32 devices in a mesh: enc: 4 (over y, core), seq: 8 (over z, x).
Axes of the slice: x: 2, y: 2, z: 4, core: 2. Of those that a mesh axis runs over, the one named last changes fastest.
Arguments:
- clip_features: bfloat16 [4, 8, 4, 16, 16, 512], P('enc', 'seq'), may hold values from -6 to 6
- clip_shape: int32 [4, 8, 3], P('enc', 'seq'), may hold values from 0 to 16, as said below
- packing: int32 [4, 8, 2, 2], P('enc', 'seq'), may hold values from -1 to 3, as said below
- conv_weight: bfloat16 [27, 16, 512], replicated, may hold values from -0.0546875 to 0.0546875
- embed_weight: bfloat16 [64, 2048], replicated, may hold values from -0.75 to 0.75
- mod_shift: float32 [2048], replicated, may hold values from -3 to 3
- mod_scale: float32 [2048], replicated, may hold values from -2 to 2
- qkv_weight: bfloat16 [3, 2048, 2048], P(None, 'seq', 'enc'), may hold values from -0.125 to 0.125
- q_gain: float32 [128], replicated, may hold values from 0.9 to 1.8
- k_gain: float32 [128], replicated, may hold values from 0.9 to 1.8
Outputs:
- attended: bfloat16 [8, 512, 2048], P('seq', 'enc')
The draws below stay inside these ranges and needn't reach their ends.
Inputs may be any that keep to these rules, and one draw needn't show every extreme that they name: `clip_shape`: Frames, height and width of each device's clip in latent pixels; height and width are even and at least 2, frames at most 4, height at most 16, width at most 16, and frames * height * width / 4 at most 256. Frames is 0 on some devices of every seq index; in every draw some device of each seq index has a clip of 4 x 16 x 16. `packing`: for each block slot: the enc index that owns it in its buffer and its block offset there, below the number of enc devices and below 1; both are -1 exactly for the slots past a clip's last token. Among the devices of one seq index no two blocks name the same owner and offset.
All inputs are finite; a program needn't handle non-finite values.
Results may differ from the reference program's by a relative error of at most 0.0075.
Values may be sent and summed in bfloat16 or wider, within the bound.
No kernel may reach another device: no remote copies, remote signals or barrier semaphores. Data moves between devices by JAX's collectives and lax.ppermute only.
A program may use at most 128 MiB of HBM per device.

```python
import jax
import jax.numpy as jnp
from jax import lax

D = 2048
HEADS = 16
HD = 128
LAT = 16
LATF = 64
FEAT = 512
BLOCK = 128
ROWS = 128
FC = 4
HC = 16
WC = 16
NBS = 2
N_ENC = 4
N_SEQ = 8


def pack_plan(key):
    half_hcap = HC // 2
    half_wcap = WC // 2
    own_blocks = ROWS // BLOCK
    slot_count = N_ENC * own_blocks
    spare_slots = slot_count - NBS
    unit_count = (N_ENC - 1) * NBS

    def column(column_key):
        key_take, key_order, key_forced, key_height, key_width, key_slots = jax.random.split(column_key, 6)
        taken_units = spare_slots - jax.random.randint(key_take, (), 0, spare_slots // 4 + 1)
        taken_units = jnp.minimum(taken_units, unit_count)
        unit_order = jax.random.permutation(key_order, unit_count)
        unit_rank = jnp.argsort(unit_order)
        chosen = (unit_rank < taken_units).astype(jnp.int32).reshape(N_ENC - 1, NBS).sum(1)
        forced = jax.random.randint(key_forced, (), 0, N_ENC)
        device_ix = jnp.arange(N_ENC)
        before = chosen[jnp.clip(device_ix, 0, N_ENC - 2)]
        shifted_up = chosen[jnp.clip(device_ix - 1, 0, N_ENC - 2)]
        block_count = jnp.where(device_ix < forced, before, jnp.where(device_ix == forced, NBS, shifted_up))
        need_tokens = (BLOCK * block_count + FC - 1) // FC
        low_h = jnp.maximum(1, (need_tokens + half_wcap - 1) // half_wcap)
        half_h = jax.random.randint(key_height, (N_ENC,), low_h, half_hcap + 1)
        low_w = jnp.maximum(1, (need_tokens + half_h - 1) // half_h)
        half_w = jax.random.randint(key_width, (N_ENC,), low_w, half_wcap + 1)
        frames = BLOCK * block_count // (half_h * half_w)
        dims = jnp.stack([frames, 2 * half_h, 2 * half_w], -1).astype(jnp.int32)
        first_rank = jnp.cumsum(block_count) - block_count
        position = first_rank[:, None] + jnp.arange(NBS)[None, :]
        is_live = jnp.arange(NBS)[None, :] < block_count[:, None]
        rest_order = jax.random.permutation(key_slots, slot_count - 1)
        slot_order = jnp.concatenate([jnp.full((1,), slot_count - 1, jnp.int32), rest_order.astype(jnp.int32)])
        slot_ix = slot_order[jnp.clip(position, 0, slot_count - 1)]
        plan_rows = jnp.stack([jnp.where(is_live, slot_ix // own_blocks, -1), jnp.where(is_live, slot_ix % own_blocks, -1)], -1)
        return (dims, plan_rows.astype(jnp.int32))
    column_keys = jax.random.split(key, N_SEQ)
    shapes, plan_all = jax.vmap(column)(column_keys)
    return (shapes.transpose(1, 0, 2), plan_all.transpose(1, 0, 2, 3))


def draw_clip_shape(key, part):
    shapes, plan_all = pack_plan(key)
    return shapes


def draw_packing(key, part):
    shapes, plan_all = pack_plan(key)
    return plan_all


def block_scale(rng, shape, cuts, smallest, largest):
    def one(dim, shards_of):
        steps = jax.random.uniform(jax.random.fold_in(jax.random.fold_in(rng, 6), dim), (shards_of,), jnp.float32, smallest / len(cuts), largest / len(cuts))
        return jnp.repeat(jnp.exp(steps), shape[dim] // shards_of).reshape((-1,) + (1,) * (len(shape) - dim - 1))

    factor_of = one(*cuts[0])
    for cut in cuts[1:]:
        factor_of = factor_of * one(*cut)
    return factor_of


def centred(key, shape, scale, bound, cuts=(), dtype=jnp.bfloat16):
    drawn = jax.random.normal(key, shape, jnp.float32) * scale
    if len(cuts) > 0:
        drawn = block_scale(key, shape, cuts, -0.22, 0.18) * drawn
    return jnp.clip(drawn, min=-bound, max=bound).astype(dtype)


def setup_inputs(seed: int = 0) -> dict:
    key_of = jax.random.split(jax.random.key(seed), 11)
    return {
        "clip_features": centred(key_of[0], (N_ENC, N_SEQ, FC, HC, WC, FEAT), 1.0, 6.0, ((0, 4), (1, 8))),
        "clip_shape": draw_clip_shape(jax.random.fold_in(key_of[10], 71), 0),
        "packing": draw_packing(jax.random.fold_in(key_of[10], 71), 0),
        "conv_weight": centred(key_of[3], (27, LAT, FEAT), (27 * FEAT) ** -0.5, 0.0546875),
        "embed_weight": centred(key_of[4], (LATF, D), LATF ** -0.5, 0.75),
        "mod_shift": centred(key_of[5], (D,), 0.5, 3.0, (), jnp.float32),
        "mod_scale": centred(key_of[6], (D,), 0.3, 2.0, (), jnp.float32),
        "qkv_weight": centred(key_of[7], (3, D, HEADS * HD), D ** -0.5, 0.125, ((1, 8), (2, 4))),
        "q_gain": jnp.clip(jax.random.uniform(key_of[8], (HD,), jnp.float32, 0.9, 1.8), 0.9, 1.8),
        "k_gain": jnp.clip(jax.random.uniform(key_of[9], (HD,), jnp.float32, 0.9, 1.8), 0.9, 1.8),
    }


eps_norm = 1e-06

def encode(features, clip_dims, conv_weight):
    frames_cap, height_cap, width_cap, feat_count = features.shape
    half_h = height_cap // 2
    half_w = width_cap // 2
    latent_ch = conv_weight.shape[1]
    frame_ix = jnp.arange(frames_cap)[:, None, None]
    row_ix = jnp.arange(height_cap)[None, :, None]
    col_ix = jnp.arange(width_cap)[None, None, :]
    inside = (frame_ix < clip_dims[0]) & (row_ix < clip_dims[1]) & (col_ix < clip_dims[2])
    masked = jnp.where(inside[..., None], features, jnp.zeros_like(features))
    padded = jnp.pad(masked, ((2, 0), (1, 1), (1, 1), (0, 0)))
    summed = jnp.zeros((latent_ch, frames_cap * height_cap * width_cap), jnp.float32)
    for tap_depth in range(3):
        for tap_row in range(3):
            for tap_col in range(3):
                shifted = padded[tap_depth:tap_depth + frames_cap, tap_row:tap_row + height_cap, tap_col:tap_col + width_cap]
                shifted = shifted.reshape(-1, feat_count)
                summed = summed + lax.dot_general(conv_weight[9 * tap_depth + 3 * tap_row + tap_col], shifted, (((1,), (1,)), ((), ())), preferred_element_type=jnp.float32)
    latent_map = summed.astype(jnp.bfloat16).reshape(latent_ch, frames_cap, half_h, 2, half_w, 2)
    patches = latent_map.transpose(0, 3, 5, 1, 2, 4).reshape(4 * latent_ch, frames_cap * half_h * half_w)
    clip_h = clip_dims[1] // 2
    clip_w = clip_dims[2] // 2
    per_frame = clip_h * clip_w
    token_ix = jnp.arange(NBS * BLOCK).astype(jnp.int32)
    frame_of = token_ix // per_frame
    within = token_ix % per_frame
    grid_ix = frame_of * (half_h * half_w) + within // clip_w * half_w + within % clip_w
    is_live = token_ix < clip_dims[0] * per_frame
    grid_ix = jnp.where(is_live, grid_ix, 0).astype(jnp.int32)
    tokens = jnp.where(is_live[None, :], jnp.take(patches, grid_ix, axis=1), jnp.zeros((), jnp.bfloat16))
    blocks = tokens.reshape(4 * latent_ch, NBS, BLOCK).transpose(1, 0, 2)
    counts = jnp.clip(clip_dims[0] * per_frame - jnp.arange(NBS).astype(jnp.int32) * BLOCK, 0, BLOCK).astype(jnp.int32)
    return (blocks, counts)

def qk_norm(projected, scale_gain, head_dim):
    per_head = projected.reshape(projected.shape[0], -1, head_dim)
    normed = per_head * lax.rsqrt(lax.optimization_barrier(jnp.mean(per_head * per_head, -1, keepdims=True)) + eps_norm) * scale_gain
    return normed.astype(jnp.bfloat16).reshape(projected.shape)

def norm_project(embedded, mod_shift, mod_scale, weights, q_gain, k_gain):
    head_dim = q_gain.shape[0]
    widened = embedded.astype(jnp.float32)
    row_mean = lax.optimization_barrier(jnp.mean(widened, -1, keepdims=True))
    centered = widened - row_mean
    row_var = lax.optimization_barrier(jnp.mean(centered * centered, -1, keepdims=True))
    normed_rows = (centered * lax.rsqrt(row_var + eps_norm) * (1.0 + mod_scale) + mod_shift).astype(jnp.bfloat16)
    query_raw = jnp.dot(normed_rows, weights[0], preferred_element_type=jnp.float32)
    key_raw = jnp.dot(normed_rows, weights[1], preferred_element_type=jnp.float32)
    value_raw = jnp.dot(normed_rows, weights[2], preferred_element_type=jnp.float32)
    return (qk_norm(query_raw, q_gain, head_dim), qk_norm(key_raw, k_gain, head_dim), value_raw.astype(jnp.bfloat16))

def reference(clip_features, clip_shape, packing, conv_weight, embed_weight, mod_shift, mod_scale, qkv_weight, q_gain, k_gain):
    head_dim = q_gain.shape[0]
    latf = embed_weight.shape[0]
    device_total = N_ENC * N_SEQ
    feats = clip_features.reshape((device_total,) + clip_features.shape[2:])
    dims_flat = clip_shape.reshape(device_total, 3)
    blocks, counts = lax.map(lambda inputs: encode(inputs[0], inputs[1], conv_weight), (feats, dims_flat))
    blocks = blocks.reshape(N_ENC, N_SEQ, NBS, latf, BLOCK).transpose(1, 0, 2, 3, 4)
    counts = counts.reshape(N_ENC, N_SEQ, NBS).transpose(1, 0, 2)
    plan_all = packing.transpose(1, 0, 2, 3)
    own_blocks = ROWS // BLOCK
    buffer_rows = N_ENC * ROWS

    def column(inputs):
        col_blocks, col_counts, col_plan = inputs
        item_count = N_ENC * NBS
        flat_blocks = col_blocks.reshape(item_count, latf, BLOCK)
        flat_counts = col_counts.reshape(item_count)
        flat_plan = col_plan.reshape(item_count, 2)
        source = (jnp.arange(item_count) // NBS).astype(jnp.int32)
        owner_ix = jnp.arange(N_ENC).astype(jnp.int32)[:, None, None]
        offset_ix = jnp.arange(own_blocks).astype(jnp.int32)[None, :, None]
        selector = (flat_plan[:, 0][None, None, :] == owner_ix) & (flat_plan[:, 1][None, None, :] == offset_ix)
        packed = jnp.einsum('eoj,jfb->eofb', selector.astype(jnp.float32), flat_blocks.astype(jnp.float32)).astype(jnp.bfloat16)
        seg_ids = lax.optimization_barrier(jnp.sum(jnp.where(selector, source[None, None, :] + 1, 0), -1))
        live_rows = lax.optimization_barrier(jnp.sum(jnp.where(selector, flat_counts[None, None, :], 0), -1))
        position = jnp.arange(BLOCK).astype(jnp.int32)[None, None, :]
        seg_rows = jnp.where(position < live_rows[..., None], seg_ids[..., None], 0).reshape(buffer_rows).astype(jnp.int32)
        row_latent = packed.transpose(0, 1, 3, 2).reshape(buffer_rows, latf)
        embedded = jnp.dot(row_latent, embed_weight, preferred_element_type=jnp.float32).astype(jnp.bfloat16)
        query_rows, key_rows, value_rows = norm_project(embedded, mod_shift, mod_scale, qkv_weight, q_gain, k_gain)
        same_seg = seg_rows[:, None] == seg_rows[None, :]

        def one_head(head_parts):
            query_head, key_head, value_head = head_parts
            scores = jnp.dot(query_head, key_head.T, preferred_element_type=jnp.float32) * head_dim ** (-0.5)
            exp_scores = jnp.where(same_seg, jnp.exp(scores), 0.0)
            attn_weights = (exp_scores / lax.optimization_barrier(jnp.sum(exp_scores, -1, keepdims=True))).astype(jnp.bfloat16)
            return jnp.dot(attn_weights, value_head, preferred_element_type=jnp.float32).astype(jnp.bfloat16)

        def split_heads(rows_in):
            return rows_in.reshape(buffer_rows, HEADS, head_dim).transpose(1, 0, 2)
        head_out = lax.map(one_head, (split_heads(query_rows), split_heads(key_rows), split_heads(value_rows)))
        return head_out.transpose(1, 0, 2).reshape(buffer_rows, HEADS * head_dim)
    return lax.map(column, (blocks, counts, plan_all))
```

```python
import functools
import math

import jax
import jax.numpy as jnp
from jax import lax
from jax.experimental import pallas as pl
from jax.experimental.pallas import tpu as pltpu
from jax.sharding import PartitionSpec as P

BLOCK = 128
NBS = 2
LANES = 128
APAD = 80
eps_norm = 1e-06
FAR = 2.0**20
VMEM_LIMIT = 48 * 1024 * 1024


def mm(a, b, dims=((1,), (0,)), precision=None):
    return lax.dot_general(a, b, (dims, ((), ())), preferred_element_type=jnp.float32, precision=precision)


def split_bf16(x):
    hi = x.astype(jnp.bfloat16)
    return hi, (x - hi.astype(jnp.float32)).astype(jnp.bfloat16)


def piece_plan(n_seq, cols):
    blocks = 3 * cols // LANES
    per = -(-blocks // n_seq)
    width = per * LANES
    assert cols % width == 0
    return width, 3 * cols // width


def fold_kernel(n_seq, embed_ref, scale_ref, shift_ref, w_ref, *outs):
    me = lax.axis_index("seq")
    _, depth, cols = w_ref.shape
    feats = embed_ref.shape[0]
    width, n_red = piece_plan(n_seq, cols)
    per_part = cols // width
    mean = jnp.sum(embed_ref[...].astype(jnp.float32), axis=1, keepdims=True) / embed_ref.shape[1]
    span = max(depth, LANES)
    chunks = span // LANES
    first = (me * depth) // LANES
    emb = embed_ref[:, pl.ds(pl.multiple_of(first * LANES, LANES), span)].astype(jnp.float32) - mean
    scale = jnp.concatenate([scale_ref[pl.ds(first + i, 1), :] for i in range(chunks)], axis=1)
    shift = jnp.concatenate([shift_ref[pl.ds(first + i, 1), :] for i in range(chunks)], axis=1)
    left = jnp.concatenate(
        [emb * (1.0 + scale), shift, jnp.zeros((APAD - feats - 1, span), jnp.float32)], axis=0
    )
    if depth < LANES:
        low = me * depth - first * LANES
        lane = lax.broadcasted_iota(jnp.int32, left.shape, 1)
        left = jnp.where((lane >= low) & (lane < low + depth), left, 0.0)
    hi, lo = split_bf16(left)
    both = jnp.concatenate([hi, lo], axis=0)
    for k in range(n_seq):
        piece = me ^ k

        @pl.when(piece < n_red)
        def _():
            part = piece // per_part
            start = pl.multiple_of((piece % per_part) * width, LANES)
            right = w_ref[part, :, pl.ds(start, width)]
            right = jnp.concatenate([right] * (span // depth), axis=0)
            total = mm(both, right)
            outs[k][...] = (total[:APAD] + total[APAD:]).astype(jnp.bfloat16)


def sum_kernel(*refs):
    total = refs[0][...].astype(jnp.float32)
    for ref in refs[1:-1]:
        total = total + ref[...].astype(jnp.float32)
    refs[-1][...] = total.astype(jnp.bfloat16)


def encode_kernel(caps, shape_ref, plan_ref, feat_ref, conv_ref, embed_ref, out_ref):
    frames_cap, height_cap, width_cap = caps
    spots = frames_cap * height_cap * width_cap
    frame_size = height_cap * width_cap
    latent_ch = conv_ref.shape[0] // 27
    feats = 4 * latent_ch
    frames, height, width = shape_ref[0, 0, 0], shape_ref[0, 0, 1], shape_ref[0, 0, 2]
    spot = lax.broadcasted_iota(jnp.int32, (1, spots), 1)
    frame_ix = spot // frame_size
    row_ix = (spot % frame_size) // width_cap
    col_ix = spot % width_cap
    inside = (frame_ix < frames) & (row_ix < height) & (col_ix < width)
    taps = mm(conv_ref[...], feat_ref[...], ((1,), (1,)))
    taps = jnp.where(inside, taps, 0.0)

    def tap(a, b, j):
        at = (9 * a + 3 * b + j) * latent_ch
        return taps[at : at + latent_ch]

    def later(x, by):
        zeros = jnp.zeros((latent_ch, by * frame_size), jnp.float32)
        return jnp.concatenate([zeros, x[:, : spots - by * frame_size]], axis=1)

    def over_frames(b, j):
        return tap(2, b, j) + later(tap(1, b, j), 1) + later(tap(0, b, j), 2)

    def over_rows(j):
        above = pltpu.roll(over_frames(0, j), width_cap, 1)
        below = pltpu.roll(over_frames(2, j), spots - width_cap, 1)
        return (
            over_frames(1, j)
            + jnp.where(row_ix >= 1, above, 0.0)
            + jnp.where(row_ix < height_cap - 1, below, 0.0)
        )

    latent = (
        over_rows(1)
        + jnp.where(col_ix >= 1, pltpu.roll(over_rows(0), 1, 1), 0.0)
        + jnp.where(col_ix < width_cap - 1, pltpu.roll(over_rows(2), spots - 1, 1), 0.0)
    )
    latent = latent.astype(jnp.bfloat16).astype(jnp.float32)
    shifted = [latent] + [pltpu.roll(latent, spots - by, 1) for by in (1, width_cap, width_cap + 1)]
    patches = jnp.concatenate(shifted, axis=0).astype(jnp.bfloat16)

    tokens = NBS * BLOCK
    half_w = (width // 2).astype(jnp.float32)
    per_frame_int = (height // 2) * (width // 2)
    per_frame = per_frame_int.astype(jnp.float32)
    live = frames * per_frame_int
    token_int = lax.broadcasted_iota(jnp.int32, (1, tokens), 1)
    token = token_int.astype(jnp.float32)
    frame_of = jnp.floor((token + 0.5) / jnp.full((1, tokens), per_frame))
    within = token - frame_of * per_frame
    row_of = jnp.floor((within + 0.5) / jnp.full((1, tokens), half_w))
    col_of = within - row_of * half_w
    source = (frame_of * frame_size + row_of * (2 * width_cap) + col_of * 2).astype(jnp.int32)
    source = jnp.where(token_int < live, source, -1)
    chosen = lax.broadcasted_iota(jnp.int32, (spots, tokens), 0) == source
    picked = mm(patches, jnp.where(chosen, 1.0, 0.0).astype(jnp.bfloat16))
    at = lax.broadcasted_iota(jnp.int32, (feats, feats), 0)
    frm = lax.broadcasted_iota(jnp.int32, (feats, feats), 1)
    order = jnp.where(frm == (at % 4) * latent_ch + at // 4, 1.0, 0.0).astype(jnp.bfloat16)
    picked = mm(order, picked.astype(jnp.bfloat16))

    emb = embed_ref[...].astype(jnp.float32)
    emb = emb - jnp.sum(emb, axis=1, keepdims=True) / emb.shape[1]
    gram = mm(emb, emb, ((1,), (1,)), lax.Precision.HIGHEST) / emb.shape[1]
    spread = mm(gram, picked, precision=lax.Precision.HIGHEST)
    variance = jnp.maximum(jnp.sum(spread * picked, axis=0, keepdims=True), 0.0)
    out_ref[:feats] = (picked * lax.rsqrt(variance + eps_norm)).astype(jnp.bfloat16)

    kind = lax.broadcasted_iota(jnp.int32, (APAD - feats, BLOCK), 0)
    for b in range(NBS):
        count = jnp.clip(live - b * BLOCK, 0, BLOCK)
        info = jnp.where(
            kind == 0,
            plan_ref[0, 0, b, 0],
            jnp.where(kind == 1, plan_ref[0, 0, b, 1], jnp.where(kind == 2, count, 0)),
        )
        out_ref[feats:, b * BLOCK : (b + 1) * BLOCK] = info.astype(jnp.float32).astype(jnp.bfloat16)


def attend_kernel(n_enc, n_seq, cols, *refs):
    blocks = refs[:n_enc]
    pieces = refs[n_enc : n_enc + n_seq]
    q_gain_ref, k_gain_ref = refs[n_enc + n_seq : n_enc + n_seq + 2]
    outs = refs[n_enc + n_seq + 2 : 2 * n_enc + n_seq + 2]
    fold_s, rows_t, keys_t, values, q_mask = refs[2 * n_enc + n_seq + 2 :]
    mine = lax.axis_index("enc")
    place = lax.axis_index("seq")
    width, n_red = piece_plan(n_seq, cols)
    per_part = cols // width
    rows = n_enc * BLOCK
    feats = blocks[0].shape[0] - (APAD - 64)
    head_dim = q_gain_ref.shape[1]
    for k in range(n_seq):
        piece = place ^ k

        @pl.when(piece < n_red)
        def _():
            fold_s[piece] = pieces[k][...]

    lane = lax.broadcasted_iota(jnp.int32, (1, BLOCK), 1).astype(jnp.float32)
    extra = lax.broadcasted_iota(jnp.int32, (APAD - feats, BLOCK), 0)
    found = []
    for k in range(n_enc):
        source = mine ^ k
        for b in range(NBS):
            tile = blocks[k][:, b * BLOCK : (b + 1) * BLOCK].astype(jnp.float32)
            owner, offset, count = tile[feats : feats + 1], tile[feats + 1 : feats + 2], tile[feats + 2 : feats + 3]
            owner = jnp.where(offset == 0.0, owner, -1.0)
            segment = jnp.where(lane < count, (source + 1).astype(jnp.float32), 0.0)
            found.append((owner, segment, tile[:feats]))
    for o in range(n_enc):
        segment = jnp.zeros((1, BLOCK), jnp.float32)
        body = jnp.zeros((feats, BLOCK), jnp.float32)
        for owner, seg_of, tile in found:
            hit = owner == float(o)
            segment = segment + jnp.where(hit, seg_of, 0.0)
            body = body + jnp.where(hit, tile, 0.0)
        tail = jnp.where(extra == 0, 1.0, jnp.where(extra == 1, segment, 0.0))
        rows_t[:, o * BLOCK : (o + 1) * BLOCK] = jnp.concatenate(
            [body, tail, jnp.zeros((LANES - APAD, BLOCK), jnp.float32)], axis=0
        )
    x_t = rows_t[...]
    x_rows = x_t.T
    seg_col = x_rows[:, feats + 1 : feats + 2]
    seg_row = x_t[feats + 1 : feats + 2]
    group = lax.broadcasted_iota(jnp.int32, (rows, LANES), 1).astype(jnp.float32)
    q_mask[...] = jnp.where(seg_col == group, -FAR, 0.0).astype(jnp.bfloat16)
    group_t = lax.broadcasted_iota(jnp.int32, (LANES, rows), 0).astype(jnp.float32)
    keys_t[head_dim:] = jnp.where(seg_row == group_t, 0.0, 1.0).astype(jnp.bfloat16)
    values[:, head_dim:] = jnp.ones((rows, LANES), jnp.bfloat16)
    x_t = x_t[:APAD].astype(jnp.bfloat16)
    x_rows = x_rows[:, :APAD].astype(jnp.bfloat16)
    gain = q_gain_ref[...] * k_gain_ref[...] * (head_dim**-0.5 * math.log2(math.e))

    def folded(part, head):
        at = part * cols + head * head_dim
        return fold_s[at // width][:, at % width : at % width + head_dim]

    for head in range(cols // head_dim):
        key = mm(folded(1, head), x_t, ((0,), (0,)))
        square = jnp.sum(key * key, axis=0, keepdims=True) / head_dim
        keys_t[:head_dim] = (key * lax.rsqrt(square + eps_norm)).astype(jnp.bfloat16)
        values[:, :head_dim] = mm(x_rows, folded(2, head)).astype(jnp.bfloat16)
        query = mm(x_rows, folded(0, head))
        square = jnp.sum(query * query, axis=1, keepdims=True) / head_dim
        query = (query * lax.rsqrt(square + eps_norm) * gain).astype(jnp.bfloat16)
        query = jnp.concatenate([query, q_mask[...]], axis=1)
        for o in range(n_enc):
            scores = mm(query[o * BLOCK : (o + 1) * BLOCK], keys_t[...])
            weight = jnp.exp2(scores).astype(jnp.bfloat16)
            mixed = mm(weight, values[...])
            result = (mixed[:, :head_dim] / mixed[:, head_dim:]).astype(jnp.bfloat16)
            for_k = mine ^ o
            for k in range(n_enc):

                @pl.when(for_k == k)
                def _():
                    outs[k][:, head * head_dim : (head + 1) * head_dim] = result


def join_kernel(n_enc, *refs):
    mine = lax.axis_index("enc")
    cols = refs[0].shape[1]
    for k in range(n_enc):
        start = pl.multiple_of((mine ^ k) * cols, LANES)
        refs[-1][0, :, pl.ds(start, cols)] = refs[k][...]


def vmem(count):
    return [pl.BlockSpec(memory_space=pltpu.VMEM)] * count


def call(kernel, ins, outs, out_shape, scratch=(), cost=(1_000_000, 1_000_000)):
    return pl.pallas_call(
        kernel,
        in_specs=ins,
        out_specs=outs,
        out_shape=out_shape,
        scratch_shapes=list(scratch),
        compiler_params=pltpu.CompilerParams(vmem_limit_bytes=VMEM_LIMIT),
        cost_estimate=pl.CostEstimate(flops=cost[0], bytes_accessed=cost[1], transcendentals=0),
    )


def exchange(x, axis, n, k):
    return lax.ppermute(x, axis, [(i, i ^ k) for i in range(n)])


def on_device(
    n_enc,
    n_seq,
    clip_features,
    clip_shape,
    packing,
    conv_weight,
    embed_weight,
    mod_shift,
    mod_scale,
    qkv_weight,
    q_gain,
    k_gain,
):
    caps = clip_features.shape[2:5]
    depth_all = clip_features.shape[5]
    cols = qkv_weight.shape[2]
    head_dim = q_gain.shape[0]
    width, n_red = piece_plan(n_seq, cols)
    smem = pl.BlockSpec(memory_space=pltpu.SMEM)
    bf16 = jnp.bfloat16

    piece_shape = jax.ShapeDtypeStruct((APAD, width), bf16)
    with jax.named_scope("fold"):
        partials = call(
            functools.partial(fold_kernel, n_seq), vmem(4), vmem(n_seq), [piece_shape] * n_seq
        )(embed_weight, mod_scale.reshape(-1, LANES), mod_shift.reshape(-1, LANES), qkv_weight)
    with jax.named_scope("fold_sum"):
        arrived = [partials[0]] + [
            lax.ppermute(partials[k], "seq", [(i, i ^ k) for i in range(n_seq) if i ^ k < n_red])
            for k in range(1, n_seq)
        ]

    with jax.named_scope("encode"):
        own = call(
            functools.partial(encode_kernel, caps),
            [smem, smem] + vmem(3),
            vmem(1)[0],
            jax.ShapeDtypeStruct((APAD, NBS * BLOCK), bf16),
            cost=(500_000_000, 2_000_000),
        )(
            clip_shape,
            packing,
            clip_features.reshape(-1, depth_all),
            conv_weight.reshape(-1, depth_all),
            embed_weight,
        )
        blocks = [own] + [exchange(own, "enc", n_enc, k) for k in range(1, n_enc)]

    with jax.named_scope("fold_sum"):
        summed = call(sum_kernel, vmem(n_seq), vmem(1)[0], piece_shape)(*arrived)
        pieces = [summed] + [
            lax.ppermute(summed, "seq", [(i, i ^ k) for i in range(n_seq) if i < n_red])
            for k in range(1, n_seq)
        ]

    rows = n_enc * BLOCK
    with jax.named_scope("attend"):
        parts = call(
            functools.partial(attend_kernel, n_enc, n_seq, cols),
            vmem(n_enc + n_seq + 2),
            vmem(n_enc),
            [jax.ShapeDtypeStruct((BLOCK, cols), bf16)] * n_enc,
            [
                pltpu.VMEM((n_red, APAD, width), bf16),
                pltpu.VMEM((LANES, rows), jnp.float32),
                pltpu.VMEM((head_dim + LANES, rows), bf16),
                pltpu.VMEM((rows, head_dim + LANES), bf16),
                pltpu.VMEM((rows, LANES), bf16),
            ],
            cost=(4_000_000_000, 3_000_000),
        )(*blocks, *pieces, q_gain.reshape(1, -1), k_gain.reshape(1, -1))
    with jax.named_scope("output"):
        got = [parts[0]] + [exchange(parts[k], "enc", n_enc, k) for k in range(1, n_enc)]
        return call(
            functools.partial(join_kernel, n_enc),
            vmem(n_enc),
            vmem(1)[0],
            jax.ShapeDtypeStruct((1, BLOCK, n_enc * cols), bf16),
        )(*got)


def solution(mesh):
    return jax.shard_map(
        functools.partial(on_device, mesh.shape["enc"], mesh.shape["seq"]),
        mesh=mesh,
        in_specs=(
            P("enc", "seq", None, None, None, None),
            P("enc", "seq", None),
            P("enc", "seq", None, None),
            P(),
            P(),
            P(),
            P(),
            P(None, "seq", "enc"),
            P(),
            P(),
        ),
        out_specs=P("seq", "enc", None),
        check_vma=False,
    )
```

```python
import functools
import math

import jax
import jax.numpy as jnp
from jax import lax
from jax.experimental import pallas as pl
from jax.experimental.pallas import tpu as pltpu
from jax.sharding import PartitionSpec as P

BLOCK = 128
NBS = 2
LANES = 128
APAD = 80
eps_norm = 1e-06
FAR = 2.0**20
VMEM_LIMIT = 48 * 1024 * 1024


def mm(a, b, dims=((1,), (0,)), precision=None):
    return lax.dot_general(a, b, (dims, ((), ())), preferred_element_type=jnp.float32, precision=precision)


def split_bf16(x):
    hi = x.astype(jnp.bfloat16)
    return hi, (x - hi.astype(jnp.float32)).astype(jnp.bfloat16)


def log2(n):
    bits = n.bit_length() - 1
    assert 1 << bits == n
    return bits


def bit_of(index, bit):
    return (index >> bit) & 1


def fetch(pairs, sems):
    copies = [pltpu.make_async_copy(src, dst, sems.at[i]) for i, (src, dst) in enumerate(pairs)]
    for copy in copies:
        copy.start()
    return copies


def fold_kernel(embed_hbm, scale_hbm, shift_hbm, w_hbm, keep_ref, send_ref, embed_ref, scale_ref, shift_ref, w_ref, sems):
    copies = fetch(
        [(embed_hbm, embed_ref), (scale_hbm, scale_ref), (shift_hbm, shift_ref), (w_hbm, w_ref)], sems
    )
    me = lax.axis_index("seq")
    _, depth, cols = w_ref.shape
    feats = embed_ref.shape[0]
    heads = cols // LANES
    for copy in copies[:3]:
        copy.wait()
    mean = jnp.sum(embed_ref[...].astype(jnp.float32), axis=1, keepdims=True) / embed_ref.shape[1]
    span = max(depth, LANES)
    chunks = span // LANES
    first = (me * depth) // LANES
    emb = embed_ref[:, pl.ds(pl.multiple_of(first * LANES, LANES), span)].astype(jnp.float32) - mean
    scale = jnp.concatenate([scale_ref[pl.ds(first + i, 1), :] for i in range(chunks)], axis=1)
    shift = jnp.concatenate([shift_ref[pl.ds(first + i, 1), :] for i in range(chunks)], axis=1)
    left = jnp.concatenate(
        [emb * (1.0 + scale), shift, jnp.zeros((APAD - feats - 1, span), jnp.float32)], axis=0
    )
    if depth < LANES:
        low = me * depth - first * LANES
        lane = lax.broadcasted_iota(jnp.int32, left.shape, 1)
        left = jnp.where((lane >= low) & (lane < low + depth), left, 0.0)
    hi, lo = split_bf16(left)
    both = jnp.concatenate([hi, lo], axis=0)
    copies[3].wait()

    def product(head):
        start = pl.multiple_of(head * LANES, LANES)
        right = jnp.concatenate([w_ref[part, :, pl.ds(start, LANES)] for part in range(3)], axis=1)
        right = jnp.concatenate([right] * (span // depth), axis=0)
        total = mm(both, right)
        return total[:APAD] + total[APAD:]

    if heads > 1:
        half = heads // 2
        mine = bit_of(me, 0) * half
        for i in range(half):
            send_ref[i] = product(half - mine + i).astype(jnp.bfloat16)
        for i in range(half):
            keep_ref[i] = product(mine + i)
    else:
        total = product(0)
        keep_ref[0] = total
        send_ref[0] = total.astype(jnp.bfloat16)


def add_kernel(bit, keep_in, got_ref, first_ref, *outs):
    count = keep_in.shape[0]
    if bit is None:
        outs[0][...] = (keep_in[...] + got_ref[...].astype(jnp.float32)).astype(jnp.bfloat16)
        return
    keep_ref, send_ref = outs
    if count == 1:
        total = keep_in[...] + got_ref[...].astype(jnp.float32)
        keep_ref[...] = total
        send_ref[...] = total.astype(jnp.bfloat16)
        return
    half = count // 2
    mine = bit_of(lax.axis_index("seq"), bit) * half
    for i in range(half):
        away = half - mine + i
        send_ref[i] = (keep_in[away] + got_ref[away].astype(jnp.float32)).astype(jnp.bfloat16)
        keep_ref[i] = keep_in[mine + i] + got_ref[mine + i].astype(jnp.float32)


def stack_kernel(first_ref, *refs):
    at = 0
    for ref in refs[:-1]:
        refs[-1][at : at + ref.shape[0]] = ref[...]
        at += ref.shape[0]


def encode_kernel(caps, shape_hbm, plan_hbm, feat_hbm, conv_hbm, embed_hbm, first_ref, out_ref, shape_ref, plan_ref, feat_ref, conv_ref, embed_ref, sems):
    copies = fetch(
        [
            (conv_hbm, conv_ref),
            (feat_hbm, feat_ref),
            (embed_hbm, embed_ref),
            (shape_hbm, shape_ref),
            (plan_hbm, plan_ref),
        ],
        sems,
    )
    frames_cap, height_cap, width_cap = caps
    spots = frames_cap * height_cap * width_cap
    frame_size = height_cap * width_cap
    latent_ch = conv_ref.shape[0] // 27
    feats = 4 * latent_ch
    copies[3].wait()
    copies[4].wait()
    frames, height, width = shape_ref[0, 0, 0], shape_ref[0, 0, 1], shape_ref[0, 0, 2]
    spot = lax.broadcasted_iota(jnp.int32, (1, spots), 1)
    frame_ix = spot // frame_size
    row_ix = (spot % frame_size) // width_cap
    col_ix = spot % width_cap
    inside = (frame_ix < frames) & (row_ix < height) & (col_ix < width)
    copies[0].wait()
    copies[1].wait()
    taps = mm(conv_ref[...], feat_ref[...], ((1,), (1,)))
    taps = jnp.where(inside, taps, 0.0)

    def tap(a, b, j):
        at = (9 * a + 3 * b + j) * latent_ch
        return taps[at : at + latent_ch]

    def later(x, by):
        zeros = jnp.zeros((latent_ch, by * frame_size), jnp.float32)
        return jnp.concatenate([zeros, x[:, : spots - by * frame_size]], axis=1)

    def over_frames(b, j):
        return tap(2, b, j) + later(tap(1, b, j), 1) + later(tap(0, b, j), 2)

    def over_rows(j):
        above = pltpu.roll(over_frames(0, j), width_cap, 1)
        below = pltpu.roll(over_frames(2, j), spots - width_cap, 1)
        return (
            over_frames(1, j)
            + jnp.where(row_ix >= 1, above, 0.0)
            + jnp.where(row_ix < height_cap - 1, below, 0.0)
        )

    latent = (
        over_rows(1)
        + jnp.where(col_ix >= 1, pltpu.roll(over_rows(0), 1, 1), 0.0)
        + jnp.where(col_ix < width_cap - 1, pltpu.roll(over_rows(2), spots - 1, 1), 0.0)
    )
    latent = latent.astype(jnp.bfloat16).astype(jnp.float32)
    shifted = [latent] + [pltpu.roll(latent, spots - by, 1) for by in (1, width_cap, width_cap + 1)]
    patches = jnp.concatenate(shifted, axis=0).astype(jnp.bfloat16)

    tokens = NBS * BLOCK
    half_w = (width // 2).astype(jnp.float32)
    per_frame_int = (height // 2) * (width // 2)
    per_frame = per_frame_int.astype(jnp.float32)
    live = frames * per_frame_int
    token_int = lax.broadcasted_iota(jnp.int32, (1, tokens), 1)
    token = token_int.astype(jnp.float32)
    frame_of = jnp.floor((token + 0.5) / jnp.full((1, tokens), per_frame))
    within = token - frame_of * per_frame
    row_of = jnp.floor((within + 0.5) / jnp.full((1, tokens), half_w))
    col_of = within - row_of * half_w
    source = (frame_of * frame_size + row_of * (2 * width_cap) + col_of * 2).astype(jnp.int32)
    source = jnp.where(token_int < live, source, -1)
    chosen = lax.broadcasted_iota(jnp.int32, (spots, tokens), 0) == source
    picked = mm(patches, jnp.where(chosen, 1.0, 0.0).astype(jnp.bfloat16))
    at = lax.broadcasted_iota(jnp.int32, (feats, feats), 0)
    frm = lax.broadcasted_iota(jnp.int32, (feats, feats), 1)
    order = jnp.where(frm == (at % 4) * latent_ch + at // 4, 1.0, 0.0).astype(jnp.bfloat16)
    picked = mm(order, picked.astype(jnp.bfloat16))

    copies[2].wait()
    emb = embed_ref[...].astype(jnp.float32)
    emb = emb - jnp.sum(emb, axis=1, keepdims=True) / emb.shape[1]
    gram = mm(emb, emb, ((1,), (1,)), lax.Precision.HIGHEST) / emb.shape[1]
    spread = mm(gram, picked, precision=lax.Precision.HIGHEST)
    variance = jnp.maximum(jnp.sum(spread * picked, axis=0, keepdims=True), 0.0)
    out_ref[:feats] = (picked * lax.rsqrt(variance + eps_norm)).astype(jnp.bfloat16)

    kind = lax.broadcasted_iota(jnp.int32, (APAD - feats, BLOCK), 0)
    for b in range(NBS):
        count = jnp.clip(live - b * BLOCK, 0, BLOCK)
        info = jnp.where(
            kind == 0,
            plan_ref[0, 0, b, 0],
            jnp.where(kind == 1, plan_ref[0, 0, b, 1], jnp.where(kind == 2, count, 0)),
        )
        out_ref[feats:, b * BLOCK : (b + 1) * BLOCK] = info.astype(jnp.float32).astype(jnp.bfloat16)


def pack_kernel(n_enc, feats, q_gain_hbm, k_gain_hbm, *refs):
    blocks = refs[:n_enc]
    x_t_ref, x_ref, own_ref, key_mask_ref, own_mask_ref, gain_ref, rows_t, q_gain_ref, k_gain_ref, sems = refs[n_enc:]
    copies = fetch([(q_gain_hbm, q_gain_ref), (k_gain_hbm, k_gain_ref)], sems)
    mine = lax.axis_index("enc")
    rows = n_enc * BLOCK
    lane = lax.broadcasted_iota(jnp.int32, (1, BLOCK), 1).astype(jnp.float32)
    extra = lax.broadcasted_iota(jnp.int32, (APAD - feats, BLOCK), 0)
    found = []
    for k in range(n_enc):
        source = mine ^ k
        for b in range(NBS):
            tile = blocks[k][:, b * BLOCK : (b + 1) * BLOCK].astype(jnp.float32)
            owner, offset, count = (tile[feats + i : feats + i + 1] for i in range(3))
            owner = jnp.where(offset == 0.0, owner, -1.0)
            segment = jnp.where(lane < count, (source + 1).astype(jnp.float32), 0.0)
            found.append((owner, segment, tile[:feats]))
    for o in range(n_enc):
        segment = jnp.zeros((1, BLOCK), jnp.float32)
        body = jnp.zeros((feats, BLOCK), jnp.float32)
        for owner, seg_of, tile in found:
            hit = owner == float(o)
            segment = segment + jnp.where(hit, seg_of, 0.0)
            body = body + jnp.where(hit, tile, 0.0)
        tail = jnp.where(extra == 0, 1.0, jnp.where(extra == 1, segment, 0.0))
        rows_t[:, o * BLOCK : (o + 1) * BLOCK] = jnp.concatenate(
            [body, tail, jnp.zeros((LANES - APAD, BLOCK), jnp.float32)], axis=0
        )
    x_t = rows_t[...]
    x_t_ref[...] = x_t[:APAD].astype(jnp.bfloat16)
    x_ref[...] = x_t.T.astype(jnp.bfloat16)
    group_t = lax.broadcasted_iota(jnp.int32, (LANES, rows), 0).astype(jnp.float32)
    key_mask_ref[...] = jnp.where(x_t[feats + 1 : feats + 2] == group_t, 0.0, 1.0).astype(jnp.bfloat16)
    own = rows_t[:, pl.ds(pl.multiple_of(mine * BLOCK, BLOCK), BLOCK)].T
    own_ref[...] = own.astype(jnp.bfloat16)
    group = lax.broadcasted_iota(jnp.int32, (BLOCK, LANES), 1).astype(jnp.float32)
    own_mask_ref[...] = jnp.where(own[:, feats + 1 : feats + 2] == group, -FAR, 0.0).astype(jnp.bfloat16)
    head_dim = q_gain_ref.shape[1]
    copies[0].wait()
    copies[1].wait()
    gain_ref[...] = q_gain_ref[...] * k_gain_ref[...] * (head_dim**-0.5 * math.log2(math.e))


def attend_head(fold, x_t, x_rows, own, key_mask, own_mask, gain):
    head_dim = LANES
    key = mm(fold[:, head_dim : 2 * head_dim], x_t, ((0,), (0,)))
    square = jnp.sum(key * key, axis=0, keepdims=True) / head_dim
    key = (key * lax.rsqrt(square + eps_norm)).astype(jnp.bfloat16)
    query = mm(own, fold[:, :head_dim])
    square = jnp.sum(query * query, axis=1, keepdims=True) / head_dim
    query = (query * lax.rsqrt(square + eps_norm) * gain).astype(jnp.bfloat16)
    scores = mm(jnp.concatenate([query, own_mask], axis=1), jnp.concatenate([key, key_mask], axis=0))
    weight = jnp.exp2(scores).astype(jnp.bfloat16)
    value = mm(x_rows, fold[:, 2 * head_dim :]).astype(jnp.bfloat16)
    value = jnp.concatenate([value, jnp.ones(value.shape, jnp.bfloat16)], axis=1)
    mixed = mm(weight, value)
    return (mixed[:, :head_dim] / mixed[:, head_dim:]).astype(jnp.bfloat16)


def attend_kernel(x_t_ref, x_ref, own_ref, key_mask_ref, own_mask_ref, gain_ref, *refs):
    folds, out_ref = refs[:-1], refs[-1]
    x_t, key_mask, own_mask, gain = x_t_ref[...], key_mask_ref[...], own_mask_ref[...], gain_ref[...]
    x_rows, own = x_ref[:, :APAD], own_ref[:, :APAD]
    at = 0
    for ref in folds:
        for i in range(ref.shape[0]):
            out_ref[:, at * LANES : (at + 1) * LANES] = attend_head(
                ref[i], x_t, x_rows, own, key_mask, own_mask, gain
            )
            at += 1


def last_kernel(seq_bits, enc_bits, early, *refs):
    x_t_ref, x_ref, own_ref, key_mask_ref, own_mask_ref, gain_ref = refs[:6]
    done = refs[6 : 6 + early]
    folds, out_ref = refs[6 + early : -1], refs[-1]
    x_t, key_mask, own_mask, gain = x_t_ref[...], key_mask_ref[...], own_mask_ref[...], gain_ref[...]
    x_rows, own = x_ref[:, :APAD], own_ref[:, :APAD]
    mine, place = lax.axis_index("enc"), lax.axis_index("seq")
    slot = 0
    for step in range(seq_bits):
        slot = slot + (bit_of(place, step) << (seq_bits - 1 - step))

    def column(at):
        flip = 0
        for t in range(enc_bits):
            flip += bit_of(at, seq_bits + t) << (enc_bits - 1 - t)
        head = ((mine ^ flip) << seq_bits) + (slot ^ (at & ((1 << seq_bits) - 1)))
        return pl.ds(pl.multiple_of(head * LANES, LANES), LANES)

    at = 0
    for ref in done:
        for i in range(ref.shape[1] // LANES):
            out_ref[0, :, column(at)] = ref[:, i * LANES : (i + 1) * LANES]
            at += 1
    for ref in folds:
        for i in range(ref.shape[0]):
            out_ref[0, :, column(at)] = attend_head(ref[i], x_t, x_rows, own, key_mask, own_mask, gain)
            at += 1


def vmem(count):
    return [pl.BlockSpec(memory_space=pltpu.VMEM)] * count


def hbm(count):
    return [pl.BlockSpec(memory_space=pltpu.HBM)] * count


def after(count):
    return [pl.BlockSpec(memory_space=pl.ANY)] * count


def call(kernel, ins, out_shape, scratch=(), cost=(1_000_000, 1_000_000)):
    return pl.pallas_call(
        kernel,
        in_specs=ins,
        out_specs=[pl.BlockSpec(memory_space=pltpu.VMEM)] * len(out_shape),
        out_shape=out_shape,
        scratch_shapes=list(scratch),
        compiler_params=pltpu.CompilerParams(vmem_limit_bytes=VMEM_LIMIT),
        cost_estimate=pl.CostEstimate(flops=cost[0], bytes_accessed=cost[1], transcendentals=0),
    )


def exchange(x, axis, n, bit):
    return lax.ppermute(x, axis, [(i, i ^ (1 << bit)) for i in range(n)])


def on_device(
    n_enc,
    n_seq,
    clip_features,
    clip_shape,
    packing,
    conv_weight,
    embed_weight,
    mod_shift,
    mod_scale,
    qkv_weight,
    q_gain,
    k_gain,
):
    caps = clip_features.shape[2:5]
    depth_all = clip_features.shape[5]
    cols = qkv_weight.shape[2]
    feats = embed_weight.shape[0]
    heads = cols // LANES
    seq_bits, enc_bits = log2(heads), log2(n_enc)
    rows = n_enc * BLOCK
    bf16, f32 = jnp.bfloat16, jnp.float32

    def folds(count, dtype):
        return jax.ShapeDtypeStruct((count, APAD, 3 * LANES), dtype)

    count = max(heads // 2, 1)
    scale_rows, shift_rows = mod_scale.reshape(-1, LANES), mod_shift.reshape(-1, LANES)
    with jax.named_scope("fold"):
        keep, send = call(
            fold_kernel,
            hbm(4),
            [folds(count, f32), folds(count, bf16)],
            [
                pltpu.VMEM(embed_weight.shape, bf16),
                pltpu.VMEM(scale_rows.shape, f32),
                pltpu.VMEM(shift_rows.shape, f32),
                pltpu.VMEM(qkv_weight.shape, bf16),
                pltpu.SemaphoreType.DMA((4,)),
            ],
            cost=(200_000_000, 1_000_000),
        )(embed_weight, scale_rows, shift_rows, qkv_weight)

    with jax.named_scope("encode"):
        features = clip_features.reshape(-1, depth_all)
        conv = conv_weight.reshape(-1, depth_all)
        own_block = call(
            functools.partial(encode_kernel, caps),
            hbm(5) + after(1),
            [jax.ShapeDtypeStruct((APAD, NBS * BLOCK), bf16)],
            [
                pltpu.SMEM(clip_shape.shape, jnp.int32),
                pltpu.SMEM(packing.shape, jnp.int32),
                pltpu.VMEM(features.shape, bf16),
                pltpu.VMEM(conv.shape, bf16),
                pltpu.VMEM(embed_weight.shape, bf16),
                pltpu.SemaphoreType.DMA((5,)),
            ],
            cost=(500_000_000, 2_000_000),
        )(clip_shape, packing, features, conv, embed_weight, keep)[0]

    with jax.named_scope("pack"):
        blocks = [own_block] + [
            lax.ppermute(own_block, "enc", [(i, i ^ k) for i in range(n_enc)]) for k in range(1, n_enc)
        ]
        packed = call(
            functools.partial(pack_kernel, n_enc, feats),
            hbm(2) + vmem(n_enc),
            [
                jax.ShapeDtypeStruct((APAD, rows), bf16),
                jax.ShapeDtypeStruct((rows, LANES), bf16),
                jax.ShapeDtypeStruct((BLOCK, LANES), bf16),
                jax.ShapeDtypeStruct((LANES, rows), bf16),
                jax.ShapeDtypeStruct((BLOCK, LANES), bf16),
                jax.ShapeDtypeStruct((1, LANES), f32),
            ],
            [
                pltpu.VMEM((LANES, rows), f32),
                pltpu.VMEM((1, LANES), f32),
                pltpu.VMEM((1, LANES), f32),
                pltpu.SemaphoreType.DMA((2,)),
            ],
        )(q_gain.reshape(1, -1), k_gain.reshape(1, -1), *blocks)

    with jax.named_scope("fold_sum"):
        for bit in range(log2(n_seq)):
            got = exchange(send, "seq", n_seq, bit)
            first = own_block if bit == 0 else packed[0]
            specs = vmem(2) + after(1)
            if bit + 1 == log2(n_seq):
                (have,) = call(functools.partial(add_kernel, None), specs, [folds(1, bf16)])(keep, got, first)
            else:
                count = max(count // 2, 1)
                keep, send = call(
                    functools.partial(add_kernel, bit + 1), specs, [folds(count, f32), folds(count, bf16)]
                )(keep, got, first)

    def stack(parts, first):
        total = sum(part.shape[0] for part in parts)
        return call(stack_kernel, after(1) + vmem(len(parts)), [folds(total, bf16)])(first, *parts)[0]

    with jax.named_scope("gather"):
        for bit in reversed(range(seq_bits)):
            have = stack([have, exchange(have, "seq", n_seq, bit)], packed[0])
    done = []
    with jax.named_scope("attend"):
        fresh = have
        for bit in reversed(range(enc_bits)):
            got = exchange(have, "enc", n_enc, bit)
            count = fresh.shape[0]
            done += call(
                attend_kernel,
                vmem(7),
                [jax.ShapeDtypeStruct((BLOCK, count * LANES), bf16)],
                cost=(count * 200_000_000, 1_000_000),
            )(*packed, fresh)
            if bit > 0:
                have = stack([have, got], done[-1])
            fresh = got
        return call(
            functools.partial(last_kernel, seq_bits, enc_bits, len(done)),
            vmem(7 + len(done)),
            [jax.ShapeDtypeStruct((1, BLOCK, n_enc * cols), bf16)],
            cost=(1_600_000_000, 2_000_000),
        )(*packed, *done, fresh)[0]


def solution(mesh):
    return jax.shard_map(
        functools.partial(on_device, mesh.shape["enc"], mesh.shape["seq"]),
        mesh=mesh,
        in_specs=(
            P("enc", "seq", None, None, None, None),
            P("enc", "seq", None),
            P("enc", "seq", None, None),
            P(),
            P(),
            P(),
            P(),
            P(None, "seq", "enc"),
            P(),
            P(),
        ),
        out_specs=P("seq", "enc", None),
        check_vma=False,
    )
```

```python
import functools
import math

import jax
import jax.numpy as jnp
from jax import lax
from jax.experimental import pallas as pl
from jax.experimental.pallas import tpu as pltpu
from jax.sharding import PartitionSpec as P

BLOCK = 128
NBS = 2
LANES = 128
APAD = 80
eps_norm = 1e-06
FAR = 2.0**20
VMEM_LIMIT = 48 * 1024 * 1024


def mm(a, b, dims=((1,), (0,)), precision=None):
    return lax.dot_general(a, b, (dims, ((), ())), preferred_element_type=jnp.float32, precision=precision)


def split_bf16(x):
    hi = x.astype(jnp.bfloat16)
    return hi, (x - hi.astype(jnp.float32)).astype(jnp.bfloat16)


def log2(n):
    bits = n.bit_length() - 1
    assert 1 << bits == n
    return bits


def fetch(pairs, sems):
    copies = [pltpu.make_async_copy(src, dst, sems.at[i]) for i, (src, dst) in enumerate(pairs)]
    for copy in copies:
        copy.start()
    return copies


def fold_kernel(embed_hbm, scale_hbm, shift_hbm, w_hbm, keep_ref, *refs):
    sends = refs[:-5]
    embed_ref, scale_ref, shift_ref, w_ref, sems = refs[-5:]
    copies = fetch(
        [(embed_hbm, embed_ref), (scale_hbm, scale_ref), (shift_hbm, shift_ref), (w_hbm, w_ref)], sems
    )
    me = lax.axis_index("seq")
    _, depth, cols = w_ref.shape
    feats = embed_ref.shape[0]
    heads = cols // LANES
    for copy in copies[:3]:
        copy.wait()
    mean = jnp.sum(embed_ref[...].astype(jnp.float32), axis=1, keepdims=True) / embed_ref.shape[1]
    span = max(depth, LANES)
    chunks = span // LANES
    first = (me * depth) // LANES
    emb = embed_ref[:, pl.ds(pl.multiple_of(first * LANES, LANES), span)].astype(jnp.float32) - mean
    scale = jnp.concatenate([scale_ref[pl.ds(first + i, 1), :] for i in range(chunks)], axis=1)
    shift = jnp.concatenate([shift_ref[pl.ds(first + i, 1), :] for i in range(chunks)], axis=1)
    left = jnp.concatenate(
        [emb * (1.0 + scale), shift, jnp.zeros((APAD - feats - 1, span), jnp.float32)], axis=0
    )
    if depth < LANES:
        low = me * depth - first * LANES
        lane = lax.broadcasted_iota(jnp.int32, left.shape, 1)
        left = jnp.where((lane >= low) & (lane < low + depth), left, 0.0)
    hi, lo = split_bf16(left)
    both = jnp.concatenate([hi, lo], axis=0)
    copies[3].wait()

    def product(head):
        start = pl.multiple_of(head * LANES, LANES)
        right = jnp.concatenate([w_ref[part, :, pl.ds(start, LANES)] for part in range(3)], axis=1)
        right = jnp.concatenate([right] * (span // depth), axis=0)
        total = mm(both, right)
        return total[:APAD] + total[APAD:]

    slot = me & (heads - 1)
    for k in range(1, heads):
        sends[k - 1][...] = product(slot ^ k).astype(jnp.bfloat16)
    total = product(slot)
    keep_ref[...] = total
    if heads == 1:
        sends[0][...] = total.astype(jnp.bfloat16)


def add_kernel(count, final, keep_in, *refs):
    total = keep_in[...]
    for ref in refs[:count]:
        total = total + ref[...].astype(jnp.float32)
    if not final:
        refs[-2][...] = total
    refs[-1][...] = total.astype(jnp.bfloat16)


def stack_kernel(count, *refs):
    for i, ref in enumerate(refs[:count]):
        refs[-1][i] = ref[...]


def load_kernel(count, *refs):
    copies = fetch([(refs[i], refs[count + 1 + i]) for i in range(count)], refs[-1])
    for copy in copies:
        copy.wait()


def gate_kernel(*refs):
    pass


def encode_kernel(caps, shape_hbm, plan_hbm, feat_ref, conv_ref, embed_ref, first_ref, out_ref, shape_ref, plan_ref, sems):
    copies = fetch([(shape_hbm, shape_ref), (plan_hbm, plan_ref)], sems)
    frames_cap, height_cap, width_cap = caps
    spots = frames_cap * height_cap * width_cap
    frame_size = height_cap * width_cap
    latent_ch = conv_ref.shape[0] // 27
    feats = 4 * latent_ch
    taps = mm(conv_ref[...], feat_ref[...], ((1,), (1,)))
    copies[0].wait()
    copies[1].wait()
    frames, height, width = shape_ref[0, 0, 0], shape_ref[0, 0, 1], shape_ref[0, 0, 2]
    spot = lax.broadcasted_iota(jnp.int32, (1, spots), 1)
    frame_ix = spot // frame_size
    row_ix = (spot % frame_size) // width_cap
    col_ix = spot % width_cap
    inside = (frame_ix < frames) & (row_ix < height) & (col_ix < width)
    taps = jnp.where(inside, taps, 0.0)

    def tap(a, b, j):
        at = (9 * a + 3 * b + j) * latent_ch
        return taps[at : at + latent_ch]

    def later(x, by):
        zeros = jnp.zeros((latent_ch, by * frame_size), jnp.float32)
        return jnp.concatenate([zeros, x[:, : spots - by * frame_size]], axis=1)

    def over_frames(b, j):
        return tap(2, b, j) + later(tap(1, b, j), 1) + later(tap(0, b, j), 2)

    def over_rows(j):
        above = pltpu.roll(over_frames(0, j), width_cap, 1)
        below = pltpu.roll(over_frames(2, j), spots - width_cap, 1)
        return (
            over_frames(1, j)
            + jnp.where(row_ix >= 1, above, 0.0)
            + jnp.where(row_ix < height_cap - 1, below, 0.0)
        )

    latent = (
        over_rows(1)
        + jnp.where(col_ix >= 1, pltpu.roll(over_rows(0), 1, 1), 0.0)
        + jnp.where(col_ix < width_cap - 1, pltpu.roll(over_rows(2), spots - 1, 1), 0.0)
    )
    latent = latent.astype(jnp.bfloat16).astype(jnp.float32)
    shifted = [latent] + [pltpu.roll(latent, spots - by, 1) for by in (1, width_cap, width_cap + 1)]
    patches = jnp.concatenate(shifted, axis=0).astype(jnp.bfloat16)

    tokens = NBS * BLOCK
    half_w = (width // 2).astype(jnp.float32)
    per_frame_int = (height // 2) * (width // 2)
    per_frame = per_frame_int.astype(jnp.float32)
    live = frames * per_frame_int
    token_int = lax.broadcasted_iota(jnp.int32, (1, tokens), 1)
    token = token_int.astype(jnp.float32)
    frame_of = jnp.floor((token + 0.5) / jnp.full((1, tokens), per_frame))
    within = token - frame_of * per_frame
    row_of = jnp.floor((within + 0.5) / jnp.full((1, tokens), half_w))
    col_of = within - row_of * half_w
    source = (frame_of * frame_size + row_of * (2 * width_cap) + col_of * 2).astype(jnp.int32)
    source = jnp.where(token_int < live, source, -1)
    chosen = lax.broadcasted_iota(jnp.int32, (spots, tokens), 0) == source
    picked = mm(patches, jnp.where(chosen, 1.0, 0.0).astype(jnp.bfloat16))
    at = lax.broadcasted_iota(jnp.int32, (feats, feats), 0)
    frm = lax.broadcasted_iota(jnp.int32, (feats, feats), 1)
    order = jnp.where(frm == (at % 4) * latent_ch + at // 4, 1.0, 0.0).astype(jnp.bfloat16)
    picked = mm(order, picked.astype(jnp.bfloat16))

    emb = embed_ref[...].astype(jnp.float32)
    emb = emb - jnp.sum(emb, axis=1, keepdims=True) / emb.shape[1]
    gram = mm(emb, emb, ((1,), (1,)), lax.Precision.HIGHEST) / emb.shape[1]
    spread = mm(gram, picked, precision=lax.Precision.HIGHEST)
    variance = jnp.maximum(jnp.sum(spread * picked, axis=0, keepdims=True), 0.0)
    out_ref[:feats] = (picked * lax.rsqrt(variance + eps_norm)).astype(jnp.bfloat16)

    kind = lax.broadcasted_iota(jnp.int32, (APAD - feats, BLOCK), 0)
    for b in range(NBS):
        count = jnp.clip(live - b * BLOCK, 0, BLOCK)
        info = jnp.where(
            kind == 0,
            plan_ref[0, 0, b, 0],
            jnp.where(kind == 1, plan_ref[0, 0, b, 1], jnp.where(kind == 2, count, 0)),
        )
        out_ref[feats:, b * BLOCK : (b + 1) * BLOCK] = info.astype(jnp.float32).astype(jnp.bfloat16)


def pack_kernel(n_enc, feats, q_gain_ref, k_gain_ref, *refs):
    blocks = refs[:n_enc]
    x_t_ref, x_ref, own_ref, key_mask_ref, own_mask_ref, gain_ref, rows_t = refs[n_enc:]
    mine = lax.axis_index("enc")
    rows = n_enc * BLOCK
    lane = lax.broadcasted_iota(jnp.int32, (1, BLOCK), 1).astype(jnp.float32)
    extra = lax.broadcasted_iota(jnp.int32, (APAD - feats, BLOCK), 0)
    found = []
    for k in range(n_enc):
        source = mine ^ k
        for b in range(NBS):
            tile = blocks[k][:, b * BLOCK : (b + 1) * BLOCK].astype(jnp.float32)
            owner, offset, count = (tile[feats + i : feats + i + 1] for i in range(3))
            owner = jnp.where(offset == 0.0, owner, -1.0)
            segment = jnp.where(lane < count, (source + 1).astype(jnp.float32), 0.0)
            found.append((owner, segment, tile[:feats]))
    for o in range(n_enc):
        segment = jnp.zeros((1, BLOCK), jnp.float32)
        body = jnp.zeros((feats, BLOCK), jnp.float32)
        for owner, seg_of, tile in found:
            hit = owner == float(o)
            segment = segment + jnp.where(hit, seg_of, 0.0)
            body = body + jnp.where(hit, tile, 0.0)
        tail = jnp.where(extra == 0, 1.0, jnp.where(extra == 1, segment, 0.0))
        rows_t[:, o * BLOCK : (o + 1) * BLOCK] = jnp.concatenate(
            [body, tail, jnp.zeros((LANES - APAD, BLOCK), jnp.float32)], axis=0
        )
    x_t = rows_t[...]
    x_t_ref[...] = x_t[:APAD].astype(jnp.bfloat16)
    x_ref[...] = x_t.T.astype(jnp.bfloat16)
    group_t = lax.broadcasted_iota(jnp.int32, (LANES, rows), 0).astype(jnp.float32)
    key_mask_ref[...] = jnp.where(x_t[feats + 1 : feats + 2] == group_t, 0.0, 1.0).astype(jnp.bfloat16)
    own = rows_t[:, pl.ds(pl.multiple_of(mine * BLOCK, BLOCK), BLOCK)].T
    own_ref[...] = own.astype(jnp.bfloat16)
    group = lax.broadcasted_iota(jnp.int32, (BLOCK, LANES), 1).astype(jnp.float32)
    own_mask_ref[...] = jnp.where(own[:, feats + 1 : feats + 2] == group, -FAR, 0.0).astype(jnp.bfloat16)
    head_dim = q_gain_ref.shape[1]
    gain_ref[...] = q_gain_ref[...] * k_gain_ref[...] * (head_dim**-0.5 * math.log2(math.e))


def attend_head(fold, x_t, x_rows, own, key_mask, own_mask, gain):
    head_dim = LANES
    key = mm(fold[:, head_dim : 2 * head_dim], x_t, ((0,), (0,)))
    square = jnp.sum(key * key, axis=0, keepdims=True) / head_dim
    key = (key * lax.rsqrt(square + eps_norm)).astype(jnp.bfloat16)
    query = mm(own, fold[:, :head_dim])
    square = jnp.sum(query * query, axis=1, keepdims=True) / head_dim
    query = (query * lax.rsqrt(square + eps_norm) * gain).astype(jnp.bfloat16)
    scores = mm(jnp.concatenate([query, own_mask], axis=1), jnp.concatenate([key, key_mask], axis=0))
    weight = jnp.exp2(scores).astype(jnp.bfloat16)
    value = mm(x_rows, fold[:, 2 * head_dim :]).astype(jnp.bfloat16)
    value = jnp.concatenate([value, jnp.ones(value.shape, jnp.bfloat16)], axis=1)
    mixed = mm(weight, value)
    return (mixed[:, :head_dim] / mixed[:, head_dim:]).astype(jnp.bfloat16)


def each_head(refs):
    for ref in refs:
        if len(ref.shape) == 2:
            yield ref[...]
        else:
            for i in range(ref.shape[0]):
                yield ref[i]


def attend_kernel(x_t_ref, x_ref, own_ref, key_mask_ref, own_mask_ref, gain_ref, *refs):
    x_t, key_mask, own_mask, gain = x_t_ref[...], key_mask_ref[...], own_mask_ref[...], gain_ref[...]
    x_rows, own = x_ref[:, :APAD], own_ref[:, :APAD]
    for at, fold in enumerate(each_head(refs[:-1])):
        refs[-1][:, at * LANES : (at + 1) * LANES] = attend_head(
            fold, x_t, x_rows, own, key_mask, own_mask, gain
        )


def last_kernel(heads, flips, early, *refs):
    x_t_ref, x_ref, own_ref, key_mask_ref, own_mask_ref, gain_ref = refs[:6]
    done = refs[6 : 6 + early]
    folds, out_ref = refs[6 + early : -1], refs[-1]
    x_t, key_mask, own_mask, gain = x_t_ref[...], key_mask_ref[...], own_mask_ref[...], gain_ref[...]
    x_rows, own = x_ref[:, :APAD], own_ref[:, :APAD]
    mine, slot = lax.axis_index("enc"), lax.axis_index("seq") & (heads - 1)

    def column(at):
        head = (mine ^ flips[at // heads]) * heads + (slot ^ (at % heads))
        return pl.ds(pl.multiple_of(head * LANES, LANES), LANES)

    at = 0
    for ref in done:
        for i in range(ref.shape[1] // LANES):
            out_ref[0, :, column(at)] = ref[:, i * LANES : (i + 1) * LANES]
            at += 1
    for fold in each_head(folds):
        out_ref[0, :, column(at)] = attend_head(fold, x_t, x_rows, own, key_mask, own_mask, gain)
        at += 1


def vmem(count):
    return [pl.BlockSpec(memory_space=pltpu.VMEM)] * count


def hbm(count):
    return [pl.BlockSpec(memory_space=pltpu.HBM)] * count


def in_hbm(x):
    return pltpu.with_memory_space_constraint(x, pltpu.HBM)


def after(count):
    return [pl.BlockSpec(memory_space=pl.ANY)] * count


def call(kernel, ins, out_shape, scratch=(), cost=(1_000_000, 1_000_000)):
    return pl.pallas_call(
        kernel,
        in_specs=ins,
        out_specs=[pl.BlockSpec(memory_space=pltpu.VMEM)] * len(out_shape),
        out_shape=out_shape,
        scratch_shapes=list(scratch),
        compiler_params=pltpu.CompilerParams(vmem_limit_bytes=VMEM_LIMIT),
        cost_estimate=pl.CostEstimate(flops=cost[0], bytes_accessed=cost[1], transcendentals=0),
    )


def gate(x, *others):
    return pl.pallas_call(
        gate_kernel,
        in_specs=after(1 + len(others)),
        out_specs=after(1)[0],
        out_shape=jax.ShapeDtypeStruct(x.shape, x.dtype),
        input_output_aliases={0: 0},
        compiler_params=pltpu.CompilerParams(vmem_limit_bytes=VMEM_LIMIT),
    )(x, *others)


def exchange(x, axis, n, k):
    return lax.ppermute(x, axis, [(i, i ^ k) for i in range(n)])


def on_device(
    n_enc,
    n_seq,
    clip_features,
    clip_shape,
    packing,
    conv_weight,
    embed_weight,
    mod_shift,
    mod_scale,
    qkv_weight,
    q_gain,
    k_gain,
):
    caps = clip_features.shape[2:5]
    depth_all = clip_features.shape[5]
    cols = qkv_weight.shape[2]
    feats = embed_weight.shape[0]
    heads = cols // LANES
    rows = n_enc * BLOCK
    bf16, f32 = jnp.bfloat16, jnp.float32

    def folds(dtype, *lead):
        return jax.ShapeDtypeStruct((*lead, APAD, 3 * LANES), dtype)

    scale_rows, shift_rows = mod_scale.reshape(-1, LANES), mod_shift.reshape(-1, LANES)
    with jax.named_scope("fold"):
        keep, *sends = call(
            fold_kernel,
            hbm(4),
            [folds(f32)] + [folds(bf16)] * max(heads - 1, 1),
            [
                pltpu.VMEM(embed_weight.shape, bf16),
                pltpu.VMEM(scale_rows.shape, f32),
                pltpu.VMEM(shift_rows.shape, f32),
                pltpu.VMEM(qkv_weight.shape, bf16),
                pltpu.SemaphoreType.DMA((4,)),
            ],
            cost=(200_000_000, 1_000_000),
        )(*map(in_hbm, (embed_weight, scale_rows, shift_rows, qkv_weight)))

    with jax.named_scope("load"):
        loads = [
            clip_features.reshape(-1, depth_all),
            conv_weight.reshape(-1, depth_all),
            embed_weight,
            q_gain.reshape(1, -1),
            k_gain.reshape(1, -1),
        ]
        features, conv, embed, q_gain, k_gain = call(
            functools.partial(load_kernel, len(loads)),
            hbm(len(loads)) + after(1),
            [jax.ShapeDtypeStruct(x.shape, x.dtype) for x in loads],
            [pltpu.SemaphoreType.DMA((len(loads),))],
        )(*map(in_hbm, loads), keep)

    def add(keep, got, final):
        shapes = [folds(bf16)] if final else [folds(f32), folds(bf16)]
        kernel = functools.partial(add_kernel, len(got), final)
        return call(kernel, vmem(1 + len(got)) + after(1), shapes)(keep, *got, own_block if final else conv)

    with jax.named_scope("fold_sum"):
        if heads > 1:
            got = [exchange(sends[k - 1], "seq", n_seq, k) for k in range(1, heads)]
            keep, send = add(keep, got, False)
        else:
            send = sends[0]

    with jax.named_scope("encode"):
        own_block = call(
            functools.partial(encode_kernel, caps),
            hbm(2) + vmem(3) + after(1),
            [jax.ShapeDtypeStruct((APAD, NBS * BLOCK), bf16)],
            [
                pltpu.SMEM(clip_shape.shape, jnp.int32),
                pltpu.SMEM(packing.shape, jnp.int32),
                pltpu.SemaphoreType.DMA((2,)),
            ],
            cost=(500_000_000, 2_000_000),
        )(
            in_hbm(clip_shape),
            in_hbm(packing),
            features,
            conv,
            embed,
            keep,
        )[0]

    with jax.named_scope("fold_sum"):
        for bit in range(log2(heads), log2(n_seq)):
            got = exchange(send, "seq", n_seq, 1 << bit)
            if bit + 1 < log2(n_seq):
                keep, send = add(keep, [got], False)
            else:
                (fresh,) = add(keep, [got], True)

    with jax.named_scope("gather"):
        have = [fresh] + [exchange(fresh, "seq", n_seq, k) for k in range(1, heads)]

    with jax.named_scope("pack"):
        blocks = [own_block] + [exchange(own_block, "enc", n_enc, k) for k in range(1, n_enc)]
        packed = call(
            functools.partial(pack_kernel, n_enc, feats),
            vmem(2 + n_enc),
            [
                jax.ShapeDtypeStruct((APAD, rows), bf16),
                jax.ShapeDtypeStruct((rows, LANES), bf16),
                jax.ShapeDtypeStruct((BLOCK, LANES), bf16),
                jax.ShapeDtypeStruct((LANES, rows), bf16),
                jax.ShapeDtypeStruct((BLOCK, LANES), bf16),
                jax.ShapeDtypeStruct((1, LANES), f32),
            ],
            [pltpu.VMEM((LANES, rows), f32)],
        )(q_gain, k_gain, *blocks)

    with jax.named_scope("gather"):
        stacked = call(
            functools.partial(stack_kernel, heads), vmem(heads) + after(n_enc - 1), [folds(bf16, heads)]
        )(*have, *blocks[1:])[0]

    def attend(group):
        count = group.shape[0]
        return call(
            attend_kernel,
            vmem(7),
            [jax.ShapeDtypeStruct((BLOCK, count * LANES), bf16)],
            cost=(count * 200_000_000, 1_000_000),
        )(*packed, group)[0]

    evens = [0]
    for bit in reversed(range(1, log2(n_enc))):
        evens += [at ^ (1 << bit) for at in evens]
    groups, flips, done = {0: stacked}, [], []
    with jax.named_scope("attend"):
        for at, here in enumerate(evens):
            flips += [here, here ^ 1]
            if at + 1 < len(evens):
                ahead = evens[at + 1]
                base = evens[at + 1 - (1 << ((at + 1).bit_length() - 1))]
                far = exchange(groups[base], "enc", n_enc, ahead ^ base)
                near = exchange(groups[here], "enc", n_enc, 1)
                done += [attend(groups[here]), attend(near)]
                groups[ahead] = gate(far, *done[-2:])
            else:
                near = exchange(groups[here], "enc", n_enc, 1)
                done.append(attend(groups[here]))
        return call(
            functools.partial(last_kernel, heads, tuple(flips), len(done)),
            vmem(7 + len(done)),
            [jax.ShapeDtypeStruct((1, BLOCK, n_enc * cols), bf16)],
            cost=(800_000_000, 2_000_000),
        )(*packed, *done, near)[0]


def solution(mesh):
    return jax.shard_map(
        functools.partial(on_device, mesh.shape["enc"], mesh.shape["seq"]),
        mesh=mesh,
        in_specs=(
            P("enc", "seq", None, None, None, None),
            P("enc", "seq", None),
            P("enc", "seq", None, None),
            P(),
            P(),
            P(),
            P(),
            P(None, "seq", "enc"),
            P(),
            P(),
        ),
        out_specs=P("seq", "enc", None),
        check_vma=False,
    )
```

```python
import functools
import math

import jax
import jax.numpy as jnp
from jax import lax
from jax.experimental import pallas as pl
from jax.experimental.pallas import tpu as pltpu
from jax.sharding import PartitionSpec as P

BLOCK = 128
NBS = 2
LANES = 128
APAD = 72
XPAD = 80
eps_norm = 1e-06
FAR = 2.0**20
VMEM_LIMIT = 48 * 1024 * 1024


def mm(a, b, dims=((1,), (0,)), precision=None):
    return lax.dot_general(a, b, (dims, ((), ())), preferred_element_type=jnp.float32, precision=precision)


def split_bf16(x):
    hi = x.astype(jnp.bfloat16)
    return hi, (x - hi.astype(jnp.float32)).astype(jnp.bfloat16)


def log2(n):
    bits = n.bit_length() - 1
    assert 1 << bits == n
    return bits


def fetch(pairs, sems):
    copies = [pltpu.make_async_copy(src, dst, sems.at[i]) for i, (src, dst) in enumerate(pairs)]
    for copy in copies:
        copy.start()
    return copies


def fold_kernel(count, embed_hbm, scale_hbm, shift_hbm, w_hbm, *refs):
    later_hbm, embed_ref, later, keep_ref, sends = refs[:count], refs[count], refs[count + 1 : 2 * count + 1], refs[2 * count + 1], refs[2 * count + 2 : -4]
    scale_ref, shift_ref, w_ref, sems = refs[-4:]
    copies = fetch(
        [(embed_hbm, embed_ref), (scale_hbm, scale_ref), (shift_hbm, shift_ref), (w_hbm, w_ref)]
        + list(zip(later_hbm, later)),
        sems,
    )
    me = lax.axis_index("seq")
    _, depth, cols = w_ref.shape
    feats = embed_ref.shape[0]
    heads = cols // LANES
    for copy in copies[:3]:
        copy.wait()
    mean = jnp.sum(embed_ref[...].astype(jnp.float32), axis=1, keepdims=True) / embed_ref.shape[1]
    span = max(depth, LANES)
    chunks = span // LANES
    first = (me * depth) // LANES
    emb = embed_ref[:, pl.ds(pl.multiple_of(first * LANES, LANES), span)].astype(jnp.float32) - mean
    scale = jnp.concatenate([scale_ref[pl.ds(first + i, 1), :] for i in range(chunks)], axis=1)
    shift = jnp.concatenate([shift_ref[pl.ds(first + i, 1), :] for i in range(chunks)], axis=1)
    left = jnp.concatenate(
        [emb * (1.0 + scale), shift, jnp.zeros((APAD - feats - 1, span), jnp.float32)], axis=0
    )
    if depth < LANES:
        low = me * depth - first * LANES
        lane = lax.broadcasted_iota(jnp.int32, left.shape, 1)
        left = jnp.where((lane >= low) & (lane < low + depth), left, 0.0)
    hi, lo = split_bf16(left)
    both = jnp.concatenate([hi, lo], axis=0)
    copies[3].wait()

    def product(head):
        start = pl.multiple_of(head * LANES, LANES)
        right = jnp.concatenate([w_ref[part, :, pl.ds(start, LANES)] for part in range(3)], axis=1)
        right = jnp.concatenate([right] * (span // depth), axis=0)
        total = mm(both, right)
        return total[:APAD] + total[APAD:]

    slot = me & (heads - 1)
    for k in range(1, heads):
        sends[k - 1][...] = product(slot ^ k).astype(jnp.bfloat16)
    total = product(slot)
    keep_ref[...] = total
    if heads == 1:
        sends[0][...] = total.astype(jnp.bfloat16)
    for copy in copies[4:]:
        copy.wait()


def add_kernel(count, final, keep_in, *refs):
    total = keep_in[...]
    for ref in refs[:count]:
        total = total + ref[...].astype(jnp.float32)
    if not final:
        refs[-2][...] = total
    refs[-1][...] = total.astype(jnp.bfloat16)


def stack_kernel(*refs):
    for i, ref in enumerate(refs[:-1]):
        refs[-1][i] = ref[...]


def gate_kernel(*refs):
    pass


def encode_kernel(caps, shape_hbm, plan_hbm, feat_ref, conv_ref, embed_ref, out_ref, shape_ref, plan_ref, sems):
    copies = fetch([(shape_hbm, shape_ref), (plan_hbm, plan_ref)], sems)
    frames_cap, height_cap, width_cap = caps
    spots = frames_cap * height_cap * width_cap
    frame_size = height_cap * width_cap
    latent_ch = conv_ref.shape[0] // 27
    feats = 4 * latent_ch
    taps = mm(conv_ref[...], feat_ref[...], ((1,), (1,)))
    copies[0].wait()
    copies[1].wait()
    frames, height, width = shape_ref[0, 0, 0], shape_ref[0, 0, 1], shape_ref[0, 0, 2]
    spot = lax.broadcasted_iota(jnp.int32, (1, spots), 1)
    frame_ix = spot // frame_size
    row_ix = (spot % frame_size) // width_cap
    col_ix = spot % width_cap
    inside = (frame_ix < frames) & (row_ix < height) & (col_ix < width)
    taps = jnp.where(inside, taps, 0.0)

    def tap(a, b, j):
        at = (9 * a + 3 * b + j) * latent_ch
        return taps[at : at + latent_ch]

    def later(x, by):
        zeros = jnp.zeros((latent_ch, by * frame_size), jnp.float32)
        return jnp.concatenate([zeros, x[:, : spots - by * frame_size]], axis=1)

    def over_frames(b, j):
        return tap(2, b, j) + later(tap(1, b, j), 1) + later(tap(0, b, j), 2)

    def over_rows(j):
        above = pltpu.roll(over_frames(0, j), width_cap, 1)
        below = pltpu.roll(over_frames(2, j), spots - width_cap, 1)
        return (
            over_frames(1, j)
            + jnp.where(row_ix >= 1, above, 0.0)
            + jnp.where(row_ix < height_cap - 1, below, 0.0)
        )

    latent = (
        over_rows(1)
        + jnp.where(col_ix >= 1, pltpu.roll(over_rows(0), 1, 1), 0.0)
        + jnp.where(col_ix < width_cap - 1, pltpu.roll(over_rows(2), spots - 1, 1), 0.0)
    )
    latent = latent.astype(jnp.bfloat16).astype(jnp.float32)
    shifted = [latent] + [pltpu.roll(latent, spots - by, 1) for by in (1, width_cap, width_cap + 1)]
    patches = jnp.concatenate(shifted, axis=0).astype(jnp.bfloat16)

    tokens = NBS * BLOCK
    half_w = (width // 2).astype(jnp.float32)
    per_frame_int = (height // 2) * (width // 2)
    per_frame = per_frame_int.astype(jnp.float32)
    live = frames * per_frame_int
    token_int = lax.broadcasted_iota(jnp.int32, (1, tokens), 1)
    token = token_int.astype(jnp.float32)
    frame_of = jnp.floor((token + 0.5) / jnp.full((1, tokens), per_frame))
    within = token - frame_of * per_frame
    row_of = jnp.floor((within + 0.5) / jnp.full((1, tokens), half_w))
    col_of = within - row_of * half_w
    source = (frame_of * frame_size + row_of * (2 * width_cap) + col_of * 2).astype(jnp.int32)
    source = jnp.where(token_int < live, source, -1)
    chosen = lax.broadcasted_iota(jnp.int32, (spots, tokens), 0) == source
    picked = mm(patches, jnp.where(chosen, 1.0, 0.0).astype(jnp.bfloat16))
    at = lax.broadcasted_iota(jnp.int32, (feats, feats), 0)
    frm = lax.broadcasted_iota(jnp.int32, (feats, feats), 1)
    order = jnp.where(frm == (at % 4) * latent_ch + at // 4, 1.0, 0.0).astype(jnp.bfloat16)
    picked = mm(order, picked.astype(jnp.bfloat16))

    emb = embed_ref[...].astype(jnp.float32)
    emb = emb - jnp.sum(emb, axis=1, keepdims=True) / emb.shape[1]
    gram = mm(emb, emb, ((1,), (1,)), lax.Precision.HIGHEST) / emb.shape[1]
    spread = mm(gram, picked, precision=lax.Precision.HIGHEST)
    variance = jnp.maximum(jnp.sum(spread * picked, axis=0, keepdims=True), 0.0)
    out_ref[:feats] = (picked * lax.rsqrt(variance + eps_norm)).astype(jnp.bfloat16)

    kind = lax.broadcasted_iota(jnp.int32, (XPAD - feats, BLOCK), 0)
    for b in range(NBS):
        count = jnp.clip(live - b * BLOCK, 0, BLOCK)
        info = jnp.where(
            kind == 0,
            plan_ref[0, 0, b, 0],
            jnp.where(kind == 1, plan_ref[0, 0, b, 1], jnp.where(kind == 2, count, 0)),
        )
        out_ref[feats:, b * BLOCK : (b + 1) * BLOCK] = info.astype(jnp.float32).astype(jnp.bfloat16)


def pack_kernel(n_enc, feats, q_gain_ref, k_gain_ref, *refs):
    blocks = refs[:n_enc]
    x_t_ref, x_ref, own_ref, key_mask_ref, own_mask_ref, gain_ref, rows_t = refs[n_enc:]
    mine = lax.axis_index("enc")
    rows = n_enc * BLOCK
    lane = lax.broadcasted_iota(jnp.int32, (1, BLOCK), 1).astype(jnp.float32)
    extra = lax.broadcasted_iota(jnp.int32, (XPAD - feats, BLOCK), 0)
    found = []
    for k in range(n_enc):
        source = mine ^ k
        for b in range(NBS):
            tile = blocks[k][:, b * BLOCK : (b + 1) * BLOCK].astype(jnp.float32)
            owner, offset, count = (tile[feats + i : feats + i + 1] for i in range(3))
            owner = jnp.where(offset == 0.0, owner, -1.0)
            segment = jnp.where(lane < count, (source + 1).astype(jnp.float32), 0.0)
            found.append((owner, segment, tile[:feats]))
    for o in range(n_enc):
        segment = jnp.zeros((1, BLOCK), jnp.float32)
        body = jnp.zeros((feats, BLOCK), jnp.float32)
        for owner, seg_of, tile in found:
            hit = owner == float(o)
            segment = segment + jnp.where(hit, seg_of, 0.0)
            body = body + jnp.where(hit, tile, 0.0)
        tail = jnp.where(extra == 0, 1.0, jnp.where(extra == 1, segment, 0.0))
        rows_t[:, o * BLOCK : (o + 1) * BLOCK] = jnp.concatenate(
            [body, tail, jnp.zeros((LANES - XPAD, BLOCK), jnp.float32)], axis=0
        )
    x_t = rows_t[...]
    x_t_ref[...] = x_t[:APAD].astype(jnp.bfloat16)
    x_ref[...] = x_t.T.astype(jnp.bfloat16)
    group_t = lax.broadcasted_iota(jnp.int32, (LANES, rows), 0).astype(jnp.float32)
    key_mask_ref[...] = jnp.where(x_t[feats + 1 : feats + 2] == group_t, 0.0, 1.0).astype(jnp.bfloat16)
    own = rows_t[:, pl.ds(pl.multiple_of(mine * BLOCK, BLOCK), BLOCK)].T
    own_ref[...] = own.astype(jnp.bfloat16)
    group = lax.broadcasted_iota(jnp.int32, (BLOCK, LANES), 1).astype(jnp.float32)
    own_mask_ref[...] = jnp.where(own[:, feats + 1 : feats + 2] == group, -FAR, 0.0).astype(jnp.bfloat16)
    head_dim = q_gain_ref.shape[1]
    gain_ref[...] = q_gain_ref[...] * k_gain_ref[...] * (head_dim**-0.5 * math.log2(math.e))


def attend_heads(folds, place, x_t_ref, x_ref, own_ref, key_mask_ref, own_mask_ref, gain_ref):
    x_t, x_rows = x_t_ref[...], x_ref[...]
    own, key_mask, own_mask, gain = own_ref[:, :APAD], key_mask_ref[...], own_mask_ref[...], gain_ref[...]
    ones_at = 64
    for i, fold in enumerate(folds):
        key = mm(fold[:, LANES : 2 * LANES], x_t, ((0,), (0,)))
        square = jnp.sum(key * key, axis=0, keepdims=True) / LANES
        key = (key * lax.rsqrt(square + eps_norm)).astype(jnp.bfloat16)
        query = mm(own, fold[:, :LANES])
        square = jnp.sum(query * query, axis=1, keepdims=True) / LANES
        query = (query * lax.rsqrt(square + eps_norm) * gain).astype(jnp.bfloat16)
        scores = mm(jnp.concatenate([query, own_mask], axis=1), jnp.concatenate([key, key_mask], axis=0))
        mixed = mm(jnp.exp2(scores).astype(jnp.bfloat16), x_rows)
        mixed = mixed / mixed[:, ones_at : ones_at + 1]
        hi, lo = split_bf16(mixed[:, :APAD])
        value = fold[:, 2 * LANES :]
        place(i, (mm(hi, value) + mm(lo, value)).astype(jnp.bfloat16))


def each_head(refs):
    for ref in refs:
        if len(ref.shape) == 2:
            yield ref[...]
        else:
            for i in range(ref.shape[0]):
                yield ref[i]


def attend_kernel(*refs):
    def place(i, result):
        refs[-1][:, i * LANES : (i + 1) * LANES] = result

    attend_heads(each_head(refs[6:-1]), place, *refs[:6])


def last_kernel(heads, flips, early, *refs):
    done, folds, out_ref = refs[6 : 6 + early], refs[6 + early : -1], refs[-1]
    mine, slot = lax.axis_index("enc"), lax.axis_index("seq") & (heads - 1)

    def put(at, result):
        head = (mine ^ flips[at // heads]) * heads + (slot ^ (at % heads))
        out_ref[0, :, pl.ds(pl.multiple_of(head * LANES, LANES), LANES)] = result

    at = 0
    for ref in done:
        for i in range(ref.shape[1] // LANES):
            put(at, ref[:, i * LANES : (i + 1) * LANES])
            at += 1
    attend_heads(each_head(folds), lambda i, result: put(at + i, result), *refs[:6])


def vmem(count):
    return [pl.BlockSpec(memory_space=pltpu.VMEM)] * count


def hbm(count):
    return [pl.BlockSpec(memory_space=pltpu.HBM)] * count


def in_hbm(x):
    return pltpu.with_memory_space_constraint(x, pltpu.HBM)


def after(count):
    return [pl.BlockSpec(memory_space=pl.ANY)] * count


def call(kernel, ins, out_shape, scratch=(), cost=(1_000_000, 1_000_000)):
    return pl.pallas_call(
        kernel,
        in_specs=ins,
        out_specs=[pl.BlockSpec(memory_space=pltpu.VMEM)] * len(out_shape),
        out_shape=out_shape,
        scratch_shapes=list(scratch),
        compiler_params=pltpu.CompilerParams(vmem_limit_bytes=VMEM_LIMIT),
        cost_estimate=pl.CostEstimate(flops=cost[0], bytes_accessed=cost[1], transcendentals=0),
    )


def gate(x, *others):
    return pl.pallas_call(
        gate_kernel,
        in_specs=after(1 + len(others)),
        out_specs=after(1)[0],
        out_shape=jax.ShapeDtypeStruct(x.shape, x.dtype),
        input_output_aliases={0: 0},
        compiler_params=pltpu.CompilerParams(vmem_limit_bytes=VMEM_LIMIT),
    )(x, *others)


def exchange(x, axis, n, k):
    return lax.ppermute(x, axis, [(i, i ^ k) for i in range(n)])


def on_device(
    n_enc,
    n_seq,
    clip_features,
    clip_shape,
    packing,
    conv_weight,
    embed_weight,
    mod_shift,
    mod_scale,
    qkv_weight,
    q_gain,
    k_gain,
):
    caps = clip_features.shape[2:5]
    depth_all = clip_features.shape[5]
    cols = qkv_weight.shape[2]
    feats = embed_weight.shape[0]
    heads = cols // LANES
    rows = n_enc * BLOCK
    bf16, f32 = jnp.bfloat16, jnp.float32

    def folds(dtype, *lead):
        return jax.ShapeDtypeStruct((*lead, APAD, 3 * LANES), dtype)

    scale_rows, shift_rows = mod_scale.reshape(-1, LANES), mod_shift.reshape(-1, LANES)
    later = [
        clip_features.reshape(-1, depth_all),
        conv_weight.reshape(-1, depth_all),
        q_gain.reshape(1, -1),
        k_gain.reshape(1, -1),
    ]
    with jax.named_scope("fold"):
        embed, features, conv, q_gain, k_gain, keep, *sends = call(
            functools.partial(fold_kernel, len(later)),
            hbm(4 + len(later)),
            [jax.ShapeDtypeStruct(x.shape, x.dtype) for x in (embed_weight, *later)]
            + [folds(f32)]
            + [folds(bf16)] * max(heads - 1, 1),
            [
                pltpu.VMEM(scale_rows.shape, f32),
                pltpu.VMEM(shift_rows.shape, f32),
                pltpu.VMEM(qkv_weight.shape, bf16),
                pltpu.SemaphoreType.DMA((4 + len(later),)),
            ],
            cost=(200_000_000, 1_000_000),
        )(*map(in_hbm, (embed_weight, scale_rows, shift_rows, qkv_weight, *later)))

    with jax.named_scope("encode"):
        own_block = call(
            functools.partial(encode_kernel, caps),
            hbm(2) + vmem(3),
            [jax.ShapeDtypeStruct((XPAD, NBS * BLOCK), bf16)],
            [
                pltpu.SMEM(clip_shape.shape, jnp.int32),
                pltpu.SMEM(packing.shape, jnp.int32),
                pltpu.SemaphoreType.DMA((2,)),
            ],
            cost=(500_000_000, 2_000_000),
        )(in_hbm(clip_shape), in_hbm(packing), features, conv, embed)[0]

    def add(keep, got, final):
        shapes = [folds(bf16)] if final else [folds(f32), folds(bf16)]
        kernel = functools.partial(add_kernel, len(got), final)
        return call(kernel, vmem(1 + len(got)) + after(1), shapes)(keep, *got, packed[0] if final else own_block)

    with jax.named_scope("fold_sum"):
        if heads > 1:
            got = [exchange(sends[k - 1], "seq", n_seq, k) for k in range(1, heads)]
            keep, send = add(keep, got, False)
        else:
            send = sends[0]

    with jax.named_scope("pack"):
        own_block = gate(own_block, keep)
        blocks = [own_block] + [exchange(own_block, "enc", n_enc, k) for k in range(1, n_enc)]
        packed = call(
            functools.partial(pack_kernel, n_enc, feats),
            vmem(2 + n_enc),
            [
                jax.ShapeDtypeStruct((APAD, rows), bf16),
                jax.ShapeDtypeStruct((rows, LANES), bf16),
                jax.ShapeDtypeStruct((BLOCK, LANES), bf16),
                jax.ShapeDtypeStruct((LANES, rows), bf16),
                jax.ShapeDtypeStruct((BLOCK, LANES), bf16),
                jax.ShapeDtypeStruct((1, LANES), f32),
            ],
            [pltpu.VMEM((LANES, rows), f32)],
        )(q_gain, k_gain, *blocks)

    with jax.named_scope("fold_sum"):
        for bit in range(log2(heads), log2(n_seq)):
            got = exchange(send, "seq", n_seq, 1 << bit)
            if bit + 1 < log2(n_seq):
                keep, send = add(keep, [got], False)
            else:
                (fresh,) = add(keep, [got], True)

    with jax.named_scope("gather"):
        have = [fresh] + [exchange(fresh, "seq", n_seq, k) for k in range(1, heads)]

    with jax.named_scope("gather"):
        stacked = call(stack_kernel, vmem(heads), [folds(bf16, heads)])(*have)[0]

    def attend(group):
        count = group.shape[0]
        return call(
            attend_kernel,
            vmem(7),
            [jax.ShapeDtypeStruct((BLOCK, count * LANES), bf16)],
            cost=(count * 200_000_000, 1_000_000),
        )(*packed, group)[0]

    evens = [0]
    for bit in reversed(range(1, log2(n_enc))):
        evens += [at ^ (1 << bit) for at in evens]
    groups, flips, done = {0: stacked}, [], []
    with jax.named_scope("attend"):
        for at, here in enumerate(evens):
            flips += [here, here ^ 1]
            if at + 1 < len(evens):
                ahead = evens[at + 1]
                base = evens[at + 1 - (1 << ((at + 1).bit_length() - 1))]
                far = exchange(groups[base], "enc", n_enc, ahead ^ base)
                near = exchange(groups[here], "enc", n_enc, 1)
                done += [attend(groups[here]), attend(near)]
                groups[ahead] = gate(far, *done[-2:])
            else:
                near = exchange(groups[here], "enc", n_enc, 1)
                done.append(attend(groups[here]))
        return call(
            functools.partial(last_kernel, heads, tuple(flips), len(done)),
            vmem(7 + len(done)),
            [jax.ShapeDtypeStruct((1, BLOCK, n_enc * cols), bf16)],
            cost=(800_000_000, 2_000_000),
        )(*packed, *done, near)[0]


def solution(mesh):
    return jax.shard_map(
        functools.partial(on_device, mesh.shape["enc"], mesh.shape["seq"]),
        mesh=mesh,
        in_specs=(
            P("enc", "seq", None, None, None, None),
            P("enc", "seq", None),
            P("enc", "seq", None, None),
            P(),
            P(),
            P(),
            P(),
            P(None, "seq", "enc"),
            P(),
            P(),
        ),
        out_specs=P("seq", "enc", None),
        check_vma=False,
    )
```

```python
import functools
import math

import jax
import jax.numpy as jnp
from jax import lax
from jax.experimental import pallas as pl
from jax.experimental.pallas import tpu as pltpu
from jax.sharding import PartitionSpec as P

BLOCK = 128
NBS = 2
LANES = 128
APAD = 72
XPAD = 80
eps_norm = 1e-06
FAR = 2.0**20
VMEM_LIMIT = 48 * 1024 * 1024


def mm(a, b, dims=((1,), (0,)), precision=None):
    return lax.dot_general(a, b, (dims, ((), ())), preferred_element_type=jnp.float32, precision=precision)


def split_bf16(x):
    hi = x.astype(jnp.bfloat16)
    return hi, (x - hi.astype(jnp.float32)).astype(jnp.bfloat16)


def log2(n):
    bits = n.bit_length() - 1
    assert 1 << bits == n
    return bits


def fetch(pairs, sems):
    copies = [pltpu.make_async_copy(src, dst, sems.at[i]) for i, (src, dst) in enumerate(pairs)]
    for copy in copies:
        copy.start()
    return copies


def fold_kernel(count, embed_hbm, scale_hbm, shift_hbm, w_hbm, *refs):
    later_hbm, embed_ref, later, keep_ref, sends = refs[:count], refs[count], refs[count + 1 : 2 * count + 1], refs[2 * count + 1], refs[2 * count + 2 : -4]
    scale_ref, shift_ref, w_ref, sems = refs[-4:]
    copies = fetch(
        [(embed_hbm, embed_ref), (scale_hbm, scale_ref), (shift_hbm, shift_ref), (w_hbm, w_ref)]
        + list(zip(later_hbm, later)),
        sems,
    )
    me = lax.axis_index("seq")
    _, depth, cols = w_ref.shape
    feats = embed_ref.shape[0]
    heads = cols // LANES
    for copy in copies[:3]:
        copy.wait()
    mean = jnp.sum(embed_ref[...].astype(jnp.float32), axis=1, keepdims=True) / embed_ref.shape[1]
    span = max(depth, LANES)
    chunks = span // LANES
    first = (me * depth) // LANES
    emb = embed_ref[:, pl.ds(pl.multiple_of(first * LANES, LANES), span)].astype(jnp.float32) - mean
    scale = jnp.concatenate([scale_ref[pl.ds(first + i, 1), :] for i in range(chunks)], axis=1)
    shift = jnp.concatenate([shift_ref[pl.ds(first + i, 1), :] for i in range(chunks)], axis=1)
    left = jnp.concatenate(
        [emb * (1.0 + scale), shift, jnp.zeros((APAD - feats - 1, span), jnp.float32)], axis=0
    )
    if depth < LANES:
        low = me * depth - first * LANES
        lane = lax.broadcasted_iota(jnp.int32, left.shape, 1)
        left = jnp.where((lane >= low) & (lane < low + depth), left, 0.0)
    hi, lo = split_bf16(left)
    both = jnp.concatenate([hi, lo], axis=0)
    copies[3].wait()

    def product(head):
        start = pl.multiple_of(head * LANES, LANES)
        right = jnp.concatenate([w_ref[part, :, pl.ds(start, LANES)] for part in range(3)], axis=1)
        right = jnp.concatenate([right] * (span // depth), axis=0)
        total = mm(both, right)
        return total[:APAD] + total[APAD:]

    slot = me & (heads - 1)
    for k in range(1, heads):
        sends[k - 1][...] = product(slot ^ k).astype(jnp.bfloat16)
    total = product(slot)
    keep_ref[...] = total
    if heads == 1:
        sends[0][...] = total.astype(jnp.bfloat16)
    for copy in copies[4:]:
        copy.wait()


def add_kernel(count, final, keep_in, *refs):
    total = keep_in[...]
    for ref in refs[:count]:
        total = total + ref[...].astype(jnp.float32)
    if not final:
        refs[-2][...] = total
    refs[-1][...] = total.astype(jnp.bfloat16)


def stack_kernel(count, *refs):
    for i, ref in enumerate(refs[:count]):
        refs[-1][i] = ref[...]


def gate_kernel(*refs):
    pass


def encode_kernel(caps, shape_hbm, plan_hbm, feat_ref, conv_ref, embed_ref, out_ref, shape_ref, plan_ref, sems):
    copies = fetch([(shape_hbm, shape_ref), (plan_hbm, plan_ref)], sems)
    frames_cap, height_cap, width_cap = caps
    spots = frames_cap * height_cap * width_cap
    frame_size = height_cap * width_cap
    latent_ch = conv_ref.shape[0] // 27
    feats = 4 * latent_ch
    taps = mm(conv_ref[...], feat_ref[...], ((1,), (1,)))
    copies[0].wait()
    copies[1].wait()
    frames, height, width = shape_ref[0, 0, 0], shape_ref[0, 0, 1], shape_ref[0, 0, 2]
    spot = lax.broadcasted_iota(jnp.int32, (1, spots), 1)
    frame_ix = spot // frame_size
    row_ix = (spot % frame_size) // width_cap
    col_ix = spot % width_cap
    inside = (frame_ix < frames) & (row_ix < height) & (col_ix < width)
    taps = jnp.where(inside, taps, 0.0)

    def tap(a, b, j):
        at = (9 * a + 3 * b + j) * latent_ch
        return taps[at : at + latent_ch]

    def later(x, by):
        zeros = jnp.zeros((latent_ch, by * frame_size), jnp.float32)
        return jnp.concatenate([zeros, x[:, : spots - by * frame_size]], axis=1)

    def over_frames(b, j):
        return tap(2, b, j) + later(tap(1, b, j), 1) + later(tap(0, b, j), 2)

    def over_rows(j):
        above = pltpu.roll(over_frames(0, j), width_cap, 1)
        below = pltpu.roll(over_frames(2, j), spots - width_cap, 1)
        return (
            over_frames(1, j)
            + jnp.where(row_ix >= 1, above, 0.0)
            + jnp.where(row_ix < height_cap - 1, below, 0.0)
        )

    latent = (
        over_rows(1)
        + jnp.where(col_ix >= 1, pltpu.roll(over_rows(0), 1, 1), 0.0)
        + jnp.where(col_ix < width_cap - 1, pltpu.roll(over_rows(2), spots - 1, 1), 0.0)
    )
    latent = latent.astype(jnp.bfloat16).astype(jnp.float32)
    shifted = [latent] + [pltpu.roll(latent, spots - by, 1) for by in (1, width_cap, width_cap + 1)]
    patches = jnp.concatenate(shifted, axis=0).astype(jnp.bfloat16)

    tokens = NBS * BLOCK
    half_w = (width // 2).astype(jnp.float32)
    per_frame_int = (height // 2) * (width // 2)
    per_frame = per_frame_int.astype(jnp.float32)
    live = frames * per_frame_int
    token_int = lax.broadcasted_iota(jnp.int32, (1, tokens), 1)
    token = token_int.astype(jnp.float32)
    frame_of = jnp.floor((token + 0.5) / jnp.full((1, tokens), per_frame))
    within = token - frame_of * per_frame
    row_of = jnp.floor((within + 0.5) / jnp.full((1, tokens), half_w))
    col_of = within - row_of * half_w
    source = (frame_of * frame_size + row_of * (2 * width_cap) + col_of * 2).astype(jnp.int32)
    source = jnp.where(token_int < live, source, -1)
    chosen = lax.broadcasted_iota(jnp.int32, (spots, tokens), 0) == source
    picked = mm(patches, jnp.where(chosen, 1.0, 0.0).astype(jnp.bfloat16))
    at = lax.broadcasted_iota(jnp.int32, (feats, feats), 0)
    frm = lax.broadcasted_iota(jnp.int32, (feats, feats), 1)
    order = jnp.where(frm == (at % 4) * latent_ch + at // 4, 1.0, 0.0).astype(jnp.bfloat16)
    picked = mm(order, picked.astype(jnp.bfloat16))

    emb = embed_ref[...].astype(jnp.float32)
    emb = emb - jnp.sum(emb, axis=1, keepdims=True) / emb.shape[1]
    gram = mm(emb, emb, ((1,), (1,)), lax.Precision.HIGHEST) / emb.shape[1]
    spread = mm(gram, picked, precision=lax.Precision.HIGHEST)
    variance = jnp.maximum(jnp.sum(spread * picked, axis=0, keepdims=True), 0.0)
    out_ref[:feats] = (picked * lax.rsqrt(variance + eps_norm)).astype(jnp.bfloat16)

    kind = lax.broadcasted_iota(jnp.int32, (XPAD - feats, BLOCK), 0)
    for b in range(NBS):
        count = jnp.clip(live - b * BLOCK, 0, BLOCK)
        info = jnp.where(
            kind == 0,
            plan_ref[0, 0, b, 0],
            jnp.where(kind == 1, plan_ref[0, 0, b, 1], jnp.where(kind == 2, count, 0)),
        )
        out_ref[feats:, b * BLOCK : (b + 1) * BLOCK] = info.astype(jnp.float32).astype(jnp.bfloat16)


def pack_kernel(n_enc, feats, q_gain_ref, k_gain_ref, *refs):
    blocks = refs[:n_enc]
    x_t_ref, x_ref, own_ref, key_mask_ref, own_mask_ref, gain_ref, rows_t = refs[n_enc:]
    mine = lax.axis_index("enc")
    rows = n_enc * BLOCK
    lane = lax.broadcasted_iota(jnp.int32, (1, BLOCK), 1).astype(jnp.float32)
    extra = lax.broadcasted_iota(jnp.int32, (XPAD - feats, BLOCK), 0)
    found = []
    for k in range(n_enc):
        source = mine ^ k
        for b in range(NBS):
            tile = blocks[k][:, b * BLOCK : (b + 1) * BLOCK].astype(jnp.float32)
            owner, offset, count = (tile[feats + i : feats + i + 1] for i in range(3))
            owner = jnp.where(offset == 0.0, owner, -1.0)
            segment = jnp.where(lane < count, (source + 1).astype(jnp.float32), 0.0)
            found.append((owner, segment, tile[:feats]))
    for o in range(n_enc):
        segment = jnp.zeros((1, BLOCK), jnp.float32)
        body = jnp.zeros((feats, BLOCK), jnp.float32)
        for owner, seg_of, tile in found:
            hit = owner == float(o)
            segment = segment + jnp.where(hit, seg_of, 0.0)
            body = body + jnp.where(hit, tile, 0.0)
        tail = jnp.where(extra == 0, 1.0, jnp.where(extra == 1, segment, 0.0))
        rows_t[:, o * BLOCK : (o + 1) * BLOCK] = jnp.concatenate(
            [body, tail, jnp.zeros((LANES - XPAD, BLOCK), jnp.float32)], axis=0
        )
    x_t = rows_t[...]
    x_t_ref[...] = x_t[:APAD].astype(jnp.bfloat16)
    x_ref[...] = x_t.T.astype(jnp.bfloat16)
    group_t = lax.broadcasted_iota(jnp.int32, (LANES, rows), 0).astype(jnp.float32)
    key_mask_ref[...] = jnp.where(x_t[feats + 1 : feats + 2] == group_t, 0.0, 1.0).astype(jnp.bfloat16)
    own = rows_t[:, pl.ds(pl.multiple_of(mine * BLOCK, BLOCK), BLOCK)].T
    own_ref[...] = own.astype(jnp.bfloat16)
    group = lax.broadcasted_iota(jnp.int32, (BLOCK, LANES), 1).astype(jnp.float32)
    own_mask_ref[...] = jnp.where(own[:, feats + 1 : feats + 2] == group, -FAR, 0.0).astype(jnp.bfloat16)
    head_dim = q_gain_ref.shape[1]
    gain_ref[...] = q_gain_ref[...] * k_gain_ref[...] * (head_dim**-0.5 * math.log2(math.e))


def attend_heads(folds, place, x_t_ref, x_ref, own_ref, key_mask_ref, own_mask_ref, gain_ref):
    folds = list(folds)
    heads = range(len(folds))

    def side(part):
        return jnp.concatenate([fold[:, part * LANES : (part + 1) * LANES] for fold in folds], axis=1)

    def of(i):
        return slice(i * LANES, (i + 1) * LANES)

    keys = mm(side(1), x_t_ref[...], ((0,), (0,)))
    queries = mm(own_ref[:, :APAD], side(0))
    values = mm(x_ref[:, :APAD], side(2)).astype(jnp.bfloat16)
    gain, own_mask, key_mask = gain_ref[...], own_mask_ref[...], key_mask_ref[...]
    left, right = [], []
    for i in heads:
        key = keys[of(i)]
        square = jnp.sum(key * key, axis=0, keepdims=True) / LANES
        key = (key * lax.rsqrt(square + eps_norm)).astype(jnp.bfloat16)
        right.append(jnp.concatenate([key, key_mask], axis=0))
        query = queries[:, of(i)]
        square = jnp.sum(query * query, axis=1, keepdims=True) / LANES
        query = (query * lax.rsqrt(square + eps_norm) * gain).astype(jnp.bfloat16)
        left.append(jnp.concatenate([query, own_mask], axis=1))
    scores = [mm(left[i], right[i]) for i in heads]
    weights = [jnp.exp2(score).astype(jnp.bfloat16) for score in scores]
    ones = jnp.ones((values.shape[0], LANES), jnp.bfloat16)
    mixed = [mm(weights[i], jnp.concatenate([values[:, of(i)], ones], axis=1)) for i in heads]
    for i in heads:
        place(i, (mixed[i][:, :LANES] / mixed[i][:, LANES:]).astype(jnp.bfloat16))


def each_head(refs):
    for ref in refs:
        if len(ref.shape) == 2:
            yield ref[...]
        else:
            for i in range(ref.shape[0]):
                yield ref[i]


def attend_kernel(*refs):
    def place(i, result):
        refs[-1][:, i * LANES : (i + 1) * LANES] = result

    attend_heads(each_head(refs[6:-1]), place, *refs[:6])


def last_kernel(heads, flips, early, *refs):
    done, folds, out_ref = refs[6 : 6 + early], refs[6 + early : -1], refs[-1]
    mine, slot = lax.axis_index("enc"), lax.axis_index("seq") & (heads - 1)

    def put(at, result):
        head = (mine ^ flips[at // heads]) * heads + (slot ^ (at % heads))
        out_ref[0, :, pl.ds(pl.multiple_of(head * LANES, LANES), LANES)] = result

    at = 0
    for ref in done:
        for i in range(ref.shape[1] // LANES):
            put(at, ref[:, i * LANES : (i + 1) * LANES])
            at += 1
    attend_heads(each_head(folds), lambda i, result: put(at + i, result), *refs[:6])


def vmem(count):
    return [pl.BlockSpec(memory_space=pltpu.VMEM)] * count


def hbm(count):
    return [pl.BlockSpec(memory_space=pltpu.HBM)] * count


def in_hbm(x):
    return pltpu.with_memory_space_constraint(x, pltpu.HBM)


def after(count):
    return [pl.BlockSpec(memory_space=pl.ANY)] * count


def call(kernel, ins, out_shape, scratch=(), cost=(1_000_000, 1_000_000)):
    return pl.pallas_call(
        kernel,
        in_specs=ins,
        out_specs=[pl.BlockSpec(memory_space=pltpu.VMEM)] * len(out_shape),
        out_shape=out_shape,
        scratch_shapes=list(scratch),
        compiler_params=pltpu.CompilerParams(vmem_limit_bytes=VMEM_LIMIT),
        cost_estimate=pl.CostEstimate(flops=cost[0], bytes_accessed=cost[1], transcendentals=0),
    )


def gate(x, *others):
    return pl.pallas_call(
        gate_kernel,
        in_specs=after(1 + len(others)),
        out_specs=after(1)[0],
        out_shape=jax.ShapeDtypeStruct(x.shape, x.dtype),
        input_output_aliases={0: 0},
        compiler_params=pltpu.CompilerParams(vmem_limit_bytes=VMEM_LIMIT),
    )(x, *others)


def exchange(x, axis, n, k):
    return lax.ppermute(x, axis, [(i, i ^ k) for i in range(n)])


def on_device(
    n_enc,
    n_seq,
    clip_features,
    clip_shape,
    packing,
    conv_weight,
    embed_weight,
    mod_shift,
    mod_scale,
    qkv_weight,
    q_gain,
    k_gain,
):
    caps = clip_features.shape[2:5]
    depth_all = clip_features.shape[5]
    cols = qkv_weight.shape[2]
    feats = embed_weight.shape[0]
    heads = cols // LANES
    rows = n_enc * BLOCK
    bf16, f32 = jnp.bfloat16, jnp.float32

    def folds(dtype, *lead):
        return jax.ShapeDtypeStruct((*lead, APAD, 3 * LANES), dtype)

    evens = [0]
    for bit in reversed(range(1, log2(n_enc))):
        evens += [at ^ (1 << bit) for at in evens]
    scale_rows, shift_rows = mod_scale.reshape(-1, LANES), mod_shift.reshape(-1, LANES)
    later = [
        clip_features.reshape(-1, depth_all),
        conv_weight.reshape(-1, depth_all),
        q_gain.reshape(1, -1),
        k_gain.reshape(1, -1),
    ]
    with jax.named_scope("fold"):
        embed, features, conv, q_gain, k_gain, keep, *sends = call(
            functools.partial(fold_kernel, len(later)),
            hbm(4 + len(later)),
            [jax.ShapeDtypeStruct(x.shape, x.dtype) for x in (embed_weight, *later)]
            + [folds(f32)]
            + [folds(bf16)] * max(heads - 1, 1),
            [
                pltpu.VMEM(scale_rows.shape, f32),
                pltpu.VMEM(shift_rows.shape, f32),
                pltpu.VMEM(qkv_weight.shape, bf16),
                pltpu.SemaphoreType.DMA((4 + len(later),)),
            ],
            cost=(200_000_000, 1_000_000),
        )(*map(in_hbm, (embed_weight, scale_rows, shift_rows, qkv_weight, *later)))

    with jax.named_scope("encode"):
        own_block = call(
            functools.partial(encode_kernel, caps),
            hbm(2) + vmem(3),
            [jax.ShapeDtypeStruct((XPAD, NBS * BLOCK), bf16)],
            [
                pltpu.SMEM(clip_shape.shape, jnp.int32),
                pltpu.SMEM(packing.shape, jnp.int32),
                pltpu.SemaphoreType.DMA((2,)),
            ],
            cost=(500_000_000, 2_000_000),
        )(in_hbm(clip_shape), in_hbm(packing), features, conv, embed)[0]

    def add(keep, got, final, *first):
        shapes = [folds(bf16)] if final else [folds(f32), folds(bf16)]
        kernel = functools.partial(add_kernel, len(got), final)
        return call(kernel, vmem(1 + len(got)) + after(len(first)), shapes)(keep, *got, *first)

    with jax.named_scope("fold_sum"):
        if heads > 1:
            got = [exchange(sends[k - 1], "seq", n_seq, k) for k in range(1, heads)]
            keep, send = add(keep, got, False, own_block)
        else:
            send = sends[0]

    with jax.named_scope("pack"):
        own_block = gate(own_block, keep)
        blocks = {0: own_block}
        for k in evens[1:]:
            blocks[k] = exchange(own_block, "enc", n_enc, k)
        for k in evens:
            blocks[k ^ 1] = exchange(blocks[k], "enc", n_enc, 1)
        packed = call(
            functools.partial(pack_kernel, n_enc, feats),
            vmem(2 + n_enc),
            [
                jax.ShapeDtypeStruct((APAD, rows), bf16),
                jax.ShapeDtypeStruct((rows, LANES), bf16),
                jax.ShapeDtypeStruct((BLOCK, LANES), bf16),
                jax.ShapeDtypeStruct((LANES, rows), bf16),
                jax.ShapeDtypeStruct((BLOCK, LANES), bf16),
                jax.ShapeDtypeStruct((1, LANES), f32),
            ],
            [pltpu.VMEM((LANES, rows), f32)],
        )(q_gain, k_gain, *[blocks[k] for k in range(n_enc)])

    with jax.named_scope("fold_sum"):
        for bit in range(log2(heads), log2(n_seq)):
            got = exchange(send, "seq", n_seq, 1 << bit)
            if bit + 1 < log2(n_seq):
                keep, send = add(keep, [got], False, own_block)
            else:
                (fresh,) = add(keep, [got], True, blocks[1], *[blocks[k] for k in evens[1:]])

    with jax.named_scope("gather"):
        have = [fresh] + [exchange(fresh, "seq", n_seq, k) for k in range(1, heads)]

    with jax.named_scope("gather"):
        last = [blocks[k ^ 1] for k in evens[1:]]
        stacked = call(
            functools.partial(stack_kernel, heads), vmem(heads) + after(len(last)), [folds(bf16, heads)]
        )(*have, *last)[0]

    def attend(group):
        count = group.shape[0]
        return call(
            attend_kernel,
            vmem(7),
            [jax.ShapeDtypeStruct((BLOCK, count * LANES), bf16)],
            cost=(count * 200_000_000, 1_000_000),
        )(*packed, group)[0]

    groups, flips, done = {0: stacked}, [], []
    with jax.named_scope("attend"):
        for at, here in enumerate(evens):
            flips += [here, here ^ 1]
            if at + 1 < len(evens):
                ahead = evens[at + 1]
                base = evens[at + 1 - (1 << ((at + 1).bit_length() - 1))]
                far = exchange(groups[base], "enc", n_enc, ahead ^ base)
                near = exchange(groups[here], "enc", n_enc, 1)
                done += [attend(groups[here]), attend(near)]
                groups[ahead] = gate(far, *done[-2:])
            else:
                near = exchange(groups[here], "enc", n_enc, 1)
                done.append(attend(groups[here]))
        return call(
            functools.partial(last_kernel, heads, tuple(flips), len(done)),
            vmem(7 + len(done)),
            [jax.ShapeDtypeStruct((1, BLOCK, n_enc * cols), bf16)],
            cost=(800_000_000, 2_000_000),
        )(*packed, *done, near)[0]


def solution(mesh):
    return jax.shard_map(
        functools.partial(on_device, mesh.shape["enc"], mesh.shape["seq"]),
        mesh=mesh,
        in_specs=(
            P("enc", "seq", None, None, None, None),
            P("enc", "seq", None),
            P("enc", "seq", None, None),
            P(),
            P(),
            P(),
            P(),
            P(None, "seq", "enc"),
            P(),
            P(),
        ),
        out_specs=P("seq", "enc", None),
        check_vma=False,
    )
```

```python
import functools
import math

import jax
import jax.numpy as jnp
from jax import lax
from jax.experimental import pallas as pl
from jax.experimental.pallas import tpu as pltpu
from jax.sharding import PartitionSpec as P

BLOCK = 128
NBS = 2
LANES = 128
APAD = 72
XPAD = 80
eps_norm = 1e-06
FAR = 2.0**20
VMEM_LIMIT = 48 * 1024 * 1024


def mm(a, b, dims=((1,), (0,)), precision=None):
    return lax.dot_general(a, b, (dims, ((), ())), preferred_element_type=jnp.float32, precision=precision)


def split_bf16(x):
    hi = x.astype(jnp.bfloat16)
    return hi, (x - hi.astype(jnp.float32)).astype(jnp.bfloat16)


def log2(n):
    bits = n.bit_length() - 1
    assert 1 << bits == n
    return bits


def fetch(pairs, sems):
    copies = [pltpu.make_async_copy(src, dst, sems.at[i]) for i, (src, dst) in enumerate(pairs)]
    for copy in copies:
        copy.start()
    return copies


def fold_kernel(count, embed_hbm, scale_hbm, shift_hbm, w_hbm, *refs):
    later_hbm, embed_ref, later, keep_ref, sends = refs[:count], refs[count], refs[count + 1 : 2 * count + 1], refs[2 * count + 1], refs[2 * count + 2 : -4]
    scale_ref, shift_ref, w_ref, sems = refs[-4:]
    copies = fetch(
        [(embed_hbm, embed_ref), (scale_hbm, scale_ref), (shift_hbm, shift_ref), (w_hbm, w_ref)]
        + list(zip(later_hbm, later)),
        sems,
    )
    me = lax.axis_index("seq")
    _, depth, cols = w_ref.shape
    feats = embed_ref.shape[0]
    heads = cols // LANES
    for copy in copies[:3]:
        copy.wait()
    mean = jnp.sum(embed_ref[...].astype(jnp.float32), axis=1, keepdims=True) / embed_ref.shape[1]
    span = max(depth, LANES)
    chunks = span // LANES
    first = (me * depth) // LANES
    emb = embed_ref[:, pl.ds(pl.multiple_of(first * LANES, LANES), span)].astype(jnp.float32) - mean
    scale = jnp.concatenate([scale_ref[pl.ds(first + i, 1), :] for i in range(chunks)], axis=1)
    shift = jnp.concatenate([shift_ref[pl.ds(first + i, 1), :] for i in range(chunks)], axis=1)
    left = jnp.concatenate(
        [emb * (1.0 + scale), shift, jnp.zeros((APAD - feats - 1, span), jnp.float32)], axis=0
    )
    if depth < LANES:
        low = me * depth - first * LANES
        lane = lax.broadcasted_iota(jnp.int32, left.shape, 1)
        left = jnp.where((lane >= low) & (lane < low + depth), left, 0.0)
    hi, lo = split_bf16(left)
    both = jnp.concatenate([hi, lo], axis=0)
    copies[3].wait()

    def product(head):
        start = pl.multiple_of(head * LANES, LANES)
        right = jnp.concatenate([w_ref[part, :, pl.ds(start, LANES)] for part in range(3)], axis=1)
        right = jnp.concatenate([right] * (span // depth), axis=0)
        total = mm(both, right)
        return total[:APAD] + total[APAD:]

    slot = me & (heads - 1)
    for k in range(1, heads):
        sends[k - 1][...] = product(slot ^ k).astype(jnp.bfloat16)
    total = product(slot)
    keep_ref[...] = total
    if heads == 1:
        sends[0][...] = total.astype(jnp.bfloat16)
    for copy in copies[4:]:
        copy.wait()


def add_kernel(count, final, keep_in, *refs):
    total = keep_in[...]
    for ref in refs[:count]:
        total = total + ref[...].astype(jnp.float32)
    if not final:
        refs[-2][...] = total
    refs[-1][...] = total.astype(jnp.bfloat16)


def stack_kernel(count, *refs):
    for i, ref in enumerate(refs[:count]):
        refs[-1][i] = ref[...]


def gate_kernel(*refs):
    pass


def encode_kernel(caps, shape_hbm, plan_hbm, feat_ref, conv_ref, embed_ref, out_ref, shape_ref, plan_ref, sems):
    copies = fetch([(shape_hbm, shape_ref), (plan_hbm, plan_ref)], sems)
    frames_cap, height_cap, width_cap = caps
    spots = frames_cap * height_cap * width_cap
    frame_size = height_cap * width_cap
    latent_ch = conv_ref.shape[0] // 27
    feats = 4 * latent_ch
    taps = mm(conv_ref[...], feat_ref[...], ((1,), (1,)))
    copies[0].wait()
    copies[1].wait()
    frames, height, width = shape_ref[0, 0, 0], shape_ref[0, 0, 1], shape_ref[0, 0, 2]
    spot = lax.broadcasted_iota(jnp.int32, (1, spots), 1)
    frame_ix = spot // frame_size
    row_ix = (spot % frame_size) // width_cap
    col_ix = spot % width_cap
    inside = (frame_ix < frames) & (row_ix < height) & (col_ix < width)
    taps = jnp.where(inside, taps, 0.0)

    def tap(a, b, j):
        at = (9 * a + 3 * b + j) * latent_ch
        return taps[at : at + latent_ch]

    def later(x, by):
        zeros = jnp.zeros((latent_ch, by * frame_size), jnp.float32)
        return jnp.concatenate([zeros, x[:, : spots - by * frame_size]], axis=1)

    def over_frames(b, j):
        return tap(2, b, j) + later(tap(1, b, j), 1) + later(tap(0, b, j), 2)

    def over_rows(j):
        above = pltpu.roll(over_frames(0, j), width_cap, 1)
        below = pltpu.roll(over_frames(2, j), spots - width_cap, 1)
        return (
            over_frames(1, j)
            + jnp.where(row_ix >= 1, above, 0.0)
            + jnp.where(row_ix < height_cap - 1, below, 0.0)
        )

    latent = (
        over_rows(1)
        + jnp.where(col_ix >= 1, pltpu.roll(over_rows(0), 1, 1), 0.0)
        + jnp.where(col_ix < width_cap - 1, pltpu.roll(over_rows(2), spots - 1, 1), 0.0)
    )
    latent = latent.astype(jnp.bfloat16).astype(jnp.float32)
    shifted = [latent] + [pltpu.roll(latent, spots - by, 1) for by in (1, width_cap, width_cap + 1)]
    patches = jnp.concatenate(shifted, axis=0).astype(jnp.bfloat16)

    tokens = NBS * BLOCK
    half_w = (width // 2).astype(jnp.float32)
    per_frame_int = (height // 2) * (width // 2)
    per_frame = per_frame_int.astype(jnp.float32)
    live = frames * per_frame_int
    token_int = lax.broadcasted_iota(jnp.int32, (1, tokens), 1)
    token = token_int.astype(jnp.float32)
    frame_of = jnp.floor((token + 0.5) / jnp.full((1, tokens), per_frame))
    within = token - frame_of * per_frame
    row_of = jnp.floor((within + 0.5) / jnp.full((1, tokens), half_w))
    col_of = within - row_of * half_w
    source = (frame_of * frame_size + row_of * (2 * width_cap) + col_of * 2).astype(jnp.int32)
    source = jnp.where(token_int < live, source, -1)
    chosen = lax.broadcasted_iota(jnp.int32, (spots, tokens), 0) == source
    picked = mm(patches, jnp.where(chosen, 1.0, 0.0).astype(jnp.bfloat16))
    at = lax.broadcasted_iota(jnp.int32, (feats, feats), 0)
    frm = lax.broadcasted_iota(jnp.int32, (feats, feats), 1)
    order = jnp.where(frm == (at % 4) * latent_ch + at // 4, 1.0, 0.0).astype(jnp.bfloat16)
    picked = mm(order, picked.astype(jnp.bfloat16))

    emb = embed_ref[...].astype(jnp.float32)
    emb = emb - jnp.sum(emb, axis=1, keepdims=True) / emb.shape[1]
    gram = mm(emb, emb, ((1,), (1,)), lax.Precision.HIGHEST) / emb.shape[1]
    spread = mm(gram, picked, precision=lax.Precision.HIGHEST)
    variance = jnp.maximum(jnp.sum(spread * picked, axis=0, keepdims=True), 0.0)
    out_ref[:feats] = (picked * lax.rsqrt(variance + eps_norm)).astype(jnp.bfloat16)

    kind = lax.broadcasted_iota(jnp.int32, (XPAD - feats, BLOCK), 0)
    for b in range(NBS):
        count = jnp.clip(live - b * BLOCK, 0, BLOCK)
        info = jnp.where(
            kind == 0,
            plan_ref[0, 0, b, 0],
            jnp.where(kind == 1, plan_ref[0, 0, b, 1], jnp.where(kind == 2, count, 0)),
        )
        out_ref[feats:, b * BLOCK : (b + 1) * BLOCK] = info.astype(jnp.float32).astype(jnp.bfloat16)


def pack_kernel(evens, feats, q_gain_ref, k_gain_ref, *refs):
    here, near = refs[: len(evens)], refs[len(evens)]
    x_t_ref, x_ref, own_ref, key_mask_ref, own_mask_ref, gain_ref, rows_t = refs[len(evens) + 1 :]
    n_enc = 2 * len(evens)
    mine = lax.axis_index("enc")
    rows = n_enc * BLOCK
    lane = lax.broadcasted_iota(jnp.int32, (1, BLOCK), 1).astype(jnp.float32)
    extra = lax.broadcasted_iota(jnp.int32, (XPAD - feats, BLOCK), 0)
    found = []
    blocks = [(at, here[i][...]) for i, at in enumerate(evens)]
    blocks += [(at ^ 1, near[i]) for i, at in enumerate(evens)]
    for distance, block in blocks:
        source = mine ^ distance
        for b in range(NBS):
            tile = block[:, b * BLOCK : (b + 1) * BLOCK].astype(jnp.float32)
            owner, offset, count = (tile[feats + i : feats + i + 1] for i in range(3))
            owner = jnp.where(offset == 0.0, owner, -1.0)
            segment = jnp.where(lane < count, (source + 1).astype(jnp.float32), 0.0)
            found.append((owner, segment, tile[:feats]))
    for o in range(n_enc):
        segment = jnp.zeros((1, BLOCK), jnp.float32)
        body = jnp.zeros((feats, BLOCK), jnp.float32)
        for owner, seg_of, tile in found:
            hit = owner == float(o)
            segment = segment + jnp.where(hit, seg_of, 0.0)
            body = body + jnp.where(hit, tile, 0.0)
        tail = jnp.where(extra == 0, 1.0, jnp.where(extra == 1, segment, 0.0))
        rows_t[:, o * BLOCK : (o + 1) * BLOCK] = jnp.concatenate(
            [body, tail, jnp.zeros((LANES - XPAD, BLOCK), jnp.float32)], axis=0
        )
    x_t = rows_t[...]
    x_t_ref[...] = x_t[:APAD].astype(jnp.bfloat16)
    x_ref[...] = x_t.T.astype(jnp.bfloat16)
    group_t = lax.broadcasted_iota(jnp.int32, (LANES, rows), 0).astype(jnp.float32)
    key_mask_ref[...] = jnp.where(x_t[feats + 1 : feats + 2] == group_t, 0.0, 1.0).astype(jnp.bfloat16)
    own = rows_t[:, pl.ds(pl.multiple_of(mine * BLOCK, BLOCK), BLOCK)].T
    own_ref[...] = own.astype(jnp.bfloat16)
    group = lax.broadcasted_iota(jnp.int32, (BLOCK, LANES), 1).astype(jnp.float32)
    own_mask_ref[...] = jnp.where(own[:, feats + 1 : feats + 2] == group, -FAR, 0.0).astype(jnp.bfloat16)
    head_dim = q_gain_ref.shape[1]
    gain_ref[...] = q_gain_ref[...] * k_gain_ref[...] * (head_dim**-0.5 * math.log2(math.e))


def attend_heads(folds, place, x_t_ref, x_ref, own_ref, key_mask_ref, own_mask_ref, gain_ref):
    folds = list(folds)
    heads = range(len(folds))

    def side(part):
        return jnp.concatenate([fold[:, part * LANES : (part + 1) * LANES] for fold in folds], axis=1)

    def of(i):
        return slice(i * LANES, (i + 1) * LANES)

    keys = mm(side(1), x_t_ref[...], ((0,), (0,)))
    queries = mm(own_ref[:, :APAD], side(0))
    values = mm(x_ref[:, :APAD], side(2)).astype(jnp.bfloat16)
    gain, own_mask, key_mask = gain_ref[...], own_mask_ref[...], key_mask_ref[...]
    left, right = [], []
    for i in heads:
        key = keys[of(i)]
        square = jnp.sum(key * key, axis=0, keepdims=True) / LANES
        key = (key * lax.rsqrt(square + eps_norm)).astype(jnp.bfloat16)
        right.append(jnp.concatenate([key, key_mask], axis=0))
        query = queries[:, of(i)]
        square = jnp.sum(query * query, axis=1, keepdims=True) / LANES
        query = (query * lax.rsqrt(square + eps_norm) * gain).astype(jnp.bfloat16)
        left.append(jnp.concatenate([query, own_mask], axis=1))
    scores = [mm(left[i], right[i]) for i in heads]
    weights = [jnp.exp2(score).astype(jnp.bfloat16) for score in scores]
    ones = jnp.ones((values.shape[0], LANES), jnp.bfloat16)
    mixed = [mm(weights[i], jnp.concatenate([values[:, of(i)], ones], axis=1)) for i in heads]
    for i in heads:
        place(i, (mixed[i][:, :LANES] / mixed[i][:, LANES:]).astype(jnp.bfloat16))


def each_head(refs):
    for ref in refs:
        if len(ref.shape) == 2:
            yield ref[...]
        else:
            for i in range(ref.shape[0]):
                yield ref[i]


def attend_kernel(*refs):
    def place(i, result):
        refs[-1][:, i * LANES : (i + 1) * LANES] = result

    attend_heads(each_head(refs[6:-1]), place, *refs[:6])


def last_kernel(heads, flips, early, *refs):
    done, folds, out_ref = refs[6 : 6 + early], refs[6 + early : -1], refs[-1]
    mine, slot = lax.axis_index("enc"), lax.axis_index("seq") & (heads - 1)

    def put(at, result):
        head = (mine ^ flips[at // heads]) * heads + (slot ^ (at % heads))
        out_ref[0, :, pl.ds(pl.multiple_of(head * LANES, LANES), LANES)] = result

    at = 0
    for ref in done:
        for i in range(ref.shape[1] // LANES):
            put(at, ref[:, i * LANES : (i + 1) * LANES])
            at += 1
    attend_heads(each_head(folds), lambda i, result: put(at + i, result), *refs[:6])


def vmem(count):
    return [pl.BlockSpec(memory_space=pltpu.VMEM)] * count


def hbm(count):
    return [pl.BlockSpec(memory_space=pltpu.HBM)] * count


def in_hbm(x):
    return pltpu.with_memory_space_constraint(x, pltpu.HBM)


def after(count):
    return [pl.BlockSpec(memory_space=pl.ANY)] * count


def call(kernel, ins, out_shape, scratch=(), cost=(1_000_000, 1_000_000)):
    return pl.pallas_call(
        kernel,
        in_specs=ins,
        out_specs=[pl.BlockSpec(memory_space=pltpu.VMEM)] * len(out_shape),
        out_shape=out_shape,
        scratch_shapes=list(scratch),
        compiler_params=pltpu.CompilerParams(vmem_limit_bytes=VMEM_LIMIT),
        cost_estimate=pl.CostEstimate(flops=cost[0], bytes_accessed=cost[1], transcendentals=0),
    )


def gate(x, *others):
    return pl.pallas_call(
        gate_kernel,
        in_specs=after(1 + len(others)),
        out_specs=after(1)[0],
        out_shape=jax.ShapeDtypeStruct(x.shape, x.dtype),
        input_output_aliases={0: 0},
        compiler_params=pltpu.CompilerParams(vmem_limit_bytes=VMEM_LIMIT),
    )(x, *others)


def exchange(x, axis, n, k):
    return lax.ppermute(x, axis, [(i, i ^ k) for i in range(n)])


def on_device(
    n_enc,
    n_seq,
    clip_features,
    clip_shape,
    packing,
    conv_weight,
    embed_weight,
    mod_shift,
    mod_scale,
    qkv_weight,
    q_gain,
    k_gain,
):
    caps = clip_features.shape[2:5]
    depth_all = clip_features.shape[5]
    cols = qkv_weight.shape[2]
    feats = embed_weight.shape[0]
    heads = cols // LANES
    rows = n_enc * BLOCK
    bf16, f32 = jnp.bfloat16, jnp.float32

    def folds(dtype, *lead):
        return jax.ShapeDtypeStruct((*lead, APAD, 3 * LANES), dtype)

    evens = [0]
    for bit in reversed(range(1, log2(n_enc))):
        evens += [at ^ (1 << bit) for at in evens]
    scale_rows, shift_rows = mod_scale.reshape(-1, LANES), mod_shift.reshape(-1, LANES)
    later = [
        clip_features.reshape(-1, depth_all),
        conv_weight.reshape(-1, depth_all),
        q_gain.reshape(1, -1),
        k_gain.reshape(1, -1),
    ]
    with jax.named_scope("fold"):
        embed, features, conv, q_gain, k_gain, keep, *sends = call(
            functools.partial(fold_kernel, len(later)),
            hbm(4 + len(later)),
            [jax.ShapeDtypeStruct(x.shape, x.dtype) for x in (embed_weight, *later)]
            + [folds(f32)]
            + [folds(bf16)] * max(heads - 1, 1),
            [
                pltpu.VMEM(scale_rows.shape, f32),
                pltpu.VMEM(shift_rows.shape, f32),
                pltpu.VMEM(qkv_weight.shape, bf16),
                pltpu.SemaphoreType.DMA((4 + len(later),)),
            ],
            cost=(200_000_000, 1_000_000),
        )(*map(in_hbm, (embed_weight, scale_rows, shift_rows, qkv_weight, *later)))

    with jax.named_scope("encode"):
        own_block = call(
            functools.partial(encode_kernel, caps),
            hbm(2) + vmem(3),
            [jax.ShapeDtypeStruct((XPAD, NBS * BLOCK), bf16)],
            [
                pltpu.SMEM(clip_shape.shape, jnp.int32),
                pltpu.SMEM(packing.shape, jnp.int32),
                pltpu.SemaphoreType.DMA((2,)),
            ],
            cost=(500_000_000, 2_000_000),
        )(in_hbm(clip_shape), in_hbm(packing), features, conv, embed)[0]

    def add(keep, got, final, *first):
        shapes = [folds(bf16)] if final else [folds(f32), folds(bf16)]
        kernel = functools.partial(add_kernel, len(got), final)
        return call(kernel, vmem(1 + len(got)) + after(len(first)), shapes)(keep, *got, *first)

    with jax.named_scope("fold_sum"):
        if heads > 1:
            got = [exchange(sends[k - 1], "seq", n_seq, k) for k in range(1, heads)]
            keep, send = add(keep, got, False, own_block)
        else:
            send = sends[0]

    with jax.named_scope("tokens"):
        own_block = gate(own_block, keep)
        blocks = [own_block] + [exchange(own_block, "enc", n_enc, k) for k in evens[1:]]

    with jax.named_scope("fold_sum"):
        for bit in range(log2(heads), log2(n_seq)):
            got = exchange(send, "seq", n_seq, 1 << bit)
            if bit + 1 < log2(n_seq):
                keep, send = add(keep, [got], False, own_block)
            else:
                (fresh,) = add(keep, [got], True, *blocks[1:])

    def stack(parts, first):
        shape = jax.ShapeDtypeStruct((len(parts), *parts[0].shape), bf16)
        kernel = functools.partial(stack_kernel, len(parts))
        return call(kernel, vmem(len(parts)) + after(len(first)), [shape])(*parts, *first)[0]

    def spread(x, far, k):
        if far == 0 or k == 0:
            return exchange(x, "seq", n_seq, k) if far == 0 else exchange(x, "enc", n_enc, far)
        pairs = [(e * n_seq + i, (e ^ far) * n_seq + (i ^ k)) for e in range(n_enc) for i in range(n_seq)]
        return lax.ppermute(x, ("enc", "seq"), pairs)

    with jax.named_scope("gather"):
        have = [fresh] + [spread(fresh, far, k) for far in evens for k in range(heads) if far or k]
        near_blocks = exchange(gate(stack(blocks, []), fresh), "enc", n_enc, 1)
        group = stack(have, [near_blocks])
        near = exchange(group, "enc", n_enc, 1)

    with jax.named_scope("pack"):
        packed = call(
            functools.partial(pack_kernel, tuple(evens), feats),
            vmem(3 + len(evens)),
            [
                jax.ShapeDtypeStruct((APAD, rows), bf16),
                jax.ShapeDtypeStruct((rows, LANES), bf16),
                jax.ShapeDtypeStruct((BLOCK, LANES), bf16),
                jax.ShapeDtypeStruct((LANES, rows), bf16),
                jax.ShapeDtypeStruct((BLOCK, LANES), bf16),
                jax.ShapeDtypeStruct((1, LANES), f32),
            ],
            [pltpu.VMEM((LANES, rows), f32)],
        )(q_gain, k_gain, *blocks, near_blocks)

    def attend(group):
        count = group.shape[0]
        return call(
            attend_kernel,
            vmem(7),
            [jax.ShapeDtypeStruct((BLOCK, count * LANES), bf16)],
            cost=(count * 200_000_000, 1_000_000),
        )(*packed, group)[0]

    flips = evens + [far ^ 1 for far in evens]
    with jax.named_scope("attend"):
        done = [attend(group)]
        return call(
            functools.partial(last_kernel, heads, tuple(flips), len(done)),
            vmem(7 + len(done)),
            [jax.ShapeDtypeStruct((1, BLOCK, n_enc * cols), bf16)],
            cost=(800_000_000, 2_000_000),
        )(*packed, *done, near)[0]


def solution(mesh):
    return jax.shard_map(
        functools.partial(on_device, mesh.shape["enc"], mesh.shape["seq"]),
        mesh=mesh,
        in_specs=(
            P("enc", "seq", None, None, None, None),
            P("enc", "seq", None),
            P("enc", "seq", None, None),
            P(),
            P(),
            P(),
            P(),
            P(None, "seq", "enc"),
            P(),
            P(),
        ),
        out_specs=P("seq", "enc", None),
        check_vma=False,
    )
```

```python
import functools
import math

import jax
import jax.numpy as jnp
from jax import lax
from jax.experimental import pallas as pl
from jax.experimental.pallas import tpu as pltpu
from jax.sharding import PartitionSpec as P

BLOCK = 128
NBS = 2
LANES = 128
APAD = 72
XPAD = 80
eps_norm = 1e-06
FAR = 2.0**20
VMEM_LIMIT = 48 * 1024 * 1024


def mm(a, b, dims=((1,), (0,)), precision=None):
    return lax.dot_general(a, b, (dims, ((), ())), preferred_element_type=jnp.float32, precision=precision)


def split_bf16(x):
    hi = x.astype(jnp.bfloat16)
    return hi, (x - hi.astype(jnp.float32)).astype(jnp.bfloat16)


def log2(n):
    bits = n.bit_length() - 1
    assert 1 << bits == n
    return bits


def fetch(pairs, sems):
    copies = [pltpu.make_async_copy(src, dst, sems.at[i]) for i, (src, dst) in enumerate(pairs)]
    for copy in copies:
        copy.start()
    return copies


def fold_kernel(count, embed_hbm, scale_hbm, shift_hbm, w_hbm, *refs):
    later_hbm, embed_ref, later, keep_ref, sends = refs[:count], refs[count], refs[count + 1 : 2 * count + 1], refs[2 * count + 1], refs[2 * count + 2 : -4]
    scale_ref, shift_ref, w_ref, sems = refs[-4:]
    copies = fetch(
        [(embed_hbm, embed_ref), (scale_hbm, scale_ref), (shift_hbm, shift_ref), (w_hbm, w_ref)]
        + list(zip(later_hbm, later)),
        sems,
    )
    me = lax.axis_index("seq")
    _, depth, cols = w_ref.shape
    feats = embed_ref.shape[0]
    heads = cols // LANES
    for copy in copies[:3]:
        copy.wait()
    mean = jnp.sum(embed_ref[...].astype(jnp.float32), axis=1, keepdims=True) / embed_ref.shape[1]
    span = max(depth, LANES)
    chunks = span // LANES
    first = (me * depth) // LANES
    emb = embed_ref[:, pl.ds(pl.multiple_of(first * LANES, LANES), span)].astype(jnp.float32) - mean
    scale = jnp.concatenate([scale_ref[pl.ds(first + i, 1), :] for i in range(chunks)], axis=1)
    shift = jnp.concatenate([shift_ref[pl.ds(first + i, 1), :] for i in range(chunks)], axis=1)
    left = jnp.concatenate(
        [emb * (1.0 + scale), shift, jnp.zeros((APAD - feats - 1, span), jnp.float32)], axis=0
    )
    if depth < LANES:
        low = me * depth - first * LANES
        lane = lax.broadcasted_iota(jnp.int32, left.shape, 1)
        left = jnp.where((lane >= low) & (lane < low + depth), left, 0.0)
    hi, lo = split_bf16(left)
    both = jnp.concatenate([hi, lo], axis=0)
    copies[3].wait()

    def product(head):
        start = pl.multiple_of(head * LANES, LANES)
        right = jnp.concatenate([w_ref[part, :, pl.ds(start, LANES)] for part in range(3)], axis=1)
        right = jnp.concatenate([right] * (span // depth), axis=0)
        total = mm(both, right)
        return total[:APAD] + total[APAD:]

    slot = me & (heads - 1)
    for k in range(1, heads):
        sends[k - 1][...] = product(slot ^ k).astype(jnp.bfloat16)
    total = product(slot)
    keep_ref[...] = total
    if heads == 1:
        sends[0][...] = total.astype(jnp.bfloat16)
    for copy in copies[4:]:
        copy.wait()


def add_kernel(count, final, keep_in, *refs):
    total = keep_in[...]
    for ref in refs[:count]:
        total = total + ref[...].astype(jnp.float32)
    if not final:
        refs[-2][...] = total
    refs[-1][...] = total.astype(jnp.bfloat16)


def stack_kernel(count, *refs):
    for i, ref in enumerate(refs[:count]):
        refs[-1][i] = ref[...]


def gate_kernel(*refs):
    pass


def encode_kernel(caps, shape_hbm, plan_hbm, feat_ref, conv_ref, embed_ref, out_ref, shape_ref, plan_ref, sems):
    copies = fetch([(shape_hbm, shape_ref), (plan_hbm, plan_ref)], sems)
    frames_cap, height_cap, width_cap = caps
    spots = frames_cap * height_cap * width_cap
    frame_size = height_cap * width_cap
    latent_ch = conv_ref.shape[0] // 27
    feats = 4 * latent_ch
    taps = mm(conv_ref[...], feat_ref[...], ((1,), (1,)))
    copies[0].wait()
    copies[1].wait()
    frames, height, width = shape_ref[0, 0, 0], shape_ref[0, 0, 1], shape_ref[0, 0, 2]
    spot = lax.broadcasted_iota(jnp.int32, (1, spots), 1)
    frame_ix = spot // frame_size
    row_ix = (spot % frame_size) // width_cap
    col_ix = spot % width_cap
    inside = (frame_ix < frames) & (row_ix < height) & (col_ix < width)
    taps = jnp.where(inside, taps, 0.0)

    def tap(a, b, j):
        at = (9 * a + 3 * b + j) * latent_ch
        return taps[at : at + latent_ch]

    def later(x, by):
        zeros = jnp.zeros((latent_ch, by * frame_size), jnp.float32)
        return jnp.concatenate([zeros, x[:, : spots - by * frame_size]], axis=1)

    def over_frames(b, j):
        return tap(2, b, j) + later(tap(1, b, j), 1) + later(tap(0, b, j), 2)

    def over_rows(j):
        above = pltpu.roll(over_frames(0, j), width_cap, 1)
        below = pltpu.roll(over_frames(2, j), spots - width_cap, 1)
        return (
            over_frames(1, j)
            + jnp.where(row_ix >= 1, above, 0.0)
            + jnp.where(row_ix < height_cap - 1, below, 0.0)
        )

    latent = (
        over_rows(1)
        + jnp.where(col_ix >= 1, pltpu.roll(over_rows(0), 1, 1), 0.0)
        + jnp.where(col_ix < width_cap - 1, pltpu.roll(over_rows(2), spots - 1, 1), 0.0)
    )
    latent = latent.astype(jnp.bfloat16).astype(jnp.float32)
    shifted = [latent] + [pltpu.roll(latent, spots - by, 1) for by in (1, width_cap, width_cap + 1)]
    patches = jnp.concatenate(shifted, axis=0).astype(jnp.bfloat16)

    tokens = NBS * BLOCK
    half_w = (width // 2).astype(jnp.float32)
    per_frame_int = (height // 2) * (width // 2)
    per_frame = per_frame_int.astype(jnp.float32)
    live = frames * per_frame_int
    token_int = lax.broadcasted_iota(jnp.int32, (1, tokens), 1)
    token = token_int.astype(jnp.float32)
    frame_of = jnp.floor((token + 0.5) / jnp.full((1, tokens), per_frame))
    within = token - frame_of * per_frame
    row_of = jnp.floor((within + 0.5) / jnp.full((1, tokens), half_w))
    col_of = within - row_of * half_w
    source = (frame_of * frame_size + row_of * (2 * width_cap) + col_of * 2).astype(jnp.int32)
    source = jnp.where(token_int < live, source, -1)
    chosen = lax.broadcasted_iota(jnp.int32, (spots, tokens), 0) == source
    picked = mm(patches, jnp.where(chosen, 1.0, 0.0).astype(jnp.bfloat16))
    at = lax.broadcasted_iota(jnp.int32, (feats, feats), 0)
    frm = lax.broadcasted_iota(jnp.int32, (feats, feats), 1)
    order = jnp.where(frm == (at % 4) * latent_ch + at // 4, 1.0, 0.0).astype(jnp.bfloat16)
    picked = mm(order, picked.astype(jnp.bfloat16))

    emb = embed_ref[...].astype(jnp.float32)
    emb = emb - jnp.sum(emb, axis=1, keepdims=True) / emb.shape[1]
    gram = mm(emb, emb, ((1,), (1,)), lax.Precision.HIGHEST) / emb.shape[1]
    spread = mm(gram, picked, precision=lax.Precision.HIGHEST)
    variance = jnp.maximum(jnp.sum(spread * picked, axis=0, keepdims=True), 0.0)
    out_ref[:feats] = (picked * lax.rsqrt(variance + eps_norm)).astype(jnp.bfloat16)

    kind = lax.broadcasted_iota(jnp.int32, (XPAD - feats, BLOCK), 0)
    for b in range(NBS):
        count = jnp.clip(live - b * BLOCK, 0, BLOCK)
        info = jnp.where(
            kind == 0,
            plan_ref[0, 0, b, 0],
            jnp.where(kind == 1, plan_ref[0, 0, b, 1], jnp.where(kind == 2, count, 0)),
        )
        out_ref[feats:, b * BLOCK : (b + 1) * BLOCK] = info.astype(jnp.float32).astype(jnp.bfloat16)


def pack_kernel(evens, feats, q_gain_ref, k_gain_ref, *refs):
    here, near = refs[: len(evens)], refs[len(evens)]
    x_t_ref, x_ref, own_ref, key_mask_ref, own_mask_ref, gain_ref, rows_t = refs[len(evens) + 1 :]
    n_enc = 2 * len(evens)
    mine = lax.axis_index("enc")
    rows = n_enc * BLOCK
    lane = lax.broadcasted_iota(jnp.int32, (1, BLOCK), 1).astype(jnp.float32)
    extra = lax.broadcasted_iota(jnp.int32, (XPAD - feats, BLOCK), 0)
    found = []
    blocks = [(at, here[i][...]) for i, at in enumerate(evens)]
    blocks += [(at ^ 1, near[i]) for i, at in enumerate(evens)]
    for distance, block in blocks:
        source = mine ^ distance
        for b in range(NBS):
            tile = block[:, b * BLOCK : (b + 1) * BLOCK].astype(jnp.float32)
            owner, offset, count = (tile[feats + i : feats + i + 1] for i in range(3))
            owner = jnp.where(offset == 0.0, owner, -1.0)
            segment = jnp.where(lane < count, (source + 1).astype(jnp.float32), 0.0)
            found.append((owner, segment, tile[:feats]))
    for o in range(n_enc):
        segment = jnp.zeros((1, BLOCK), jnp.float32)
        body = jnp.zeros((feats, BLOCK), jnp.float32)
        for owner, seg_of, tile in found:
            hit = owner == float(o)
            segment = segment + jnp.where(hit, seg_of, 0.0)
            body = body + jnp.where(hit, tile, 0.0)
        tail = jnp.where(extra == 0, 1.0, jnp.where(extra == 1, segment, 0.0))
        rows_t[:, o * BLOCK : (o + 1) * BLOCK] = jnp.concatenate(
            [body, tail, jnp.zeros((LANES - XPAD, BLOCK), jnp.float32)], axis=0
        )
    x_t = rows_t[...]
    x_t_ref[...] = x_t[:APAD].astype(jnp.bfloat16)
    x_ref[...] = x_t.T.astype(jnp.bfloat16)
    group_t = lax.broadcasted_iota(jnp.int32, (LANES, rows), 0).astype(jnp.float32)
    key_mask_ref[...] = jnp.where(x_t[feats + 1 : feats + 2] == group_t, 0.0, 1.0).astype(jnp.bfloat16)
    own = rows_t[:, pl.ds(pl.multiple_of(mine * BLOCK, BLOCK), BLOCK)].T
    own_ref[...] = own.astype(jnp.bfloat16)
    group = lax.broadcasted_iota(jnp.int32, (BLOCK, LANES), 1).astype(jnp.float32)
    own_mask_ref[...] = jnp.where(own[:, feats + 1 : feats + 2] == group, -FAR, 0.0).astype(jnp.bfloat16)
    head_dim = q_gain_ref.shape[1]
    gain_ref[...] = q_gain_ref[...] * k_gain_ref[...] * (head_dim**-0.5 * math.log2(math.e))


def attend_heads(folds, place, x_t_ref, x_ref, own_ref, key_mask_ref, own_mask_ref, gain_ref):
    folds = list(folds)
    heads = range(len(folds))

    def side(part):
        return jnp.concatenate([fold[:, part * LANES : (part + 1) * LANES] for fold in folds], axis=1)

    def of(i):
        return slice(i * LANES, (i + 1) * LANES)

    keys = mm(side(1), x_t_ref[...], ((0,), (0,)))
    queries = mm(own_ref[:, :APAD], side(0))
    values = mm(x_ref[:, :APAD], side(2)).astype(jnp.bfloat16)
    gain, own_mask, key_mask = gain_ref[...], own_mask_ref[...], key_mask_ref[...]
    left, right = [], []
    for i in heads:
        key = keys[of(i)]
        square = jnp.sum(key * key, axis=0, keepdims=True) / LANES
        key = (key * lax.rsqrt(square + eps_norm)).astype(jnp.bfloat16)
        right.append(jnp.concatenate([key, key_mask], axis=0))
        query = queries[:, of(i)]
        square = jnp.sum(query * query, axis=1, keepdims=True) / LANES
        query = (query * lax.rsqrt(square + eps_norm) * gain).astype(jnp.bfloat16)
        left.append(jnp.concatenate([query, own_mask], axis=1))
    scores = [mm(left[i], right[i]) for i in heads]
    weights = [jnp.exp2(score).astype(jnp.bfloat16) for score in scores]
    ones = jnp.ones((values.shape[0], LANES), jnp.bfloat16)
    mixed = [mm(weights[i], jnp.concatenate([values[:, of(i)], ones], axis=1)) for i in heads]
    for i in heads:
        place(i, (mixed[i][:, :LANES] / mixed[i][:, LANES:]).astype(jnp.bfloat16))


def each_head(refs):
    for ref in refs:
        if len(ref.shape) == 2:
            yield ref[...]
        else:
            for i in range(ref.shape[0]):
                yield ref[i]


def attend_kernel(*refs):
    def place(i, result):
        refs[-1][:, i * LANES : (i + 1) * LANES] = result

    attend_heads(each_head(refs[6:-1]), place, *refs[:6])


def last_kernel(heads, flips, early, *refs):
    done, folds, out_ref = refs[6 : 6 + early], refs[6 + early : -1], refs[-1]
    mine, slot = lax.axis_index("enc"), lax.axis_index("seq") & (heads - 1)

    def put(at, result):
        head = (mine ^ flips[at // heads]) * heads + (slot ^ (at % heads))
        out_ref[0, :, pl.ds(pl.multiple_of(head * LANES, LANES), LANES)] = result

    at = 0
    for ref in done:
        for i in range(ref.shape[1] // LANES):
            put(at, ref[:, i * LANES : (i + 1) * LANES])
            at += 1
    attend_heads(each_head(folds), lambda i, result: put(at + i, result), *refs[:6])


def vmem(count):
    return [pl.BlockSpec(memory_space=pltpu.VMEM)] * count


def hbm(count):
    return [pl.BlockSpec(memory_space=pltpu.HBM)] * count


def in_hbm(x):
    return pltpu.with_memory_space_constraint(x, pltpu.HBM)


def after(count):
    return [pl.BlockSpec(memory_space=pl.ANY)] * count


def call(kernel, ins, out_shape, scratch=(), cost=(1_000_000, 1_000_000)):
    return pl.pallas_call(
        kernel,
        in_specs=ins,
        out_specs=[pl.BlockSpec(memory_space=pltpu.VMEM)] * len(out_shape),
        out_shape=out_shape,
        scratch_shapes=list(scratch),
        compiler_params=pltpu.CompilerParams(vmem_limit_bytes=VMEM_LIMIT),
        cost_estimate=pl.CostEstimate(flops=cost[0], bytes_accessed=cost[1], transcendentals=0),
    )


def gate(x, *others):
    return pl.pallas_call(
        gate_kernel,
        in_specs=after(1 + len(others)),
        out_specs=after(1)[0],
        out_shape=jax.ShapeDtypeStruct(x.shape, x.dtype),
        input_output_aliases={0: 0},
        compiler_params=pltpu.CompilerParams(vmem_limit_bytes=VMEM_LIMIT),
    )(x, *others)


def exchange(x, axis, n, k):
    return lax.ppermute(x, axis, [(i, i ^ k) for i in range(n)])


def on_device(
    n_enc,
    n_seq,
    clip_features,
    clip_shape,
    packing,
    conv_weight,
    embed_weight,
    mod_shift,
    mod_scale,
    qkv_weight,
    q_gain,
    k_gain,
):
    caps = clip_features.shape[2:5]
    depth_all = clip_features.shape[5]
    cols = qkv_weight.shape[2]
    feats = embed_weight.shape[0]
    heads = cols // LANES
    rows = n_enc * BLOCK
    bf16, f32 = jnp.bfloat16, jnp.float32

    def folds(dtype, *lead):
        return jax.ShapeDtypeStruct((*lead, APAD, 3 * LANES), dtype)

    evens = [0]
    for bit in reversed(range(1, log2(n_enc))):
        evens += [at ^ (1 << bit) for at in evens]
    scale_rows, shift_rows = mod_scale.reshape(-1, LANES), mod_shift.reshape(-1, LANES)
    later = [
        clip_features.reshape(-1, depth_all),
        conv_weight.reshape(-1, depth_all),
        q_gain.reshape(1, -1),
        k_gain.reshape(1, -1),
    ]
    with jax.named_scope("fold"):
        embed, features, conv, q_gain, k_gain, keep, *sends = call(
            functools.partial(fold_kernel, len(later)),
            hbm(4 + len(later)),
            [jax.ShapeDtypeStruct(x.shape, x.dtype) for x in (embed_weight, *later)]
            + [folds(f32)]
            + [folds(bf16)] * max(heads - 1, 1),
            [
                pltpu.VMEM(scale_rows.shape, f32),
                pltpu.VMEM(shift_rows.shape, f32),
                pltpu.VMEM(qkv_weight.shape, bf16),
                pltpu.SemaphoreType.DMA((4 + len(later),)),
            ],
            cost=(200_000_000, 1_000_000),
        )(*map(in_hbm, (embed_weight, scale_rows, shift_rows, qkv_weight, *later)))

    with jax.named_scope("encode"):
        own_block = call(
            functools.partial(encode_kernel, caps),
            hbm(2) + vmem(3),
            [jax.ShapeDtypeStruct((XPAD, NBS * BLOCK), bf16)],
            [
                pltpu.SMEM(clip_shape.shape, jnp.int32),
                pltpu.SMEM(packing.shape, jnp.int32),
                pltpu.SemaphoreType.DMA((2,)),
            ],
            cost=(500_000_000, 2_000_000),
        )(in_hbm(clip_shape), in_hbm(packing), features, conv, embed)[0]

    def add(keep, got, final, *first):
        shapes = [folds(bf16)] if final else [folds(f32), folds(bf16)]
        kernel = functools.partial(add_kernel, len(got), final)
        return call(kernel, vmem(1 + len(got)) + after(len(first)), shapes)(keep, *got, *first)

    with jax.named_scope("fold_sum"):
        if heads > 1:
            got = [exchange(sends[k - 1], "seq", n_seq, k) for k in range(1, heads)]
            keep, send = add(keep, got, False, own_block)
        else:
            send = sends[0]

    with jax.named_scope("tokens"):
        own_block = gate(own_block, keep)
        blocks = [own_block] + [exchange(own_block, "enc", n_enc, k) for k in evens[1:]]

    with jax.named_scope("fold_sum"):
        for bit in range(log2(heads), log2(n_seq)):
            got = exchange(send, "seq", n_seq, 1 << bit)
            if bit + 1 < log2(n_seq):
                keep, send = add(keep, [got], False, own_block)
            else:
                (fresh,) = add(keep, [got], True, *blocks[1:])

    def stack(parts, first):
        shape = jax.ShapeDtypeStruct((len(parts), *parts[0].shape), bf16)
        kernel = functools.partial(stack_kernel, len(parts))
        return call(kernel, vmem(len(parts)) + after(len(first)), [shape])(*parts, *first)[0]

    def spread(x, far, k):
        if far == 0 or k == 0:
            return exchange(x, "seq", n_seq, k) if far == 0 else exchange(x, "enc", n_enc, far)
        pairs = [(e * n_seq + i, (e ^ far) * n_seq + (i ^ k)) for e in range(n_enc) for i in range(n_seq)]
        return lax.ppermute(x, ("enc", "seq"), pairs)

    with jax.named_scope("gather"):
        have = [fresh] + [spread(fresh, far, k) for far in evens for k in range(heads) if far or k]
        group = stack(have, [])
        near_blocks = exchange(gate(stack(blocks, []), group), "enc", n_enc, 1)
        group = gate(group, near_blocks)
        near = exchange(group, "enc", n_enc, 1)

    with jax.named_scope("pack"):
        packed = call(
            functools.partial(pack_kernel, tuple(evens), feats),
            vmem(3 + len(evens)),
            [
                jax.ShapeDtypeStruct((APAD, rows), bf16),
                jax.ShapeDtypeStruct((rows, LANES), bf16),
                jax.ShapeDtypeStruct((BLOCK, LANES), bf16),
                jax.ShapeDtypeStruct((LANES, rows), bf16),
                jax.ShapeDtypeStruct((BLOCK, LANES), bf16),
                jax.ShapeDtypeStruct((1, LANES), f32),
            ],
            [pltpu.VMEM((LANES, rows), f32)],
        )(q_gain, k_gain, *blocks, near_blocks)

    def attend(group):
        count = group.shape[0]
        return call(
            attend_kernel,
            vmem(7),
            [jax.ShapeDtypeStruct((BLOCK, count * LANES), bf16)],
            cost=(count * 200_000_000, 1_000_000),
        )(*packed, group)[0]

    flips = evens + [far ^ 1 for far in evens]
    with jax.named_scope("attend"):
        done = [attend(group)]
        return call(
            functools.partial(last_kernel, heads, tuple(flips), len(done)),
            vmem(7 + len(done)),
            [jax.ShapeDtypeStruct((1, BLOCK, n_enc * cols), bf16)],
            cost=(800_000_000, 2_000_000),
        )(*packed, *done, near)[0]


def solution(mesh):
    return jax.shard_map(
        functools.partial(on_device, mesh.shape["enc"], mesh.shape["seq"]),
        mesh=mesh,
        in_specs=(
            P("enc", "seq", None, None, None, None),
            P("enc", "seq", None),
            P("enc", "seq", None, None),
            P(),
            P(),
            P(),
            P(),
            P(None, "seq", "enc"),
            P(),
            P(),
        ),
        out_specs=P("seq", "enc", None),
        check_vma=False,
    )
```

```python
import functools
import math

import jax
import jax.numpy as jnp
from jax import lax
from jax.experimental import pallas as pl
from jax.experimental.pallas import tpu as pltpu
from jax.sharding import PartitionSpec as P

BLOCK = 128
NBS = 2
LANES = 128
APAD = 72
XPAD = 80
eps_norm = 1e-06
FAR = 2.0**20
VMEM_LIMIT = 48 * 1024 * 1024


def mm(a, b, dims=((1,), (0,)), precision=None):
    return lax.dot_general(a, b, (dims, ((), ())), preferred_element_type=jnp.float32, precision=precision)


def split_bf16(x):
    hi = x.astype(jnp.bfloat16)
    return hi, (x - hi.astype(jnp.float32)).astype(jnp.bfloat16)


def log2(n):
    bits = n.bit_length() - 1
    assert 1 << bits == n
    return bits


def fetch(pairs, sems):
    copies = [pltpu.make_async_copy(src, dst, sems.at[i]) for i, (src, dst) in enumerate(pairs)]
    for copy in copies:
        copy.start()
    return copies


def fold_kernel(count, embed_hbm, scale_hbm, shift_hbm, w_hbm, *refs):
    later_hbm, embed_ref, later, keep_ref, sends = refs[:count], refs[count], refs[count + 1 : 2 * count + 1], refs[2 * count + 1], refs[2 * count + 2 : -4]
    scale_ref, shift_ref, w_ref, sems = refs[-4:]
    copies = fetch(
        [(embed_hbm, embed_ref), (scale_hbm, scale_ref), (shift_hbm, shift_ref), (w_hbm, w_ref)]
        + list(zip(later_hbm, later)),
        sems,
    )
    me = lax.axis_index("seq")
    _, depth, cols = w_ref.shape
    feats = embed_ref.shape[0]
    heads = cols // LANES
    for copy in copies[:3]:
        copy.wait()
    mean = jnp.sum(embed_ref[...].astype(jnp.float32), axis=1, keepdims=True) / embed_ref.shape[1]
    span = max(depth, LANES)
    chunks = span // LANES
    first = (me * depth) // LANES
    emb = embed_ref[:, pl.ds(pl.multiple_of(first * LANES, LANES), span)].astype(jnp.float32) - mean
    scale = jnp.concatenate([scale_ref[pl.ds(first + i, 1), :] for i in range(chunks)], axis=1)
    shift = jnp.concatenate([shift_ref[pl.ds(first + i, 1), :] for i in range(chunks)], axis=1)
    left = jnp.concatenate(
        [emb * (1.0 + scale), shift, jnp.zeros((APAD - feats - 1, span), jnp.float32)], axis=0
    )
    if depth < LANES:
        low = me * depth - first * LANES
        lane = lax.broadcasted_iota(jnp.int32, left.shape, 1)
        left = jnp.where((lane >= low) & (lane < low + depth), left, 0.0)
    hi, lo = split_bf16(left)
    both = jnp.concatenate([hi, lo], axis=0)
    copies[3].wait()

    def product(head):
        start = pl.multiple_of(head * LANES, LANES)
        right = jnp.concatenate([w_ref[part, :, pl.ds(start, LANES)] for part in range(3)], axis=1)
        right = jnp.concatenate([right] * (span // depth), axis=0)
        total = mm(both, right)
        return total[:APAD] + total[APAD:]

    slot = me & (heads - 1)
    for k in range(1, heads):
        sends[k - 1][...] = product(slot ^ k).astype(jnp.bfloat16)
    total = product(slot)
    keep_ref[...] = total
    if heads == 1:
        sends[0][...] = total.astype(jnp.bfloat16)
    for copy in copies[4:]:
        copy.wait()


def add_kernel(count, final, keep_in, *refs):
    total = keep_in[...]
    for ref in refs[:count]:
        total = total + ref[...].astype(jnp.float32)
    if not final:
        refs[-2][...] = total
    refs[-1][...] = total.astype(jnp.bfloat16)


def stack_kernel(count, *refs):
    for i, ref in enumerate(refs[:count]):
        refs[-1][i] = ref[...]


def gate_kernel(*refs):
    pass


def encode_kernel(caps, shape_hbm, plan_hbm, feat_ref, conv_ref, out_ref, shape_ref, plan_ref, sems):
    copies = fetch([(shape_hbm, shape_ref), (plan_hbm, plan_ref)], sems)
    frames_cap, height_cap, width_cap = caps
    spots = frames_cap * height_cap * width_cap
    frame_size = height_cap * width_cap
    latent_ch = conv_ref.shape[0] // 27
    feats = 4 * latent_ch
    taps = mm(conv_ref[...], feat_ref[...], ((1,), (1,)))
    copies[0].wait()
    copies[1].wait()
    frames, height, width = shape_ref[0, 0, 0], shape_ref[0, 0, 1], shape_ref[0, 0, 2]
    spot = lax.broadcasted_iota(jnp.int32, (1, spots), 1)
    frame_ix = spot // frame_size
    row_ix = (spot % frame_size) // width_cap
    col_ix = spot % width_cap
    inside = (frame_ix < frames) & (row_ix < height) & (col_ix < width)
    taps = jnp.where(inside, taps, 0.0)

    def tap(a, b, j):
        at = (9 * a + 3 * b + j) * latent_ch
        return taps[at : at + latent_ch]

    def later(x, by):
        zeros = jnp.zeros((latent_ch, by * frame_size), jnp.float32)
        return jnp.concatenate([zeros, x[:, : spots - by * frame_size]], axis=1)

    def over_frames(b, j):
        return tap(2, b, j) + later(tap(1, b, j), 1) + later(tap(0, b, j), 2)

    def over_rows(j):
        above = pltpu.roll(over_frames(0, j), width_cap, 1)
        below = pltpu.roll(over_frames(2, j), spots - width_cap, 1)
        return (
            over_frames(1, j)
            + jnp.where(row_ix >= 1, above, 0.0)
            + jnp.where(row_ix < height_cap - 1, below, 0.0)
        )

    latent = (
        over_rows(1)
        + jnp.where(col_ix >= 1, pltpu.roll(over_rows(0), 1, 1), 0.0)
        + jnp.where(col_ix < width_cap - 1, pltpu.roll(over_rows(2), spots - 1, 1), 0.0)
    )
    latent = latent.astype(jnp.bfloat16).astype(jnp.float32)
    shifted = [latent] + [pltpu.roll(latent, spots - by, 1) for by in (1, width_cap, width_cap + 1)]
    patches = jnp.concatenate(shifted, axis=0).astype(jnp.bfloat16)

    tokens = NBS * BLOCK
    half_w = (width // 2).astype(jnp.float32)
    per_frame_int = (height // 2) * (width // 2)
    per_frame = per_frame_int.astype(jnp.float32)
    live = frames * per_frame_int
    token_int = lax.broadcasted_iota(jnp.int32, (1, tokens), 1)
    token = token_int.astype(jnp.float32)
    frame_of = jnp.floor((token + 0.5) / jnp.full((1, tokens), per_frame))
    within = token - frame_of * per_frame
    row_of = jnp.floor((within + 0.5) / jnp.full((1, tokens), half_w))
    col_of = within - row_of * half_w
    source = (frame_of * frame_size + row_of * (2 * width_cap) + col_of * 2).astype(jnp.int32)
    source = jnp.where(token_int < live, source, -1)
    chosen = lax.broadcasted_iota(jnp.int32, (spots, tokens), 0) == source
    picked = mm(patches, jnp.where(chosen, 1.0, 0.0).astype(jnp.bfloat16))
    out_ref[:feats] = picked.astype(jnp.bfloat16)

    kind = lax.broadcasted_iota(jnp.int32, (XPAD - feats, BLOCK), 0)
    for b in range(NBS):
        count = jnp.clip(live - b * BLOCK, 0, BLOCK)
        info = jnp.where(
            kind == 0,
            plan_ref[0, 0, b, 0],
            jnp.where(kind == 1, plan_ref[0, 0, b, 1], jnp.where(kind == 2, count, 0)),
        )
        out_ref[feats:, b * BLOCK : (b + 1) * BLOCK] = info.astype(jnp.float32).astype(jnp.bfloat16)


def gram_kernel(embed_ref, first_ref, out_ref):
    feats, width = embed_ref.shape
    emb = embed_ref[...].astype(jnp.float32)
    emb = emb - jnp.sum(emb, axis=1, keepdims=True) / width
    both = jnp.concatenate(split_bf16(emb), axis=0)
    gram = mm(both, both, ((1,), (1,))) / width
    gram = gram[:feats] + gram[feats:]
    out_ref[...] = jnp.concatenate(split_bf16(gram[:, :feats] + gram[:, feats:]), axis=0)


def pack_kernel(evens, feats, q_gain_ref, k_gain_ref, gram_ref, *refs):
    here, near = refs[: len(evens)], refs[len(evens)]
    x_t_ref, x_ref, own_ref, key_mask_ref, own_mask_ref, gain_ref, rows_t = refs[len(evens) + 1 :]
    n_enc = 2 * len(evens)
    mine = lax.axis_index("enc")
    rows = n_enc * BLOCK
    lane = lax.broadcasted_iota(jnp.int32, (1, BLOCK), 1).astype(jnp.float32)
    extra = lax.broadcasted_iota(jnp.int32, (XPAD - feats, BLOCK), 0)
    found = []
    blocks = [(at, here[i][...]) for i, at in enumerate(evens)]
    blocks += [(at ^ 1, near[i]) for i, at in enumerate(evens)]
    for distance, block in blocks:
        source = mine ^ distance
        for b in range(NBS):
            tile = block[:, b * BLOCK : (b + 1) * BLOCK].astype(jnp.float32)
            owner, offset, count = (tile[feats + i : feats + i + 1] for i in range(3))
            owner = jnp.where(offset == 0.0, owner, -1.0)
            segment = jnp.where(lane < count, (source + 1).astype(jnp.float32), 0.0)
            found.append((owner, segment, tile[:feats]))
    at = lax.broadcasted_iota(jnp.int32, (feats, feats), 0)
    frm = lax.broadcasted_iota(jnp.int32, (feats, feats), 1)
    order = jnp.where(frm == (at % 4) * (feats // 4) + at // 4, 1.0, 0.0).astype(jnp.bfloat16)
    for o in range(n_enc):
        segment = jnp.zeros((1, BLOCK), jnp.float32)
        body = jnp.zeros((feats, BLOCK), jnp.float32)
        for owner, seg_of, tile in found:
            hit = owner == float(o)
            segment = segment + jnp.where(hit, seg_of, 0.0)
            body = body + jnp.where(hit, tile, 0.0)
        tail = jnp.where(extra == 0, 1.0, jnp.where(extra == 1, segment, 0.0))
        rows_t[:, o * BLOCK : (o + 1) * BLOCK] = jnp.concatenate(
            [body, tail, jnp.zeros((LANES - XPAD, BLOCK), jnp.float32)], axis=0
        )
    picked = mm(order, rows_t[:feats].astype(jnp.bfloat16))
    spread = mm(gram_ref[...], picked.astype(jnp.bfloat16))
    variance = jnp.sum((spread[:feats] + spread[feats:]) * picked, axis=0, keepdims=True)
    rows_t[:feats] = picked * lax.rsqrt(jnp.maximum(variance, 0.0) + eps_norm)
    x_t = rows_t[...]
    x_t_ref[...] = x_t[:APAD].astype(jnp.bfloat16)
    x_ref[...] = x_t.T.astype(jnp.bfloat16)
    group_t = lax.broadcasted_iota(jnp.int32, (LANES, rows), 0).astype(jnp.float32)
    key_mask_ref[...] = jnp.where(x_t[feats + 1 : feats + 2] == group_t, 0.0, 1.0).astype(jnp.bfloat16)
    own = rows_t[:, pl.ds(pl.multiple_of(mine * BLOCK, BLOCK), BLOCK)].T
    own_ref[...] = own.astype(jnp.bfloat16)
    group = lax.broadcasted_iota(jnp.int32, (BLOCK, LANES), 1).astype(jnp.float32)
    own_mask_ref[...] = jnp.where(own[:, feats + 1 : feats + 2] == group, -FAR, 0.0).astype(jnp.bfloat16)
    head_dim = q_gain_ref.shape[1]
    gain_ref[...] = q_gain_ref[...] * k_gain_ref[...] * (head_dim**-0.5 * math.log2(math.e))


def attend_heads(folds, place, x_t_ref, x_ref, own_ref, key_mask_ref, own_mask_ref, gain_ref):
    folds = list(folds)
    heads = range(len(folds))

    def side(part):
        return jnp.concatenate([fold[:, part * LANES : (part + 1) * LANES] for fold in folds], axis=1)

    def of(i):
        return slice(i * LANES, (i + 1) * LANES)

    keys = mm(side(1), x_t_ref[...], ((0,), (0,)))
    queries = mm(own_ref[:, :APAD], side(0))
    values = mm(x_ref[:, :APAD], side(2)).astype(jnp.bfloat16)
    gain, own_mask, key_mask = gain_ref[...], own_mask_ref[...], key_mask_ref[...]
    left, right = [], []
    for i in heads:
        key = keys[of(i)]
        square = jnp.sum(key * key, axis=0, keepdims=True) / LANES
        key = (key * lax.rsqrt(square + eps_norm)).astype(jnp.bfloat16)
        right.append(jnp.concatenate([key, key_mask], axis=0))
        query = queries[:, of(i)]
        square = jnp.sum(query * query, axis=1, keepdims=True) / LANES
        query = (query * lax.rsqrt(square + eps_norm) * gain).astype(jnp.bfloat16)
        left.append(jnp.concatenate([query, own_mask], axis=1))
    scores = [mm(left[i], right[i]) for i in heads]
    weights = [jnp.exp2(score).astype(jnp.bfloat16) for score in scores]
    ones = jnp.ones((values.shape[0], LANES), jnp.bfloat16)
    mixed = [mm(weights[i], jnp.concatenate([values[:, of(i)], ones], axis=1)) for i in heads]
    for i in heads:
        place(i, (mixed[i][:, :LANES] / mixed[i][:, LANES:]).astype(jnp.bfloat16))


def attend_kernel(heads, flips, *refs):
    folds, out_ref, done, sems = refs[6], refs[-3], refs[-2], refs[-1]
    mine, slot = lax.axis_index("enc"), lax.axis_index("seq") & (heads - 1)
    copies = []

    def place(i, result):
        head = (mine ^ flips[i // heads]) * heads + (slot ^ (i % heads))
        column = pl.ds(pl.multiple_of(head * LANES, LANES), LANES)
        done[i] = result
        copies.append(pltpu.make_async_copy(done.at[i], out_ref.at[0, :, column], sems.at[i]))
        copies[-1].start()

    attend_heads([folds[i] for i in range(folds.shape[0])], place, *refs[:6])
    for copy in copies:
        copy.wait()


def vmem(count):
    return [pl.BlockSpec(memory_space=pltpu.VMEM)] * count


def hbm(count):
    return [pl.BlockSpec(memory_space=pltpu.HBM)] * count


def in_hbm(x):
    return pltpu.with_memory_space_constraint(x, pltpu.HBM)


def after(count):
    return [pl.BlockSpec(memory_space=pl.ANY)] * count


def call(kernel, ins, out_shape, scratch=(), cost=(1_000_000, 1_000_000)):
    return pl.pallas_call(
        kernel,
        in_specs=ins,
        out_specs=[pl.BlockSpec(memory_space=pltpu.VMEM)] * len(out_shape),
        out_shape=out_shape,
        scratch_shapes=list(scratch),
        compiler_params=pltpu.CompilerParams(vmem_limit_bytes=VMEM_LIMIT),
        cost_estimate=pl.CostEstimate(flops=cost[0], bytes_accessed=cost[1], transcendentals=0),
    )


def gate(x, *others):
    return pl.pallas_call(
        gate_kernel,
        in_specs=after(1 + len(others)),
        out_specs=after(1)[0],
        out_shape=jax.ShapeDtypeStruct(x.shape, x.dtype),
        input_output_aliases={0: 0},
        compiler_params=pltpu.CompilerParams(vmem_limit_bytes=VMEM_LIMIT),
    )(x, *others)


def exchange(x, axis, n, k):
    return lax.ppermute(x, axis, [(i, i ^ k) for i in range(n)])


def on_device(
    n_enc,
    n_seq,
    clip_features,
    clip_shape,
    packing,
    conv_weight,
    embed_weight,
    mod_shift,
    mod_scale,
    qkv_weight,
    q_gain,
    k_gain,
):
    caps = clip_features.shape[2:5]
    depth_all = clip_features.shape[5]
    cols = qkv_weight.shape[2]
    feats = embed_weight.shape[0]
    heads = cols // LANES
    rows = n_enc * BLOCK
    bf16, f32 = jnp.bfloat16, jnp.float32

    def folds(dtype, *lead):
        return jax.ShapeDtypeStruct((*lead, APAD, 3 * LANES), dtype)

    evens = [0]
    for bit in reversed(range(1, log2(n_enc))):
        evens += [at ^ (1 << bit) for at in evens]
    scale_rows, shift_rows = mod_scale.reshape(-1, LANES), mod_shift.reshape(-1, LANES)
    later = [
        clip_features.reshape(-1, depth_all),
        conv_weight.reshape(-1, depth_all),
        q_gain.reshape(1, -1),
        k_gain.reshape(1, -1),
    ]
    with jax.named_scope("fold"):
        embed, features, conv, q_gain, k_gain, keep, *sends = call(
            functools.partial(fold_kernel, len(later)),
            hbm(4 + len(later)),
            [jax.ShapeDtypeStruct(x.shape, x.dtype) for x in (embed_weight, *later)]
            + [folds(f32)]
            + [folds(bf16)] * max(heads - 1, 1),
            [
                pltpu.VMEM(scale_rows.shape, f32),
                pltpu.VMEM(shift_rows.shape, f32),
                pltpu.VMEM(qkv_weight.shape, bf16),
                pltpu.SemaphoreType.DMA((4 + len(later),)),
            ],
            cost=(200_000_000, 1_000_000),
        )(*map(in_hbm, (embed_weight, scale_rows, shift_rows, qkv_weight, *later)))

    with jax.named_scope("encode"):
        own_block = call(
            functools.partial(encode_kernel, caps),
            hbm(2) + vmem(2),
            [jax.ShapeDtypeStruct((XPAD, NBS * BLOCK), bf16)],
            [
                pltpu.SMEM(clip_shape.shape, jnp.int32),
                pltpu.SMEM(packing.shape, jnp.int32),
                pltpu.SemaphoreType.DMA((2,)),
            ],
            cost=(500_000_000, 2_000_000),
        )(in_hbm(clip_shape), in_hbm(packing), features, conv)[0]

    def add(keep, got, final, *first):
        shapes = [folds(bf16)] if final else [folds(f32), folds(bf16)]
        kernel = functools.partial(add_kernel, len(got), final)
        return call(kernel, vmem(1 + len(got)) + after(len(first)), shapes)(keep, *got, *first)

    with jax.named_scope("fold_sum"):
        if heads > 1:
            got = [exchange(sends[k - 1], "seq", n_seq, k) for k in range(1, heads)]
            keep, send = add(keep, got, False, own_block)
        else:
            send = sends[0]

    with jax.named_scope("gram"):
        gram = call(gram_kernel, vmem(1) + after(1), [jax.ShapeDtypeStruct((2 * feats, feats), bf16)])(embed, keep)[0]

    with jax.named_scope("tokens"):
        own_block = gate(own_block, keep)
        blocks = [own_block] + [exchange(own_block, "enc", n_enc, k) for k in evens[1:]]

    with jax.named_scope("fold_sum"):
        for bit in range(log2(heads), log2(n_seq)):
            got = exchange(send, "seq", n_seq, 1 << bit)
            if bit + 1 < log2(n_seq):
                keep, send = add(keep, [got], False, own_block)
            else:
                (fresh,) = add(keep, [got], True, gram, *blocks[1:])

    def stack(parts, first):
        shape = jax.ShapeDtypeStruct((len(parts), *parts[0].shape), bf16)
        kernel = functools.partial(stack_kernel, len(parts))
        return call(kernel, vmem(len(parts)) + after(len(first)), [shape])(*parts, *first)[0]

    def spread(x, far, k):
        if far == 0 or k == 0:
            return exchange(x, "seq", n_seq, k) if far == 0 else exchange(x, "enc", n_enc, far)
        pairs = [(e * n_seq + i, (e ^ far) * n_seq + (i ^ k)) for e in range(n_enc) for i in range(n_seq)]
        return lax.ppermute(x, ("enc", "seq"), pairs)

    with jax.named_scope("gather"):
        have = {(0, 0): fresh}
        for far in reversed(evens):
            for k in range(heads):
                if far or k:
                    have[far, k] = spread(fresh, far, k)
        near_blocks = exchange(gate(stack(blocks, []), fresh), "enc", n_enc, 1)

    with jax.named_scope("pack"):
        packed = call(
            functools.partial(pack_kernel, tuple(evens), feats),
            vmem(4 + len(evens)),
            [
                jax.ShapeDtypeStruct((APAD, rows), bf16),
                jax.ShapeDtypeStruct((rows, LANES), bf16),
                jax.ShapeDtypeStruct((BLOCK, LANES), bf16),
                jax.ShapeDtypeStruct((LANES, rows), bf16),
                jax.ShapeDtypeStruct((BLOCK, LANES), bf16),
                jax.ShapeDtypeStruct((1, LANES), f32),
            ],
            [pltpu.VMEM((LANES, rows), f32)],
        )(q_gain, k_gain, gram, *blocks, near_blocks)

    def attend(group, flips, out):
        count = group.shape[0]
        olds = [] if out is None else [out]
        return pl.pallas_call(
            functools.partial(attend_kernel, heads, tuple(flips)),
            in_specs=vmem(7) + hbm(len(olds)),
            out_specs=hbm(1)[0],
            out_shape=jax.ShapeDtypeStruct((1, BLOCK, n_enc * cols), bf16),
            scratch_shapes=[pltpu.VMEM((count, BLOCK, LANES), bf16), pltpu.SemaphoreType.DMA((count,))],
            input_output_aliases={7: 0} if olds else {},
            compiler_params=pltpu.CompilerParams(vmem_limit_bytes=VMEM_LIMIT),
            cost_estimate=pl.CostEstimate(flops=count * 200_000_000, bytes_accessed=1_000_000, transcendentals=0),
        )(*packed, group, *map(in_hbm, olds))

    with jax.named_scope("attend"):
        out, parts = None, []
        for far in evens:
            parts += [have[far, k] for k in range(heads)]
            if far == 0:
                out = attend(stack(parts, []), [0], out)
        group = stack(parts, [in_hbm(out)])
        near = exchange(group, "enc", n_enc, 1)
        out = attend(stack(parts[heads:], [group]), evens[1:], out)
        return attend(near, [far ^ 1 for far in evens], out)


def solution(mesh):
    return jax.shard_map(
        functools.partial(on_device, mesh.shape["enc"], mesh.shape["seq"]),
        mesh=mesh,
        in_specs=(
            P("enc", "seq", None, None, None, None),
            P("enc", "seq", None),
            P("enc", "seq", None, None),
            P(),
            P(),
            P(),
            P(),
            P(None, "seq", "enc"),
            P(),
            P(),
        ),
        out_specs=P("seq", "enc", None),
        check_vma=False,
    )
```

```python
import functools
import math

import jax
import jax.numpy as jnp
from jax import lax
from jax.experimental import pallas as pl
from jax.experimental.pallas import tpu as pltpu
from jax.sharding import PartitionSpec as P

BLOCK = 128
NBS = 2
LANES = 128
APAD = 72
XPAD = 80
eps_norm = 1e-06
FAR = 2.0**20
VMEM_LIMIT = 48 * 1024 * 1024


def mm(a, b, dims=((1,), (0,)), precision=None):
    return lax.dot_general(a, b, (dims, ((), ())), preferred_element_type=jnp.float32, precision=precision)


def split_bf16(x):
    hi = x.astype(jnp.bfloat16)
    return hi, (x - hi.astype(jnp.float32)).astype(jnp.bfloat16)


def log2(n):
    bits = n.bit_length() - 1
    assert 1 << bits == n
    return bits


def fetch(pairs, sems):
    copies = [pltpu.make_async_copy(src, dst, sems.at[i]) for i, (src, dst) in enumerate(pairs)]
    for copy in copies:
        copy.start()
    return copies


def fold_kernel(count, embed_hbm, scale_hbm, shift_hbm, w_hbm, *refs):
    later_hbm, embed_ref, later, keep_ref, sends = refs[:count], refs[count], refs[count + 1 : 2 * count + 1], refs[2 * count + 1], refs[2 * count + 2 : -4]
    scale_ref, shift_ref, w_ref, sems = refs[-4:]
    copies = fetch(
        [(embed_hbm, embed_ref), (scale_hbm, scale_ref), (shift_hbm, shift_ref), (w_hbm, w_ref)]
        + list(zip(later_hbm, later)),
        sems,
    )
    me = lax.axis_index("seq")
    _, depth, cols = w_ref.shape
    feats = embed_ref.shape[0]
    heads = cols // LANES
    for copy in copies[:3]:
        copy.wait()
    mean = jnp.sum(embed_ref[...].astype(jnp.float32), axis=1, keepdims=True) / embed_ref.shape[1]
    span = max(depth, LANES)
    chunks = span // LANES
    first = (me * depth) // LANES
    emb = embed_ref[:, pl.ds(pl.multiple_of(first * LANES, LANES), span)].astype(jnp.float32) - mean
    scale = jnp.concatenate([scale_ref[pl.ds(first + i, 1), :] for i in range(chunks)], axis=1)
    shift = jnp.concatenate([shift_ref[pl.ds(first + i, 1), :] for i in range(chunks)], axis=1)
    left = jnp.concatenate(
        [emb * (1.0 + scale), shift, jnp.zeros((APAD - feats - 1, span), jnp.float32)], axis=0
    )
    if depth < LANES:
        low = me * depth - first * LANES
        lane = lax.broadcasted_iota(jnp.int32, left.shape, 1)
        left = jnp.where((lane >= low) & (lane < low + depth), left, 0.0)
    hi, lo = split_bf16(left)
    both = jnp.concatenate([hi, lo], axis=0)
    copies[3].wait()

    def product(head):
        start = pl.multiple_of(head * LANES, LANES)
        right = jnp.concatenate([w_ref[part, :, pl.ds(start, LANES)] for part in range(3)], axis=1)
        right = jnp.concatenate([right] * (span // depth), axis=0)
        total = mm(both, right)
        return total[:APAD] + total[APAD:]

    slot = me & (heads - 1)
    for k in range(1, heads):
        sends[k - 1][...] = product(slot ^ k).astype(jnp.bfloat16)
    total = product(slot)
    keep_ref[...] = total
    if heads == 1:
        sends[0][...] = total.astype(jnp.bfloat16)
    for copy in copies[4:]:
        copy.wait()


def add_kernel(count, final, keep_in, *refs):
    total = keep_in[...]
    for ref in refs[:count]:
        total = total + ref[...].astype(jnp.float32)
    if not final:
        refs[-2][...] = total
    refs[-1][...] = total.astype(jnp.bfloat16)


def stack_kernel(count, *refs):
    for i, ref in enumerate(refs[:count]):
        refs[-1][i] = ref[...]


def gate_kernel(*refs):
    pass


def encode_kernel(caps, shape_hbm, plan_hbm, feat_ref, conv_ref, out_ref, shape_ref, plan_ref, sems):
    copies = fetch([(shape_hbm, shape_ref), (plan_hbm, plan_ref)], sems)
    frames_cap, height_cap, width_cap = caps
    spots = frames_cap * height_cap * width_cap
    frame_size = height_cap * width_cap
    latent_ch = conv_ref.shape[0] // 27
    feats = 4 * latent_ch
    taps = mm(conv_ref[...], feat_ref[...], ((1,), (1,)))
    copies[0].wait()
    copies[1].wait()
    frames, height, width = shape_ref[0, 0, 0], shape_ref[0, 0, 1], shape_ref[0, 0, 2]
    spot = lax.broadcasted_iota(jnp.int32, (1, spots), 1)
    frame_ix = spot // frame_size
    row_ix = (spot % frame_size) // width_cap
    col_ix = spot % width_cap
    inside = (frame_ix < frames) & (row_ix < height) & (col_ix < width)
    taps = jnp.where(inside, taps, 0.0)

    def tap(a, b, j):
        at = (9 * a + 3 * b + j) * latent_ch
        return taps[at : at + latent_ch]

    def later(x, by):
        zeros = jnp.zeros((latent_ch, by * frame_size), jnp.float32)
        return jnp.concatenate([zeros, x[:, : spots - by * frame_size]], axis=1)

    def over_frames(b, j):
        return tap(2, b, j) + later(tap(1, b, j), 1) + later(tap(0, b, j), 2)

    def over_rows(j):
        above = pltpu.roll(over_frames(0, j), width_cap, 1)
        below = pltpu.roll(over_frames(2, j), spots - width_cap, 1)
        return (
            over_frames(1, j)
            + jnp.where(row_ix >= 1, above, 0.0)
            + jnp.where(row_ix < height_cap - 1, below, 0.0)
        )

    latent = (
        over_rows(1)
        + jnp.where(col_ix >= 1, pltpu.roll(over_rows(0), 1, 1), 0.0)
        + jnp.where(col_ix < width_cap - 1, pltpu.roll(over_rows(2), spots - 1, 1), 0.0)
    )
    latent = latent.astype(jnp.bfloat16).astype(jnp.float32)
    shifted = [latent] + [pltpu.roll(latent, spots - by, 1) for by in (1, width_cap, width_cap + 1)]
    patches = jnp.concatenate(shifted, axis=0).astype(jnp.bfloat16)

    tokens = NBS * BLOCK
    half_w = (width // 2).astype(jnp.float32)
    per_frame_int = (height // 2) * (width // 2)
    per_frame = per_frame_int.astype(jnp.float32)
    live = frames * per_frame_int
    token_int = lax.broadcasted_iota(jnp.int32, (1, tokens), 1)
    token = token_int.astype(jnp.float32)
    frame_of = jnp.floor((token + 0.5) / jnp.full((1, tokens), per_frame))
    within = token - frame_of * per_frame
    row_of = jnp.floor((within + 0.5) / jnp.full((1, tokens), half_w))
    col_of = within - row_of * half_w
    source = (frame_of * frame_size + row_of * (2 * width_cap) + col_of * 2).astype(jnp.int32)
    source = jnp.where(token_int < live, source, -1)
    chosen = lax.broadcasted_iota(jnp.int32, (spots, tokens), 0) == source
    picked = mm(patches, jnp.where(chosen, 1.0, 0.0).astype(jnp.bfloat16))
    out_ref[:feats] = picked.astype(jnp.bfloat16)

    kind = lax.broadcasted_iota(jnp.int32, (XPAD - feats, BLOCK), 0)
    for b in range(NBS):
        count = jnp.clip(live - b * BLOCK, 0, BLOCK)
        info = jnp.where(
            kind == 0,
            plan_ref[0, 0, b, 0],
            jnp.where(kind == 1, plan_ref[0, 0, b, 1], jnp.where(kind == 2, count, 0)),
        )
        out_ref[feats:, b * BLOCK : (b + 1) * BLOCK] = info.astype(jnp.float32).astype(jnp.bfloat16)


def gram_kernel(embed_ref, first_ref, out_ref):
    feats, width = embed_ref.shape
    emb = embed_ref[...].astype(jnp.float32)
    emb = emb - jnp.sum(emb, axis=1, keepdims=True) / width
    both = jnp.concatenate(split_bf16(emb), axis=0)
    gram = mm(both, both, ((1,), (1,))) / width
    gram = gram[:feats] + gram[feats:]
    out_ref[...] = jnp.concatenate(split_bf16(gram[:, :feats] + gram[:, feats:]), axis=0)


def pack_kernel(evens, feats, q_gain_ref, k_gain_ref, gram_ref, *refs):
    here, near = refs[: len(evens)], refs[len(evens)]
    x_t_ref, x_ref, own_ref, key_mask_ref, own_mask_ref, gain_ref, rows_t = refs[len(evens) + 1 :]
    n_enc = 2 * len(evens)
    mine = lax.axis_index("enc")
    rows = n_enc * BLOCK
    lane = lax.broadcasted_iota(jnp.int32, (1, BLOCK), 1).astype(jnp.float32)
    extra = lax.broadcasted_iota(jnp.int32, (XPAD - feats, BLOCK), 0)
    found = []
    blocks = [(at, here[i][...]) for i, at in enumerate(evens)]
    blocks += [(at ^ 1, near[i]) for i, at in enumerate(evens)]
    for distance, block in blocks:
        source = mine ^ distance
        for b in range(NBS):
            tile = block[:, b * BLOCK : (b + 1) * BLOCK].astype(jnp.float32)
            owner, offset, count = (tile[feats + i : feats + i + 1] for i in range(3))
            owner = jnp.where(offset == 0.0, owner, -1.0)
            segment = jnp.where(lane < count, (source + 1).astype(jnp.float32), 0.0)
            found.append((owner, segment, tile[:feats]))
    at = lax.broadcasted_iota(jnp.int32, (feats, feats), 0)
    frm = lax.broadcasted_iota(jnp.int32, (feats, feats), 1)
    order = jnp.where(frm == (at % 4) * (feats // 4) + at // 4, 1.0, 0.0).astype(jnp.bfloat16)
    for o in range(n_enc):
        segment = jnp.zeros((1, BLOCK), jnp.float32)
        body = jnp.zeros((feats, BLOCK), jnp.float32)
        for owner, seg_of, tile in found:
            hit = owner == float(o)
            segment = segment + jnp.where(hit, seg_of, 0.0)
            body = body + jnp.where(hit, tile, 0.0)
        tail = jnp.where(extra == 0, 1.0, jnp.where(extra == 1, segment, 0.0))
        rows_t[:, o * BLOCK : (o + 1) * BLOCK] = jnp.concatenate(
            [body, tail, jnp.zeros((LANES - XPAD, BLOCK), jnp.float32)], axis=0
        )
    picked = mm(order, rows_t[:feats].astype(jnp.bfloat16))
    spread = mm(gram_ref[...], picked.astype(jnp.bfloat16))
    variance = jnp.sum((spread[:feats] + spread[feats:]) * picked, axis=0, keepdims=True)
    rows_t[:feats] = picked * lax.rsqrt(jnp.maximum(variance, 0.0) + eps_norm)
    x_t = rows_t[...]
    x_t_ref[...] = x_t[:APAD].astype(jnp.bfloat16)
    x_ref[...] = x_t.T.astype(jnp.bfloat16)
    group_t = lax.broadcasted_iota(jnp.int32, (LANES, rows), 0).astype(jnp.float32)
    key_mask_ref[...] = jnp.where(x_t[feats + 1 : feats + 2] == group_t, 0.0, 1.0).astype(jnp.bfloat16)
    own = rows_t[:, pl.ds(pl.multiple_of(mine * BLOCK, BLOCK), BLOCK)].T
    own_ref[...] = own.astype(jnp.bfloat16)
    group = lax.broadcasted_iota(jnp.int32, (BLOCK, LANES), 1).astype(jnp.float32)
    own_mask_ref[...] = jnp.where(own[:, feats + 1 : feats + 2] == group, -FAR, 0.0).astype(jnp.bfloat16)
    head_dim = q_gain_ref.shape[1]
    gain_ref[...] = q_gain_ref[...] * k_gain_ref[...] * (head_dim**-0.5 * math.log2(math.e))


def attend_heads(folds, place, x_t_ref, x_ref, own_ref, key_mask_ref, own_mask_ref, gain_ref):
    folds = list(folds)
    heads = range(len(folds))

    def side(part):
        return jnp.concatenate([fold[:, part * LANES : (part + 1) * LANES] for fold in folds], axis=1)

    def of(i):
        return slice(i * LANES, (i + 1) * LANES)

    keys = mm(side(1), x_t_ref[...], ((0,), (0,)))
    queries = mm(own_ref[:, :APAD], side(0))
    values = mm(x_ref[:, :APAD], side(2)).astype(jnp.bfloat16)
    gain, own_mask, key_mask = gain_ref[...], own_mask_ref[...], key_mask_ref[...]
    left, right = [], []
    for i in heads:
        key = keys[of(i)]
        square = jnp.sum(key * key, axis=0, keepdims=True) / LANES
        key = (key * lax.rsqrt(square + eps_norm)).astype(jnp.bfloat16)
        right.append(jnp.concatenate([key, key_mask], axis=0))
        query = queries[:, of(i)]
        square = jnp.sum(query * query, axis=1, keepdims=True) / LANES
        query = (query * lax.rsqrt(square + eps_norm) * gain).astype(jnp.bfloat16)
        left.append(jnp.concatenate([query, own_mask], axis=1))
    scores = [mm(left[i], right[i]) for i in heads]
    weights = [jnp.exp2(score).astype(jnp.bfloat16) for score in scores]
    ones = jnp.ones((values.shape[0], LANES), jnp.bfloat16)
    mixed = [mm(weights[i], jnp.concatenate([values[:, of(i)], ones], axis=1)) for i in heads]
    for i in heads:
        place(i, (mixed[i][:, :LANES] / mixed[i][:, LANES:]).astype(jnp.bfloat16))


def each_head(refs):
    for ref in refs:
        for i in range(ref.shape[0]):
            yield ref[i]


def attend_kernel(*refs):
    def place(i, result):
        refs[-1][:, i * LANES : (i + 1) * LANES] = result

    attend_heads(each_head(refs[6:-1]), place, *refs[:6])


def last_kernel(heads, lists, own_ref, got_ref, *refs):
    last_ref, near_ref, out_ref = refs[-3:]
    mine, slot = lax.axis_index("enc"), lax.axis_index("seq") & (heads - 1)
    core = mine & 1

    def put(base, partner, second, result):
        far, k = partner
        head = (base ^ far ^ second) * heads + (slot ^ k)
        out_ref[0, :, pl.ds(pl.multiple_of(head * LANES, LANES), LANES)] = result

    def partner(core, at):
        return tuple(jnp.where(core == 0, a, b) for a, b in zip(lists[0][at], lists[1][at]))

    for i in range(2):
        put(mine, (0, 0), i, own_ref[:, i * LANES : (i + 1) * LANES])
    for i in range(2 * len(lists[0])):
        put(mine, partner(core, i // 2), i % 2, got_ref[:, i * LANES : (i + 1) * LANES])

    def place(i, result):
        if i < 2 * len(lists[0]):
            put(mine ^ 1, partner(core ^ 1, i // 2), i % 2, result)
        else:
            put(mine | 1, lists[1][-1], i % 2, result)

    folds = list(each_head([near_ref.at[j] for j in range(len(lists[0]))]))
    for i in range(2):
        folds.append(jnp.where(core == 0, near_ref[len(lists[0]), i], last_ref[i]))
    attend_heads(folds, place, *refs[:6])


def vmem(count):
    return [pl.BlockSpec(memory_space=pltpu.VMEM)] * count


def hbm(count):
    return [pl.BlockSpec(memory_space=pltpu.HBM)] * count


def in_hbm(x):
    return pltpu.with_memory_space_constraint(x, pltpu.HBM)


def after(count):
    return [pl.BlockSpec(memory_space=pl.ANY)] * count


def call(kernel, ins, out_shape, scratch=(), cost=(1_000_000, 1_000_000)):
    return pl.pallas_call(
        kernel,
        in_specs=ins,
        out_specs=[pl.BlockSpec(memory_space=pltpu.VMEM)] * len(out_shape),
        out_shape=out_shape,
        scratch_shapes=list(scratch),
        compiler_params=pltpu.CompilerParams(vmem_limit_bytes=VMEM_LIMIT),
        cost_estimate=pl.CostEstimate(flops=cost[0], bytes_accessed=cost[1], transcendentals=0),
    )


def gate(x, *others):
    return pl.pallas_call(
        gate_kernel,
        in_specs=after(1 + len(others)),
        out_specs=after(1)[0],
        out_shape=jax.ShapeDtypeStruct(x.shape, x.dtype),
        input_output_aliases={0: 0},
        compiler_params=pltpu.CompilerParams(vmem_limit_bytes=VMEM_LIMIT),
    )(x, *others)


def exchange(x, axis, n, k):
    return lax.ppermute(x, axis, [(i, i ^ k) for i in range(n)])


def on_device(
    n_enc,
    n_seq,
    clip_features,
    clip_shape,
    packing,
    conv_weight,
    embed_weight,
    mod_shift,
    mod_scale,
    qkv_weight,
    q_gain,
    k_gain,
):
    caps = clip_features.shape[2:5]
    depth_all = clip_features.shape[5]
    cols = qkv_weight.shape[2]
    feats = embed_weight.shape[0]
    heads = cols // LANES
    rows = n_enc * BLOCK
    bf16, f32 = jnp.bfloat16, jnp.float32

    def folds(dtype, *lead):
        return jax.ShapeDtypeStruct((*lead, APAD, 3 * LANES), dtype)

    evens = [0]
    for bit in reversed(range(1, log2(n_enc))):
        evens += [at ^ (1 << bit) for at in evens]
    scale_rows, shift_rows = mod_scale.reshape(-1, LANES), mod_shift.reshape(-1, LANES)
    later = [
        clip_features.reshape(-1, depth_all),
        conv_weight.reshape(-1, depth_all),
        q_gain.reshape(1, -1),
        k_gain.reshape(1, -1),
    ]
    with jax.named_scope("fold"):
        embed, features, conv, q_gain, k_gain, keep, *sends = call(
            functools.partial(fold_kernel, len(later)),
            hbm(4 + len(later)),
            [jax.ShapeDtypeStruct(x.shape, x.dtype) for x in (embed_weight, *later)]
            + [folds(f32)]
            + [folds(bf16)] * max(heads - 1, 1),
            [
                pltpu.VMEM(scale_rows.shape, f32),
                pltpu.VMEM(shift_rows.shape, f32),
                pltpu.VMEM(qkv_weight.shape, bf16),
                pltpu.SemaphoreType.DMA((4 + len(later),)),
            ],
            cost=(200_000_000, 1_000_000),
        )(*map(in_hbm, (embed_weight, scale_rows, shift_rows, qkv_weight, *later)))

    with jax.named_scope("encode"):
        own_block = call(
            functools.partial(encode_kernel, caps),
            hbm(2) + vmem(2),
            [jax.ShapeDtypeStruct((XPAD, NBS * BLOCK), bf16)],
            [
                pltpu.SMEM(clip_shape.shape, jnp.int32),
                pltpu.SMEM(packing.shape, jnp.int32),
                pltpu.SemaphoreType.DMA((2,)),
            ],
            cost=(500_000_000, 2_000_000),
        )(in_hbm(clip_shape), in_hbm(packing), features, conv)[0]

    def add(keep, got, final, *first):
        shapes = [folds(bf16)] if final else [folds(f32), folds(bf16)]
        kernel = functools.partial(add_kernel, len(got), final)
        return call(kernel, vmem(1 + len(got)) + after(len(first)), shapes)(keep, *got, *first)

    with jax.named_scope("fold_sum"):
        if heads > 1:
            got = [exchange(sends[k - 1], "seq", n_seq, k) for k in range(1, heads)]
            keep, send = add(keep, got, False, own_block)
        else:
            send = sends[0]

    with jax.named_scope("gram"):
        gram = call(gram_kernel, vmem(1) + after(1), [jax.ShapeDtypeStruct((2 * feats, feats), bf16)])(embed, keep)[0]

    with jax.named_scope("tokens"):
        own_block = gate(own_block, keep)
        blocks = [own_block] + [exchange(own_block, "enc", n_enc, k) for k in evens[1:]]

    with jax.named_scope("fold_sum"):
        for bit in range(log2(heads), log2(n_seq)):
            got = exchange(send, "seq", n_seq, 1 << bit)
            if bit + 1 < log2(n_seq):
                keep, send = add(keep, [got], False, own_block)
            else:
                (fresh,) = add(keep, [got], True, gram, *blocks[1:])

    def stack(parts, first):
        shape = jax.ShapeDtypeStruct((len(parts), *parts[0].shape), bf16)
        kernel = functools.partial(stack_kernel, len(parts))
        return call(kernel, vmem(len(parts)) + after(len(first)), [shape])(*parts, *first)[0]

    partners = [(far, k) for far in evens for k in range(heads) if far or k]
    partners.sort(key=lambda p: p[0].bit_count() + p[1].bit_count())
    lists = (tuple(partners[: len(partners) // 2]), tuple(partners[len(partners) // 2 :]))
    assert len(lists[1]) == len(lists[0]) + 1

    def spread(x, at):
        pairs = []
        for e in range(n_enc):
            if at < len(lists[e & 1]):
                far, k = lists[e & 1][at]
                pairs += [(e * n_seq + i, (e ^ far) * n_seq + (i ^ k)) for i in range(n_seq)]
        return lax.ppermute(x, ("enc", "seq"), pairs)

    with jax.named_scope("gather"):
        near_blocks = exchange(gate(stack(blocks, []), fresh), "enc", n_enc, 1)
        pair = stack([fresh, exchange(fresh, "enc", n_enc, 1)], [])
        got = [spread(pair, at) for at in range(len(lists[1]))]

    with jax.named_scope("pack"):
        packed = call(
            functools.partial(pack_kernel, tuple(evens), feats),
            vmem(4 + len(evens)),
            [
                jax.ShapeDtypeStruct((APAD, rows), bf16),
                jax.ShapeDtypeStruct((rows, LANES), bf16),
                jax.ShapeDtypeStruct((BLOCK, LANES), bf16),
                jax.ShapeDtypeStruct((LANES, rows), bf16),
                jax.ShapeDtypeStruct((BLOCK, LANES), bf16),
                jax.ShapeDtypeStruct((1, LANES), f32),
            ],
            [pltpu.VMEM((LANES, rows), f32)],
        )(q_gain, k_gain, gram, *blocks, near_blocks)

    def attend(groups):
        count = sum(group.shape[0] for group in groups)
        return call(
            attend_kernel,
            vmem(6 + len(groups)),
            [jax.ShapeDtypeStruct((BLOCK, count * LANES), bf16)],
            cost=(count * 200_000_000, 1_000_000),
        )(*packed, *groups)[0]

    with jax.named_scope("attend"):
        own_done = attend([pair])
        near = exchange(stack(got, [own_done]), "enc", n_enc, 1)
        got_done = attend(got[:-1])
        return call(
            functools.partial(last_kernel, heads, lists),
            vmem(10),
            [jax.ShapeDtypeStruct((1, BLOCK, n_enc * cols), bf16)],
            cost=(1_600_000_000, 2_000_000),
        )(own_done, got_done, *packed, got[-1], near)[0]


def solution(mesh):
    return jax.shard_map(
        functools.partial(on_device, mesh.shape["enc"], mesh.shape["seq"]),
        mesh=mesh,
        in_specs=(
            P("enc", "seq", None, None, None, None),
            P("enc", "seq", None),
            P("enc", "seq", None, None),
            P(),
            P(),
            P(),
            P(),
            P(None, "seq", "enc"),
            P(),
            P(),
        ),
        out_specs=P("seq", "enc", None),
        check_vma=False,
    )
```

```python
import functools
import math

import jax
import jax.numpy as jnp
from jax import lax
from jax.experimental import pallas as pl
from jax.experimental.pallas import tpu as pltpu
from jax.sharding import PartitionSpec as P

BLOCK = 128
NBS = 2
LANES = 128
APAD = 72
eps_norm = 1e-06
FAR = 2.0**20
VMEM_LIMIT = 48 * 1024 * 1024


def mm(a, b, dims=((1,), (0,)), precision=None):
    return lax.dot_general(a, b, (dims, ((), ())), preferred_element_type=jnp.float32, precision=precision)


def split_bf16(x):
    hi = x.astype(jnp.bfloat16)
    return hi, (x - hi.astype(jnp.float32)).astype(jnp.bfloat16)


def log2(n):
    bits = n.bit_length() - 1
    assert 1 << bits == n
    return bits


def fetch(pairs, sems):
    copies = [pltpu.make_async_copy(src, dst, sems.at[i]) for i, (src, dst) in enumerate(pairs)]
    for copy in copies:
        copy.start()
    return copies


def fold_kernel(count, embed_hbm, scale_hbm, shift_hbm, w_hbm, *refs):
    later_hbm, embed_ref, later, keep_ref, sends = refs[:count], refs[count], refs[count + 1 : 2 * count + 1], refs[2 * count + 1], refs[2 * count + 2 : -4]
    scale_ref, shift_ref, w_ref, sems = refs[-4:]
    copies = fetch(
        [(embed_hbm, embed_ref), (scale_hbm, scale_ref), (shift_hbm, shift_ref), (w_hbm, w_ref)]
        + list(zip(later_hbm, later)),
        sems,
    )
    me = lax.axis_index("seq")
    _, depth, cols = w_ref.shape
    feats = embed_ref.shape[0]
    heads = cols // LANES
    for copy in copies[:3]:
        copy.wait()
    mean = jnp.sum(embed_ref[...].astype(jnp.float32), axis=1, keepdims=True) / embed_ref.shape[1]
    span = max(depth, LANES)
    chunks = span // LANES
    first = (me * depth) // LANES
    emb = embed_ref[:, pl.ds(pl.multiple_of(first * LANES, LANES), span)].astype(jnp.float32) - mean
    scale = jnp.concatenate([scale_ref[pl.ds(first + i, 1), :] for i in range(chunks)], axis=1)
    shift = jnp.concatenate([shift_ref[pl.ds(first + i, 1), :] for i in range(chunks)], axis=1)
    left = jnp.concatenate(
        [emb * (1.0 + scale), shift, jnp.zeros((APAD - feats - 1, span), jnp.float32)], axis=0
    )
    if depth < LANES:
        low = me * depth - first * LANES
        lane = lax.broadcasted_iota(jnp.int32, left.shape, 1)
        left = jnp.where((lane >= low) & (lane < low + depth), left, 0.0)
    hi, lo = split_bf16(left)
    both = jnp.concatenate([hi, lo], axis=0)
    copies[3].wait()

    def product(head):
        start = pl.multiple_of(head * LANES, LANES)
        right = jnp.concatenate([w_ref[part, :, pl.ds(start, LANES)] for part in range(3)], axis=1)
        right = jnp.concatenate([right] * (span // depth), axis=0)
        total = mm(both, right)
        return total[:APAD] + total[APAD:]

    slot = me & (heads - 1)
    for k in range(1, heads):
        sends[k - 1][...] = product(slot ^ k).astype(jnp.bfloat16)
    total = product(slot)
    keep_ref[...] = total
    if heads == 1:
        sends[0][...] = total.astype(jnp.bfloat16)
    for copy in copies[4:]:
        copy.wait()


def add_kernel(count, keep_in, *refs):
    total = keep_in[...]
    for ref in refs[:count]:
        total = total + ref[...].astype(jnp.float32)
    refs[-2][...] = total
    refs[-1][...] = total.astype(jnp.bfloat16)


def last_add_kernel(count, keep_in, got_ref, *refs):
    total = (keep_in[...] + got_ref[...].astype(jnp.float32)).astype(jnp.bfloat16)
    out_ref, swap_ref = refs[-2:]
    out_ref[...] = total
    swap_ref[0] = total
    for i in range(count):
        width = refs[i].shape[1]
        swap_ref[1 + i, :, :width] = refs[i][...]
        swap_ref[1 + i, :, width:] = jnp.zeros((total.shape[0], total.shape[1] - width), jnp.bfloat16)


def stack_kernel(count, *refs):
    for i, ref in enumerate(refs[:count]):
        refs[-1][i] = ref[...]


def pair_kernel(own_ref, swapped_ref, out_ref):
    out_ref[0] = own_ref[...]
    out_ref[1] = swapped_ref[0]


def gate_kernel(*refs):
    pass


def encode_kernel(caps, shape_hbm, plan_hbm, feat_ref, conv_ref, out_ref, shape_ref, plan_ref, sems):
    copies = fetch([(shape_hbm, shape_ref), (plan_hbm, plan_ref)], sems)
    frames_cap, height_cap, width_cap = caps
    spots = frames_cap * height_cap * width_cap
    frame_size = height_cap * width_cap
    latent_ch = conv_ref.shape[0] // 27
    feats = 4 * latent_ch
    taps = mm(conv_ref[...], feat_ref[...], ((1,), (1,)))
    copies[0].wait()
    copies[1].wait()
    frames, height, width = shape_ref[0, 0, 0], shape_ref[0, 0, 1], shape_ref[0, 0, 2]
    spot = lax.broadcasted_iota(jnp.int32, (1, spots), 1)
    frame_ix = spot // frame_size
    row_ix = (spot % frame_size) // width_cap
    col_ix = spot % width_cap
    inside = (frame_ix < frames) & (row_ix < height) & (col_ix < width)
    taps = jnp.where(inside, taps, 0.0)

    def tap(a, b, j):
        at = (9 * a + 3 * b + j) * latent_ch
        return taps[at : at + latent_ch]

    def later(x, by):
        zeros = jnp.zeros((latent_ch, by * frame_size), jnp.float32)
        return jnp.concatenate([zeros, x[:, : spots - by * frame_size]], axis=1)

    def over_frames(b, j):
        return tap(2, b, j) + later(tap(1, b, j), 1) + later(tap(0, b, j), 2)

    def over_rows(j):
        above = pltpu.roll(over_frames(0, j), width_cap, 1)
        below = pltpu.roll(over_frames(2, j), spots - width_cap, 1)
        return (
            over_frames(1, j)
            + jnp.where(row_ix >= 1, above, 0.0)
            + jnp.where(row_ix < height_cap - 1, below, 0.0)
        )

    latent = (
        over_rows(1)
        + jnp.where(col_ix >= 1, pltpu.roll(over_rows(0), 1, 1), 0.0)
        + jnp.where(col_ix < width_cap - 1, pltpu.roll(over_rows(2), spots - 1, 1), 0.0)
    )
    latent = latent.astype(jnp.bfloat16).astype(jnp.float32)
    shifted = [latent] + [pltpu.roll(latent, spots - by, 1) for by in (1, width_cap, width_cap + 1)]
    patches = jnp.concatenate(shifted, axis=0).astype(jnp.bfloat16)

    tokens = NBS * BLOCK
    half_w = (width // 2).astype(jnp.float32)
    per_frame_int = (height // 2) * (width // 2)
    per_frame = per_frame_int.astype(jnp.float32)
    live = frames * per_frame_int
    token_int = lax.broadcasted_iota(jnp.int32, (1, tokens), 1)
    token = token_int.astype(jnp.float32)
    frame_of = jnp.floor((token + 0.5) / jnp.full((1, tokens), per_frame))
    within = token - frame_of * per_frame
    row_of = jnp.floor((within + 0.5) / jnp.full((1, tokens), half_w))
    col_of = within - row_of * half_w
    source = (frame_of * frame_size + row_of * (2 * width_cap) + col_of * 2).astype(jnp.int32)
    source = jnp.where(token_int < live, source, -1)
    chosen = lax.broadcasted_iota(jnp.int32, (spots, tokens), 0) == source
    picked = mm(patches, jnp.where(chosen, 1.0, 0.0).astype(jnp.bfloat16))
    kind = lax.broadcasted_iota(jnp.int32, (APAD - feats, BLOCK), 0)
    infos = []
    for b in range(NBS):
        count = jnp.clip(live - b * BLOCK, 0, BLOCK)
        info = jnp.where(
            kind == 0,
            plan_ref[0, 0, b, 0],
            jnp.where(kind == 1, plan_ref[0, 0, b, 1], jnp.where(kind == 2, count, 0)),
        )
        infos.append(info.astype(jnp.float32))
    info = jnp.concatenate(infos, axis=1)
    out_ref[...] = jnp.concatenate([picked, info], axis=0).astype(jnp.bfloat16)


def gram_kernel(embed_ref, first_ref, out_ref):
    feats, width = embed_ref.shape
    emb = embed_ref[...].astype(jnp.float32)
    emb = emb - jnp.sum(emb, axis=1, keepdims=True) / width
    both = jnp.concatenate(split_bf16(emb), axis=0)
    gram = mm(both, both, ((1,), (1,))) / width
    gram = gram[:feats] + gram[feats:]
    out_ref[...] = jnp.concatenate(split_bf16(gram[:, :feats] + gram[:, feats:]), axis=0)


def pack_kernel(evens, feats, q_gain_ref, k_gain_ref, gram_ref, *refs):
    here, near = refs[: len(evens)], refs[len(evens)]
    x_t_ref, x_ref, own_ref, key_mask_ref, own_mask_ref, gain_ref, rows_t = refs[len(evens) + 1 :]
    n_enc = 2 * len(evens)
    mine = lax.axis_index("enc")
    rows = n_enc * BLOCK
    lane = lax.broadcasted_iota(jnp.int32, (1, BLOCK), 1).astype(jnp.float32)
    extra = lax.broadcasted_iota(jnp.int32, (APAD - feats, BLOCK), 0)
    found = []
    blocks = [(at, here[i][...]) for i, at in enumerate(evens)]
    blocks += [(at ^ 1, near[1 + i]) for i, at in enumerate(evens)]
    for distance, block in blocks:
        source = mine ^ distance
        for b in range(NBS):
            tile = block[:, b * BLOCK : (b + 1) * BLOCK].astype(jnp.float32)
            owner, offset, count = (tile[feats + i : feats + i + 1] for i in range(3))
            owner = jnp.where(offset == 0.0, owner, -1.0)
            segment = jnp.where(lane < count, (source + 1).astype(jnp.float32), 0.0)
            found.append((owner, segment, tile[:feats]))
    at = lax.broadcasted_iota(jnp.int32, (feats, feats), 0)
    frm = lax.broadcasted_iota(jnp.int32, (feats, feats), 1)
    order = jnp.where(frm == (at % 4) * (feats // 4) + at // 4, 1.0, 0.0).astype(jnp.bfloat16)
    for o in range(n_enc):
        segment = jnp.zeros((1, BLOCK), jnp.float32)
        body = jnp.zeros((feats, BLOCK), jnp.float32)
        for owner, seg_of, tile in found:
            hit = owner == float(o)
            segment = segment + jnp.where(hit, seg_of, 0.0)
            body = body + jnp.where(hit, tile, 0.0)
        tail = jnp.where(extra == 0, 1.0, jnp.where(extra == 1, segment, 0.0))
        rows_t[:, o * BLOCK : (o + 1) * BLOCK] = jnp.concatenate(
            [body, tail, jnp.zeros((LANES - APAD, BLOCK), jnp.float32)], axis=0
        )
    picked = mm(order, rows_t[:feats].astype(jnp.bfloat16))
    spread = mm(gram_ref[...], picked.astype(jnp.bfloat16))
    variance = jnp.sum((spread[:feats] + spread[feats:]) * picked, axis=0, keepdims=True)
    rows_t[:feats] = picked * lax.rsqrt(jnp.maximum(variance, 0.0) + eps_norm)
    x_t = rows_t[...]
    x_t_ref[...] = x_t[:APAD].astype(jnp.bfloat16)
    x_ref[...] = x_t.T.astype(jnp.bfloat16)
    group_t = lax.broadcasted_iota(jnp.int32, (LANES, rows), 0).astype(jnp.float32)
    key_mask_ref[...] = jnp.where(x_t[feats + 1 : feats + 2] == group_t, 0.0, 1.0).astype(jnp.bfloat16)
    own = rows_t[:, pl.ds(pl.multiple_of(mine * BLOCK, BLOCK), BLOCK)].T
    own_ref[...] = own.astype(jnp.bfloat16)
    group = lax.broadcasted_iota(jnp.int32, (BLOCK, LANES), 1).astype(jnp.float32)
    own_mask_ref[...] = jnp.where(own[:, feats + 1 : feats + 2] == group, -FAR, 0.0).astype(jnp.bfloat16)
    head_dim = q_gain_ref.shape[1]
    gain_ref[...] = q_gain_ref[...] * k_gain_ref[...] * (head_dim**-0.5 * math.log2(math.e))


def attend_heads(folds, place, x_t_ref, x_ref, own_ref, key_mask_ref, own_mask_ref, gain_ref):
    folds = list(folds)
    heads = range(len(folds))

    def side(part):
        return jnp.concatenate([fold[:, part * LANES : (part + 1) * LANES] for fold in folds], axis=1)

    def of(i):
        return slice(i * LANES, (i + 1) * LANES)

    keys = mm(side(1), x_t_ref[...], ((0,), (0,)))
    queries = mm(own_ref[:, :APAD], side(0))
    values = mm(x_ref[:, :APAD], side(2)).astype(jnp.bfloat16)
    gain, own_mask, key_mask = gain_ref[...], own_mask_ref[...], key_mask_ref[...]
    left, right = [], []
    for i in heads:
        key = keys[of(i)]
        square = jnp.sum(key * key, axis=0, keepdims=True) / LANES
        key = (key * lax.rsqrt(square + eps_norm)).astype(jnp.bfloat16)
        right.append(jnp.concatenate([key, key_mask], axis=0))
        query = queries[:, of(i)]
        square = jnp.sum(query * query, axis=1, keepdims=True) / LANES
        query = (query * lax.rsqrt(square + eps_norm) * gain).astype(jnp.bfloat16)
        left.append(jnp.concatenate([query, own_mask], axis=1))
    scores = [mm(left[i], right[i]) for i in heads]
    weights = [jnp.exp2(score).astype(jnp.bfloat16) for score in scores]
    ones = jnp.ones((values.shape[0], LANES), jnp.bfloat16)
    mixed = [mm(weights[i], jnp.concatenate([values[:, of(i)], ones], axis=1)) for i in heads]
    for i in heads:
        place(i, (mixed[i][:, :LANES] / mixed[i][:, LANES:]).astype(jnp.bfloat16))


def each_head(refs):
    for ref in refs:
        for i in range(ref.shape[0]):
            yield ref[i]


def attend_kernel(*refs):
    def place(i, result):
        refs[-1][:, i * LANES : (i + 1) * LANES] = result

    attend_heads(each_head(refs[6:-1]), place, *refs[:6])


def last_kernel(heads, lists, own_ref, got_ref, *refs):
    last_ref, near_ref, out_ref, done, sems = refs[-5:]
    mine, slot = lax.axis_index("enc"), lax.axis_index("seq") & (heads - 1)
    core, half = mine & 1, len(lists[1])
    copies = []

    def put(base, partner, second, result):
        far, k = partner
        head = (base ^ far ^ second) * heads + (slot ^ k)
        column = pl.ds(pl.multiple_of(head * LANES, LANES), LANES)
        copies.append(pltpu.make_async_copy(result, out_ref.at[0, :, column], sems.at[len(copies)]))
        copies[-1].start()

    def partner(core, at):
        return tuple(jnp.where(core == 0, a, b) for a, b in zip(lists[0][at], lists[1][at]))

    for i in range(2):
        put(mine, (0, 0), i, own_ref.at[:, i * LANES : (i + 1) * LANES])
    for i in range(2 * half):
        put(mine, partner(core, i // 2), i % 2, got_ref.at[:, i * LANES : (i + 1) * LANES])

    def place(i, result):
        done[i] = result
        if i < 2 * half:
            put(mine ^ 1, partner(core ^ 1, i // 2), i % 2, done.at[i])
        else:
            put(mine & ~1, lists[0][-1], i % 2, done.at[i])

    folds = list(each_head([near_ref.at[j] for j in range(half)]))
    for i in range(2):
        folds.append(jnp.where(core == 0, last_ref[i], near_ref[half, i]))
    attend_heads(folds, place, *refs[:6])
    for copy in copies:
        copy.wait()


def vmem(count):
    return [pl.BlockSpec(memory_space=pltpu.VMEM)] * count


def hbm(count):
    return [pl.BlockSpec(memory_space=pltpu.HBM)] * count


def in_hbm(x):
    return pltpu.with_memory_space_constraint(x, pltpu.HBM)


def after(count):
    return [pl.BlockSpec(memory_space=pl.ANY)] * count


def call(kernel, ins, out_shape, scratch=(), cost=(1_000_000, 1_000_000)):
    return pl.pallas_call(
        kernel,
        in_specs=ins,
        out_specs=[pl.BlockSpec(memory_space=pltpu.VMEM)] * len(out_shape),
        out_shape=out_shape,
        scratch_shapes=list(scratch),
        compiler_params=pltpu.CompilerParams(vmem_limit_bytes=VMEM_LIMIT),
        cost_estimate=pl.CostEstimate(flops=cost[0], bytes_accessed=cost[1], transcendentals=0),
    )


def gate(x, *others):
    return pl.pallas_call(
        gate_kernel,
        in_specs=after(1 + len(others)),
        out_specs=after(1)[0],
        out_shape=jax.ShapeDtypeStruct(x.shape, x.dtype),
        input_output_aliases={0: 0},
        compiler_params=pltpu.CompilerParams(vmem_limit_bytes=VMEM_LIMIT),
    )(x, *others)


def exchange(x, axis, n, k):
    return lax.ppermute(x, axis, [(i, i ^ k) for i in range(n)])


def on_device(
    n_enc,
    n_seq,
    clip_features,
    clip_shape,
    packing,
    conv_weight,
    embed_weight,
    mod_shift,
    mod_scale,
    qkv_weight,
    q_gain,
    k_gain,
):
    caps = clip_features.shape[2:5]
    depth_all = clip_features.shape[5]
    cols = qkv_weight.shape[2]
    feats = embed_weight.shape[0]
    heads = cols // LANES
    rows = n_enc * BLOCK
    bf16, f32 = jnp.bfloat16, jnp.float32

    def folds(dtype, *lead):
        return jax.ShapeDtypeStruct((*lead, APAD, 3 * LANES), dtype)

    evens = [0]
    for bit in reversed(range(1, log2(n_enc))):
        evens += [at ^ (1 << bit) for at in evens]
    scale_rows, shift_rows = mod_scale.reshape(-1, LANES), mod_shift.reshape(-1, LANES)
    later = [
        clip_features.reshape(-1, depth_all),
        conv_weight.reshape(-1, depth_all),
        q_gain.reshape(1, -1),
        k_gain.reshape(1, -1),
    ]
    with jax.named_scope("fold"):
        embed, features, conv, q_gain, k_gain, keep, *sends = call(
            functools.partial(fold_kernel, len(later)),
            hbm(4 + len(later)),
            [jax.ShapeDtypeStruct(x.shape, x.dtype) for x in (embed_weight, *later)]
            + [folds(f32)]
            + [folds(bf16)] * max(heads - 1, 1),
            [
                pltpu.VMEM(scale_rows.shape, f32),
                pltpu.VMEM(shift_rows.shape, f32),
                pltpu.VMEM(qkv_weight.shape, bf16),
                pltpu.SemaphoreType.DMA((4 + len(later),)),
            ],
            cost=(200_000_000, 1_000_000),
        )(*map(in_hbm, (embed_weight, scale_rows, shift_rows, qkv_weight, *later)))

    with jax.named_scope("encode"):
        own_block = call(
            functools.partial(encode_kernel, caps),
            hbm(2) + vmem(2),
            [jax.ShapeDtypeStruct((APAD, NBS * BLOCK), bf16)],
            [
                pltpu.SMEM(clip_shape.shape, jnp.int32),
                pltpu.SMEM(packing.shape, jnp.int32),
                pltpu.SemaphoreType.DMA((2,)),
            ],
            cost=(500_000_000, 2_000_000),
        )(in_hbm(clip_shape), in_hbm(packing), features, conv)[0]

    def add(keep, got, first):
        kernel = functools.partial(add_kernel, len(got))
        return call(kernel, vmem(1 + len(got)) + after(1), [folds(f32), folds(bf16)])(keep, *got, first)

    with jax.named_scope("fold_sum"):
        if heads > 1:
            got = [exchange(sends[k - 1], "seq", n_seq, k) for k in range(1, heads)]
            keep, send = add(keep, got, own_block)
        else:
            send = sends[0]

    with jax.named_scope("gram"):
        gram = call(gram_kernel, vmem(1) + after(1), [jax.ShapeDtypeStruct((2 * feats, feats), bf16)])(embed, keep)[0]

    with jax.named_scope("tokens"):
        own_block = gate(own_block, keep)
        blocks = [own_block] + [exchange(own_block, "enc", n_enc, k) for k in evens[1:]]

    with jax.named_scope("fold_sum"):
        for bit in range(log2(heads), log2(n_seq)):
            got = exchange(send, "seq", n_seq, 1 << bit)
            if bit + 1 < log2(n_seq):
                keep, send = add(keep, [got], own_block)
            else:
                fresh, swap = call(
                    functools.partial(last_add_kernel, len(blocks)),
                    vmem(2 + len(blocks)) + after(1),
                    [folds(bf16), folds(bf16, 1 + len(blocks))],
                )(keep, got, *blocks, gram)

    def stack(parts, first):
        shape = jax.ShapeDtypeStruct((len(parts), *parts[0].shape), bf16)
        kernel = functools.partial(stack_kernel, len(parts))
        return call(kernel, vmem(len(parts)) + after(len(first)), [shape])(*parts, *first)[0]

    partners = [(far, k) for far in evens for k in range(heads) if far or k]
    partners.sort(key=lambda p: (p[0].bit_count() + p[1].bit_count(), p[0]))
    half = len(partners) // 2
    lists = (tuple(partners[: half + 1]), tuple(partners[half + 1 :]))
    assert len(lists[1]) == half

    def spread(x, at):
        pairs = []
        for e in range(n_enc):
            if at < len(lists[e & 1]):
                far, k = lists[e & 1][at]
                pairs += [(e * n_seq + i, (e ^ far) * n_seq + (i ^ k)) for i in range(n_seq)]
        return lax.ppermute(x, ("enc", "seq"), pairs)

    with jax.named_scope("gather"):
        swapped = exchange(swap, "enc", n_enc, 1)
        pair = call(pair_kernel, vmem(2), [folds(bf16, 2)])(fresh, swapped)[0]
        got = [spread(pair, at) for at in range(half + 1)]

    with jax.named_scope("pack"):
        packed = call(
            functools.partial(pack_kernel, tuple(evens), feats),
            vmem(4 + len(evens)),
            [
                jax.ShapeDtypeStruct((APAD, rows), bf16),
                jax.ShapeDtypeStruct((rows, LANES), bf16),
                jax.ShapeDtypeStruct((BLOCK, LANES), bf16),
                jax.ShapeDtypeStruct((LANES, rows), bf16),
                jax.ShapeDtypeStruct((BLOCK, LANES), bf16),
                jax.ShapeDtypeStruct((1, LANES), f32),
            ],
            [pltpu.VMEM((LANES, rows), f32)],
        )(q_gain, k_gain, gram, *blocks, swapped)

    def attend(groups):
        count = sum(group.shape[0] for group in groups)
        return call(
            attend_kernel,
            vmem(6 + len(groups)),
            [jax.ShapeDtypeStruct((BLOCK, count * LANES), bf16)],
            cost=(count * 200_000_000, 1_000_000),
        )(*packed, *groups)[0]

    with jax.named_scope("attend"):
        own_done = attend([pair])
        near = exchange(stack(got, [own_done]), "enc", n_enc, 1)
        got_done = attend(got[:-1])
        total = n_enc * heads
        return pl.pallas_call(
            functools.partial(last_kernel, heads, lists),
            in_specs=vmem(10),
            out_specs=hbm(1)[0],
            out_shape=jax.ShapeDtypeStruct((1, BLOCK, n_enc * cols), bf16),
            scratch_shapes=[pltpu.VMEM((2 * half + 2, BLOCK, LANES), bf16), pltpu.SemaphoreType.DMA((total,))],
            compiler_params=pltpu.CompilerParams(vmem_limit_bytes=VMEM_LIMIT),
            cost_estimate=pl.CostEstimate(flops=1_600_000_000, bytes_accessed=2_000_000, transcendentals=0),
        )(own_done, got_done, *packed, got[-1], near)


def solution(mesh):
    return jax.shard_map(
        functools.partial(on_device, mesh.shape["enc"], mesh.shape["seq"]),
        mesh=mesh,
        in_specs=(
            P("enc", "seq", None, None, None, None),
            P("enc", "seq", None),
            P("enc", "seq", None, None),
            P(),
            P(),
            P(),
            P(),
            P(None, "seq", "enc"),
            P(),
            P(),
        ),
        out_specs=P("seq", "enc", None),
        check_vma=False,
    )
```

```python
import functools
import math

import jax
import jax.numpy as jnp
from jax import lax
from jax.experimental import pallas as pl
from jax.experimental.pallas import tpu as pltpu
from jax.sharding import PartitionSpec as P

BLOCK = 128
NBS = 2
LANES = 128
APAD = 72
eps_norm = 1e-06
FAR = 2.0**20
VMEM_LIMIT = 48 * 1024 * 1024


def mm(a, b, dims=((1,), (0,)), precision=None):
    return lax.dot_general(a, b, (dims, ((), ())), preferred_element_type=jnp.float32, precision=precision)


def split_bf16(x):
    hi = x.astype(jnp.bfloat16)
    return hi, (x - hi.astype(jnp.float32)).astype(jnp.bfloat16)


def log2(n):
    bits = n.bit_length() - 1
    assert 1 << bits == n
    return bits


def fetch(pairs, sems):
    copies = [pltpu.make_async_copy(src, dst, sems.at[i]) for i, (src, dst) in enumerate(pairs)]
    for copy in copies:
        copy.start()
    return copies


def fold_kernel(count, embed_hbm, scale_hbm, shift_hbm, w_hbm, *refs):
    later_hbm, embed_ref, later, keep_ref, sends = refs[:count], refs[count], refs[count + 1 : 2 * count + 1], refs[2 * count + 1], refs[2 * count + 2 : -4]
    scale_ref, shift_ref, w_ref, sems = refs[-4:]
    copies = fetch(
        [(embed_hbm, embed_ref), (scale_hbm, scale_ref), (shift_hbm, shift_ref), (w_hbm, w_ref)]
        + list(zip(later_hbm, later)),
        sems,
    )
    me = lax.axis_index("seq")
    _, depth, cols = w_ref.shape
    feats = embed_ref.shape[0]
    heads = cols // LANES
    for copy in copies[:3]:
        copy.wait()
    mean = jnp.sum(embed_ref[...].astype(jnp.float32), axis=1, keepdims=True) / embed_ref.shape[1]
    span = max(depth, LANES)
    chunks = span // LANES
    first = (me * depth) // LANES
    emb = embed_ref[:, pl.ds(pl.multiple_of(first * LANES, LANES), span)].astype(jnp.float32) - mean
    scale = jnp.concatenate([scale_ref[pl.ds(first + i, 1), :] for i in range(chunks)], axis=1)
    shift = jnp.concatenate([shift_ref[pl.ds(first + i, 1), :] for i in range(chunks)], axis=1)
    left = jnp.concatenate(
        [emb * (1.0 + scale), shift, jnp.zeros((APAD - feats - 1, span), jnp.float32)], axis=0
    )
    if depth < LANES:
        low = me * depth - first * LANES
        lane = lax.broadcasted_iota(jnp.int32, left.shape, 1)
        left = jnp.where((lane >= low) & (lane < low + depth), left, 0.0)
    hi, lo = split_bf16(left)
    both = jnp.concatenate([hi, lo], axis=0)
    copies[3].wait()

    def product(head):
        start = pl.multiple_of(head * LANES, LANES)
        right = jnp.concatenate([w_ref[part, :, pl.ds(start, LANES)] for part in range(3)], axis=1)
        right = jnp.concatenate([right] * (span // depth), axis=0)
        total = mm(both, right)
        return total[:APAD] + total[APAD:]

    slot = me & (heads - 1)
    for k in range(1, heads):
        sends[k - 1][...] = product(slot ^ k).astype(jnp.bfloat16)
    total = product(slot)
    keep_ref[...] = total
    if heads == 1:
        sends[0][...] = total.astype(jnp.bfloat16)
    for copy in copies[4:]:
        copy.wait()


def add_kernel(count, keep_in, *refs):
    total = keep_in[...]
    for ref in refs[:count]:
        total = total + ref[...].astype(jnp.float32)
    refs[-2][...] = total
    refs[-1][...] = total.astype(jnp.bfloat16)


def last_add_kernel(count, keep_in, got_ref, *refs):
    total = (keep_in[...] + got_ref[...].astype(jnp.float32)).astype(jnp.bfloat16)
    out_ref, swap_ref = refs[-2:]
    out_ref[...] = total
    swap_ref[0] = total
    for i in range(count):
        width = refs[i].shape[1]
        swap_ref[1 + i, :, :width] = refs[i][...]
        swap_ref[1 + i, :, width:] = jnp.zeros((total.shape[0], total.shape[1] - width), jnp.bfloat16)


def bundle_kernel(count, *refs):
    at = 0
    for ref in refs[:count]:
        for i in range(ref.shape[0] if len(ref.shape) == 3 else 1):
            refs[-1][at] = ref[i] if len(ref.shape) == 3 else ref[...]
            at += 1


def pair_kernel(own_ref, swapped_ref, out_ref):
    out_ref[0] = own_ref[...]
    out_ref[1] = swapped_ref[0]


def gate_kernel(*refs):
    pass


def encode_kernel(caps, shape_hbm, plan_hbm, feat_ref, conv_ref, out_ref, shape_ref, plan_ref, sems):
    copies = fetch([(shape_hbm, shape_ref), (plan_hbm, plan_ref)], sems)
    frames_cap, height_cap, width_cap = caps
    spots = frames_cap * height_cap * width_cap
    frame_size = height_cap * width_cap
    latent_ch = conv_ref.shape[0] // 27
    feats = 4 * latent_ch
    taps = mm(conv_ref[...], feat_ref[...], ((1,), (1,)))
    copies[0].wait()
    copies[1].wait()
    frames, height, width = shape_ref[0, 0, 0], shape_ref[0, 0, 1], shape_ref[0, 0, 2]
    spot = lax.broadcasted_iota(jnp.int32, (1, spots), 1)
    frame_ix = spot // frame_size
    row_ix = (spot % frame_size) // width_cap
    col_ix = spot % width_cap
    inside = (frame_ix < frames) & (row_ix < height) & (col_ix < width)
    taps = jnp.where(inside, taps, 0.0)

    def tap(a, b, j):
        at = (9 * a + 3 * b + j) * latent_ch
        return taps[at : at + latent_ch]

    def later(x, by):
        zeros = jnp.zeros((latent_ch, by * frame_size), jnp.float32)
        return jnp.concatenate([zeros, x[:, : spots - by * frame_size]], axis=1)

    def over_frames(b, j):
        return tap(2, b, j) + later(tap(1, b, j), 1) + later(tap(0, b, j), 2)

    def over_rows(j):
        above = pltpu.roll(over_frames(0, j), width_cap, 1)
        below = pltpu.roll(over_frames(2, j), spots - width_cap, 1)
        return (
            over_frames(1, j)
            + jnp.where(row_ix >= 1, above, 0.0)
            + jnp.where(row_ix < height_cap - 1, below, 0.0)
        )

    latent = (
        over_rows(1)
        + jnp.where(col_ix >= 1, pltpu.roll(over_rows(0), 1, 1), 0.0)
        + jnp.where(col_ix < width_cap - 1, pltpu.roll(over_rows(2), spots - 1, 1), 0.0)
    )
    latent = latent.astype(jnp.bfloat16).astype(jnp.float32)
    shifted = [latent] + [pltpu.roll(latent, spots - by, 1) for by in (1, width_cap, width_cap + 1)]
    patches = jnp.concatenate(shifted, axis=0).astype(jnp.bfloat16)

    tokens = NBS * BLOCK
    half_w = (width // 2).astype(jnp.float32)
    per_frame_int = (height // 2) * (width // 2)
    per_frame = per_frame_int.astype(jnp.float32)
    live = frames * per_frame_int
    token_int = lax.broadcasted_iota(jnp.int32, (1, tokens), 1)
    token = token_int.astype(jnp.float32)
    frame_of = jnp.floor((token + 0.5) / jnp.full((1, tokens), per_frame))
    within = token - frame_of * per_frame
    row_of = jnp.floor((within + 0.5) / jnp.full((1, tokens), half_w))
    col_of = within - row_of * half_w
    source = (frame_of * frame_size + row_of * (2 * width_cap) + col_of * 2).astype(jnp.int32)
    source = jnp.where(token_int < live, source, -1)
    chosen = lax.broadcasted_iota(jnp.int32, (spots, tokens), 0) == source
    picked = mm(patches, jnp.where(chosen, 1.0, 0.0).astype(jnp.bfloat16))
    kind = lax.broadcasted_iota(jnp.int32, (APAD - feats, BLOCK), 0)
    infos = []
    for b in range(NBS):
        count = jnp.clip(live - b * BLOCK, 0, BLOCK)
        info = jnp.where(
            kind == 0,
            plan_ref[0, 0, b, 0],
            jnp.where(kind == 1, plan_ref[0, 0, b, 1], jnp.where(kind == 2, count, 0)),
        )
        infos.append(info.astype(jnp.float32))
    info = jnp.concatenate(infos, axis=1)
    out_ref[...] = jnp.concatenate([picked, info], axis=0).astype(jnp.bfloat16)


def gram_kernel(embed_ref, first_ref, out_ref):
    feats, width = embed_ref.shape
    emb = embed_ref[...].astype(jnp.float32)
    emb = emb - jnp.sum(emb, axis=1, keepdims=True) / width
    both = jnp.concatenate(split_bf16(emb), axis=0)
    gram = mm(both, both, ((1,), (1,))) / width
    gram = gram[:feats] + gram[feats:]
    out_ref[...] = jnp.concatenate(split_bf16(gram[:, :feats] + gram[:, feats:]), axis=0)


def pack_kernel(evens, feats, q_gain_ref, k_gain_ref, gram_ref, *refs):
    here, near = refs[: len(evens)], refs[len(evens)]
    x_t_ref, x_ref, own_ref, key_mask_ref, own_mask_ref, gain_ref, rows_t = refs[len(evens) + 1 :]
    n_enc = 2 * len(evens)
    mine = lax.axis_index("enc")
    rows = n_enc * BLOCK
    lane = lax.broadcasted_iota(jnp.int32, (1, BLOCK), 1).astype(jnp.float32)
    extra = lax.broadcasted_iota(jnp.int32, (APAD - feats, BLOCK), 0)
    found = []
    blocks = [(at, here[i][...]) for i, at in enumerate(evens)]
    blocks += [(at ^ 1, near[1 + i]) for i, at in enumerate(evens)]
    for distance, block in blocks:
        source = mine ^ distance
        for b in range(NBS):
            tile = block[:, b * BLOCK : (b + 1) * BLOCK].astype(jnp.float32)
            owner, offset, count = (tile[feats + i : feats + i + 1] for i in range(3))
            owner = jnp.where(offset == 0.0, owner, -1.0)
            segment = jnp.where(lane < count, (source + 1).astype(jnp.float32), 0.0)
            found.append((owner, segment, tile[:feats]))
    at = lax.broadcasted_iota(jnp.int32, (feats, feats), 0)
    frm = lax.broadcasted_iota(jnp.int32, (feats, feats), 1)
    order = jnp.where(frm == (at % 4) * (feats // 4) + at // 4, 1.0, 0.0).astype(jnp.bfloat16)
    for o in range(n_enc):
        segment = jnp.zeros((1, BLOCK), jnp.float32)
        body = jnp.zeros((feats, BLOCK), jnp.float32)
        for owner, seg_of, tile in found:
            hit = owner == float(o)
            segment = segment + jnp.where(hit, seg_of, 0.0)
            body = body + jnp.where(hit, tile, 0.0)
        tail = jnp.where(extra == 0, 1.0, jnp.where(extra == 1, segment, 0.0))
        rows_t[:, o * BLOCK : (o + 1) * BLOCK] = jnp.concatenate(
            [body, tail, jnp.zeros((LANES - APAD, BLOCK), jnp.float32)], axis=0
        )
    picked = mm(order, rows_t[:feats].astype(jnp.bfloat16))
    spread = mm(gram_ref[...], picked.astype(jnp.bfloat16))
    variance = jnp.sum((spread[:feats] + spread[feats:]) * picked, axis=0, keepdims=True)
    rows_t[:feats] = picked * lax.rsqrt(jnp.maximum(variance, 0.0) + eps_norm)
    x_t = rows_t[...]
    x_t_ref[...] = x_t[:APAD].astype(jnp.bfloat16)
    x_ref[...] = x_t.T.astype(jnp.bfloat16)
    group_t = lax.broadcasted_iota(jnp.int32, (LANES, rows), 0).astype(jnp.float32)
    key_mask_ref[...] = jnp.where(x_t[feats + 1 : feats + 2] == group_t, 0.0, 1.0).astype(jnp.bfloat16)
    own = rows_t[:, pl.ds(pl.multiple_of(mine * BLOCK, BLOCK), BLOCK)].T
    own_ref[...] = own.astype(jnp.bfloat16)
    group = lax.broadcasted_iota(jnp.int32, (BLOCK, LANES), 1).astype(jnp.float32)
    own_mask_ref[...] = jnp.where(own[:, feats + 1 : feats + 2] == group, -FAR, 0.0).astype(jnp.bfloat16)
    head_dim = q_gain_ref.shape[1]
    gain_ref[...] = q_gain_ref[...] * k_gain_ref[...] * (head_dim**-0.5 * math.log2(math.e))


def attend_heads(folds, place, x_t_ref, x_ref, own_ref, key_mask_ref, own_mask_ref, gain_ref):
    folds = list(folds)
    heads = range(len(folds))

    def side(part):
        return jnp.concatenate([fold[:, part * LANES : (part + 1) * LANES] for fold in folds], axis=1)

    def of(i):
        return slice(i * LANES, (i + 1) * LANES)

    keys = mm(side(1), x_t_ref[...], ((0,), (0,)))
    queries = mm(own_ref[:, :APAD], side(0))
    values = mm(x_ref[:, :APAD], side(2)).astype(jnp.bfloat16)
    gain, own_mask, key_mask = gain_ref[...], own_mask_ref[...], key_mask_ref[...]
    left, right = [], []
    for i in heads:
        key = keys[of(i)]
        square = jnp.sum(key * key, axis=0, keepdims=True) / LANES
        key = (key * lax.rsqrt(square + eps_norm)).astype(jnp.bfloat16)
        right.append(jnp.concatenate([key, key_mask], axis=0))
        query = queries[:, of(i)]
        square = jnp.sum(query * query, axis=1, keepdims=True) / LANES
        query = (query * lax.rsqrt(square + eps_norm) * gain).astype(jnp.bfloat16)
        left.append(jnp.concatenate([query, own_mask], axis=1))
    scores = [mm(left[i], right[i]) for i in heads]
    weights = [jnp.exp2(score).astype(jnp.bfloat16) for score in scores]
    ones = jnp.ones((values.shape[0], LANES), jnp.bfloat16)
    mixed = [mm(weights[i], jnp.concatenate([values[:, of(i)], ones], axis=1)) for i in heads]
    for i in heads:
        place(i, (mixed[i][:, :LANES] / mixed[i][:, LANES:]).astype(jnp.bfloat16))


def each_head(refs):
    for ref in refs:
        if len(ref.shape) == 2:
            yield ref[...]
        else:
            for i in range(ref.shape[0]):
                yield ref[i]


def attend_kernel(*refs):
    def place(i, result):
        refs[-1][:, i * LANES : (i + 1) * LANES] = result

    attend_heads(each_head(refs[6:-1]), place, *refs[:6])


def last_kernel(heads, lists, both, own_ref, got_ref, *refs):
    near_ref, out_ref, done, sems = refs[-4:]
    mine, slot = lax.axis_index("enc"), lax.axis_index("seq") & (heads - 1)
    core, half = mine & 1, len(lists[0])
    copies = []

    def put(base, partner, second, result):
        far, k = partner
        head = (base ^ far ^ second) * heads + (slot ^ k)
        column = pl.ds(pl.multiple_of(head * LANES, LANES), LANES)
        copies.append(pltpu.make_async_copy(result, out_ref.at[0, :, column], sems.at[len(copies)]))
        copies[-1].start()

    def put_got(core, base, at, result):
        if at < 2 * half:
            far, k = (jnp.where(core == 0, a, b) for a, b in zip(lists[0][at // 2], lists[1][at // 2]))
            put(base, (far, k), at % 2, result)
        else:
            put(base, both, 0, result)

    for i in range(2):
        put(mine, (0, 0), i, own_ref.at[:, i * LANES : (i + 1) * LANES])
    for i in range(2 * half + 1):
        put_got(core, mine, i, got_ref.at[:, i * LANES : (i + 1) * LANES])

    def place(i, result):
        done[i] = result
        put_got(core ^ 1, mine ^ 1, i, done.at[i])

    attend_heads(each_head([near_ref]), place, *refs[:6])
    for copy in copies:
        copy.wait()


def vmem(count):
    return [pl.BlockSpec(memory_space=pltpu.VMEM)] * count


def hbm(count):
    return [pl.BlockSpec(memory_space=pltpu.HBM)] * count


def in_hbm(x):
    return pltpu.with_memory_space_constraint(x, pltpu.HBM)


def after(count):
    return [pl.BlockSpec(memory_space=pl.ANY)] * count


def call(kernel, ins, out_shape, scratch=(), cost=(1_000_000, 1_000_000)):
    return pl.pallas_call(
        kernel,
        in_specs=ins,
        out_specs=[pl.BlockSpec(memory_space=pltpu.VMEM)] * len(out_shape),
        out_shape=out_shape,
        scratch_shapes=list(scratch),
        compiler_params=pltpu.CompilerParams(vmem_limit_bytes=VMEM_LIMIT),
        cost_estimate=pl.CostEstimate(flops=cost[0], bytes_accessed=cost[1], transcendentals=0),
    )


def gate(x, *others):
    return pl.pallas_call(
        gate_kernel,
        in_specs=after(1 + len(others)),
        out_specs=after(1)[0],
        out_shape=jax.ShapeDtypeStruct(x.shape, x.dtype),
        input_output_aliases={0: 0},
        compiler_params=pltpu.CompilerParams(vmem_limit_bytes=VMEM_LIMIT),
    )(x, *others)


def exchange(x, axis, n, k):
    return lax.ppermute(x, axis, [(i, i ^ k) for i in range(n)])


def on_device(
    n_enc,
    n_seq,
    clip_features,
    clip_shape,
    packing,
    conv_weight,
    embed_weight,
    mod_shift,
    mod_scale,
    qkv_weight,
    q_gain,
    k_gain,
):
    caps = clip_features.shape[2:5]
    depth_all = clip_features.shape[5]
    cols = qkv_weight.shape[2]
    feats = embed_weight.shape[0]
    heads = cols // LANES
    rows = n_enc * BLOCK
    bf16, f32 = jnp.bfloat16, jnp.float32

    def folds(dtype, *lead):
        return jax.ShapeDtypeStruct((*lead, APAD, 3 * LANES), dtype)

    evens = [0]
    for bit in reversed(range(1, log2(n_enc))):
        evens += [at ^ (1 << bit) for at in evens]
    scale_rows, shift_rows = mod_scale.reshape(-1, LANES), mod_shift.reshape(-1, LANES)
    later = [
        clip_features.reshape(-1, depth_all),
        conv_weight.reshape(-1, depth_all),
        q_gain.reshape(1, -1),
        k_gain.reshape(1, -1),
    ]
    with jax.named_scope("fold"):
        embed, features, conv, q_gain, k_gain, keep, *sends = call(
            functools.partial(fold_kernel, len(later)),
            hbm(4 + len(later)),
            [jax.ShapeDtypeStruct(x.shape, x.dtype) for x in (embed_weight, *later)]
            + [folds(f32)]
            + [folds(bf16)] * max(heads - 1, 1),
            [
                pltpu.VMEM(scale_rows.shape, f32),
                pltpu.VMEM(shift_rows.shape, f32),
                pltpu.VMEM(qkv_weight.shape, bf16),
                pltpu.SemaphoreType.DMA((4 + len(later),)),
            ],
            cost=(200_000_000, 1_000_000),
        )(*map(in_hbm, (embed_weight, scale_rows, shift_rows, qkv_weight, *later)))

    with jax.named_scope("encode"):
        own_block = call(
            functools.partial(encode_kernel, caps),
            hbm(2) + vmem(2),
            [jax.ShapeDtypeStruct((APAD, NBS * BLOCK), bf16)],
            [
                pltpu.SMEM(clip_shape.shape, jnp.int32),
                pltpu.SMEM(packing.shape, jnp.int32),
                pltpu.SemaphoreType.DMA((2,)),
            ],
            cost=(500_000_000, 2_000_000),
        )(in_hbm(clip_shape), in_hbm(packing), features, conv)[0]

    def add(keep, got, first):
        kernel = functools.partial(add_kernel, len(got))
        return call(kernel, vmem(1 + len(got)) + after(1), [folds(f32), folds(bf16)])(keep, *got, first)

    with jax.named_scope("fold_sum"):
        if heads > 1:
            got = [exchange(sends[k - 1], "seq", n_seq, k) for k in range(1, heads)]
            keep, send = add(keep, got, own_block)
        else:
            send = sends[0]

    with jax.named_scope("gram"):
        gram = call(gram_kernel, vmem(1) + after(1), [jax.ShapeDtypeStruct((2 * feats, feats), bf16)])(embed, keep)[0]

    with jax.named_scope("tokens"):
        own_block = gate(own_block, keep)
        blocks = [own_block] + [exchange(own_block, "enc", n_enc, k) for k in evens[1:]]

    with jax.named_scope("fold_sum"):
        for bit in range(log2(heads), log2(n_seq)):
            got = exchange(send, "seq", n_seq, 1 << bit)
            if bit + 1 < log2(n_seq):
                keep, send = add(keep, [got], own_block)
            else:
                fresh, swap = call(
                    functools.partial(last_add_kernel, len(blocks)),
                    vmem(2 + len(blocks)) + after(1),
                    [folds(bf16), folds(bf16, 1 + len(blocks))],
                )(keep, got, *blocks, gram)

    def bundle(parts, first):
        total = sum(part.size for part in parts) // (APAD * 3 * LANES)
        kernel = functools.partial(bundle_kernel, len(parts))
        return call(kernel, vmem(len(parts)) + after(1), [folds(bf16, total)])(*parts, first)[0]

    partners = [(far, k) for far in evens for k in range(heads) if far or k]
    partners.sort(key=lambda p: (p[0].bit_count() + p[1].bit_count(), p[0]))
    half = len(partners) // 2
    assert len(partners) == 2 * half + 1
    both, lists = partners[half], (tuple(partners[:half]), tuple(partners[half + 1 :]))

    def spread(x, partner_of):
        pairs = []
        for e in range(n_enc):
            far, k = partner_of[e & 1]
            pairs += [(e * n_seq + i, (e ^ far) * n_seq + (i ^ k)) for i in range(n_seq)]
        return lax.ppermute(x, ("enc", "seq"), pairs)

    with jax.named_scope("gather"):
        single = spread(fresh, (both, both))
        swapped = exchange(swap, "enc", n_enc, 1)
        pair = call(pair_kernel, vmem(2), [folds(bf16, 2)])(fresh, swapped)[0]
        got = [spread(pair, partner_of) for partner_of in zip(*lists)] + [single]

    with jax.named_scope("pack"):
        packed = call(
            functools.partial(pack_kernel, tuple(evens), feats),
            vmem(4 + len(evens)),
            [
                jax.ShapeDtypeStruct((APAD, rows), bf16),
                jax.ShapeDtypeStruct((rows, LANES), bf16),
                jax.ShapeDtypeStruct((BLOCK, LANES), bf16),
                jax.ShapeDtypeStruct((LANES, rows), bf16),
                jax.ShapeDtypeStruct((BLOCK, LANES), bf16),
                jax.ShapeDtypeStruct((1, LANES), f32),
            ],
            [pltpu.VMEM((LANES, rows), f32)],
        )(q_gain, k_gain, gram, *blocks, swapped)

    def attend(groups):
        count = sum(group.size for group in groups) // (APAD * 3 * LANES)
        return call(
            attend_kernel,
            vmem(6 + len(groups)),
            [jax.ShapeDtypeStruct((BLOCK, count * LANES), bf16)],
            cost=(count * 200_000_000, 1_000_000),
        )(*packed, *groups)[0]

    with jax.named_scope("attend"):
        own_done = attend([pair])
        near = exchange(bundle(got, own_done), "enc", n_enc, 1)
        got_done = attend(got)
        total = n_enc * heads
        return pl.pallas_call(
            functools.partial(last_kernel, heads, lists, both),
            in_specs=vmem(9),
            out_specs=hbm(1)[0],
            out_shape=jax.ShapeDtypeStruct((1, BLOCK, n_enc * cols), bf16),
            scratch_shapes=[pltpu.VMEM((2 * half + 1, BLOCK, LANES), bf16), pltpu.SemaphoreType.DMA((total,))],
            compiler_params=pltpu.CompilerParams(vmem_limit_bytes=VMEM_LIMIT),
            cost_estimate=pl.CostEstimate(flops=1_600_000_000, bytes_accessed=2_000_000, transcendentals=0),
        )(own_done, got_done, *packed, near)


def solution(mesh):
    return jax.shard_map(
        functools.partial(on_device, mesh.shape["enc"], mesh.shape["seq"]),
        mesh=mesh,
        in_specs=(
            P("enc", "seq", None, None, None, None),
            P("enc", "seq", None),
            P("enc", "seq", None, None),
            P(),
            P(),
            P(),
            P(),
            P(None, "seq", "enc"),
            P(),
            P(),
        ),
        out_specs=P("seq", "enc", None),
        check_vma=False,
    )
```

```python
import functools
import math

import jax
import jax.numpy as jnp
from jax import lax
from jax.experimental import pallas as pl
from jax.experimental.pallas import tpu as pltpu
from jax.sharding import PartitionSpec as P

BLOCK = 128
NBS = 2
LANES = 128
APAD = 72
eps_norm = 1e-06
FAR = 2.0**20
VMEM_LIMIT = 48 * 1024 * 1024


def mm(a, b, dims=((1,), (0,)), precision=None):
    return lax.dot_general(a, b, (dims, ((), ())), preferred_element_type=jnp.float32, precision=precision)


def split_bf16(x):
    hi = x.astype(jnp.bfloat16)
    return hi, (x - hi.astype(jnp.float32)).astype(jnp.bfloat16)


def log2(n):
    bits = n.bit_length() - 1
    assert 1 << bits == n
    return bits


def fetch(pairs, sems):
    copies = [pltpu.make_async_copy(src, dst, sems.at[i]) for i, (src, dst) in enumerate(pairs)]
    for copy in copies:
        copy.start()
    return copies


def fold_kernel(count, embed_hbm, scale_hbm, shift_hbm, w_hbm, *refs):
    later_hbm, embed_ref, later, keep_ref, sends = refs[:count], refs[count], refs[count + 1 : 2 * count + 1], refs[2 * count + 1], refs[2 * count + 2 : -4]
    scale_ref, shift_ref, w_ref, sems = refs[-4:]
    copies = fetch(
        [(embed_hbm, embed_ref), (scale_hbm, scale_ref), (shift_hbm, shift_ref), (w_hbm, w_ref)]
        + list(zip(later_hbm, later)),
        sems,
    )
    me = lax.axis_index("seq")
    _, depth, cols = w_ref.shape
    feats = embed_ref.shape[0]
    heads = cols // LANES
    for copy in copies[:3]:
        copy.wait()
    mean = jnp.sum(embed_ref[...].astype(jnp.float32), axis=1, keepdims=True) / embed_ref.shape[1]
    span = max(depth, LANES)
    chunks = span // LANES
    first = (me * depth) // LANES
    emb = embed_ref[:, pl.ds(pl.multiple_of(first * LANES, LANES), span)].astype(jnp.float32) - mean
    scale = jnp.concatenate([scale_ref[pl.ds(first + i, 1), :] for i in range(chunks)], axis=1)
    shift = jnp.concatenate([shift_ref[pl.ds(first + i, 1), :] for i in range(chunks)], axis=1)
    left = jnp.concatenate(
        [emb * (1.0 + scale), shift, jnp.zeros((APAD - feats - 1, span), jnp.float32)], axis=0
    )
    if depth < LANES:
        low = me * depth - first * LANES
        lane = lax.broadcasted_iota(jnp.int32, left.shape, 1)
        left = jnp.where((lane >= low) & (lane < low + depth), left, 0.0)
    hi, lo = split_bf16(left)
    both = jnp.concatenate([hi, lo], axis=0)
    copies[3].wait()

    def product(head):
        start = pl.multiple_of(head * LANES, LANES)
        right = jnp.concatenate([w_ref[part, :, pl.ds(start, LANES)] for part in range(3)], axis=1)
        right = jnp.concatenate([right] * (span // depth), axis=0)
        total = mm(both, right)
        return total[:APAD] + total[APAD:]

    slot = me & (heads - 1)
    for k in range(1, heads):
        sends[k - 1][...] = product(slot ^ k).astype(jnp.bfloat16)
    total = product(slot)
    keep_ref[...] = total
    if heads == 1:
        sends[0][...] = total.astype(jnp.bfloat16)
    for copy in copies[4:]:
        copy.wait()


def add_kernel(count, keep_in, *refs):
    total = keep_in[...]
    for ref in refs[:count]:
        total = total + ref[...].astype(jnp.float32)
    refs[-2][...] = total
    refs[-1][...] = total.astype(jnp.bfloat16)


def last_add_kernel(count, keep_in, got_ref, *refs):
    total = (keep_in[...] + got_ref[...].astype(jnp.float32)).astype(jnp.bfloat16)
    out_ref, swap_ref = refs[-2:]
    out_ref[...] = total
    swap_ref[0] = total
    for i in range(count):
        width = refs[i].shape[1]
        swap_ref[1 + i, :, :width] = refs[i][...]
        swap_ref[1 + i, :, width:] = jnp.zeros((total.shape[0], total.shape[1] - width), jnp.bfloat16)


def bundle_kernel(count, *refs):
    at = 0
    for ref in refs[:count]:
        for i in range(ref.shape[0] if len(ref.shape) == 3 else 1):
            refs[-1][at] = ref[i] if len(ref.shape) == 3 else ref[...]
            at += 1


def pair_kernel(own_ref, swapped_ref, out_ref):
    out_ref[0] = own_ref[...]
    out_ref[1] = swapped_ref[0]


def gate_kernel(*refs):
    pass


def encode_kernel(caps, shape_hbm, plan_hbm, feat_ref, conv_ref, out_ref, shape_ref, plan_ref, sems):
    copies = fetch([(shape_hbm, shape_ref), (plan_hbm, plan_ref)], sems)
    frames_cap, height_cap, width_cap = caps
    spots = frames_cap * height_cap * width_cap
    frame_size = height_cap * width_cap
    latent_ch = conv_ref.shape[0] // 27
    feats = 4 * latent_ch
    taps = mm(conv_ref[...], feat_ref[...], ((1,), (1,)))
    copies[0].wait()
    copies[1].wait()
    frames, height, width = shape_ref[0, 0, 0], shape_ref[0, 0, 1], shape_ref[0, 0, 2]
    spot = lax.broadcasted_iota(jnp.int32, (1, spots), 1)
    frame_ix = spot // frame_size
    row_ix = (spot % frame_size) // width_cap
    col_ix = spot % width_cap
    inside = (frame_ix < frames) & (row_ix < height) & (col_ix < width)
    taps = jnp.where(inside, taps, 0.0)

    def tap(a, b, j):
        at = (9 * a + 3 * b + j) * latent_ch
        return taps[at : at + latent_ch]

    def later(x, by):
        zeros = jnp.zeros((latent_ch, by * frame_size), jnp.float32)
        return jnp.concatenate([zeros, x[:, : spots - by * frame_size]], axis=1)

    def over_frames(b, j):
        return tap(2, b, j) + later(tap(1, b, j), 1) + later(tap(0, b, j), 2)

    def over_rows(j):
        above = pltpu.roll(over_frames(0, j), width_cap, 1)
        below = pltpu.roll(over_frames(2, j), spots - width_cap, 1)
        return (
            over_frames(1, j)
            + jnp.where(row_ix >= 1, above, 0.0)
            + jnp.where(row_ix < height_cap - 1, below, 0.0)
        )

    latent = (
        over_rows(1)
        + jnp.where(col_ix >= 1, pltpu.roll(over_rows(0), 1, 1), 0.0)
        + jnp.where(col_ix < width_cap - 1, pltpu.roll(over_rows(2), spots - 1, 1), 0.0)
    )
    latent = latent.astype(jnp.bfloat16).astype(jnp.float32)
    shifted = [latent] + [pltpu.roll(latent, spots - by, 1) for by in (1, width_cap, width_cap + 1)]
    patches = jnp.concatenate(shifted, axis=0).astype(jnp.bfloat16)

    tokens = NBS * BLOCK
    half_w = (width // 2).astype(jnp.float32)
    per_frame_int = (height // 2) * (width // 2)
    per_frame = per_frame_int.astype(jnp.float32)
    live = frames * per_frame_int
    token_int = lax.broadcasted_iota(jnp.int32, (1, tokens), 1)
    token = token_int.astype(jnp.float32)
    frame_of = jnp.floor((token + 0.5) / jnp.full((1, tokens), per_frame))
    within = token - frame_of * per_frame
    row_of = jnp.floor((within + 0.5) / jnp.full((1, tokens), half_w))
    col_of = within - row_of * half_w
    source = (frame_of * frame_size + row_of * (2 * width_cap) + col_of * 2).astype(jnp.int32)
    source = jnp.where(token_int < live, source, -1)
    chosen = lax.broadcasted_iota(jnp.int32, (spots, tokens), 0) == source
    picked = mm(patches, jnp.where(chosen, 1.0, 0.0).astype(jnp.bfloat16))
    kind = lax.broadcasted_iota(jnp.int32, (APAD - feats, BLOCK), 0)
    infos = []
    for b in range(NBS):
        count = jnp.clip(live - b * BLOCK, 0, BLOCK)
        info = jnp.where(
            kind == 0,
            plan_ref[0, 0, b, 0],
            jnp.where(kind == 1, plan_ref[0, 0, b, 1], jnp.where(kind == 2, count, 0)),
        )
        infos.append(info.astype(jnp.float32))
    info = jnp.concatenate(infos, axis=1)
    out_ref[...] = jnp.concatenate([picked, info], axis=0).astype(jnp.bfloat16)


def gram_kernel(embed_ref, first_ref, out_ref):
    feats, width = embed_ref.shape
    emb = embed_ref[...].astype(jnp.float32)
    emb = emb - jnp.sum(emb, axis=1, keepdims=True) / width
    both = jnp.concatenate(split_bf16(emb), axis=0)
    gram = mm(both, both, ((1,), (1,))) / width
    gram = gram[:feats] + gram[feats:]
    out_ref[...] = jnp.concatenate(split_bf16(gram[:, :feats] + gram[:, feats:]), axis=0)


def pack_kernel(evens, feats, q_gain_ref, k_gain_ref, gram_ref, *refs):
    here, near = refs[: len(evens)], refs[len(evens)]
    x_t_ref, x_ref, own_ref, key_mask_ref, own_mask_ref, gain_ref, rows_t = refs[len(evens) + 1 :]
    n_enc = 2 * len(evens)
    mine = lax.axis_index("enc")
    rows = n_enc * BLOCK
    lane = lax.broadcasted_iota(jnp.int32, (1, BLOCK), 1).astype(jnp.float32)
    extra = lax.broadcasted_iota(jnp.int32, (APAD - feats, BLOCK), 0)
    found = []
    blocks = [(at, here[i][...]) for i, at in enumerate(evens)]
    blocks += [(at ^ 1, near[1 + i]) for i, at in enumerate(evens)]
    for distance, block in blocks:
        source = mine ^ distance
        for b in range(NBS):
            tile = block[:, b * BLOCK : (b + 1) * BLOCK].astype(jnp.float32)
            owner, offset, count = (tile[feats + i : feats + i + 1] for i in range(3))
            owner = jnp.where(offset == 0.0, owner, -1.0)
            segment = jnp.where(lane < count, (source + 1).astype(jnp.float32), 0.0)
            found.append((owner, segment, tile[:feats]))
    at = lax.broadcasted_iota(jnp.int32, (feats, feats), 0)
    frm = lax.broadcasted_iota(jnp.int32, (feats, feats), 1)
    order = jnp.where(frm == (at % 4) * (feats // 4) + at // 4, 1.0, 0.0).astype(jnp.bfloat16)
    for o in range(n_enc):
        segment = jnp.zeros((1, BLOCK), jnp.float32)
        body = jnp.zeros((feats, BLOCK), jnp.float32)
        for owner, seg_of, tile in found:
            hit = owner == float(o)
            segment = segment + jnp.where(hit, seg_of, 0.0)
            body = body + jnp.where(hit, tile, 0.0)
        tail = jnp.where(extra == 0, 1.0, jnp.where(extra == 1, segment, 0.0))
        rows_t[:, o * BLOCK : (o + 1) * BLOCK] = jnp.concatenate(
            [body, tail, jnp.zeros((LANES - APAD, BLOCK), jnp.float32)], axis=0
        )
    picked = mm(order, rows_t[:feats].astype(jnp.bfloat16))
    spread = mm(gram_ref[...], picked.astype(jnp.bfloat16))
    variance = jnp.sum((spread[:feats] + spread[feats:]) * picked, axis=0, keepdims=True)
    rows_t[:feats] = picked * lax.rsqrt(jnp.maximum(variance, 0.0) + eps_norm)
    x_t = rows_t[...]
    x_t_ref[...] = x_t[:APAD].astype(jnp.bfloat16)
    x_ref[...] = x_t.T.astype(jnp.bfloat16)
    group_t = lax.broadcasted_iota(jnp.int32, (LANES, rows), 0).astype(jnp.float32)
    key_mask_ref[...] = jnp.where(x_t[feats + 1 : feats + 2] == group_t, 0.0, 1.0).astype(jnp.bfloat16)
    own = rows_t[:, pl.ds(pl.multiple_of(mine * BLOCK, BLOCK), BLOCK)].T
    own_ref[...] = own.astype(jnp.bfloat16)
    group = lax.broadcasted_iota(jnp.int32, (BLOCK, LANES), 1).astype(jnp.float32)
    own_mask_ref[...] = jnp.where(own[:, feats + 1 : feats + 2] == group, -FAR, 0.0).astype(jnp.bfloat16)
    head_dim = q_gain_ref.shape[1]
    gain_ref[...] = q_gain_ref[...] * k_gain_ref[...] * (head_dim**-0.5 * math.log2(math.e))


def attend_heads(folds, place, x_t_ref, x_ref, own_ref, key_mask_ref, own_mask_ref, gain_ref):
    folds = list(folds)
    heads = range(len(folds))

    def side(part):
        return jnp.concatenate([fold[:, part * LANES : (part + 1) * LANES] for fold in folds], axis=1)

    def of(i):
        return slice(i * LANES, (i + 1) * LANES)

    keys = mm(side(1), x_t_ref[...], ((0,), (0,)))
    queries = mm(own_ref[:, :APAD], side(0))
    values = mm(x_ref[:, :APAD], side(2)).astype(jnp.bfloat16)
    gain, own_mask, key_mask = gain_ref[...], own_mask_ref[...], key_mask_ref[...]
    left, right = [], []
    for i in heads:
        key = keys[of(i)]
        square = jnp.sum(key * key, axis=0, keepdims=True) / LANES
        key = (key * lax.rsqrt(square + eps_norm)).astype(jnp.bfloat16)
        right.append(jnp.concatenate([key, key_mask], axis=0))
        query = queries[:, of(i)]
        square = jnp.sum(query * query, axis=1, keepdims=True) / LANES
        query = (query * lax.rsqrt(square + eps_norm) * gain).astype(jnp.bfloat16)
        left.append(jnp.concatenate([query, own_mask], axis=1))
    scores = [mm(left[i], right[i]) for i in heads]
    weights = [jnp.exp2(score).astype(jnp.bfloat16) for score in scores]
    ones = jnp.ones((values.shape[0], LANES), jnp.bfloat16)
    mixed = [mm(weights[i], jnp.concatenate([values[:, of(i)], ones], axis=1)) for i in heads]
    for i in heads:
        place(i, (mixed[i][:, :LANES] / mixed[i][:, LANES:]).astype(jnp.bfloat16))


def each_head(refs):
    for ref in refs:
        if len(ref.shape) == 2:
            yield ref[...]
        else:
            for i in range(ref.shape[0]):
                yield ref[i]


def attend_kernel(*refs):
    def place(i, result):
        refs[-1][:, i * LANES : (i + 1) * LANES] = result

    attend_heads(each_head(refs[6:-1]), place, *refs[:6])


def last_kernel(heads, lists, both, own_ref, got_ref, *refs):
    near_ref, out_ref, done, sems = refs[-4:]
    mine, slot = lax.axis_index("enc"), lax.axis_index("seq") & (heads - 1)
    core, half = mine & 1, len(lists[0])
    copies = []

    def put(base, partner, second, result):
        far, k = partner
        head = (base ^ far ^ second) * heads + (slot ^ k)
        column = pl.ds(pl.multiple_of(head * LANES, LANES), LANES)
        copies.append(pltpu.make_async_copy(result, out_ref.at[0, :, column], sems.at[len(copies)]))
        copies[-1].start()

    def put_got(core, base, at, result):
        if at < 2 * half:
            far, k = (jnp.where(core == 0, a, b) for a, b in zip(lists[0][at // 2], lists[1][at // 2]))
            put(base, (far, k), at % 2, result)
        else:
            put(base, both, 0, result)

    for i in range(2):
        put(mine, (0, 0), i, own_ref.at[:, i * LANES : (i + 1) * LANES])
    for i in range(2 * half + 1):
        put_got(core, mine, i, got_ref.at[:, i * LANES : (i + 1) * LANES])

    def place(i, result):
        done[i] = result
        put_got(core ^ 1, mine ^ 1, i, done.at[i])

    attend_heads(each_head([near_ref]), place, *refs[:6])
    for copy in copies:
        copy.wait()


def vmem(count):
    return [pl.BlockSpec(memory_space=pltpu.VMEM)] * count


def hbm(count):
    return [pl.BlockSpec(memory_space=pltpu.HBM)] * count


def in_hbm(x):
    return pltpu.with_memory_space_constraint(x, pltpu.HBM)


def after(count):
    return [pl.BlockSpec(memory_space=pl.ANY)] * count


def call(kernel, ins, out_shape, scratch=(), cost=(1_000_000, 1_000_000)):
    return pl.pallas_call(
        kernel,
        in_specs=ins,
        out_specs=[pl.BlockSpec(memory_space=pltpu.VMEM)] * len(out_shape),
        out_shape=out_shape,
        scratch_shapes=list(scratch),
        compiler_params=pltpu.CompilerParams(vmem_limit_bytes=VMEM_LIMIT),
        cost_estimate=pl.CostEstimate(flops=cost[0], bytes_accessed=cost[1], transcendentals=0),
    )


def gate(x, *others):
    return pl.pallas_call(
        gate_kernel,
        in_specs=after(1 + len(others)),
        out_specs=after(1)[0],
        out_shape=jax.ShapeDtypeStruct(x.shape, x.dtype),
        input_output_aliases={0: 0},
        compiler_params=pltpu.CompilerParams(vmem_limit_bytes=VMEM_LIMIT),
    )(x, *others)


def exchange(x, axis, n, k):
    return lax.ppermute(x, axis, [(i, i ^ k) for i in range(n)])


def on_device(
    n_enc,
    n_seq,
    clip_features,
    clip_shape,
    packing,
    conv_weight,
    embed_weight,
    mod_shift,
    mod_scale,
    qkv_weight,
    q_gain,
    k_gain,
):
    caps = clip_features.shape[2:5]
    depth_all = clip_features.shape[5]
    cols = qkv_weight.shape[2]
    feats = embed_weight.shape[0]
    heads = cols // LANES
    rows = n_enc * BLOCK
    bf16, f32 = jnp.bfloat16, jnp.float32

    def folds(dtype, *lead):
        return jax.ShapeDtypeStruct((*lead, APAD, 3 * LANES), dtype)

    evens = [0]
    for bit in reversed(range(1, log2(n_enc))):
        evens += [at ^ (1 << bit) for at in evens]
    scale_rows, shift_rows = mod_scale.reshape(-1, LANES), mod_shift.reshape(-1, LANES)
    later = [
        clip_features.reshape(-1, depth_all),
        conv_weight.reshape(-1, depth_all),
        q_gain.reshape(1, -1),
        k_gain.reshape(1, -1),
    ]
    with jax.named_scope("fold"):
        embed, features, conv, q_gain, k_gain, keep, *sends = call(
            functools.partial(fold_kernel, len(later)),
            hbm(4 + len(later)),
            [jax.ShapeDtypeStruct(x.shape, x.dtype) for x in (embed_weight, *later)]
            + [folds(f32)]
            + [folds(bf16)] * max(heads - 1, 1),
            [
                pltpu.VMEM(scale_rows.shape, f32),
                pltpu.VMEM(shift_rows.shape, f32),
                pltpu.VMEM(qkv_weight.shape, bf16),
                pltpu.SemaphoreType.DMA((4 + len(later),)),
            ],
            cost=(200_000_000, 1_000_000),
        )(*map(in_hbm, (embed_weight, scale_rows, shift_rows, qkv_weight, *later)))

    with jax.named_scope("encode"):
        own_block = call(
            functools.partial(encode_kernel, caps),
            hbm(2) + vmem(2),
            [jax.ShapeDtypeStruct((APAD, NBS * BLOCK), bf16)],
            [
                pltpu.SMEM(clip_shape.shape, jnp.int32),
                pltpu.SMEM(packing.shape, jnp.int32),
                pltpu.SemaphoreType.DMA((2,)),
            ],
            cost=(500_000_000, 2_000_000),
        )(in_hbm(clip_shape), in_hbm(packing), features, conv)[0]

    def add(keep, got, first):
        kernel = functools.partial(add_kernel, len(got))
        return call(kernel, vmem(1 + len(got)) + after(1), [folds(f32), folds(bf16)])(keep, *got, first)

    with jax.named_scope("fold_sum"):
        if heads > 1:
            got = [exchange(sends[k - 1], "seq", n_seq, k) for k in reversed(range(1, heads))]
            keep, send = add(keep, got, own_block)
        else:
            send = sends[0]

    with jax.named_scope("gram"):
        gram = call(gram_kernel, vmem(1) + after(1), [jax.ShapeDtypeStruct((2 * feats, feats), bf16)])(embed, keep)[0]

    with jax.named_scope("tokens"):
        own_block = gate(own_block, keep)
        blocks = [own_block] + [exchange(own_block, "enc", n_enc, k) for k in evens[1:]]

    with jax.named_scope("fold_sum"):
        for bit in range(log2(heads), log2(n_seq)):
            got = exchange(send, "seq", n_seq, 1 << bit)
            if bit + 1 < log2(n_seq):
                keep, send = add(keep, [got], own_block)
            else:
                fresh, swap = call(
                    functools.partial(last_add_kernel, len(blocks)),
                    vmem(2 + len(blocks)) + after(1),
                    [folds(bf16), folds(bf16, 1 + len(blocks))],
                )(keep, got, *blocks, gram)

    def bundle(parts, first):
        total = sum(part.size for part in parts) // (APAD * 3 * LANES)
        kernel = functools.partial(bundle_kernel, len(parts))
        return call(kernel, vmem(len(parts)) + after(1), [folds(bf16, total)])(*parts, first)[0]

    partners = [(far, k) for far in evens for k in range(heads) if far or k]
    partners.sort(key=lambda p: (p[0].bit_count() + p[1].bit_count(), p[0]))
    half = len(partners) // 2
    assert len(partners) == 2 * half + 1
    both, lists = partners[0], (tuple(partners[1 : half + 1]), tuple(partners[half + 1 :]))

    def spread(x, partner_of):
        pairs = []
        for e in range(n_enc):
            far, k = partner_of[e & 1]
            pairs += [(e * n_seq + i, (e ^ far) * n_seq + (i ^ k)) for i in range(n_seq)]
        return lax.ppermute(x, ("enc", "seq"), pairs)

    with jax.named_scope("gather"):
        single = spread(fresh, (both, both))
        swapped = exchange(swap, "enc", n_enc, 1)
        pair = call(pair_kernel, vmem(2), [folds(bf16, 2)])(fresh, swapped)[0]
        got = [spread(pair, partner_of) for partner_of in zip(*lists)] + [single]

    with jax.named_scope("pack"):
        packed = call(
            functools.partial(pack_kernel, tuple(evens), feats),
            vmem(4 + len(evens)),
            [
                jax.ShapeDtypeStruct((APAD, rows), bf16),
                jax.ShapeDtypeStruct((rows, LANES), bf16),
                jax.ShapeDtypeStruct((BLOCK, LANES), bf16),
                jax.ShapeDtypeStruct((LANES, rows), bf16),
                jax.ShapeDtypeStruct((BLOCK, LANES), bf16),
                jax.ShapeDtypeStruct((1, LANES), f32),
            ],
            [pltpu.VMEM((LANES, rows), f32)],
        )(q_gain, k_gain, gram, *blocks, swapped)

    def attend(groups):
        count = sum(group.size for group in groups) // (APAD * 3 * LANES)
        return call(
            attend_kernel,
            vmem(6 + len(groups)),
            [jax.ShapeDtypeStruct((BLOCK, count * LANES), bf16)],
            cost=(count * 200_000_000, 1_000_000),
        )(*packed, *groups)[0]

    with jax.named_scope("attend"):
        own_done = attend([pair])
        near = exchange(bundle(got, own_done), "enc", n_enc, 1)
        got_done = attend(got)
        total = n_enc * heads
        return pl.pallas_call(
            functools.partial(last_kernel, heads, lists, both),
            in_specs=vmem(9),
            out_specs=hbm(1)[0],
            out_shape=jax.ShapeDtypeStruct((1, BLOCK, n_enc * cols), bf16),
            scratch_shapes=[pltpu.VMEM((2 * half + 1, BLOCK, LANES), bf16), pltpu.SemaphoreType.DMA((total,))],
            compiler_params=pltpu.CompilerParams(vmem_limit_bytes=VMEM_LIMIT),
            cost_estimate=pl.CostEstimate(flops=1_600_000_000, bytes_accessed=2_000_000, transcendentals=0),
        )(own_done, got_done, *packed, near)


def solution(mesh):
    return jax.shard_map(
        functools.partial(on_device, mesh.shape["enc"], mesh.shape["seq"]),
        mesh=mesh,
        in_specs=(
            P("enc", "seq", None, None, None, None),
            P("enc", "seq", None),
            P("enc", "seq", None, None),
            P(),
            P(),
            P(),
            P(),
            P(None, "seq", "enc"),
            P(),
            P(),
        ),
        out_specs=P("seq", "enc", None),
        check_vma=False,
    )
```

```python
import functools
import math

import jax
import jax.numpy as jnp
from jax import lax
from jax.experimental import pallas as pl
from jax.experimental.pallas import tpu as pltpu
from jax.sharding import PartitionSpec as P

BLOCK = 128
NBS = 2
LANES = 128
APAD = 72
eps_norm = 1e-06
FAR = 2.0**20
VMEM_LIMIT = 48 * 1024 * 1024


def mm(a, b, dims=((1,), (0,)), precision=None):
    return lax.dot_general(a, b, (dims, ((), ())), preferred_element_type=jnp.float32, precision=precision)


def split_bf16(x):
    hi = x.astype(jnp.bfloat16)
    return hi, (x - hi.astype(jnp.float32)).astype(jnp.bfloat16)


def log2(n):
    bits = n.bit_length() - 1
    assert 1 << bits == n
    return bits


def fetch(pairs, sems):
    copies = [pltpu.make_async_copy(src, dst, sems.at[i]) for i, (src, dst) in enumerate(pairs)]
    for copy in copies:
        copy.start()
    return copies


def fold_kernel(count, embed_hbm, scale_hbm, shift_hbm, w_hbm, *refs):
    later_hbm, embed_ref, later, keep_ref, sends = refs[:count], refs[count], refs[count + 1 : 2 * count + 1], refs[2 * count + 1], refs[2 * count + 2 : -4]
    scale_ref, shift_ref, w_ref, sems = refs[-4:]
    copies = fetch(
        [(embed_hbm, embed_ref), (scale_hbm, scale_ref), (shift_hbm, shift_ref), (w_hbm, w_ref)]
        + list(zip(later_hbm, later)),
        sems,
    )
    me = lax.axis_index("seq")
    _, depth, cols = w_ref.shape
    feats = embed_ref.shape[0]
    heads = cols // LANES
    for copy in copies[:3]:
        copy.wait()
    mean = jnp.sum(embed_ref[...].astype(jnp.float32), axis=1, keepdims=True) / embed_ref.shape[1]
    span = max(depth, LANES)
    chunks = span // LANES
    first = (me * depth) // LANES
    emb = embed_ref[:, pl.ds(pl.multiple_of(first * LANES, LANES), span)].astype(jnp.float32) - mean
    scale = jnp.concatenate([scale_ref[pl.ds(first + i, 1), :] for i in range(chunks)], axis=1)
    shift = jnp.concatenate([shift_ref[pl.ds(first + i, 1), :] for i in range(chunks)], axis=1)
    left = jnp.concatenate(
        [emb * (1.0 + scale), shift, jnp.zeros((APAD - feats - 1, span), jnp.float32)], axis=0
    )
    if depth < LANES:
        low = me * depth - first * LANES
        lane = lax.broadcasted_iota(jnp.int32, left.shape, 1)
        left = jnp.where((lane >= low) & (lane < low + depth), left, 0.0)
    hi, lo = split_bf16(left)
    both = jnp.concatenate([hi, lo], axis=0)
    copies[3].wait()

    def product(head):
        start = pl.multiple_of(head * LANES, LANES)
        right = jnp.concatenate([w_ref[part, :, pl.ds(start, LANES)] for part in range(3)], axis=1)
        right = jnp.concatenate([right] * (span // depth), axis=0)
        total = mm(both, right)
        return total[:APAD] + total[APAD:]

    slot = me & (heads - 1)
    for k in range(1, heads):
        sends[k - 1][...] = product(slot ^ k).astype(jnp.bfloat16)
    total = product(slot)
    keep_ref[...] = total
    if heads == 1:
        sends[0][...] = total.astype(jnp.bfloat16)
    for copy in copies[4:]:
        copy.wait()


def add_kernel(count, keep_in, *refs):
    total = keep_in[...]
    for ref in refs[:count]:
        total = total + ref[...].astype(jnp.float32)
    refs[-2][...] = total
    refs[-1][...] = total.astype(jnp.bfloat16)


def last_add_kernel(count, keep_in, got_ref, *refs):
    total = (keep_in[...] + got_ref[...].astype(jnp.float32)).astype(jnp.bfloat16)
    out_ref, swap_ref = refs[-2:]
    out_ref[...] = total
    swap_ref[0] = total
    for i in range(count):
        width = refs[i].shape[1]
        swap_ref[1 + i, :, :width] = refs[i][...]
        swap_ref[1 + i, :, width:] = jnp.zeros((total.shape[0], total.shape[1] - width), jnp.bfloat16)


def pair_kernel(own_ref, swapped_ref, out_ref):
    out_ref[0] = own_ref[...]
    out_ref[1] = swapped_ref[0]


def gate_kernel(*refs):
    pass


def encode_kernel(caps, shape_hbm, plan_hbm, feat_ref, conv_ref, out_ref, shape_ref, plan_ref, sems):
    copies = fetch([(shape_hbm, shape_ref), (plan_hbm, plan_ref)], sems)
    frames_cap, height_cap, width_cap = caps
    spots = frames_cap * height_cap * width_cap
    frame_size = height_cap * width_cap
    latent_ch = conv_ref.shape[0] // 27
    feats = 4 * latent_ch
    taps = mm(conv_ref[...], feat_ref[...], ((1,), (1,)))
    copies[0].wait()
    copies[1].wait()
    frames, height, width = shape_ref[0, 0, 0], shape_ref[0, 0, 1], shape_ref[0, 0, 2]
    spot = lax.broadcasted_iota(jnp.int32, (1, spots), 1)
    frame_ix = spot // frame_size
    row_ix = (spot % frame_size) // width_cap
    col_ix = spot % width_cap
    inside = (frame_ix < frames) & (row_ix < height) & (col_ix < width)
    taps = jnp.where(inside, taps, 0.0)

    def tap(a, b, j):
        at = (9 * a + 3 * b + j) * latent_ch
        return taps[at : at + latent_ch]

    def later(x, by):
        zeros = jnp.zeros((latent_ch, by * frame_size), jnp.float32)
        return jnp.concatenate([zeros, x[:, : spots - by * frame_size]], axis=1)

    def over_frames(b, j):
        return tap(2, b, j) + later(tap(1, b, j), 1) + later(tap(0, b, j), 2)

    def over_rows(j):
        above = pltpu.roll(over_frames(0, j), width_cap, 1)
        below = pltpu.roll(over_frames(2, j), spots - width_cap, 1)
        return (
            over_frames(1, j)
            + jnp.where(row_ix >= 1, above, 0.0)
            + jnp.where(row_ix < height_cap - 1, below, 0.0)
        )

    latent = (
        over_rows(1)
        + jnp.where(col_ix >= 1, pltpu.roll(over_rows(0), 1, 1), 0.0)
        + jnp.where(col_ix < width_cap - 1, pltpu.roll(over_rows(2), spots - 1, 1), 0.0)
    )
    latent = latent.astype(jnp.bfloat16).astype(jnp.float32)
    shifted = [latent] + [pltpu.roll(latent, spots - by, 1) for by in (1, width_cap, width_cap + 1)]
    patches = jnp.concatenate(shifted, axis=0).astype(jnp.bfloat16)

    tokens = NBS * BLOCK
    half_w = (width // 2).astype(jnp.float32)
    per_frame_int = (height // 2) * (width // 2)
    per_frame = per_frame_int.astype(jnp.float32)
    live = frames * per_frame_int
    token_int = lax.broadcasted_iota(jnp.int32, (1, tokens), 1)
    token = token_int.astype(jnp.float32)
    frame_of = jnp.floor((token + 0.5) / jnp.full((1, tokens), per_frame))
    within = token - frame_of * per_frame
    row_of = jnp.floor((within + 0.5) / jnp.full((1, tokens), half_w))
    col_of = within - row_of * half_w
    source = (frame_of * frame_size + row_of * (2 * width_cap) + col_of * 2).astype(jnp.int32)
    source = jnp.where(token_int < live, source, -1)
    chosen = lax.broadcasted_iota(jnp.int32, (spots, tokens), 0) == source
    picked = mm(patches, jnp.where(chosen, 1.0, 0.0).astype(jnp.bfloat16))
    kind = lax.broadcasted_iota(jnp.int32, (APAD - feats, BLOCK), 0)
    infos = []
    for b in range(NBS):
        count = jnp.clip(live - b * BLOCK, 0, BLOCK)
        info = jnp.where(
            kind == 0,
            plan_ref[0, 0, b, 0],
            jnp.where(kind == 1, plan_ref[0, 0, b, 1], jnp.where(kind == 2, count, 0)),
        )
        infos.append(info.astype(jnp.float32))
    info = jnp.concatenate(infos, axis=1)
    out_ref[...] = jnp.concatenate([picked, info], axis=0).astype(jnp.bfloat16)


def gram_kernel(embed_ref, first_ref, out_ref):
    feats, width = embed_ref.shape
    emb = embed_ref[...].astype(jnp.float32)
    emb = emb - jnp.sum(emb, axis=1, keepdims=True) / width
    both = jnp.concatenate(split_bf16(emb), axis=0)
    gram = mm(both, both, ((1,), (1,))) / width
    gram = gram[:feats] + gram[feats:]
    out_ref[...] = jnp.concatenate(split_bf16(gram[:, :feats] + gram[:, feats:]), axis=0)


def pack_kernel(evens, feats, q_gain_ref, k_gain_ref, gram_ref, *refs):
    here, near = refs[: len(evens)], refs[len(evens)]
    x_t_ref, x_ref, key_mask_ref, gain_ref, *row_refs, rows_t = refs[len(evens) + 1 :]
    n_enc = 2 * len(evens)
    mine = lax.axis_index("enc")
    rows = n_enc * BLOCK
    lane = lax.broadcasted_iota(jnp.int32, (1, BLOCK), 1).astype(jnp.float32)
    extra = lax.broadcasted_iota(jnp.int32, (APAD - feats, BLOCK), 0)
    found = []
    blocks = [(at, here[i][...]) for i, at in enumerate(evens)]
    blocks += [(at ^ 1, near[1 + i]) for i, at in enumerate(evens)]
    for distance, block in blocks:
        source = mine ^ distance
        for b in range(NBS):
            tile = block[:, b * BLOCK : (b + 1) * BLOCK].astype(jnp.float32)
            owner, offset, count = (tile[feats + i : feats + i + 1] for i in range(3))
            owner = jnp.where(offset == 0.0, owner, -1.0)
            segment = jnp.where(lane < count, (source + 1).astype(jnp.float32), 0.0)
            found.append((owner, segment, tile[:feats]))
    at = lax.broadcasted_iota(jnp.int32, (feats, feats), 0)
    frm = lax.broadcasted_iota(jnp.int32, (feats, feats), 1)
    order = jnp.where(frm == (at % 4) * (feats // 4) + at // 4, 1.0, 0.0).astype(jnp.bfloat16)
    for o in range(n_enc):
        segment = jnp.zeros((1, BLOCK), jnp.float32)
        body = jnp.zeros((feats, BLOCK), jnp.float32)
        for owner, seg_of, tile in found:
            hit = owner == float(o)
            segment = segment + jnp.where(hit, seg_of, 0.0)
            body = body + jnp.where(hit, tile, 0.0)
        tail = jnp.where(extra == 0, 1.0, jnp.where(extra == 1, segment, 0.0))
        rows_t[:, o * BLOCK : (o + 1) * BLOCK] = jnp.concatenate(
            [body, tail, jnp.zeros((LANES - APAD, BLOCK), jnp.float32)], axis=0
        )
    picked = mm(order, rows_t[:feats].astype(jnp.bfloat16))
    spread = mm(gram_ref[...], picked.astype(jnp.bfloat16))
    variance = jnp.sum((spread[:feats] + spread[feats:]) * picked, axis=0, keepdims=True)
    rows_t[:feats] = picked * lax.rsqrt(jnp.maximum(variance, 0.0) + eps_norm)
    x_t = rows_t[...]
    x_t_ref[...] = x_t[:APAD].astype(jnp.bfloat16)
    x_ref[...] = x_t.T.astype(jnp.bfloat16)
    group_t = lax.broadcasted_iota(jnp.int32, (LANES, rows), 0).astype(jnp.float32)
    key_mask_ref[...] = jnp.where(x_t[feats + 1 : feats + 2] == group_t, 0.0, 1.0).astype(jnp.bfloat16)
    group = lax.broadcasted_iota(jnp.int32, (BLOCK, LANES), 1).astype(jnp.float32)
    for core in range(2):
        rows_ref, mask_ref = row_refs[2 * core : 2 * core + 2]
        own = rows_t[:, pl.ds(pl.multiple_of((mine ^ core) * BLOCK, BLOCK), BLOCK)].T
        rows_ref[...] = own.astype(jnp.bfloat16)
        mask_ref[...] = jnp.where(own[:, feats + 1 : feats + 2] == group, -FAR, 0.0).astype(jnp.bfloat16)
    head_dim = q_gain_ref.shape[1]
    gain_ref[...] = q_gain_ref[...] * k_gain_ref[...] * (head_dim**-0.5 * math.log2(math.e))


def attend_heads(folds, place, x_t_ref, x_ref, key_mask_ref, gain_ref, own_ref, own_mask_ref):
    folds = list(folds)
    heads = range(len(folds))

    def side(part):
        return jnp.concatenate([fold[:, part * LANES : (part + 1) * LANES] for fold in folds], axis=1)

    def of(i):
        return slice(i * LANES, (i + 1) * LANES)

    keys = mm(side(1), x_t_ref[...], ((0,), (0,)))
    queries = mm(own_ref[:, :APAD], side(0))
    values = mm(x_ref[:, :APAD], side(2)).astype(jnp.bfloat16)
    gain, own_mask, key_mask = gain_ref[...], own_mask_ref[...], key_mask_ref[...]
    left, right = [], []
    for i in heads:
        key = keys[of(i)]
        square = jnp.sum(key * key, axis=0, keepdims=True) / LANES
        key = (key * lax.rsqrt(square + eps_norm)).astype(jnp.bfloat16)
        right.append(jnp.concatenate([key, key_mask], axis=0))
        query = queries[:, of(i)]
        square = jnp.sum(query * query, axis=1, keepdims=True) / LANES
        query = (query * lax.rsqrt(square + eps_norm) * gain).astype(jnp.bfloat16)
        left.append(jnp.concatenate([query, own_mask], axis=1))
    scores = [mm(left[i], right[i]) for i in heads]
    weights = [jnp.exp2(score).astype(jnp.bfloat16) for score in scores]
    ones = jnp.ones((values.shape[0], LANES), jnp.bfloat16)
    mixed = [mm(weights[i], jnp.concatenate([values[:, of(i)], ones], axis=1)) for i in heads]
    for i in heads:
        place(i, (mixed[i][:, :LANES] / mixed[i][:, LANES:]).astype(jnp.bfloat16))


def each_head(refs):
    for ref in refs:
        if len(ref.shape) == 2:
            yield ref[...]
        else:
            for i in range(ref.shape[0]):
                yield ref[i]


def attend_kernel(count, *refs):
    folds, out_ref = refs[6 : 6 + count], refs[-1]
    first = 0
    if len(refs) > 7 + count:
        done_ref = refs[6 + count]
        first = done_ref.shape[1] // LANES
        out_ref[:, : first * LANES] = done_ref[...]

    def place(i, result):
        out_ref[:, (first + i) * LANES : (first + i + 1) * LANES] = result

    attend_heads(each_head(folds), place, *refs[:6])


def output_kernel(heads, lists, both, own_ref, near_ref, out_ref, sems):
    mine, slot = lax.axis_index("enc"), lax.axis_index("seq") & (heads - 1)
    half = len(lists[0])
    order = [half - 1, *range(half - 1)]
    copies = []

    def put(ref, at, base, far, k):
        head = (base ^ far) * heads + (slot ^ k)
        column = pl.ds(pl.multiple_of(head * LANES, LANES), LANES)
        result = ref.at[:, at * LANES : (at + 1) * LANES]
        copies.append(pltpu.make_async_copy(result, out_ref.at[0, :, column], sems.at[len(copies)]))
        copies[-1].start()

    for ref, base in ((near_ref, mine ^ 1), (own_ref, mine)):
        put(ref, 0, base, 0, 0)
        for i, at in enumerate(order):
            pair = zip(lists[0][at], lists[1][at])
            far, k = (jnp.where(base & 1 == 0, zero, one) for zero, one in pair)
            put(ref, 1 + 2 * i, base, far, k)
            put(ref, 2 + 2 * i, base, far ^ 1, k)
        put(ref, 1 + 2 * half, base, *both)
    for copy in copies:
        copy.wait()


def vmem(count):
    return [pl.BlockSpec(memory_space=pltpu.VMEM)] * count


def hbm(count):
    return [pl.BlockSpec(memory_space=pltpu.HBM)] * count


def in_hbm(x):
    return pltpu.with_memory_space_constraint(x, pltpu.HBM)


def after(count):
    return [pl.BlockSpec(memory_space=pl.ANY)] * count


def call(kernel, ins, out_shape, scratch=(), cost=(1_000_000, 1_000_000)):
    return pl.pallas_call(
        kernel,
        in_specs=ins,
        out_specs=[pl.BlockSpec(memory_space=pltpu.VMEM)] * len(out_shape),
        out_shape=out_shape,
        scratch_shapes=list(scratch),
        compiler_params=pltpu.CompilerParams(vmem_limit_bytes=VMEM_LIMIT),
        cost_estimate=pl.CostEstimate(flops=cost[0], bytes_accessed=cost[1], transcendentals=0),
    )


def gate(x, *others):
    return pl.pallas_call(
        gate_kernel,
        in_specs=after(1 + len(others)),
        out_specs=after(1)[0],
        out_shape=jax.ShapeDtypeStruct(x.shape, x.dtype),
        input_output_aliases={0: 0},
        compiler_params=pltpu.CompilerParams(vmem_limit_bytes=VMEM_LIMIT),
    )(x, *others)


def exchange(x, axis, n, k):
    return lax.ppermute(x, axis, [(i, i ^ k) for i in range(n)])


def on_device(
    n_enc,
    n_seq,
    clip_features,
    clip_shape,
    packing,
    conv_weight,
    embed_weight,
    mod_shift,
    mod_scale,
    qkv_weight,
    q_gain,
    k_gain,
):
    caps = clip_features.shape[2:5]
    depth_all = clip_features.shape[5]
    cols = qkv_weight.shape[2]
    feats = embed_weight.shape[0]
    heads = cols // LANES
    rows = n_enc * BLOCK
    bf16, f32 = jnp.bfloat16, jnp.float32

    def folds(dtype, *lead):
        return jax.ShapeDtypeStruct((*lead, APAD, 3 * LANES), dtype)

    evens = [0]
    for bit in reversed(range(1, log2(n_enc))):
        evens += [at ^ (1 << bit) for at in evens]
    scale_rows, shift_rows = mod_scale.reshape(-1, LANES), mod_shift.reshape(-1, LANES)
    later = [
        clip_features.reshape(-1, depth_all),
        conv_weight.reshape(-1, depth_all),
        q_gain.reshape(1, -1),
        k_gain.reshape(1, -1),
    ]
    with jax.named_scope("fold"):
        embed, features, conv, q_gain, k_gain, keep, *sends = call(
            functools.partial(fold_kernel, len(later)),
            hbm(4 + len(later)),
            [jax.ShapeDtypeStruct(x.shape, x.dtype) for x in (embed_weight, *later)]
            + [folds(f32)]
            + [folds(bf16)] * max(heads - 1, 1),
            [
                pltpu.VMEM(scale_rows.shape, f32),
                pltpu.VMEM(shift_rows.shape, f32),
                pltpu.VMEM(qkv_weight.shape, bf16),
                pltpu.SemaphoreType.DMA((4 + len(later),)),
            ],
            cost=(200_000_000, 1_000_000),
        )(*map(in_hbm, (embed_weight, scale_rows, shift_rows, qkv_weight, *later)))

    with jax.named_scope("encode"):
        own_block = call(
            functools.partial(encode_kernel, caps),
            hbm(2) + vmem(2),
            [jax.ShapeDtypeStruct((APAD, NBS * BLOCK), bf16)],
            [
                pltpu.SMEM(clip_shape.shape, jnp.int32),
                pltpu.SMEM(packing.shape, jnp.int32),
                pltpu.SemaphoreType.DMA((2,)),
            ],
            cost=(500_000_000, 2_000_000),
        )(in_hbm(clip_shape), in_hbm(packing), features, conv)[0]

    def add(keep, got, first):
        kernel = functools.partial(add_kernel, len(got))
        return call(kernel, vmem(1 + len(got)) + after(1), [folds(f32), folds(bf16)])(keep, *got, first)

    with jax.named_scope("fold_sum"):
        if heads > 1:
            got = [exchange(sends[k - 1], "seq", n_seq, k) for k in reversed(range(1, heads))]
            keep, send = add(keep, got, own_block)
        else:
            send = sends[0]

    with jax.named_scope("gram"):
        gram = call(gram_kernel, vmem(1) + after(1), [jax.ShapeDtypeStruct((2 * feats, feats), bf16)])(embed, keep)[0]

    with jax.named_scope("tokens"):
        own_block = gate(own_block, keep)
        blocks = [own_block] + [exchange(own_block, "enc", n_enc, k) for k in evens[1:]]

    with jax.named_scope("fold_sum"):
        for bit in range(log2(heads), log2(n_seq)):
            got = exchange(send, "seq", n_seq, 1 << bit)
            if bit + 1 < log2(n_seq):
                keep, send = add(keep, [got], own_block)
            else:
                fresh, swap = call(
                    functools.partial(last_add_kernel, len(blocks)),
                    vmem(2 + len(blocks)) + after(1),
                    [folds(bf16), folds(bf16, 1 + len(blocks))],
                )(keep, got, *blocks, gram)

    partners = [(far, k) for far in evens for k in range(heads) if far or k]
    partners.sort(key=lambda p: (p[0].bit_count() + p[1].bit_count(), p[0]))
    half = len(partners) // 2
    assert len(partners) == 2 * half + 1
    both, lists = partners[0], (tuple(partners[1 : half + 1]), tuple(partners[half + 1 :]))

    def spread(x, partner_of):
        pairs = []
        for e in range(n_enc):
            far, k = partner_of[e & 1]
            pairs += [(e * n_seq + i, (e ^ far) * n_seq + (i ^ k)) for i in range(n_seq)]
        return lax.ppermute(x, ("enc", "seq"), pairs)

    with jax.named_scope("gather"):
        single = spread(fresh, (both, both))
        swapped = exchange(swap, "enc", n_enc, 1)
        pair = call(pair_kernel, vmem(2), [folds(bf16, 2)])(fresh, swapped)[0]
        got = [spread(pair, partner_of) for partner_of in zip(*lists)]

    with jax.named_scope("pack"):
        *shared, own_rows, own_mask, far_rows, far_mask = call(
            functools.partial(pack_kernel, tuple(evens), feats),
            vmem(4 + len(evens)),
            [
                jax.ShapeDtypeStruct((APAD, rows), bf16),
                jax.ShapeDtypeStruct((rows, LANES), bf16),
                jax.ShapeDtypeStruct((LANES, rows), bf16),
                jax.ShapeDtypeStruct((1, LANES), f32),
            ]
            + [jax.ShapeDtypeStruct((BLOCK, LANES), bf16)] * 4,
            [pltpu.VMEM((LANES, rows), f32)],
        )(q_gain, k_gain, gram, *blocks, swapped)

    def attend(rows_here, groups, done=(), first=()):
        count = sum(group.size for group in groups) // (APAD * 3 * LANES)
        total = count + sum(x.shape[1] for x in done) // LANES
        return call(
            functools.partial(attend_kernel, len(groups)),
            vmem(6 + len(groups) + len(done)) + after(len(first)),
            [jax.ShapeDtypeStruct((BLOCK, total * LANES), bf16)],
            cost=(count * 200_000_000, 1_000_000),
        )(*shared, *rows_here, *groups, *done, *first)[0]

    with jax.named_scope("attend"):
        own, other = (own_rows, own_mask), (far_rows, far_mask)
        early = [fresh, got[half - 1]]
        rest = got[: half - 1] + [single]
        early_other, early_own = attend(other, early), attend(own, early)
        near = exchange(attend(other, rest, [early_other], [early_own]), "enc", n_enc, 1)
        own_done = attend(own, rest, [early_own])
        return pl.pallas_call(
            functools.partial(output_kernel, heads, lists, both),
            in_specs=vmem(2),
            out_specs=hbm(1)[0],
            out_shape=jax.ShapeDtypeStruct((1, BLOCK, n_enc * cols), bf16),
            scratch_shapes=[pltpu.SemaphoreType.DMA((n_enc * heads,))],
            compiler_params=pltpu.CompilerParams(vmem_limit_bytes=VMEM_LIMIT),
        )(own_done, near)


def solution(mesh):
    return jax.shard_map(
        functools.partial(on_device, mesh.shape["enc"], mesh.shape["seq"]),
        mesh=mesh,
        in_specs=(
            P("enc", "seq", None, None, None, None),
            P("enc", "seq", None),
            P("enc", "seq", None, None),
            P(),
            P(),
            P(),
            P(),
            P(None, "seq", "enc"),
            P(),
            P(),
        ),
        out_specs=P("seq", "enc", None),
        check_vma=False,
    )
```

```python
import functools
import math

import jax
import jax.numpy as jnp
from jax import lax
from jax.experimental import pallas as pl
from jax.experimental.pallas import tpu as pltpu
from jax.sharding import PartitionSpec as P

BLOCK = 128
NBS = 2
LANES = 128
APAD = 72
eps_norm = 1e-06
FAR = 2.0**20
VMEM_LIMIT = 48 * 1024 * 1024


def mm(a, b, dims=((1,), (0,)), precision=None):
    return lax.dot_general(a, b, (dims, ((), ())), preferred_element_type=jnp.float32, precision=precision)


def split_bf16(x):
    hi = x.astype(jnp.bfloat16)
    return hi, (x - hi.astype(jnp.float32)).astype(jnp.bfloat16)


def log2(n):
    bits = n.bit_length() - 1
    assert 1 << bits == n
    return bits


def fetch(pairs, sems):
    copies = [pltpu.make_async_copy(src, dst, sems.at[i]) for i, (src, dst) in enumerate(pairs)]
    for copy in copies:
        copy.start()
    return copies


def fold_kernel(count, embed_hbm, scale_hbm, shift_hbm, w_hbm, *refs):
    later_hbm, embed_ref, later, keep_ref, sends = refs[:count], refs[count], refs[count + 1 : 2 * count + 1], refs[2 * count + 1], refs[2 * count + 2 : -4]
    scale_ref, shift_ref, w_ref, sems = refs[-4:]
    copies = fetch(
        [(embed_hbm, embed_ref), (scale_hbm, scale_ref), (shift_hbm, shift_ref), (w_hbm, w_ref)]
        + list(zip(later_hbm, later)),
        sems,
    )
    me = lax.axis_index("seq")
    _, depth, cols = w_ref.shape
    feats = embed_ref.shape[0]
    heads = cols // LANES
    for copy in copies[:3]:
        copy.wait()
    mean = jnp.sum(embed_ref[...].astype(jnp.float32), axis=1, keepdims=True) / embed_ref.shape[1]
    span = max(depth, LANES)
    chunks = span // LANES
    first = (me * depth) // LANES
    emb = embed_ref[:, pl.ds(pl.multiple_of(first * LANES, LANES), span)].astype(jnp.float32) - mean
    scale = jnp.concatenate([scale_ref[pl.ds(first + i, 1), :] for i in range(chunks)], axis=1)
    shift = jnp.concatenate([shift_ref[pl.ds(first + i, 1), :] for i in range(chunks)], axis=1)
    left = jnp.concatenate(
        [emb * (1.0 + scale), shift, jnp.zeros((APAD - feats - 1, span), jnp.float32)], axis=0
    )
    if depth < LANES:
        low = me * depth - first * LANES
        lane = lax.broadcasted_iota(jnp.int32, left.shape, 1)
        left = jnp.where((lane >= low) & (lane < low + depth), left, 0.0)
    hi, lo = split_bf16(left)
    both = jnp.concatenate([hi, lo], axis=0)
    copies[3].wait()

    def product(head):
        start = pl.multiple_of(head * LANES, LANES)
        right = jnp.concatenate([w_ref[part, :, pl.ds(start, LANES)] for part in range(3)], axis=1)
        right = jnp.concatenate([right] * (span // depth), axis=0)
        total = mm(both, right)
        return total[:APAD] + total[APAD:]

    slot = me & (heads - 1)
    for k in range(1, heads):
        sends[k - 1][...] = product(slot ^ k).astype(jnp.bfloat16)
    total = product(slot)
    keep_ref[...] = total
    if heads == 1:
        sends[0][...] = total.astype(jnp.bfloat16)
    for copy in copies[4:]:
        copy.wait()


def add_kernel(count, keep_in, *refs):
    total = keep_in[...]
    for ref in refs[:count]:
        total = total + ref[...].astype(jnp.float32)
    refs[-2][...] = total
    refs[-1][...] = total.astype(jnp.bfloat16)


def last_add_kernel(count, keep_in, got_ref, *refs):
    total = (keep_in[...] + got_ref[...].astype(jnp.float32)).astype(jnp.bfloat16)
    out_ref, swap_ref = refs[-2:]
    out_ref[...] = total
    swap_ref[0] = total
    for i in range(count):
        width = refs[i].shape[1]
        swap_ref[1 + i, :, :width] = refs[i][...]
        swap_ref[1 + i, :, width:] = jnp.zeros((total.shape[0], total.shape[1] - width), jnp.bfloat16)


def pair_kernel(own_ref, swapped_ref, out_ref):
    out_ref[0] = own_ref[...]
    out_ref[1] = swapped_ref[0]


def gate_kernel(*refs):
    pass


def encode_kernel(caps, shape_hbm, plan_hbm, feat_ref, conv_ref, out_ref, shape_ref, plan_ref, sems):
    copies = fetch([(shape_hbm, shape_ref), (plan_hbm, plan_ref)], sems)
    frames_cap, height_cap, width_cap = caps
    spots = frames_cap * height_cap * width_cap
    frame_size = height_cap * width_cap
    latent_ch = conv_ref.shape[0] // 27
    feats = 4 * latent_ch
    taps = mm(conv_ref[...], feat_ref[...], ((1,), (1,)))
    copies[0].wait()
    copies[1].wait()
    frames, height, width = shape_ref[0, 0, 0], shape_ref[0, 0, 1], shape_ref[0, 0, 2]
    spot = lax.broadcasted_iota(jnp.int32, (1, spots), 1)
    frame_ix = spot // frame_size
    row_ix = (spot % frame_size) // width_cap
    col_ix = spot % width_cap
    inside = (frame_ix < frames) & (row_ix < height) & (col_ix < width)
    taps = jnp.where(inside, taps, 0.0)

    def tap(a, b, j):
        at = (9 * a + 3 * b + j) * latent_ch
        return taps[at : at + latent_ch]

    def later(x, by):
        zeros = jnp.zeros((latent_ch, by * frame_size), jnp.float32)
        return jnp.concatenate([zeros, x[:, : spots - by * frame_size]], axis=1)

    def over_frames(b, j):
        return tap(2, b, j) + later(tap(1, b, j), 1) + later(tap(0, b, j), 2)

    def over_rows(j):
        above = pltpu.roll(over_frames(0, j), width_cap, 1)
        below = pltpu.roll(over_frames(2, j), spots - width_cap, 1)
        return (
            over_frames(1, j)
            + jnp.where(row_ix >= 1, above, 0.0)
            + jnp.where(row_ix < height_cap - 1, below, 0.0)
        )

    latent = (
        over_rows(1)
        + jnp.where(col_ix >= 1, pltpu.roll(over_rows(0), 1, 1), 0.0)
        + jnp.where(col_ix < width_cap - 1, pltpu.roll(over_rows(2), spots - 1, 1), 0.0)
    )
    latent = latent.astype(jnp.bfloat16).astype(jnp.float32)
    shifted = [latent] + [pltpu.roll(latent, spots - by, 1) for by in (1, width_cap, width_cap + 1)]
    patches = jnp.concatenate(shifted, axis=0).astype(jnp.bfloat16)

    tokens = NBS * BLOCK
    half_w = (width // 2).astype(jnp.float32)
    per_frame_int = (height // 2) * (width // 2)
    per_frame = per_frame_int.astype(jnp.float32)
    live = frames * per_frame_int
    token_int = lax.broadcasted_iota(jnp.int32, (1, tokens), 1)
    token = token_int.astype(jnp.float32)
    frame_of = jnp.floor((token + 0.5) / jnp.full((1, tokens), per_frame))
    within = token - frame_of * per_frame
    row_of = jnp.floor((within + 0.5) / jnp.full((1, tokens), half_w))
    col_of = within - row_of * half_w
    source = (frame_of * frame_size + row_of * (2 * width_cap) + col_of * 2).astype(jnp.int32)
    source = jnp.where(token_int < live, source, -1)
    chosen = lax.broadcasted_iota(jnp.int32, (spots, tokens), 0) == source
    picked = mm(patches, jnp.where(chosen, 1.0, 0.0).astype(jnp.bfloat16))
    kind = lax.broadcasted_iota(jnp.int32, (APAD - feats, BLOCK), 0)
    infos = []
    for b in range(NBS):
        count = jnp.clip(live - b * BLOCK, 0, BLOCK)
        info = jnp.where(
            kind == 0,
            plan_ref[0, 0, b, 0],
            jnp.where(kind == 1, plan_ref[0, 0, b, 1], jnp.where(kind == 2, count, 0)),
        )
        infos.append(info.astype(jnp.float32))
    info = jnp.concatenate(infos, axis=1)
    out_ref[...] = jnp.concatenate([picked, info], axis=0).astype(jnp.bfloat16)


def gram_kernel(embed_ref, first_ref, out_ref):
    feats, width = embed_ref.shape
    emb = embed_ref[...].astype(jnp.float32)
    emb = emb - jnp.sum(emb, axis=1, keepdims=True) / width
    both = jnp.concatenate(split_bf16(emb), axis=0)
    gram = mm(both, both, ((1,), (1,))) / width
    gram = gram[:feats] + gram[feats:]
    out_ref[...] = jnp.concatenate(split_bf16(gram[:, :feats] + gram[:, feats:]), axis=0)


def pack_kernel(evens, feats, q_gain_ref, k_gain_ref, gram_ref, *refs):
    here, near = refs[: len(evens)], refs[len(evens)]
    x_t_ref, x_ref, key_mask_ref, gain_ref, *row_refs, rows_t = refs[len(evens) + 1 :]
    n_enc = 2 * len(evens)
    mine = lax.axis_index("enc")
    rows = n_enc * BLOCK
    lane = lax.broadcasted_iota(jnp.int32, (1, BLOCK), 1).astype(jnp.float32)
    extra = lax.broadcasted_iota(jnp.int32, (APAD - feats, BLOCK), 0)
    found = []
    blocks = [(at, here[i][...]) for i, at in enumerate(evens)]
    blocks += [(at ^ 1, near[1 + i]) for i, at in enumerate(evens)]
    for distance, block in blocks:
        source = mine ^ distance
        for b in range(NBS):
            tile = block[:, b * BLOCK : (b + 1) * BLOCK].astype(jnp.float32)
            owner, offset, count = (tile[feats + i : feats + i + 1] for i in range(3))
            owner = jnp.where(offset == 0.0, owner, -1.0)
            segment = jnp.where(lane < count, (source + 1).astype(jnp.float32), 0.0)
            found.append((owner, segment, tile[:feats]))
    at = lax.broadcasted_iota(jnp.int32, (feats, feats), 0)
    frm = lax.broadcasted_iota(jnp.int32, (feats, feats), 1)
    order = jnp.where(frm == (at % 4) * (feats // 4) + at // 4, 1.0, 0.0).astype(jnp.bfloat16)
    for o in range(n_enc):
        segment = jnp.zeros((1, BLOCK), jnp.float32)
        body = jnp.zeros((feats, BLOCK), jnp.float32)
        for owner, seg_of, tile in found:
            hit = owner == float(o)
            segment = segment + jnp.where(hit, seg_of, 0.0)
            body = body + jnp.where(hit, tile, 0.0)
        tail = jnp.where(extra == 0, 1.0, jnp.where(extra == 1, segment, 0.0))
        rows_t[:, o * BLOCK : (o + 1) * BLOCK] = jnp.concatenate(
            [body, tail, jnp.zeros((LANES - APAD, BLOCK), jnp.float32)], axis=0
        )
    picked = mm(order, rows_t[:feats].astype(jnp.bfloat16))
    spread = mm(gram_ref[...], picked.astype(jnp.bfloat16))
    variance = jnp.sum((spread[:feats] + spread[feats:]) * picked, axis=0, keepdims=True)
    rows_t[:feats] = picked * lax.rsqrt(jnp.maximum(variance, 0.0) + eps_norm)
    x_t = rows_t[...]
    x_t_ref[...] = x_t[:APAD].astype(jnp.bfloat16)
    x_ref[...] = x_t.T.astype(jnp.bfloat16)
    group_t = lax.broadcasted_iota(jnp.int32, (LANES, rows), 0).astype(jnp.float32)
    key_mask_ref[...] = jnp.where(x_t[feats + 1 : feats + 2] == group_t, 0.0, 1.0).astype(jnp.bfloat16)
    group = lax.broadcasted_iota(jnp.int32, (BLOCK, LANES), 1).astype(jnp.float32)
    for core in range(2):
        rows_ref, mask_ref = row_refs[2 * core : 2 * core + 2]
        own = rows_t[:, pl.ds(pl.multiple_of((mine ^ core) * BLOCK, BLOCK), BLOCK)].T
        rows_ref[...] = own.astype(jnp.bfloat16)
        mask_ref[...] = jnp.where(own[:, feats + 1 : feats + 2] == group, -FAR, 0.0).astype(jnp.bfloat16)
    head_dim = q_gain_ref.shape[1]
    gain_ref[...] = q_gain_ref[...] * k_gain_ref[...] * (head_dim**-0.5 * math.log2(math.e))


def attend_heads(folds, place, x_t_ref, x_ref, key_mask_ref, gain_ref, own_ref, own_mask_ref):
    folds = list(folds)
    heads = range(len(folds))

    def side(part):
        return jnp.concatenate([fold[:, part * LANES : (part + 1) * LANES] for fold in folds], axis=1)

    def of(i):
        return slice(i * LANES, (i + 1) * LANES)

    keys = mm(side(1), x_t_ref[...], ((0,), (0,)))
    queries = mm(own_ref[:, :APAD], side(0))
    values = mm(x_ref[:, :APAD], side(2)).astype(jnp.bfloat16)
    gain, own_mask, key_mask = gain_ref[...], own_mask_ref[...], key_mask_ref[...]
    left, right = [], []
    for i in heads:
        key = keys[of(i)]
        square = jnp.sum(key * key, axis=0, keepdims=True) / LANES
        key = (key * lax.rsqrt(square + eps_norm)).astype(jnp.bfloat16)
        right.append(jnp.concatenate([key, key_mask], axis=0))
        query = queries[:, of(i)]
        square = jnp.sum(query * query, axis=1, keepdims=True) / LANES
        query = (query * lax.rsqrt(square + eps_norm) * gain).astype(jnp.bfloat16)
        left.append(jnp.concatenate([query, own_mask], axis=1))
    scores = [mm(left[i], right[i]) for i in heads]
    weights = [jnp.exp2(score).astype(jnp.bfloat16) for score in scores]
    ones = jnp.ones((values.shape[0], LANES), jnp.bfloat16)
    mixed = [mm(weights[i], jnp.concatenate([values[:, of(i)], ones], axis=1)) for i in heads]
    for i in heads:
        place(i, (mixed[i][:, :LANES] / mixed[i][:, LANES:]).astype(jnp.bfloat16))


def each_head(refs):
    for ref in refs:
        if len(ref.shape) == 2:
            yield ref[...]
        else:
            for i in range(ref.shape[0]):
                yield ref[i]


def attend_kernel(count, *refs):
    folds, out_ref = refs[6 : 6 + count], refs[-1]
    first = 0
    if len(refs) > 7 + count:
        done_ref = refs[6 + count]
        first = done_ref.shape[1] // LANES
        out_ref[:, : first * LANES] = done_ref[...]

    def place(i, result):
        out_ref[:, (first + i) * LANES : (first + i + 1) * LANES] = result

    attend_heads(each_head(folds), place, *refs[:6])


def output_kernel(heads, lists, both, own_ref, near_ref, out_ref, sems):
    mine, slot = lax.axis_index("enc"), lax.axis_index("seq") & (heads - 1)
    half = len(lists[0])
    copies = []

    def put(ref, at, base, far, k):
        head = (base ^ far) * heads + (slot ^ k)
        column = pl.ds(pl.multiple_of(head * LANES, LANES), LANES)
        result = ref.at[:, at * LANES : (at + 1) * LANES]
        copies.append(pltpu.make_async_copy(result, out_ref.at[0, :, column], sems.at[len(copies)]))
        copies[-1].start()

    for ref, base in ((near_ref, mine ^ 1), (own_ref, mine)):
        put(ref, 0, base, 0, 0)
        put(ref, 1, base, *both)
        for i in range(half):
            pair = zip(lists[0][i], lists[1][i])
            far, k = (jnp.where(base & 1 == 0, zero, one) for zero, one in pair)
            put(ref, 2 + 2 * i, base, far, k)
            put(ref, 3 + 2 * i, base, far ^ 1, k)
    for copy in copies:
        copy.wait()


def vmem(count):
    return [pl.BlockSpec(memory_space=pltpu.VMEM)] * count


def hbm(count):
    return [pl.BlockSpec(memory_space=pltpu.HBM)] * count


def in_hbm(x):
    return pltpu.with_memory_space_constraint(x, pltpu.HBM)


def after(count):
    return [pl.BlockSpec(memory_space=pl.ANY)] * count


def call(kernel, ins, out_shape, scratch=(), cost=(1_000_000, 1_000_000)):
    return pl.pallas_call(
        kernel,
        in_specs=ins,
        out_specs=[pl.BlockSpec(memory_space=pltpu.VMEM)] * len(out_shape),
        out_shape=out_shape,
        scratch_shapes=list(scratch),
        compiler_params=pltpu.CompilerParams(vmem_limit_bytes=VMEM_LIMIT),
        cost_estimate=pl.CostEstimate(flops=cost[0], bytes_accessed=cost[1], transcendentals=0),
    )


def gate(x, *others):
    return pl.pallas_call(
        gate_kernel,
        in_specs=after(1 + len(others)),
        out_specs=after(1)[0],
        out_shape=jax.ShapeDtypeStruct(x.shape, x.dtype),
        input_output_aliases={0: 0},
        compiler_params=pltpu.CompilerParams(vmem_limit_bytes=VMEM_LIMIT),
    )(x, *others)


def exchange(x, axis, n, k):
    return lax.ppermute(x, axis, [(i, i ^ k) for i in range(n)])


def on_device(
    n_enc,
    n_seq,
    clip_features,
    clip_shape,
    packing,
    conv_weight,
    embed_weight,
    mod_shift,
    mod_scale,
    qkv_weight,
    q_gain,
    k_gain,
):
    caps = clip_features.shape[2:5]
    depth_all = clip_features.shape[5]
    cols = qkv_weight.shape[2]
    feats = embed_weight.shape[0]
    heads = cols // LANES
    rows = n_enc * BLOCK
    bf16, f32 = jnp.bfloat16, jnp.float32

    def folds(dtype, *lead):
        return jax.ShapeDtypeStruct((*lead, APAD, 3 * LANES), dtype)

    evens = [0]
    for bit in reversed(range(1, log2(n_enc))):
        evens += [at ^ (1 << bit) for at in evens]
    scale_rows, shift_rows = mod_scale.reshape(-1, LANES), mod_shift.reshape(-1, LANES)
    later = [
        clip_features.reshape(-1, depth_all),
        conv_weight.reshape(-1, depth_all),
        q_gain.reshape(1, -1),
        k_gain.reshape(1, -1),
    ]
    with jax.named_scope("fold"):
        embed, features, conv, q_gain, k_gain, keep, *sends = call(
            functools.partial(fold_kernel, len(later)),
            hbm(4 + len(later)),
            [jax.ShapeDtypeStruct(x.shape, x.dtype) for x in (embed_weight, *later)]
            + [folds(f32)]
            + [folds(bf16)] * max(heads - 1, 1),
            [
                pltpu.VMEM(scale_rows.shape, f32),
                pltpu.VMEM(shift_rows.shape, f32),
                pltpu.VMEM(qkv_weight.shape, bf16),
                pltpu.SemaphoreType.DMA((4 + len(later),)),
            ],
            cost=(200_000_000, 1_000_000),
        )(*map(in_hbm, (embed_weight, scale_rows, shift_rows, qkv_weight, *later)))

    with jax.named_scope("encode"):
        own_block = call(
            functools.partial(encode_kernel, caps),
            hbm(2) + vmem(2),
            [jax.ShapeDtypeStruct((APAD, NBS * BLOCK), bf16)],
            [
                pltpu.SMEM(clip_shape.shape, jnp.int32),
                pltpu.SMEM(packing.shape, jnp.int32),
                pltpu.SemaphoreType.DMA((2,)),
            ],
            cost=(500_000_000, 2_000_000),
        )(in_hbm(clip_shape), in_hbm(packing), features, conv)[0]

    def add(keep, got, first):
        kernel = functools.partial(add_kernel, len(got))
        return call(kernel, vmem(1 + len(got)) + after(1), [folds(f32), folds(bf16)])(keep, *got, first)

    with jax.named_scope("fold_sum"):
        if heads > 1:
            got = [exchange(sends[k - 1], "seq", n_seq, k) for k in reversed(range(1, heads))]
            keep, send = add(keep, got, own_block)
        else:
            send = sends[0]

    with jax.named_scope("gram"):
        gram = call(gram_kernel, vmem(1) + after(1), [jax.ShapeDtypeStruct((2 * feats, feats), bf16)])(embed, keep)[0]

    with jax.named_scope("tokens"):
        own_block = gate(own_block, keep)
        blocks = [own_block] + [exchange(own_block, "enc", n_enc, k) for k in evens[1:]]

    with jax.named_scope("fold_sum"):
        for bit in range(log2(heads), log2(n_seq)):
            got = exchange(send, "seq", n_seq, 1 << bit)
            if bit + 1 < log2(n_seq):
                keep, send = add(keep, [got], own_block)
            else:
                fresh, swap = call(
                    functools.partial(last_add_kernel, len(blocks)),
                    vmem(2 + len(blocks)) + after(1),
                    [folds(bf16), folds(bf16, 1 + len(blocks))],
                )(keep, got, *blocks, gram)

    partners = [(far, k) for far in evens for k in range(heads) if far or k]
    partners.sort(key=lambda p: (p[0].bit_count() + p[1].bit_count(), p[0]))
    half = len(partners) // 2
    assert len(partners) == 2 * half + 1
    both, lists = partners[0], (tuple(partners[1 : half + 1]), tuple(partners[half + 1 :]))

    def spread(x, partner_of):
        pairs = []
        for e in range(n_enc):
            far, k = partner_of[e & 1]
            pairs += [(e * n_seq + i, (e ^ far) * n_seq + (i ^ k)) for i in range(n_seq)]
        return lax.ppermute(x, ("enc", "seq"), pairs)

    with jax.named_scope("gather"):
        single = spread(fresh, (both, both))
        swapped = exchange(swap, "enc", n_enc, 1)
        pair = call(pair_kernel, vmem(2), [folds(bf16, 2)])(fresh, swapped)[0]
        got = [spread(pair, partner_of) for partner_of in zip(*lists)]

    with jax.named_scope("pack"):
        *shared, own_rows, own_mask, far_rows, far_mask = call(
            functools.partial(pack_kernel, tuple(evens), feats),
            vmem(4 + len(evens)),
            [
                jax.ShapeDtypeStruct((APAD, rows), bf16),
                jax.ShapeDtypeStruct((rows, LANES), bf16),
                jax.ShapeDtypeStruct((LANES, rows), bf16),
                jax.ShapeDtypeStruct((1, LANES), f32),
            ]
            + [jax.ShapeDtypeStruct((BLOCK, LANES), bf16)] * 4,
            [pltpu.VMEM((LANES, rows), f32)],
        )(q_gain, k_gain, gram, *blocks, swapped)

    def attend(rows_here, groups, done=(), first=()):
        count = sum(group.size for group in groups) // (APAD * 3 * LANES)
        total = count + sum(x.shape[1] for x in done) // LANES
        return call(
            functools.partial(attend_kernel, len(groups)),
            vmem(6 + len(groups) + len(done)) + after(len(first)),
            [jax.ShapeDtypeStruct((BLOCK, total * LANES), bf16)],
            cost=(count * 200_000_000, 1_000_000),
        )(*shared, *rows_here, *groups, *done, *first)[0]

    with jax.named_scope("attend"):
        own, other = (own_rows, own_mask), (far_rows, far_mask)
        early, rest = [fresh, single], got
        early_other, early_own = attend(other, early), attend(own, early)
        near = exchange(attend(other, rest, [early_other], [early_own]), "enc", n_enc, 1)
        own_done = attend(own, rest, [early_own])
        return pl.pallas_call(
            functools.partial(output_kernel, heads, lists, both),
            in_specs=vmem(2),
            out_specs=hbm(1)[0],
            out_shape=jax.ShapeDtypeStruct((1, BLOCK, n_enc * cols), bf16),
            scratch_shapes=[pltpu.SemaphoreType.DMA((n_enc * heads,))],
            compiler_params=pltpu.CompilerParams(vmem_limit_bytes=VMEM_LIMIT),
        )(own_done, near)


def solution(mesh):
    return jax.shard_map(
        functools.partial(on_device, mesh.shape["enc"], mesh.shape["seq"]),
        mesh=mesh,
        in_specs=(
            P("enc", "seq", None, None, None, None),
            P("enc", "seq", None),
            P("enc", "seq", None, None),
            P(),
            P(),
            P(),
            P(),
            P(None, "seq", "enc"),
            P(),
            P(),
        ),
        out_specs=P("seq", "enc", None),
        check_vma=False,
    )
```

```python
import functools
import math

import jax
import jax.numpy as jnp
from jax import lax
from jax.experimental import pallas as pl
from jax.experimental.pallas import tpu as pltpu
from jax.sharding import PartitionSpec as P

BLOCK = 128
NBS = 2
LANES = 128
APAD = 72
eps_norm = 1e-06
FAR = 2.0**20
VMEM_LIMIT = 48 * 1024 * 1024


def mm(a, b, dims=((1,), (0,)), precision=None):
    return lax.dot_general(a, b, (dims, ((), ())), preferred_element_type=jnp.float32, precision=precision)


def split_bf16(x):
    hi = x.astype(jnp.bfloat16)
    return hi, (x - hi.astype(jnp.float32)).astype(jnp.bfloat16)


def log2(n):
    bits = n.bit_length() - 1
    assert 1 << bits == n
    return bits


def fetch(pairs, sems):
    copies = [pltpu.make_async_copy(src, dst, sems.at[i]) for i, (src, dst) in enumerate(pairs)]
    for copy in copies:
        copy.start()
    return copies


def fold_kernel(count, embed_hbm, scale_hbm, shift_hbm, w_hbm, *refs):
    later_hbm, embed_ref, later, keep_ref, sends = refs[:count], refs[count], refs[count + 1 : 2 * count + 1], refs[2 * count + 1], refs[2 * count + 2 : -4]
    scale_ref, shift_ref, w_ref, sems = refs[-4:]
    copies = fetch(
        [(embed_hbm, embed_ref), (scale_hbm, scale_ref), (shift_hbm, shift_ref), (w_hbm, w_ref)]
        + list(zip(later_hbm, later)),
        sems,
    )
    me = lax.axis_index("seq")
    _, depth, cols = w_ref.shape
    feats = embed_ref.shape[0]
    heads = cols // LANES
    for copy in copies[:3]:
        copy.wait()
    mean = jnp.sum(embed_ref[...].astype(jnp.float32), axis=1, keepdims=True) / embed_ref.shape[1]
    span = max(depth, LANES)
    chunks = span // LANES
    first = (me * depth) // LANES
    emb = embed_ref[:, pl.ds(pl.multiple_of(first * LANES, LANES), span)].astype(jnp.float32) - mean
    scale = jnp.concatenate([scale_ref[pl.ds(first + i, 1), :] for i in range(chunks)], axis=1)
    shift = jnp.concatenate([shift_ref[pl.ds(first + i, 1), :] for i in range(chunks)], axis=1)
    left = jnp.concatenate(
        [emb * (1.0 + scale), shift, jnp.zeros((APAD - feats - 1, span), jnp.float32)], axis=0
    )
    if depth < LANES:
        low = me * depth - first * LANES
        lane = lax.broadcasted_iota(jnp.int32, left.shape, 1)
        left = jnp.where((lane >= low) & (lane < low + depth), left, 0.0)
    hi, lo = split_bf16(left)
    both = jnp.concatenate([hi, lo], axis=0)
    copies[3].wait()

    def product(head):
        start = pl.multiple_of(head * LANES, LANES)
        right = jnp.concatenate([w_ref[part, :, pl.ds(start, LANES)] for part in range(3)], axis=1)
        right = jnp.concatenate([right] * (span // depth), axis=0)
        total = mm(both, right)
        return total[:APAD] + total[APAD:]

    slot = me & (heads - 1)
    for k in range(1, heads):
        sends[k - 1][...] = product(slot ^ k).astype(jnp.bfloat16)
    total = product(slot)
    keep_ref[...] = total
    if heads == 1:
        sends[0][...] = total.astype(jnp.bfloat16)
    for copy in copies[4:]:
        copy.wait()


def add_kernel(count, keep_in, *refs):
    total = keep_in[...]
    for ref in refs[:count]:
        total = total + ref[...].astype(jnp.float32)
    refs[-2][...] = total
    refs[-1][...] = total.astype(jnp.bfloat16)


def last_add_kernel(count, keep_in, got_ref, *refs):
    total = (keep_in[...] + got_ref[...].astype(jnp.float32)).astype(jnp.bfloat16)
    out_ref, swap_ref = refs[-2:]
    out_ref[...] = total
    swap_ref[0] = total
    for i in range(count):
        width = refs[i].shape[1]
        swap_ref[1 + i, :, :width] = refs[i][...]
        swap_ref[1 + i, :, width:] = jnp.zeros((total.shape[0], total.shape[1] - width), jnp.bfloat16)


def pair_kernel(own_ref, swapped_ref, out_ref):
    out_ref[0] = own_ref[...]
    out_ref[1] = swapped_ref[0]


def gate_kernel(*refs):
    pass


def encode_kernel(caps, shape_hbm, plan_hbm, feat_ref, conv_ref, out_ref, shape_ref, plan_ref, sems):
    copies = fetch([(shape_hbm, shape_ref), (plan_hbm, plan_ref)], sems)
    frames_cap, height_cap, width_cap = caps
    spots = frames_cap * height_cap * width_cap
    frame_size = height_cap * width_cap
    latent_ch = conv_ref.shape[0] // 27
    feats = 4 * latent_ch
    taps = mm(conv_ref[...], feat_ref[...], ((1,), (1,)))
    copies[0].wait()
    copies[1].wait()
    frames, height, width = shape_ref[0, 0, 0], shape_ref[0, 0, 1], shape_ref[0, 0, 2]
    spot = lax.broadcasted_iota(jnp.int32, (1, spots), 1)
    frame_ix = spot // frame_size
    row_ix = (spot % frame_size) // width_cap
    col_ix = spot % width_cap
    inside = (frame_ix < frames) & (row_ix < height) & (col_ix < width)
    taps = jnp.where(inside, taps, 0.0)

    def tap(a, b, j):
        at = (9 * a + 3 * b + j) * latent_ch
        return taps[at : at + latent_ch]

    def later(x, by):
        zeros = jnp.zeros((latent_ch, by * frame_size), jnp.float32)
        return jnp.concatenate([zeros, x[:, : spots - by * frame_size]], axis=1)

    def over_frames(b, j):
        return tap(2, b, j) + later(tap(1, b, j), 1) + later(tap(0, b, j), 2)

    def over_rows(j):
        above = pltpu.roll(over_frames(0, j), width_cap, 1)
        below = pltpu.roll(over_frames(2, j), spots - width_cap, 1)
        return (
            over_frames(1, j)
            + jnp.where(row_ix >= 1, above, 0.0)
            + jnp.where(row_ix < height_cap - 1, below, 0.0)
        )

    latent = (
        over_rows(1)
        + jnp.where(col_ix >= 1, pltpu.roll(over_rows(0), 1, 1), 0.0)
        + jnp.where(col_ix < width_cap - 1, pltpu.roll(over_rows(2), spots - 1, 1), 0.0)
    )
    latent = latent.astype(jnp.bfloat16).astype(jnp.float32)
    shifted = [latent] + [pltpu.roll(latent, spots - by, 1) for by in (1, width_cap, width_cap + 1)]
    patches = jnp.concatenate(shifted, axis=0).astype(jnp.bfloat16)

    tokens = NBS * BLOCK
    half_w = (width // 2).astype(jnp.float32)
    per_frame_int = (height // 2) * (width // 2)
    per_frame = per_frame_int.astype(jnp.float32)
    live = frames * per_frame_int
    token_int = lax.broadcasted_iota(jnp.int32, (1, tokens), 1)
    token = token_int.astype(jnp.float32)
    frame_of = jnp.floor((token + 0.5) / jnp.full((1, tokens), per_frame))
    within = token - frame_of * per_frame
    row_of = jnp.floor((within + 0.5) / jnp.full((1, tokens), half_w))
    col_of = within - row_of * half_w
    source = (frame_of * frame_size + row_of * (2 * width_cap) + col_of * 2).astype(jnp.int32)
    source = jnp.where(token_int < live, source, -1)
    chosen = lax.broadcasted_iota(jnp.int32, (spots, tokens), 0) == source
    picked = mm(patches, jnp.where(chosen, 1.0, 0.0).astype(jnp.bfloat16))
    kind = lax.broadcasted_iota(jnp.int32, (APAD - feats, BLOCK), 0)
    infos = []
    for b in range(NBS):
        count = jnp.clip(live - b * BLOCK, 0, BLOCK)
        info = jnp.where(
            kind == 0,
            plan_ref[0, 0, b, 0],
            jnp.where(kind == 1, plan_ref[0, 0, b, 1], jnp.where(kind == 2, count, 0)),
        )
        infos.append(info.astype(jnp.float32))
    info = jnp.concatenate(infos, axis=1)
    out_ref[...] = jnp.concatenate([picked, info], axis=0).astype(jnp.bfloat16)


def gram_kernel(embed_ref, first_ref, out_ref):
    feats, width = embed_ref.shape
    emb = embed_ref[...].astype(jnp.float32)
    emb = emb - jnp.sum(emb, axis=1, keepdims=True) / width
    both = jnp.concatenate(split_bf16(emb), axis=0)
    gram = mm(both, both, ((1,), (1,))) / width
    gram = gram[:feats] + gram[feats:]
    out_ref[...] = jnp.concatenate(split_bf16(gram[:, :feats] + gram[:, feats:]), axis=0)


def pack_kernel(evens, feats, q_gain_ref, k_gain_ref, gram_ref, *refs):
    here, near = refs[: len(evens)], refs[len(evens)]
    x_t_ref, x_ref, key_mask_ref, gain_ref, *row_refs, rows_t = refs[len(evens) + 1 :]
    n_enc = 2 * len(evens)
    mine = lax.axis_index("enc")
    rows = n_enc * BLOCK
    lane = lax.broadcasted_iota(jnp.int32, (1, BLOCK), 1).astype(jnp.float32)
    extra = lax.broadcasted_iota(jnp.int32, (APAD - feats, BLOCK), 0)
    found = []
    blocks = [(at, here[i][...]) for i, at in enumerate(evens)]
    blocks += [(at ^ 1, near[1 + i]) for i, at in enumerate(evens)]
    for distance, block in blocks:
        source = mine ^ distance
        for b in range(NBS):
            tile = block[:, b * BLOCK : (b + 1) * BLOCK].astype(jnp.float32)
            owner, offset, count = (tile[feats + i : feats + i + 1] for i in range(3))
            owner = jnp.where(offset == 0.0, owner, -1.0)
            segment = jnp.where(lane < count, (source + 1).astype(jnp.float32), 0.0)
            found.append((owner, segment, tile[:feats]))
    at = lax.broadcasted_iota(jnp.int32, (feats, feats), 0)
    frm = lax.broadcasted_iota(jnp.int32, (feats, feats), 1)
    order = jnp.where(frm == (at % 4) * (feats // 4) + at // 4, 1.0, 0.0).astype(jnp.bfloat16)
    for o in range(n_enc):
        segment = jnp.zeros((1, BLOCK), jnp.float32)
        body = jnp.zeros((feats, BLOCK), jnp.float32)
        for owner, seg_of, tile in found:
            hit = owner == float(o)
            segment = segment + jnp.where(hit, seg_of, 0.0)
            body = body + jnp.where(hit, tile, 0.0)
        tail = jnp.where(extra == 0, 1.0, jnp.where(extra == 1, segment, 0.0))
        rows_t[:, o * BLOCK : (o + 1) * BLOCK] = jnp.concatenate(
            [body, tail, jnp.zeros((LANES - APAD, BLOCK), jnp.float32)], axis=0
        )
    picked = mm(order, rows_t[:feats].astype(jnp.bfloat16))
    spread = mm(gram_ref[...], picked.astype(jnp.bfloat16))
    variance = jnp.sum((spread[:feats] + spread[feats:]) * picked, axis=0, keepdims=True)
    rows_t[:feats] = picked * lax.rsqrt(jnp.maximum(variance, 0.0) + eps_norm)
    x_t = rows_t[...]
    x_t_ref[...] = x_t[:APAD].astype(jnp.bfloat16)
    x_ref[...] = x_t.T.astype(jnp.bfloat16)
    group_t = lax.broadcasted_iota(jnp.int32, (LANES, rows), 0).astype(jnp.float32)
    key_mask_ref[...] = jnp.where(x_t[feats + 1 : feats + 2] == group_t, 0.0, 1.0).astype(jnp.bfloat16)
    group = lax.broadcasted_iota(jnp.int32, (BLOCK, LANES), 1).astype(jnp.float32)
    for core in range(2):
        rows_ref, mask_ref = row_refs[2 * core : 2 * core + 2]
        own = rows_t[:, pl.ds(pl.multiple_of((mine ^ core) * BLOCK, BLOCK), BLOCK)].T
        rows_ref[...] = own.astype(jnp.bfloat16)
        mask_ref[...] = jnp.where(own[:, feats + 1 : feats + 2] == group, -FAR, 0.0).astype(jnp.bfloat16)
    head_dim = q_gain_ref.shape[1]
    gain_ref[...] = q_gain_ref[...] * k_gain_ref[...] * (head_dim**-0.5 * math.log2(math.e))


def attend_heads(folds, place, x_t_ref, x_ref, key_mask_ref, gain_ref, own_ref, own_mask_ref):
    folds = list(folds)
    heads = range(len(folds))

    def side(part):
        return jnp.concatenate([fold[:, part * LANES : (part + 1) * LANES] for fold in folds], axis=1)

    def of(i):
        return slice(i * LANES, (i + 1) * LANES)

    keys = mm(side(1), x_t_ref[...], ((0,), (0,)))
    queries = mm(own_ref[:, :APAD], side(0))
    values = mm(x_ref[:, :APAD], side(2)).astype(jnp.bfloat16)
    gain, own_mask, key_mask = gain_ref[...], own_mask_ref[...], key_mask_ref[...]
    left, right = [], []
    for i in heads:
        key = keys[of(i)]
        square = jnp.sum(key * key, axis=0, keepdims=True) / LANES
        key = (key * lax.rsqrt(square + eps_norm)).astype(jnp.bfloat16)
        right.append(jnp.concatenate([key, key_mask], axis=0))
        query = queries[:, of(i)]
        square = jnp.sum(query * query, axis=1, keepdims=True) / LANES
        query = (query * lax.rsqrt(square + eps_norm) * gain).astype(jnp.bfloat16)
        left.append(jnp.concatenate([query, own_mask], axis=1))
    scores = [mm(left[i], right[i]) for i in heads]
    weights = [jnp.exp2(score).astype(jnp.bfloat16) for score in scores]
    ones = jnp.ones((values.shape[0], LANES), jnp.bfloat16)
    mixed = [mm(weights[i], jnp.concatenate([values[:, of(i)], ones], axis=1)) for i in heads]
    for i in heads:
        place(i, (mixed[i][:, :LANES] / mixed[i][:, LANES:]).astype(jnp.bfloat16))


def each_head(refs):
    for ref in refs:
        if len(ref.shape) == 2:
            yield ref[...]
        else:
            for i in range(ref.shape[0]):
                yield ref[i]


def attend_kernel(count, *refs):
    folds, out_ref = refs[6 : 6 + count], refs[-1]
    first = 0
    if len(refs) > 7 + count:
        done_ref = refs[6 + count]
        first = done_ref.shape[1] // LANES
        out_ref[:, : first * LANES] = done_ref[...]

    def place(i, result):
        out_ref[:, (first + i) * LANES : (first + i + 1) * LANES] = result

    attend_heads(each_head(folds), place, *refs[:6])


def output_kernel(heads, neighbours, lists, own_ref, near_ref, out_ref, sems):
    mine, slot = lax.axis_index("enc"), lax.axis_index("seq") & (heads - 1)
    copies = []

    def put(ref, at, base, far, k):
        head = (base ^ far) * heads + (slot ^ k)
        column = pl.ds(pl.multiple_of(head * LANES, LANES), LANES)
        result = ref.at[:, at * LANES : (at + 1) * LANES]
        copies.append(pltpu.make_async_copy(result, out_ref.at[0, :, column], sems.at[len(copies)]))
        copies[-1].start()

    for ref, base in ((near_ref, mine ^ 1), (own_ref, mine)):
        first = 1 + len(neighbours)
        for at, partner in enumerate(((0, 0), *neighbours)):
            put(ref, at, base, *partner)
        for i, pair in enumerate(zip(*lists)):
            far, k = (jnp.where(base & 1 == 0, zero, one) for zero, one in zip(*pair))
            put(ref, first + 2 * i, base, far, k)
            put(ref, first + 2 * i + 1, base, far ^ 1, k)
    for copy in copies:
        copy.wait()


def vmem(count):
    return [pl.BlockSpec(memory_space=pltpu.VMEM)] * count


def hbm(count):
    return [pl.BlockSpec(memory_space=pltpu.HBM)] * count


def in_hbm(x):
    return pltpu.with_memory_space_constraint(x, pltpu.HBM)


def after(count):
    return [pl.BlockSpec(memory_space=pl.ANY)] * count


def call(kernel, ins, out_shape, scratch=(), cost=(1_000_000, 1_000_000)):
    return pl.pallas_call(
        kernel,
        in_specs=ins,
        out_specs=[pl.BlockSpec(memory_space=pltpu.VMEM)] * len(out_shape),
        out_shape=out_shape,
        scratch_shapes=list(scratch),
        compiler_params=pltpu.CompilerParams(vmem_limit_bytes=VMEM_LIMIT),
        cost_estimate=pl.CostEstimate(flops=cost[0], bytes_accessed=cost[1], transcendentals=0),
    )


def gate(x, *others):
    return pl.pallas_call(
        gate_kernel,
        in_specs=after(1 + len(others)),
        out_specs=after(1)[0],
        out_shape=jax.ShapeDtypeStruct(x.shape, x.dtype),
        input_output_aliases={0: 0},
        compiler_params=pltpu.CompilerParams(vmem_limit_bytes=VMEM_LIMIT),
    )(x, *others)


def exchange(x, axis, n, k):
    return lax.ppermute(x, axis, [(i, i ^ k) for i in range(n)])


def on_device(
    n_enc,
    n_seq,
    clip_features,
    clip_shape,
    packing,
    conv_weight,
    embed_weight,
    mod_shift,
    mod_scale,
    qkv_weight,
    q_gain,
    k_gain,
):
    caps = clip_features.shape[2:5]
    depth_all = clip_features.shape[5]
    cols = qkv_weight.shape[2]
    feats = embed_weight.shape[0]
    heads = cols // LANES
    rows = n_enc * BLOCK
    bf16, f32 = jnp.bfloat16, jnp.float32

    def folds(dtype, *lead):
        return jax.ShapeDtypeStruct((*lead, APAD, 3 * LANES), dtype)

    evens = [0]
    for bit in reversed(range(1, log2(n_enc))):
        evens += [at ^ (1 << bit) for at in evens]
    scale_rows, shift_rows = mod_scale.reshape(-1, LANES), mod_shift.reshape(-1, LANES)
    later = [
        clip_features.reshape(-1, depth_all),
        conv_weight.reshape(-1, depth_all),
        q_gain.reshape(1, -1),
        k_gain.reshape(1, -1),
    ]
    with jax.named_scope("fold"):
        embed, features, conv, q_gain, k_gain, keep, *sends = call(
            functools.partial(fold_kernel, len(later)),
            hbm(4 + len(later)),
            [jax.ShapeDtypeStruct(x.shape, x.dtype) for x in (embed_weight, *later)]
            + [folds(f32)]
            + [folds(bf16)] * max(heads - 1, 1),
            [
                pltpu.VMEM(scale_rows.shape, f32),
                pltpu.VMEM(shift_rows.shape, f32),
                pltpu.VMEM(qkv_weight.shape, bf16),
                pltpu.SemaphoreType.DMA((4 + len(later),)),
            ],
            cost=(200_000_000, 1_000_000),
        )(*map(in_hbm, (embed_weight, scale_rows, shift_rows, qkv_weight, *later)))

    with jax.named_scope("encode"):
        own_block = call(
            functools.partial(encode_kernel, caps),
            hbm(2) + vmem(2),
            [jax.ShapeDtypeStruct((APAD, NBS * BLOCK), bf16)],
            [
                pltpu.SMEM(clip_shape.shape, jnp.int32),
                pltpu.SMEM(packing.shape, jnp.int32),
                pltpu.SemaphoreType.DMA((2,)),
            ],
            cost=(500_000_000, 2_000_000),
        )(in_hbm(clip_shape), in_hbm(packing), features, conv)[0]

    def add(keep, got, first):
        kernel = functools.partial(add_kernel, len(got))
        return call(kernel, vmem(1 + len(got)) + after(1), [folds(f32), folds(bf16)])(keep, *got, first)

    with jax.named_scope("fold_sum"):
        if heads > 1:
            got = [exchange(sends[k - 1], "seq", n_seq, k) for k in reversed(range(1, heads))]
            keep, send = add(keep, got, own_block)
        else:
            send = sends[0]

    with jax.named_scope("gram"):
        gram = call(gram_kernel, vmem(1) + after(1), [jax.ShapeDtypeStruct((2 * feats, feats), bf16)])(embed, keep)[0]

    with jax.named_scope("tokens"):
        own_block = gate(own_block, keep)
        blocks = [own_block] + [exchange(own_block, "enc", n_enc, k) for k in evens[1:]]

    with jax.named_scope("fold_sum"):
        for bit in range(log2(heads), log2(n_seq)):
            got = exchange(send, "seq", n_seq, 1 << bit)
            if bit + 1 < log2(n_seq):
                keep, send = add(keep, [got], own_block)
            else:
                fresh, swap = call(
                    functools.partial(last_add_kernel, len(blocks)),
                    vmem(2 + len(blocks)) + after(1),
                    [folds(bf16), folds(bf16, 1 + len(blocks))],
                )(keep, got, *blocks, gram)

    partners = [(far, k) for far in evens for k in range(heads) if far or k]
    partners.sort(key=lambda p: (p[0].bit_count() + p[1].bit_count(), p[0]))
    near_count = min(3, len(partners))
    half = (len(partners) - near_count) // 2
    assert len(partners) == near_count + 2 * half
    neighbours = tuple(partners[:near_count])
    lists = (tuple(partners[near_count : near_count + half]), tuple(partners[near_count + half :]))

    def spread(x, partner_of):
        pairs = []
        for e in range(n_enc):
            far, k = partner_of[e & 1]
            pairs += [(e * n_seq + i, (e ^ far) * n_seq + (i ^ k)) for i in range(n_seq)]
        return lax.ppermute(x, ("enc", "seq"), pairs)

    with jax.named_scope("gather"):
        singles = [spread(fresh, (partner, partner)) for partner in neighbours]
        swapped = exchange(swap, "enc", n_enc, 1)
        pair = call(pair_kernel, vmem(2), [folds(bf16, 2)])(fresh, swapped)[0]
        got = [spread(pair, partner_of) for partner_of in zip(*lists)]

    with jax.named_scope("pack"):
        *shared, own_rows, own_mask, far_rows, far_mask = call(
            functools.partial(pack_kernel, tuple(evens), feats),
            vmem(4 + len(evens)),
            [
                jax.ShapeDtypeStruct((APAD, rows), bf16),
                jax.ShapeDtypeStruct((rows, LANES), bf16),
                jax.ShapeDtypeStruct((LANES, rows), bf16),
                jax.ShapeDtypeStruct((1, LANES), f32),
            ]
            + [jax.ShapeDtypeStruct((BLOCK, LANES), bf16)] * 4,
            [pltpu.VMEM((LANES, rows), f32)],
        )(q_gain, k_gain, gram, *blocks, swapped)

    def attend(rows_here, groups, done=(), first=()):
        count = sum(group.size for group in groups) // (APAD * 3 * LANES)
        total = count + sum(x.shape[1] for x in done) // LANES
        return call(
            functools.partial(attend_kernel, len(groups)),
            vmem(6 + len(groups) + len(done)) + after(len(first)),
            [jax.ShapeDtypeStruct((BLOCK, total * LANES), bf16)],
            cost=(count * 200_000_000, 1_000_000),
        )(*shared, *rows_here, *groups, *done, *first)[0]

    with jax.named_scope("attend"):
        own, other = (own_rows, own_mask), (far_rows, far_mask)
        early, rest = [fresh, *singles], got
        early_other, early_own = attend(other, early), attend(own, early)
        near = exchange(attend(other, rest, [early_other], [early_own]), "enc", n_enc, 1)
        own_done = attend(own, rest, [early_own])
        return pl.pallas_call(
            functools.partial(output_kernel, heads, neighbours, lists),
            in_specs=vmem(2),
            out_specs=hbm(1)[0],
            out_shape=jax.ShapeDtypeStruct((1, BLOCK, n_enc * cols), bf16),
            scratch_shapes=[pltpu.SemaphoreType.DMA((n_enc * heads,))],
            compiler_params=pltpu.CompilerParams(vmem_limit_bytes=VMEM_LIMIT),
        )(own_done, near)


def solution(mesh):
    return jax.shard_map(
        functools.partial(on_device, mesh.shape["enc"], mesh.shape["seq"]),
        mesh=mesh,
        in_specs=(
            P("enc", "seq", None, None, None, None),
            P("enc", "seq", None),
            P("enc", "seq", None, None),
            P(),
            P(),
            P(),
            P(),
            P(None, "seq", "enc"),
            P(),
            P(),
        ),
        out_specs=P("seq", "enc", None),
        check_vma=False,
    )
```

```python
import functools
import math

import jax
import jax.numpy as jnp
from jax import lax
from jax.experimental import pallas as pl
from jax.experimental.pallas import tpu as pltpu
from jax.sharding import PartitionSpec as P

BLOCK = 128
NBS = 2
LANES = 128
APAD = 72
TAIL = 8
TOKEN_ROWS = 80
eps_norm = 1e-06
FAR = 2.0**20
VMEM_LIMIT = 48 * 1024 * 1024


def mm(a, b, dims=((1,), (0,)), precision=None):
    return lax.dot_general(a, b, (dims, ((), ())), preferred_element_type=jnp.float32, precision=precision)


def split_bf16(x):
    hi = x.astype(jnp.bfloat16)
    return hi, (x - hi.astype(jnp.float32)).astype(jnp.bfloat16)


def log2(n):
    bits = n.bit_length() - 1
    assert 1 << bits == n
    return bits


def fetch(pairs, sems):
    copies = [pltpu.make_async_copy(src, dst, sems.at[i]) for i, (src, dst) in enumerate(pairs)]
    for copy in copies:
        copy.start()
    return copies


def fold_kernel(count, embed_hbm, scale_hbm, shift_hbm, w_hbm, *refs):
    later_hbm, embed_ref, later, keep_ref, sends = refs[:count], refs[count], refs[count + 1 : 2 * count + 1], refs[2 * count + 1], refs[2 * count + 2 : -4]
    scale_ref, shift_ref, w_ref, sems = refs[-4:]
    copies = fetch(
        [(embed_hbm, embed_ref), (scale_hbm, scale_ref), (shift_hbm, shift_ref), (w_hbm, w_ref)]
        + list(zip(later_hbm, later)),
        sems,
    )
    me = lax.axis_index("seq")
    _, depth, cols = w_ref.shape
    feats = embed_ref.shape[0]
    heads = cols // LANES
    for copy in copies[:3]:
        copy.wait()
    mean = jnp.sum(embed_ref[...].astype(jnp.float32), axis=1, keepdims=True) / embed_ref.shape[1]
    span = max(depth, LANES)
    chunks = span // LANES
    first = (me * depth) // LANES
    emb = embed_ref[:, pl.ds(pl.multiple_of(first * LANES, LANES), span)].astype(jnp.float32) - mean
    scale = jnp.concatenate([scale_ref[pl.ds(first + i, 1), :] for i in range(chunks)], axis=1)
    shift = jnp.concatenate([shift_ref[pl.ds(first + i, 1), :] for i in range(chunks)], axis=1)
    left = jnp.concatenate(
        [emb * (1.0 + scale), shift, jnp.zeros((APAD - feats - 1, span), jnp.float32)], axis=0
    )
    if depth < LANES:
        low = me * depth - first * LANES
        lane = lax.broadcasted_iota(jnp.int32, left.shape, 1)
        left = jnp.where((lane >= low) & (lane < low + depth), left, 0.0)
    hi, lo = split_bf16(left)
    both = jnp.concatenate([hi, lo], axis=0)
    copies[3].wait()

    def product(head):
        start = pl.multiple_of(head * LANES, LANES)
        right = jnp.concatenate([w_ref[part, :, pl.ds(start, LANES)] for part in range(3)], axis=1)
        right = jnp.concatenate([right] * (span // depth), axis=0)
        total = mm(both, right)
        total = total[:APAD] + total[APAD:]
        parts = [total[:, part * LANES : (part + 1) * LANES] for part in range(3)]
        row = lax.broadcasted_iota(jnp.int32, (TAIL, LANES), 0)
        tail = jnp.zeros((TAIL, LANES), jnp.float32)
        for part in range(3):
            tail = jnp.where(row == part, parts[part][feats : feats + 1], tail)
        return jnp.concatenate([part[:feats] for part in parts] + [tail], axis=0)

    slot = me & (heads - 1)
    for k in range(1, heads):
        sends[k - 1][...] = product(slot ^ k).astype(jnp.bfloat16)
    total = product(slot)
    keep_ref[...] = total
    if heads == 1:
        sends[0][...] = total.astype(jnp.bfloat16)
    for copy in copies[4:]:
        copy.wait()


def add_kernel(count, keep_in, *refs):
    total = keep_in[...]
    for ref in refs[:count]:
        total = total + ref[...].astype(jnp.float32)
    refs[-2][...] = total
    refs[-1][...] = total.astype(jnp.bfloat16)


def last_add_kernel(count, keep_in, got_ref, *refs):
    total = (keep_in[...] + got_ref[...].astype(jnp.float32)).astype(jnp.bfloat16)
    out_ref, swap_ref = refs[-2:]
    out_ref[...] = total
    swap_ref[0] = total
    for i in range(count):
        block = refs[i][...]
        rest = jnp.zeros((total.shape[0] - block.shape[0], LANES), jnp.bfloat16)
        swap_ref[1 + i] = jnp.concatenate([block, rest], axis=0)


def pair_kernel(own_ref, swapped_ref, out_ref):
    out_ref[0] = own_ref[...]
    out_ref[1] = swapped_ref[0]


def gate_kernel(*refs):
    pass


def encode_kernel(caps, shape_hbm, plan_hbm, feat_ref, conv_ref, out_ref, shape_ref, plan_ref, sems):
    copies = fetch([(shape_hbm, shape_ref), (plan_hbm, plan_ref)], sems)
    frames_cap, height_cap, width_cap = caps
    spots = frames_cap * height_cap * width_cap
    frame_size = height_cap * width_cap
    latent_ch = conv_ref.shape[0] // 27
    feats = 4 * latent_ch
    taps = mm(conv_ref[...], feat_ref[...], ((1,), (1,)))
    copies[0].wait()
    copies[1].wait()
    frames, height, width = shape_ref[0, 0, 0], shape_ref[0, 0, 1], shape_ref[0, 0, 2]
    spot = lax.broadcasted_iota(jnp.int32, (1, spots), 1)
    frame_ix = spot // frame_size
    row_ix = (spot % frame_size) // width_cap
    col_ix = spot % width_cap
    inside = (frame_ix < frames) & (row_ix < height) & (col_ix < width)
    taps = jnp.where(inside, taps, 0.0)

    def tap(a, b, j):
        at = (9 * a + 3 * b + j) * latent_ch
        return taps[at : at + latent_ch]

    def later(x, by):
        zeros = jnp.zeros((latent_ch, by * frame_size), jnp.float32)
        return jnp.concatenate([zeros, x[:, : spots - by * frame_size]], axis=1)

    def over_frames(b, j):
        return tap(2, b, j) + later(tap(1, b, j), 1) + later(tap(0, b, j), 2)

    def over_rows(j):
        above = pltpu.roll(over_frames(0, j), width_cap, 1)
        below = pltpu.roll(over_frames(2, j), spots - width_cap, 1)
        return (
            over_frames(1, j)
            + jnp.where(row_ix >= 1, above, 0.0)
            + jnp.where(row_ix < height_cap - 1, below, 0.0)
        )

    latent = (
        over_rows(1)
        + jnp.where(col_ix >= 1, pltpu.roll(over_rows(0), 1, 1), 0.0)
        + jnp.where(col_ix < width_cap - 1, pltpu.roll(over_rows(2), spots - 1, 1), 0.0)
    )
    latent = latent.astype(jnp.bfloat16).astype(jnp.float32)
    shifted = [latent] + [pltpu.roll(latent, spots - by, 1) for by in (1, width_cap, width_cap + 1)]
    patches = jnp.concatenate(shifted, axis=0).astype(jnp.bfloat16)

    tokens = NBS * BLOCK
    half_w = (width // 2).astype(jnp.float32)
    per_frame_int = (height // 2) * (width // 2)
    per_frame = per_frame_int.astype(jnp.float32)
    live = frames * per_frame_int
    token_int = lax.broadcasted_iota(jnp.int32, (1, tokens), 1)
    token = token_int.astype(jnp.float32)
    frame_of = jnp.floor((token + 0.5) / jnp.full((1, tokens), per_frame))
    within = token - frame_of * per_frame
    row_of = jnp.floor((within + 0.5) / jnp.full((1, tokens), half_w))
    col_of = within - row_of * half_w
    source = (frame_of * frame_size + row_of * (2 * width_cap) + col_of * 2).astype(jnp.int32)
    source = jnp.where(token_int < live, source, -1)
    chosen = lax.broadcasted_iota(jnp.int32, (spots, tokens), 0) == source
    picked = mm(patches, jnp.where(chosen, 1.0, 0.0).astype(jnp.bfloat16))
    kind = lax.broadcasted_iota(jnp.int32, (TOKEN_ROWS - feats, BLOCK), 0)
    pieces = []
    for b in range(NBS):
        count = jnp.clip(live - b * BLOCK, 0, BLOCK)
        info = jnp.where(
            kind == 0,
            plan_ref[0, 0, b, 0],
            jnp.where(kind == 1, plan_ref[0, 0, b, 1], jnp.where(kind == 2, count, 0)),
        )
        pieces += [picked[:, b * BLOCK : (b + 1) * BLOCK], info.astype(jnp.float32)]
    out_ref[...] = jnp.concatenate(pieces, axis=0).astype(jnp.bfloat16)


def gram_kernel(embed_ref, first_ref, out_ref):
    feats, width = embed_ref.shape
    emb = embed_ref[...].astype(jnp.float32)
    emb = emb - jnp.sum(emb, axis=1, keepdims=True) / width
    both = jnp.concatenate(split_bf16(emb), axis=0)
    gram = mm(both, both, ((1,), (1,))) / width
    gram = gram[:feats] + gram[feats:]
    out_ref[...] = jnp.concatenate(split_bf16(gram[:, :feats] + gram[:, feats:]), axis=0)


def pack_kernel(evens, feats, q_gain_ref, k_gain_ref, gram_ref, *refs):
    here, near = refs[: len(evens)], refs[len(evens)]
    x_t_ref, x_ref, key_mask_ref, gain_ref, *row_refs, rows_t = refs[len(evens) + 1 :]
    n_enc = 2 * len(evens)
    mine = lax.axis_index("enc")
    rows = n_enc * BLOCK
    lane = lax.broadcasted_iota(jnp.int32, (1, BLOCK), 1).astype(jnp.float32)
    extra = lax.broadcasted_iota(jnp.int32, (APAD - feats, BLOCK), 0)
    found = []
    blocks = [(at, here[i][...]) for i, at in enumerate(evens)]
    blocks += [(at ^ 1, near[1 + i]) for i, at in enumerate(evens)]
    for distance, block in blocks:
        source = mine ^ distance
        for b in range(NBS):
            tile = block.astype(jnp.float32)[b * TOKEN_ROWS : (b + 1) * TOKEN_ROWS]
            owner, offset, count = (tile[feats + i : feats + i + 1] for i in range(3))
            owner = jnp.where(offset == 0.0, owner, -1.0)
            segment = jnp.where(lane < count, (source + 1).astype(jnp.float32), 0.0)
            found.append((owner, segment, tile[:feats]))
    at = lax.broadcasted_iota(jnp.int32, (feats, feats), 0)
    frm = lax.broadcasted_iota(jnp.int32, (feats, feats), 1)
    order = jnp.where(frm == (at % 4) * (feats // 4) + at // 4, 1.0, 0.0).astype(jnp.bfloat16)
    for o in range(n_enc):
        segment = jnp.zeros((1, BLOCK), jnp.float32)
        body = jnp.zeros((feats, BLOCK), jnp.float32)
        for owner, seg_of, tile in found:
            hit = owner == float(o)
            segment = segment + jnp.where(hit, seg_of, 0.0)
            body = body + jnp.where(hit, tile, 0.0)
        tail = jnp.where(extra == 0, 1.0, jnp.where(extra == 1, segment, 0.0))
        rows_t[:, o * BLOCK : (o + 1) * BLOCK] = jnp.concatenate(
            [body, tail, jnp.zeros((LANES - APAD, BLOCK), jnp.float32)], axis=0
        )
    picked = mm(order, rows_t[:feats].astype(jnp.bfloat16))
    spread = mm(gram_ref[...], picked.astype(jnp.bfloat16))
    variance = jnp.sum((spread[:feats] + spread[feats:]) * picked, axis=0, keepdims=True)
    rows_t[:feats] = picked * lax.rsqrt(jnp.maximum(variance, 0.0) + eps_norm)
    x_t = rows_t[...]
    x_t_ref[...] = x_t[:APAD].astype(jnp.bfloat16)
    x_ref[...] = x_t.T.astype(jnp.bfloat16)
    group_t = lax.broadcasted_iota(jnp.int32, (LANES, rows), 0).astype(jnp.float32)
    key_mask_ref[...] = jnp.where(x_t[feats + 1 : feats + 2] == group_t, 0.0, 1.0).astype(jnp.bfloat16)
    group = lax.broadcasted_iota(jnp.int32, (BLOCK, LANES), 1).astype(jnp.float32)
    for core in range(2):
        rows_ref, mask_ref = row_refs[2 * core : 2 * core + 2]
        own = rows_t[:, pl.ds(pl.multiple_of((mine ^ core) * BLOCK, BLOCK), BLOCK)].T
        rows_ref[...] = own.astype(jnp.bfloat16)
        mask_ref[...] = jnp.where(own[:, feats + 1 : feats + 2] == group, -FAR, 0.0).astype(jnp.bfloat16)
    head_dim = q_gain_ref.shape[1]
    gain_ref[...] = q_gain_ref[...] * k_gain_ref[...] * (head_dim**-0.5 * math.log2(math.e))


def attend_heads(folds, place, x_t_ref, x_ref, key_mask_ref, gain_ref, own_ref, own_mask_ref):
    folds = list(folds)
    heads = range(len(folds))
    feats = (folds[0].shape[0] - TAIL) // 3
    tails = jnp.concatenate([fold[3 * feats :].astype(jnp.float32) for fold in folds], axis=1)
    row = lax.broadcasted_iota(jnp.int32, tails.shape, 0)

    def side(part):
        body = jnp.concatenate([fold[part * feats : (part + 1) * feats] for fold in folds], axis=1)
        shift = jnp.where(row == 0, tails[part : part + 1], 0.0).astype(jnp.bfloat16)
        return jnp.concatenate([body, shift], axis=0)

    def of(i):
        return slice(i * LANES, (i + 1) * LANES)

    keys = mm(side(1), x_t_ref[...], ((0,), (0,)))
    queries = mm(own_ref[:, :APAD], side(0))
    values = mm(x_ref[:, :APAD], side(2)).astype(jnp.bfloat16)
    gain, own_mask, key_mask = gain_ref[...], own_mask_ref[...], key_mask_ref[...]
    left, right = [], []
    for i in heads:
        key = keys[of(i)]
        square = jnp.sum(key * key, axis=0, keepdims=True) / LANES
        key = (key * lax.rsqrt(square + eps_norm)).astype(jnp.bfloat16)
        right.append(jnp.concatenate([key, key_mask], axis=0))
        query = queries[:, of(i)]
        square = jnp.sum(query * query, axis=1, keepdims=True) / LANES
        query = (query * lax.rsqrt(square + eps_norm) * gain).astype(jnp.bfloat16)
        left.append(jnp.concatenate([query, own_mask], axis=1))
    scores = [mm(left[i], right[i]) for i in heads]
    weights = [jnp.exp2(score).astype(jnp.bfloat16) for score in scores]
    ones = jnp.ones((values.shape[0], LANES), jnp.bfloat16)
    mixed = [mm(weights[i], jnp.concatenate([values[:, of(i)], ones], axis=1)) for i in heads]
    for i in heads:
        place(i, (mixed[i][:, :LANES] / mixed[i][:, LANES:]).astype(jnp.bfloat16))


def each_head(refs):
    for ref in refs:
        if len(ref.shape) == 2:
            yield ref[...]
        else:
            for i in range(ref.shape[0]):
                yield ref[i]


def attend_kernel(count, *refs):
    folds, out_ref = refs[6 : 6 + count], refs[-1]
    first = 0
    if len(refs) > 7 + count:
        done_ref = refs[6 + count]
        first = done_ref.shape[1] // LANES
        out_ref[:, : first * LANES] = done_ref[...]

    def place(i, result):
        out_ref[:, (first + i) * LANES : (first + i + 1) * LANES] = result

    attend_heads(each_head(folds), place, *refs[:6])


def output_kernel(heads, neighbours, lists, own_ref, near_ref, out_ref, sems):
    mine, slot = lax.axis_index("enc"), lax.axis_index("seq") & (heads - 1)
    copies = []

    def put(ref, at, base, far, k):
        head = (base ^ far) * heads + (slot ^ k)
        column = pl.ds(pl.multiple_of(head * LANES, LANES), LANES)
        result = ref.at[:, at * LANES : (at + 1) * LANES]
        copies.append(pltpu.make_async_copy(result, out_ref.at[0, :, column], sems.at[len(copies)]))
        copies[-1].start()

    for ref, base in ((near_ref, mine ^ 1), (own_ref, mine)):
        first = 1 + len(neighbours)
        for at, partner in enumerate(((0, 0), *neighbours)):
            put(ref, at, base, *partner)
        for i, pair in enumerate(zip(*lists)):
            far, k = (jnp.where(base & 1 == 0, zero, one) for zero, one in zip(*pair))
            put(ref, first + 2 * i, base, far, k)
            put(ref, first + 2 * i + 1, base, far ^ 1, k)
    for copy in copies:
        copy.wait()


def vmem(count):
    return [pl.BlockSpec(memory_space=pltpu.VMEM)] * count


def hbm(count):
    return [pl.BlockSpec(memory_space=pltpu.HBM)] * count


def in_hbm(x):
    return pltpu.with_memory_space_constraint(x, pltpu.HBM)


def after(count):
    return [pl.BlockSpec(memory_space=pl.ANY)] * count


def call(kernel, ins, out_shape, scratch=(), cost=(1_000_000, 1_000_000)):
    return pl.pallas_call(
        kernel,
        in_specs=ins,
        out_specs=[pl.BlockSpec(memory_space=pltpu.VMEM)] * len(out_shape),
        out_shape=out_shape,
        scratch_shapes=list(scratch),
        compiler_params=pltpu.CompilerParams(vmem_limit_bytes=VMEM_LIMIT),
        cost_estimate=pl.CostEstimate(flops=cost[0], bytes_accessed=cost[1], transcendentals=0),
    )


def gate(x, *others):
    return pl.pallas_call(
        gate_kernel,
        in_specs=after(1 + len(others)),
        out_specs=after(1)[0],
        out_shape=jax.ShapeDtypeStruct(x.shape, x.dtype),
        input_output_aliases={0: 0},
        compiler_params=pltpu.CompilerParams(vmem_limit_bytes=VMEM_LIMIT),
    )(x, *others)


def exchange(x, axis, n, k):
    return lax.ppermute(x, axis, [(i, i ^ k) for i in range(n)])


def on_device(
    n_enc,
    n_seq,
    clip_features,
    clip_shape,
    packing,
    conv_weight,
    embed_weight,
    mod_shift,
    mod_scale,
    qkv_weight,
    q_gain,
    k_gain,
):
    caps = clip_features.shape[2:5]
    depth_all = clip_features.shape[5]
    cols = qkv_weight.shape[2]
    feats = embed_weight.shape[0]
    heads = cols // LANES
    rows = n_enc * BLOCK
    bf16, f32 = jnp.bfloat16, jnp.float32

    def folds(dtype, *lead):
        return jax.ShapeDtypeStruct((*lead, 3 * feats + TAIL, LANES), dtype)

    evens = [0]
    for bit in reversed(range(1, log2(n_enc))):
        evens += [at ^ (1 << bit) for at in evens]
    scale_rows, shift_rows = mod_scale.reshape(-1, LANES), mod_shift.reshape(-1, LANES)
    later = [
        clip_features.reshape(-1, depth_all),
        conv_weight.reshape(-1, depth_all),
        q_gain.reshape(1, -1),
        k_gain.reshape(1, -1),
    ]
    with jax.named_scope("fold"):
        embed, features, conv, q_gain, k_gain, keep, *sends = call(
            functools.partial(fold_kernel, len(later)),
            hbm(4 + len(later)),
            [jax.ShapeDtypeStruct(x.shape, x.dtype) for x in (embed_weight, *later)]
            + [folds(f32)]
            + [folds(bf16)] * max(heads - 1, 1),
            [
                pltpu.VMEM(scale_rows.shape, f32),
                pltpu.VMEM(shift_rows.shape, f32),
                pltpu.VMEM(qkv_weight.shape, bf16),
                pltpu.SemaphoreType.DMA((4 + len(later),)),
            ],
            cost=(200_000_000, 1_000_000),
        )(*map(in_hbm, (embed_weight, scale_rows, shift_rows, qkv_weight, *later)))

    with jax.named_scope("encode"):
        own_block = call(
            functools.partial(encode_kernel, caps),
            hbm(2) + vmem(2),
            [jax.ShapeDtypeStruct((NBS * TOKEN_ROWS, BLOCK), bf16)],
            [
                pltpu.SMEM(clip_shape.shape, jnp.int32),
                pltpu.SMEM(packing.shape, jnp.int32),
                pltpu.SemaphoreType.DMA((2,)),
            ],
            cost=(500_000_000, 2_000_000),
        )(in_hbm(clip_shape), in_hbm(packing), features, conv)[0]

    def add(keep, got, first):
        kernel = functools.partial(add_kernel, len(got))
        return call(kernel, vmem(1 + len(got)) + after(1), [folds(f32), folds(bf16)])(keep, *got, first)

    with jax.named_scope("fold_sum"):
        if heads > 1:
            got = [exchange(sends[k - 1], "seq", n_seq, k) for k in reversed(range(1, heads))]
            keep, send = add(keep, got, own_block)
        else:
            send = sends[0]

    with jax.named_scope("gram"):
        gram = call(gram_kernel, vmem(1) + after(1), [jax.ShapeDtypeStruct((2 * feats, feats), bf16)])(embed, keep)[0]

    with jax.named_scope("tokens"):
        own_block = gate(own_block, keep)
        blocks = [own_block] + [exchange(own_block, "enc", n_enc, k) for k in evens[1:]]

    with jax.named_scope("fold_sum"):
        for bit in range(log2(heads), log2(n_seq)):
            got = exchange(send, "seq", n_seq, 1 << bit)
            if bit + 1 < log2(n_seq):
                keep, send = add(keep, [got], own_block)
            else:
                fresh, swap = call(
                    functools.partial(last_add_kernel, len(blocks)),
                    vmem(2 + len(blocks)) + after(1),
                    [folds(bf16), folds(bf16, 1 + len(blocks))],
                )(keep, got, *blocks, gram)

    partners = [(far, k) for far in evens for k in range(heads) if far or k]
    partners.sort(key=lambda p: (p[0].bit_count() + p[1].bit_count(), p[0]))
    near_count = min(3, len(partners))
    half = (len(partners) - near_count) // 2
    assert len(partners) == near_count + 2 * half
    neighbours = tuple(partners[:near_count])
    lists = (tuple(partners[near_count : near_count + half]), tuple(partners[near_count + half :]))

    def spread(x, partner_of):
        pairs = []
        for e in range(n_enc):
            far, k = partner_of[e & 1]
            pairs += [(e * n_seq + i, (e ^ far) * n_seq + (i ^ k)) for i in range(n_seq)]
        return lax.ppermute(x, ("enc", "seq"), pairs)

    with jax.named_scope("gather"):
        singles = [spread(fresh, (partner, partner)) for partner in neighbours]
        swapped = exchange(swap, "enc", n_enc, 1)
        pair = call(pair_kernel, vmem(2), [folds(bf16, 2)])(fresh, swapped)[0]
        got = [spread(pair, partner_of) for partner_of in zip(*lists)]

    with jax.named_scope("pack"):
        *shared, own_rows, own_mask, far_rows, far_mask = call(
            functools.partial(pack_kernel, tuple(evens), feats),
            vmem(4 + len(evens)),
            [
                jax.ShapeDtypeStruct((APAD, rows), bf16),
                jax.ShapeDtypeStruct((rows, LANES), bf16),
                jax.ShapeDtypeStruct((LANES, rows), bf16),
                jax.ShapeDtypeStruct((1, LANES), f32),
            ]
            + [jax.ShapeDtypeStruct((BLOCK, LANES), bf16)] * 4,
            [pltpu.VMEM((LANES, rows), f32)],
        )(q_gain, k_gain, gram, *blocks, swapped)

    def attend(rows_here, groups, done=(), first=()):
        count = sum(group.size for group in groups) // ((3 * feats + TAIL) * LANES)
        total = count + sum(x.shape[1] for x in done) // LANES
        return call(
            functools.partial(attend_kernel, len(groups)),
            vmem(6 + len(groups) + len(done)) + after(len(first)),
            [jax.ShapeDtypeStruct((BLOCK, total * LANES), bf16)],
            cost=(count * 200_000_000, 1_000_000),
        )(*shared, *rows_here, *groups, *done, *first)[0]

    with jax.named_scope("attend"):
        own, other = (own_rows, own_mask), (far_rows, far_mask)
        early, rest = [fresh, *singles], got
        early_other, early_own = attend(other, early), attend(own, early)
        near = exchange(attend(other, rest, [early_other], [early_own]), "enc", n_enc, 1)
        own_done = attend(own, rest, [early_own])
        return pl.pallas_call(
            functools.partial(output_kernel, heads, neighbours, lists),
            in_specs=vmem(2),
            out_specs=hbm(1)[0],
            out_shape=jax.ShapeDtypeStruct((1, BLOCK, n_enc * cols), bf16),
            scratch_shapes=[pltpu.SemaphoreType.DMA((n_enc * heads,))],
            compiler_params=pltpu.CompilerParams(vmem_limit_bytes=VMEM_LIMIT),
        )(own_done, near)


def solution(mesh):
    return jax.shard_map(
        functools.partial(on_device, mesh.shape["enc"], mesh.shape["seq"]),
        mesh=mesh,
        in_specs=(
            P("enc", "seq", None, None, None, None),
            P("enc", "seq", None),
            P("enc", "seq", None, None),
            P(),
            P(),
            P(),
            P(),
            P(None, "seq", "enc"),
            P(),
            P(),
        ),
        out_specs=P("seq", "enc", None),
        check_vma=False,
    )
```

```python
import functools
import math

import jax
import jax.numpy as jnp
from jax import lax
from jax.experimental import pallas as pl
from jax.experimental.pallas import tpu as pltpu
from jax.sharding import PartitionSpec as P

BLOCK = 128
NBS = 2
LANES = 128
APAD = 72
TAIL = 8
TOKEN_ROWS = 80
eps_norm = 1e-06
FAR = 2.0**20
VMEM_LIMIT = 48 * 1024 * 1024


def mm(a, b, dims=((1,), (0,)), precision=None):
    return lax.dot_general(a, b, (dims, ((), ())), preferred_element_type=jnp.float32, precision=precision)


def split_bf16(x):
    hi = x.astype(jnp.bfloat16)
    return hi, (x - hi.astype(jnp.float32)).astype(jnp.bfloat16)


def log2(n):
    bits = n.bit_length() - 1
    assert 1 << bits == n
    return bits


def fetch(pairs, sems):
    copies = [pltpu.make_async_copy(src, dst, sems.at[i]) for i, (src, dst) in enumerate(pairs)]
    for copy in copies:
        copy.start()
    return copies


def fold_kernel(count, embed_hbm, scale_hbm, shift_hbm, w_hbm, *refs):
    later_hbm, embed_ref, later, keep_ref, sends = refs[:count], refs[count], refs[count + 1 : 2 * count + 1], refs[2 * count + 1], refs[2 * count + 2 : -4]
    scale_ref, shift_ref, w_ref, sems = refs[-4:]
    copies = fetch(
        [(embed_hbm, embed_ref), (scale_hbm, scale_ref), (shift_hbm, shift_ref), (w_hbm, w_ref)]
        + list(zip(later_hbm, later)),
        sems,
    )
    me = lax.axis_index("seq")
    _, depth, cols = w_ref.shape
    feats = embed_ref.shape[0]
    heads = cols // LANES
    for copy in copies[:3]:
        copy.wait()
    mean = jnp.sum(embed_ref[...].astype(jnp.float32), axis=1, keepdims=True) / embed_ref.shape[1]
    span = max(depth, LANES)
    chunks = span // LANES
    first = (me * depth) // LANES
    emb = embed_ref[:, pl.ds(pl.multiple_of(first * LANES, LANES), span)].astype(jnp.float32) - mean
    scale = jnp.concatenate([scale_ref[pl.ds(first + i, 1), :] for i in range(chunks)], axis=1)
    shift = jnp.concatenate([shift_ref[pl.ds(first + i, 1), :] for i in range(chunks)], axis=1)
    left = jnp.concatenate(
        [emb * (1.0 + scale), shift, jnp.zeros((APAD - feats - 1, span), jnp.float32)], axis=0
    )
    if depth < LANES:
        low = me * depth - first * LANES
        lane = lax.broadcasted_iota(jnp.int32, left.shape, 1)
        left = jnp.where((lane >= low) & (lane < low + depth), left, 0.0)
    hi, lo = split_bf16(left)
    both = jnp.concatenate([hi, lo], axis=0)
    copies[3].wait()

    def product(head):
        start = pl.multiple_of(head * LANES, LANES)
        right = jnp.concatenate([w_ref[part, :, pl.ds(start, LANES)] for part in range(3)], axis=1)
        right = jnp.concatenate([right] * (span // depth), axis=0)
        total = mm(both, right)
        total = total[:APAD] + total[APAD:]
        parts = [total[:, part * LANES : (part + 1) * LANES] for part in range(3)]
        row = lax.broadcasted_iota(jnp.int32, (TAIL, LANES), 0)
        tail = jnp.zeros((TAIL, LANES), jnp.float32)
        for part in range(3):
            tail = jnp.where(row == part, parts[part][feats : feats + 1], tail)
        return jnp.concatenate([part[:feats] for part in parts] + [tail], axis=0)

    slot = me & (heads - 1)
    for k in range(1, heads):
        sends[k - 1][...] = product(slot ^ k).astype(jnp.bfloat16)
    total = product(slot)
    keep_ref[...] = total
    if heads == 1:
        sends[0][...] = total.astype(jnp.bfloat16)
    for copy in copies[4:]:
        copy.wait()


def add_kernel(count, keep_in, *refs):
    total = keep_in[...]
    for ref in refs[:count]:
        total = total + ref[...].astype(jnp.float32)
    refs[-2][...] = total
    refs[-1][...] = total.astype(jnp.bfloat16)


def last_add_kernel(count, keep_in, got_ref, *refs):
    total = (keep_in[...] + got_ref[...].astype(jnp.float32)).astype(jnp.bfloat16)
    out_ref, swap_ref = refs[-2:]
    out_ref[...] = total
    swap_ref[0] = total
    for i in range(count):
        block = refs[i][...]
        rest = jnp.zeros((total.shape[0] - block.shape[0], LANES), jnp.bfloat16)
        swap_ref[1 + i] = jnp.concatenate([block, rest], axis=0)


def pair_kernel(own_ref, swapped_ref, out_ref):
    out_ref[0] = own_ref[...]
    out_ref[1] = swapped_ref[0]


def gate_kernel(*refs):
    pass


def encode_kernel(caps, shape_hbm, plan_hbm, feat_ref, conv_ref, out_ref, shape_ref, plan_ref, sems):
    copies = fetch([(shape_hbm, shape_ref), (plan_hbm, plan_ref)], sems)
    frames_cap, height_cap, width_cap = caps
    spots = frames_cap * height_cap * width_cap
    frame_size = height_cap * width_cap
    latent_ch = conv_ref.shape[0] // 27
    feats = 4 * latent_ch
    taps = mm(conv_ref[...], feat_ref[...], ((1,), (1,)))
    copies[0].wait()
    copies[1].wait()
    frames, height, width = shape_ref[0, 0, 0], shape_ref[0, 0, 1], shape_ref[0, 0, 2]
    spot = lax.broadcasted_iota(jnp.int32, (1, spots), 1)
    frame_ix = spot // frame_size
    row_ix = (spot % frame_size) // width_cap
    col_ix = spot % width_cap
    inside = (frame_ix < frames) & (row_ix < height) & (col_ix < width)
    taps = jnp.where(inside, taps, 0.0)

    def tap(a, b, j):
        at = (9 * a + 3 * b + j) * latent_ch
        return taps[at : at + latent_ch]

    def later(x, by):
        zeros = jnp.zeros((latent_ch, by * frame_size), jnp.float32)
        return jnp.concatenate([zeros, x[:, : spots - by * frame_size]], axis=1)

    def over_frames(b, j):
        return tap(2, b, j) + later(tap(1, b, j), 1) + later(tap(0, b, j), 2)

    def over_rows(j):
        above = pltpu.roll(over_frames(0, j), width_cap, 1)
        below = pltpu.roll(over_frames(2, j), spots - width_cap, 1)
        return (
            over_frames(1, j)
            + jnp.where(row_ix >= 1, above, 0.0)
            + jnp.where(row_ix < height_cap - 1, below, 0.0)
        )

    latent = (
        over_rows(1)
        + jnp.where(col_ix >= 1, pltpu.roll(over_rows(0), 1, 1), 0.0)
        + jnp.where(col_ix < width_cap - 1, pltpu.roll(over_rows(2), spots - 1, 1), 0.0)
    )
    latent = latent.astype(jnp.bfloat16).astype(jnp.float32)
    shifted = [latent] + [pltpu.roll(latent, spots - by, 1) for by in (1, width_cap, width_cap + 1)]
    patches = jnp.concatenate(shifted, axis=0).astype(jnp.bfloat16)

    tokens = NBS * BLOCK
    half_w = (width // 2).astype(jnp.float32)
    per_frame_int = (height // 2) * (width // 2)
    per_frame = per_frame_int.astype(jnp.float32)
    live = frames * per_frame_int
    token_int = lax.broadcasted_iota(jnp.int32, (1, tokens), 1)
    token = token_int.astype(jnp.float32)
    frame_of = jnp.floor((token + 0.5) / jnp.full((1, tokens), per_frame))
    within = token - frame_of * per_frame
    row_of = jnp.floor((within + 0.5) / jnp.full((1, tokens), half_w))
    col_of = within - row_of * half_w
    source = (frame_of * frame_size + row_of * (2 * width_cap) + col_of * 2).astype(jnp.int32)
    source = jnp.where(token_int < live, source, -1)
    chosen = lax.broadcasted_iota(jnp.int32, (spots, tokens), 0) == source
    picked = mm(patches, jnp.where(chosen, 1.0, 0.0).astype(jnp.bfloat16))
    kind = lax.broadcasted_iota(jnp.int32, (TOKEN_ROWS - feats, BLOCK), 0)
    pieces = []
    for b in range(NBS):
        count = jnp.clip(live - b * BLOCK, 0, BLOCK)
        info = jnp.where(
            kind == 0,
            plan_ref[0, 0, b, 0],
            jnp.where(kind == 1, plan_ref[0, 0, b, 1], jnp.where(kind == 2, count, 0)),
        )
        pieces += [picked[:, b * BLOCK : (b + 1) * BLOCK], info.astype(jnp.float32)]
    out_ref[...] = jnp.concatenate(pieces, axis=0).astype(jnp.bfloat16)


def gram_kernel(embed_ref, first_ref, out_ref):
    feats, width = embed_ref.shape
    emb = embed_ref[...].astype(jnp.float32)
    emb = emb - jnp.sum(emb, axis=1, keepdims=True) / width
    both = jnp.concatenate(split_bf16(emb), axis=0)
    gram = mm(both, both, ((1,), (1,))) / width
    gram = gram[:feats] + gram[feats:]
    out_ref[...] = jnp.concatenate(split_bf16(gram[:, :feats] + gram[:, feats:]), axis=0)


def pack_kernel(evens, feats, q_gain_ref, k_gain_ref, gram_ref, *refs):
    here, near = refs[: len(evens)], refs[len(evens)]
    x_t_ref, x_ref, key_mask_ref, gain_ref, *row_refs, rows_t = refs[len(evens) + 1 :]
    n_enc = 2 * len(evens)
    mine = lax.axis_index("enc")
    rows = n_enc * BLOCK
    lane = lax.broadcasted_iota(jnp.int32, (1, BLOCK), 1).astype(jnp.float32)
    extra = lax.broadcasted_iota(jnp.int32, (APAD - feats, BLOCK), 0)
    found = []
    blocks = [(at, here[i][...]) for i, at in enumerate(evens)]
    blocks += [(at ^ 1, near[1 + i]) for i, at in enumerate(evens)]
    for distance, block in blocks:
        source = mine ^ distance
        for b in range(NBS):
            tile = block.astype(jnp.float32)[b * TOKEN_ROWS : (b + 1) * TOKEN_ROWS]
            owner, offset, count = (tile[feats + i : feats + i + 1] for i in range(3))
            owner = jnp.where(offset == 0.0, owner, -1.0)
            segment = jnp.where(lane < count, (source + 1).astype(jnp.float32), 0.0)
            found.append((owner, segment, tile[:feats]))
    at = lax.broadcasted_iota(jnp.int32, (feats, feats), 0)
    frm = lax.broadcasted_iota(jnp.int32, (feats, feats), 1)
    order = jnp.where(frm == (at % 4) * (feats // 4) + at // 4, 1.0, 0.0).astype(jnp.bfloat16)
    for o in range(n_enc):
        segment = jnp.zeros((1, BLOCK), jnp.float32)
        body = jnp.zeros((feats, BLOCK), jnp.float32)
        for owner, seg_of, tile in found:
            hit = owner == float(o)
            segment = segment + jnp.where(hit, seg_of, 0.0)
            body = body + jnp.where(hit, tile, 0.0)
        tail = jnp.where(extra == 0, 1.0, jnp.where(extra == 1, segment, 0.0))
        rows_t[:, o * BLOCK : (o + 1) * BLOCK] = jnp.concatenate(
            [body, tail, jnp.zeros((LANES - APAD, BLOCK), jnp.float32)], axis=0
        )
    picked = mm(order, rows_t[:feats].astype(jnp.bfloat16))
    spread = mm(gram_ref[...], picked.astype(jnp.bfloat16))
    variance = jnp.sum((spread[:feats] + spread[feats:]) * picked, axis=0, keepdims=True)
    rows_t[:feats] = picked * lax.rsqrt(jnp.maximum(variance, 0.0) + eps_norm)
    x_t = rows_t[...]
    x_t_ref[...] = x_t[:APAD].astype(jnp.bfloat16)
    x_ref[...] = x_t.T.astype(jnp.bfloat16)
    group_t = lax.broadcasted_iota(jnp.int32, (LANES, rows), 0).astype(jnp.float32)
    key_mask_ref[...] = jnp.where(x_t[feats + 1 : feats + 2] == group_t, 0.0, 1.0).astype(jnp.bfloat16)
    group = lax.broadcasted_iota(jnp.int32, (BLOCK, LANES), 1).astype(jnp.float32)
    for core in range(2):
        rows_ref, mask_ref = row_refs[2 * core : 2 * core + 2]
        own = rows_t[:, pl.ds(pl.multiple_of((mine ^ core) * BLOCK, BLOCK), BLOCK)].T
        rows_ref[...] = own.astype(jnp.bfloat16)
        mask_ref[...] = jnp.where(own[:, feats + 1 : feats + 2] == group, -FAR, 0.0).astype(jnp.bfloat16)
    head_dim = q_gain_ref.shape[1]
    gain_ref[...] = q_gain_ref[...] * k_gain_ref[...] * (head_dim**-0.5 * math.log2(math.e))


def attend_heads(folds, place, x_t_ref, x_ref, key_mask_ref, gain_ref, own_ref, own_mask_ref):
    folds = list(folds)
    heads = range(len(folds))
    feats = (folds[0].shape[0] - TAIL) // 3
    tails = jnp.concatenate([fold[3 * feats :].astype(jnp.float32) for fold in folds], axis=1)
    row = lax.broadcasted_iota(jnp.int32, tails.shape, 0)

    def side(part):
        body = jnp.concatenate([fold[part * feats : (part + 1) * feats] for fold in folds], axis=1)
        shift = jnp.where(row == 0, tails[part : part + 1], 0.0).astype(jnp.bfloat16)
        return jnp.concatenate([body, shift], axis=0)

    def of(i):
        return slice(i * LANES, (i + 1) * LANES)

    keys = mm(side(1), x_t_ref[...], ((0,), (0,)))
    queries = mm(own_ref[:, :APAD], side(0))
    values = mm(x_ref[:, :APAD], side(2)).astype(jnp.bfloat16)
    gain, own_mask, key_mask = gain_ref[...], own_mask_ref[...], key_mask_ref[...]
    left, right = [], []
    for i in heads:
        key = keys[of(i)]
        square = jnp.sum(key * key, axis=0, keepdims=True) / LANES
        key = (key * lax.rsqrt(square + eps_norm)).astype(jnp.bfloat16)
        right.append(jnp.concatenate([key, key_mask], axis=0))
        query = queries[:, of(i)]
        square = jnp.sum(query * query, axis=1, keepdims=True) / LANES
        query = (query * lax.rsqrt(square + eps_norm) * gain).astype(jnp.bfloat16)
        left.append(jnp.concatenate([query, own_mask], axis=1))
    scores = [mm(left[i], right[i]) for i in heads]
    weights = [jnp.exp2(score).astype(jnp.bfloat16) for score in scores]
    ones = jnp.ones((values.shape[0], LANES), jnp.bfloat16)
    mixed = [mm(weights[i], jnp.concatenate([values[:, of(i)], ones], axis=1)) for i in heads]
    for i in heads:
        place(i, (mixed[i][:, :LANES] / mixed[i][:, LANES:]).astype(jnp.bfloat16))


def each_head(refs):
    for ref in refs:
        if len(ref.shape) == 2:
            yield ref[...]
        else:
            for i in range(ref.shape[0]):
                yield ref[i]


def attend_kernel(count, *refs):
    folds, out_ref = refs[6 : 6 + count], refs[-1]

    def place(i, result):
        out_ref[:, i * LANES : (i + 1) * LANES] = result

    attend_heads(each_head(folds), place, *refs[:6])


def output_kernel(heads, neighbours, lists, near_early_ref, near_rest_ref, own_early_ref, own_rest_ref, out_ref, sems):
    mine, slot = lax.axis_index("enc"), lax.axis_index("seq") & (heads - 1)
    copies = []

    def put(ref, at, base, far, k):
        head = (base ^ far) * heads + (slot ^ k)
        column = pl.ds(pl.multiple_of(head * LANES, LANES), LANES)
        result = ref.at[:, at * LANES : (at + 1) * LANES]
        copies.append(pltpu.make_async_copy(result, out_ref.at[0, :, column], sems.at[len(copies)]))
        copies[-1].start()

    for early, rest, base in (
        (near_early_ref, near_rest_ref, mine ^ 1),
        (own_early_ref, own_rest_ref, mine),
    ):
        for at, partner in enumerate(((0, 0), *neighbours)):
            put(early, at, base, *partner)
        for i, pair in enumerate(zip(*lists)):
            far, k = (jnp.where(base & 1 == 0, zero, one) for zero, one in zip(*pair))
            put(rest, 2 * i, base, far, k)
            put(rest, 2 * i + 1, base, far ^ 1, k)
    for copy in copies:
        copy.wait()


def vmem(count):
    return [pl.BlockSpec(memory_space=pltpu.VMEM)] * count


def hbm(count):
    return [pl.BlockSpec(memory_space=pltpu.HBM)] * count


def in_hbm(x):
    return pltpu.with_memory_space_constraint(x, pltpu.HBM)


def after(count):
    return [pl.BlockSpec(memory_space=pl.ANY)] * count


def call(kernel, ins, out_shape, scratch=(), cost=(1_000_000, 1_000_000)):
    return pl.pallas_call(
        kernel,
        in_specs=ins,
        out_specs=[pl.BlockSpec(memory_space=pltpu.VMEM)] * len(out_shape),
        out_shape=out_shape,
        scratch_shapes=list(scratch),
        compiler_params=pltpu.CompilerParams(vmem_limit_bytes=VMEM_LIMIT),
        cost_estimate=pl.CostEstimate(flops=cost[0], bytes_accessed=cost[1], transcendentals=0),
    )


def gate(x, *others):
    return pl.pallas_call(
        gate_kernel,
        in_specs=after(1 + len(others)),
        out_specs=after(1)[0],
        out_shape=jax.ShapeDtypeStruct(x.shape, x.dtype),
        input_output_aliases={0: 0},
        compiler_params=pltpu.CompilerParams(vmem_limit_bytes=VMEM_LIMIT),
    )(x, *others)


def exchange(x, axis, n, k):
    return lax.ppermute(x, axis, [(i, i ^ k) for i in range(n)])


def on_device(
    n_enc,
    n_seq,
    clip_features,
    clip_shape,
    packing,
    conv_weight,
    embed_weight,
    mod_shift,
    mod_scale,
    qkv_weight,
    q_gain,
    k_gain,
):
    caps = clip_features.shape[2:5]
    depth_all = clip_features.shape[5]
    cols = qkv_weight.shape[2]
    feats = embed_weight.shape[0]
    heads = cols // LANES
    rows = n_enc * BLOCK
    bf16, f32 = jnp.bfloat16, jnp.float32

    def folds(dtype, *lead):
        return jax.ShapeDtypeStruct((*lead, 3 * feats + TAIL, LANES), dtype)

    evens = [0]
    for bit in reversed(range(1, log2(n_enc))):
        evens += [at ^ (1 << bit) for at in evens]
    scale_rows, shift_rows = mod_scale.reshape(-1, LANES), mod_shift.reshape(-1, LANES)
    later = [
        clip_features.reshape(-1, depth_all),
        conv_weight.reshape(-1, depth_all),
        q_gain.reshape(1, -1),
        k_gain.reshape(1, -1),
    ]
    with jax.named_scope("fold"):
        embed, features, conv, q_gain, k_gain, keep, *sends = call(
            functools.partial(fold_kernel, len(later)),
            hbm(4 + len(later)),
            [jax.ShapeDtypeStruct(x.shape, x.dtype) for x in (embed_weight, *later)]
            + [folds(f32)]
            + [folds(bf16)] * max(heads - 1, 1),
            [
                pltpu.VMEM(scale_rows.shape, f32),
                pltpu.VMEM(shift_rows.shape, f32),
                pltpu.VMEM(qkv_weight.shape, bf16),
                pltpu.SemaphoreType.DMA((4 + len(later),)),
            ],
            cost=(200_000_000, 1_000_000),
        )(*map(in_hbm, (embed_weight, scale_rows, shift_rows, qkv_weight, *later)))

    with jax.named_scope("encode"):
        own_block = call(
            functools.partial(encode_kernel, caps),
            hbm(2) + vmem(2),
            [jax.ShapeDtypeStruct((NBS * TOKEN_ROWS, BLOCK), bf16)],
            [
                pltpu.SMEM(clip_shape.shape, jnp.int32),
                pltpu.SMEM(packing.shape, jnp.int32),
                pltpu.SemaphoreType.DMA((2,)),
            ],
            cost=(500_000_000, 2_000_000),
        )(in_hbm(clip_shape), in_hbm(packing), features, conv)[0]

    def add(keep, got, first):
        kernel = functools.partial(add_kernel, len(got))
        return call(kernel, vmem(1 + len(got)) + after(1), [folds(f32), folds(bf16)])(keep, *got, first)

    with jax.named_scope("fold_sum"):
        if heads > 1:
            got = [exchange(sends[k - 1], "seq", n_seq, k) for k in reversed(range(1, heads))]
            keep, send = add(keep, got, own_block)
        else:
            send = sends[0]

    with jax.named_scope("gram"):
        gram = call(gram_kernel, vmem(1) + after(1), [jax.ShapeDtypeStruct((2 * feats, feats), bf16)])(embed, keep)[0]

    with jax.named_scope("tokens"):
        own_block = gate(own_block, keep)
        blocks = [own_block] + [exchange(own_block, "enc", n_enc, k) for k in evens[1:]]

    with jax.named_scope("fold_sum"):
        for bit in range(log2(heads), log2(n_seq)):
            got = exchange(send, "seq", n_seq, 1 << bit)
            if bit + 1 < log2(n_seq):
                keep, send = add(keep, [got], own_block)
            else:
                fresh, swap = call(
                    functools.partial(last_add_kernel, len(blocks)),
                    vmem(2 + len(blocks)) + after(1),
                    [folds(bf16), folds(bf16, 1 + len(blocks))],
                )(keep, got, *blocks, gram)

    partners = [(far, k) for far in evens for k in range(heads) if far or k]
    partners.sort(key=lambda p: (p[0].bit_count() + p[1].bit_count(), p[0]))
    near_count = min(3, len(partners))
    half = (len(partners) - near_count) // 2
    assert len(partners) == near_count + 2 * half
    neighbours = tuple(partners[:near_count])
    lists = (tuple(partners[near_count : near_count + half]), tuple(partners[near_count + half :]))

    def spread(x, partner_of):
        pairs = []
        for e in range(n_enc):
            far, k = partner_of[e & 1]
            pairs += [(e * n_seq + i, (e ^ far) * n_seq + (i ^ k)) for i in range(n_seq)]
        return lax.ppermute(x, ("enc", "seq"), pairs)

    with jax.named_scope("gather"):
        singles = [spread(fresh, (partner, partner)) for partner in neighbours]
        swapped = exchange(swap, "enc", n_enc, 1)
        pair = call(pair_kernel, vmem(2), [folds(bf16, 2)])(fresh, swapped)[0]
        got = [spread(pair, partner_of) for partner_of in zip(*lists)]

    with jax.named_scope("pack"):
        *shared, own_rows, own_mask, far_rows, far_mask = call(
            functools.partial(pack_kernel, tuple(evens), feats),
            vmem(4 + len(evens)),
            [
                jax.ShapeDtypeStruct((APAD, rows), bf16),
                jax.ShapeDtypeStruct((rows, LANES), bf16),
                jax.ShapeDtypeStruct((LANES, rows), bf16),
                jax.ShapeDtypeStruct((1, LANES), f32),
            ]
            + [jax.ShapeDtypeStruct((BLOCK, LANES), bf16)] * 4,
            [pltpu.VMEM((LANES, rows), f32)],
        )(q_gain, k_gain, gram, *blocks, swapped)

    def attend(rows_here, groups, first=()):
        count = sum(group.size for group in groups) // ((3 * feats + TAIL) * LANES)
        return call(
            functools.partial(attend_kernel, len(groups)),
            vmem(6 + len(groups)) + after(len(first)),
            [jax.ShapeDtypeStruct((BLOCK, count * LANES), bf16)],
            cost=(count * 200_000_000, 1_000_000),
        )(*shared, *rows_here, *groups, *first)[0]

    with jax.named_scope("attend"):
        own, other = (own_rows, own_mask), (far_rows, far_mask)
        early, rest = [fresh, *singles], got
        early_other = attend(other, early)
        early_own = attend(own, early, [early_other])
        near_early = exchange(gate(early_other, early_own), "enc", n_enc, 1)
        near_rest = exchange(attend(other, rest, [early_own]), "enc", n_enc, 1)
        rest_own = attend(own, rest)
        return pl.pallas_call(
            functools.partial(output_kernel, heads, neighbours, lists),
            in_specs=vmem(4),
            out_specs=hbm(1)[0],
            out_shape=jax.ShapeDtypeStruct((1, BLOCK, n_enc * cols), bf16),
            scratch_shapes=[pltpu.SemaphoreType.DMA((n_enc * heads,))],
            compiler_params=pltpu.CompilerParams(vmem_limit_bytes=VMEM_LIMIT),
        )(near_early, near_rest, early_own, rest_own)


def solution(mesh):
    return jax.shard_map(
        functools.partial(on_device, mesh.shape["enc"], mesh.shape["seq"]),
        mesh=mesh,
        in_specs=(
            P("enc", "seq", None, None, None, None),
            P("enc", "seq", None),
            P("enc", "seq", None, None),
            P(),
            P(),
            P(),
            P(),
            P(None, "seq", "enc"),
            P(),
            P(),
        ),
        out_specs=P("seq", "enc", None),
        check_vma=False,
    )
```

```python
import functools
import math

import jax
import jax.numpy as jnp
from jax import lax
from jax.experimental import pallas as pl
from jax.experimental.pallas import tpu as pltpu
from jax.sharding import PartitionSpec as P

BLOCK = 128
NBS = 2
LANES = 128
APAD = 72
TAIL = 8
TOKEN_ROWS = 80
eps_norm = 1e-06
FAR = 2.0**20
VMEM_LIMIT = 48 * 1024 * 1024


def mm(a, b, dims=((1,), (0,)), precision=None):
    return lax.dot_general(a, b, (dims, ((), ())), preferred_element_type=jnp.float32, precision=precision)


def split_bf16(x):
    hi = x.astype(jnp.bfloat16)
    return hi, (x - hi.astype(jnp.float32)).astype(jnp.bfloat16)


def log2(n):
    bits = n.bit_length() - 1
    assert 1 << bits == n
    return bits


def fetch(pairs, sems):
    copies = [pltpu.make_async_copy(src, dst, sems.at[i]) for i, (src, dst) in enumerate(pairs)]
    for copy in copies:
        copy.start()
    return copies


def fold_kernel(count, embed_hbm, scale_hbm, shift_hbm, w_hbm, *refs):
    later_hbm, embed_ref, later, keep_ref, sends = refs[:count], refs[count], refs[count + 1 : 2 * count + 1], refs[2 * count + 1], refs[2 * count + 2 : -4]
    scale_ref, shift_ref, w_ref, sems = refs[-4:]
    copies = fetch(
        [(embed_hbm, embed_ref), (scale_hbm, scale_ref), (shift_hbm, shift_ref), (w_hbm, w_ref)]
        + list(zip(later_hbm, later)),
        sems,
    )
    me = lax.axis_index("seq")
    _, depth, cols = w_ref.shape
    feats = embed_ref.shape[0]
    heads = cols // LANES
    for copy in copies[:3]:
        copy.wait()
    mean = jnp.sum(embed_ref[...].astype(jnp.float32), axis=1, keepdims=True) / embed_ref.shape[1]
    span = max(depth, LANES)
    chunks = span // LANES
    first = (me * depth) // LANES
    emb = embed_ref[:, pl.ds(pl.multiple_of(first * LANES, LANES), span)].astype(jnp.float32) - mean
    scale = jnp.concatenate([scale_ref[pl.ds(first + i, 1), :] for i in range(chunks)], axis=1)
    shift = jnp.concatenate([shift_ref[pl.ds(first + i, 1), :] for i in range(chunks)], axis=1)
    left = jnp.concatenate(
        [emb * (1.0 + scale), shift, jnp.zeros((APAD - feats - 1, span), jnp.float32)], axis=0
    )
    if depth < LANES:
        low = me * depth - first * LANES
        lane = lax.broadcasted_iota(jnp.int32, left.shape, 1)
        left = jnp.where((lane >= low) & (lane < low + depth), left, 0.0)
    hi, lo = split_bf16(left)
    both = jnp.concatenate([hi, lo], axis=0)
    copies[3].wait()

    def product(head):
        start = pl.multiple_of(head * LANES, LANES)
        right = jnp.concatenate([w_ref[part, :, pl.ds(start, LANES)] for part in range(3)], axis=1)
        right = jnp.concatenate([right] * (span // depth), axis=0)
        total = mm(both, right)
        total = total[:APAD] + total[APAD:]
        parts = [total[:, part * LANES : (part + 1) * LANES] for part in range(3)]
        row = lax.broadcasted_iota(jnp.int32, (TAIL, LANES), 0)
        tail = jnp.zeros((TAIL, LANES), jnp.float32)
        for part in range(3):
            tail = jnp.where(row == part, parts[part][feats : feats + 1], tail)
        return jnp.concatenate([part[:feats] for part in parts] + [tail], axis=0)

    slot = me & (heads - 1)
    for k in range(1, heads):
        sends[k - 1][...] = product(slot ^ k).astype(jnp.bfloat16)
    total = product(slot)
    keep_ref[...] = total
    if heads == 1:
        sends[0][...] = total.astype(jnp.bfloat16)
    for copy in copies[4:]:
        copy.wait()


def add_kernel(count, keep_in, *refs):
    total = keep_in[...]
    for ref in refs[:count]:
        total = total + ref[...].astype(jnp.float32)
    refs[-2][...] = total
    refs[-1][...] = total.astype(jnp.bfloat16)


def last_add_kernel(count, keep_in, got_ref, *refs):
    total = (keep_in[...] + got_ref[...].astype(jnp.float32)).astype(jnp.bfloat16)
    out_ref, swap_ref = refs[-2:]
    out_ref[...] = total
    swap_ref[0] = total
    for i in range(count):
        block = refs[i][...]
        rest = jnp.zeros((total.shape[0] - block.shape[0], LANES), jnp.bfloat16)
        swap_ref[1 + i] = jnp.concatenate([block, rest], axis=0)


def pair_kernel(own_ref, swapped_ref, out_ref):
    out_ref[0] = own_ref[...]
    out_ref[1] = swapped_ref[0]


def gate_kernel(*refs):
    pass


def encode_kernel(caps, *refs):
    hbm_refs, out_ref, refs, sems = refs[:4], refs[5], refs[6:10], refs[10]
    copies = fetch(list(zip(hbm_refs, refs)), sems)
    shape_ref, plan_ref, feat_ref, conv_ref = refs
    frames_cap, height_cap, width_cap = caps
    spots = frames_cap * height_cap * width_cap
    frame_size = height_cap * width_cap
    latent_ch = conv_ref.shape[0] // 27
    feats = 4 * latent_ch
    copies[0].wait()
    copies[1].wait()
    frames, height, width = shape_ref[0, 0, 0], shape_ref[0, 0, 1], shape_ref[0, 0, 2]
    spot = lax.broadcasted_iota(jnp.int32, (1, spots), 1)
    frame_ix = spot // frame_size
    row_ix = (spot % frame_size) // width_cap
    col_ix = spot % width_cap
    inside = (frame_ix < frames) & (row_ix < height) & (col_ix < width)
    tokens = NBS * BLOCK
    half_w = (width // 2).astype(jnp.float32)
    per_frame_int = (height // 2) * (width // 2)
    per_frame = per_frame_int.astype(jnp.float32)
    live = frames * per_frame_int
    token_int = lax.broadcasted_iota(jnp.int32, (1, tokens), 1)
    token = token_int.astype(jnp.float32)
    frame_of = jnp.floor((token + 0.5) / jnp.full((1, tokens), per_frame))
    within = token - frame_of * per_frame
    row_of = jnp.floor((within + 0.5) / jnp.full((1, tokens), half_w))
    col_of = within - row_of * half_w
    source = (frame_of * frame_size + row_of * (2 * width_cap) + col_of * 2).astype(jnp.int32)
    source = jnp.where(token_int < live, source, -1)
    chosen = lax.broadcasted_iota(jnp.int32, (spots, tokens), 0) == source
    chosen = jnp.where(chosen, 1.0, 0.0).astype(jnp.bfloat16)
    copies[2].wait()
    copies[3].wait()
    taps = mm(conv_ref[...], feat_ref[...], ((1,), (1,)))
    taps = jnp.where(inside, taps, 0.0)

    def tap(a, b, j):
        at = (9 * a + 3 * b + j) * latent_ch
        return taps[at : at + latent_ch]

    def later(x, by):
        zeros = jnp.zeros((latent_ch, by * frame_size), jnp.float32)
        return jnp.concatenate([zeros, x[:, : spots - by * frame_size]], axis=1)

    def over_frames(b, j):
        return tap(2, b, j) + later(tap(1, b, j), 1) + later(tap(0, b, j), 2)

    def over_rows(j):
        above = pltpu.roll(over_frames(0, j), width_cap, 1)
        below = pltpu.roll(over_frames(2, j), spots - width_cap, 1)
        return (
            over_frames(1, j)
            + jnp.where(row_ix >= 1, above, 0.0)
            + jnp.where(row_ix < height_cap - 1, below, 0.0)
        )

    latent = (
        over_rows(1)
        + jnp.where(col_ix >= 1, pltpu.roll(over_rows(0), 1, 1), 0.0)
        + jnp.where(col_ix < width_cap - 1, pltpu.roll(over_rows(2), spots - 1, 1), 0.0)
    )
    latent = latent.astype(jnp.bfloat16).astype(jnp.float32)
    shifted = [latent] + [pltpu.roll(latent, spots - by, 1) for by in (1, width_cap, width_cap + 1)]
    patches = jnp.concatenate(shifted, axis=0).astype(jnp.bfloat16)

    picked = mm(patches, chosen)
    kind = lax.broadcasted_iota(jnp.int32, (TOKEN_ROWS - feats, BLOCK), 0)
    pieces = []
    for b in range(NBS):
        count = jnp.clip(live - b * BLOCK, 0, BLOCK)
        info = jnp.where(
            kind == 0,
            plan_ref[0, 0, b, 0],
            jnp.where(kind == 1, plan_ref[0, 0, b, 1], jnp.where(kind == 2, count, 0)),
        )
        pieces += [picked[:, b * BLOCK : (b + 1) * BLOCK], info.astype(jnp.float32)]
    out_ref[...] = jnp.concatenate(pieces, axis=0).astype(jnp.bfloat16)


def gram_kernel(embed_ref, first_ref, out_ref):
    feats, width = embed_ref.shape
    emb = embed_ref[...].astype(jnp.float32)
    emb = emb - jnp.sum(emb, axis=1, keepdims=True) / width
    both = jnp.concatenate(split_bf16(emb), axis=0)
    gram = mm(both, both, ((1,), (1,))) / width
    gram = gram[:feats] + gram[feats:]
    out_ref[...] = jnp.concatenate(split_bf16(gram[:, :feats] + gram[:, feats:]), axis=0)


def pack_kernel(evens, feats, q_gain_ref, k_gain_ref, gram_ref, *refs):
    here, near = refs[: len(evens)], refs[len(evens)]
    x_t_ref, x_ref, key_mask_ref, gain_ref, *row_refs, rows_t = refs[len(evens) + 1 :]
    n_enc = 2 * len(evens)
    mine = lax.axis_index("enc")
    rows = n_enc * BLOCK
    lane = lax.broadcasted_iota(jnp.int32, (1, BLOCK), 1).astype(jnp.float32)
    extra = lax.broadcasted_iota(jnp.int32, (APAD - feats, BLOCK), 0)
    found = []
    blocks = [(at, here[i][...]) for i, at in enumerate(evens)]
    blocks += [(at ^ 1, near[1 + i]) for i, at in enumerate(evens)]
    for distance, block in blocks:
        source = mine ^ distance
        for b in range(NBS):
            tile = block.astype(jnp.float32)[b * TOKEN_ROWS : (b + 1) * TOKEN_ROWS]
            owner, offset, count = (tile[feats + i : feats + i + 1] for i in range(3))
            owner = jnp.where(offset == 0.0, owner, -1.0)
            segment = jnp.where(lane < count, (source + 1).astype(jnp.float32), 0.0)
            found.append((owner, segment, tile[:feats]))
    at = lax.broadcasted_iota(jnp.int32, (feats, feats), 0)
    frm = lax.broadcasted_iota(jnp.int32, (feats, feats), 1)
    order = jnp.where(frm == (at % 4) * (feats // 4) + at // 4, 1.0, 0.0).astype(jnp.bfloat16)
    for o in range(n_enc):
        segment = jnp.zeros((1, BLOCK), jnp.float32)
        body = jnp.zeros((feats, BLOCK), jnp.float32)
        for owner, seg_of, tile in found:
            hit = owner == float(o)
            segment = segment + jnp.where(hit, seg_of, 0.0)
            body = body + jnp.where(hit, tile, 0.0)
        tail = jnp.where(extra == 0, 1.0, jnp.where(extra == 1, segment, 0.0))
        rows_t[:, o * BLOCK : (o + 1) * BLOCK] = jnp.concatenate(
            [body, tail, jnp.zeros((LANES - APAD, BLOCK), jnp.float32)], axis=0
        )
    picked = mm(order, rows_t[:feats].astype(jnp.bfloat16))
    spread = mm(gram_ref[...], picked.astype(jnp.bfloat16))
    variance = jnp.sum((spread[:feats] + spread[feats:]) * picked, axis=0, keepdims=True)
    rows_t[:feats] = picked * lax.rsqrt(jnp.maximum(variance, 0.0) + eps_norm)
    x_t = rows_t[...]
    x_t_ref[...] = x_t[:APAD].astype(jnp.bfloat16)
    x_ref[...] = x_t.T.astype(jnp.bfloat16)
    group_t = lax.broadcasted_iota(jnp.int32, (LANES, rows), 0).astype(jnp.float32)
    key_mask_ref[...] = jnp.where(x_t[feats + 1 : feats + 2] == group_t, 0.0, 1.0).astype(jnp.bfloat16)
    group = lax.broadcasted_iota(jnp.int32, (BLOCK, LANES), 1).astype(jnp.float32)
    for core in range(2):
        rows_ref, mask_ref = row_refs[2 * core : 2 * core + 2]
        own = rows_t[:, pl.ds(pl.multiple_of((mine ^ core) * BLOCK, BLOCK), BLOCK)].T
        rows_ref[...] = own.astype(jnp.bfloat16)
        mask_ref[...] = jnp.where(own[:, feats + 1 : feats + 2] == group, -FAR, 0.0).astype(jnp.bfloat16)
    head_dim = q_gain_ref.shape[1]
    gain_ref[...] = q_gain_ref[...] * k_gain_ref[...] * (head_dim**-0.5 * math.log2(math.e))


def attend_heads(folds, place, x_t_ref, x_ref, key_mask_ref, gain_ref, own_ref, own_mask_ref):
    folds = list(folds)
    heads = range(len(folds))
    feats = (folds[0].shape[0] - TAIL) // 3
    tails = jnp.concatenate([fold[3 * feats :].astype(jnp.float32) for fold in folds], axis=1)
    row = lax.broadcasted_iota(jnp.int32, tails.shape, 0)

    def side(part):
        body = jnp.concatenate([fold[part * feats : (part + 1) * feats] for fold in folds], axis=1)
        shift = jnp.where(row == 0, tails[part : part + 1], 0.0).astype(jnp.bfloat16)
        return jnp.concatenate([body, shift], axis=0)

    def of(i):
        return slice(i * LANES, (i + 1) * LANES)

    keys = mm(side(1), x_t_ref[...], ((0,), (0,)))
    queries = mm(own_ref[:, :APAD], side(0))
    values = mm(x_ref[:, :APAD], side(2)).astype(jnp.bfloat16)
    gain, own_mask, key_mask = gain_ref[...], own_mask_ref[...], key_mask_ref[...]
    left, right = [], []
    for i in heads:
        key = keys[of(i)]
        square = jnp.sum(key * key, axis=0, keepdims=True) / LANES
        key = (key * lax.rsqrt(square + eps_norm)).astype(jnp.bfloat16)
        right.append(jnp.concatenate([key, key_mask], axis=0))
        query = queries[:, of(i)]
        square = jnp.sum(query * query, axis=1, keepdims=True) / LANES
        query = (query * lax.rsqrt(square + eps_norm) * gain).astype(jnp.bfloat16)
        left.append(jnp.concatenate([query, own_mask], axis=1))
    scores = [mm(left[i], right[i]) for i in heads]
    weights = [jnp.exp2(score).astype(jnp.bfloat16) for score in scores]
    ones = jnp.ones((values.shape[0], LANES), jnp.bfloat16)
    mixed = [mm(weights[i], jnp.concatenate([values[:, of(i)], ones], axis=1)) for i in heads]
    for i in heads:
        place(i, (mixed[i][:, :LANES] / mixed[i][:, LANES:]).astype(jnp.bfloat16))


def each_head(refs):
    for ref in refs:
        if len(ref.shape) == 2:
            yield ref[...]
        else:
            for i in range(ref.shape[0]):
                yield ref[i]


def attend_kernel(count, *refs):
    folds, out_ref = refs[6 : 6 + count], refs[-1]

    def place(i, result):
        out_ref[:, i * LANES : (i + 1) * LANES] = result

    attend_heads(each_head(folds), place, *refs[:6])


def output_kernel(heads, neighbours, lists, near_early_ref, near_rest_ref, own_early_ref, own_rest_ref, out_ref, sems):
    mine, slot = lax.axis_index("enc"), lax.axis_index("seq") & (heads - 1)
    copies = []

    def put(ref, at, base, far, k):
        head = (base ^ far) * heads + (slot ^ k)
        column = pl.ds(pl.multiple_of(head * LANES, LANES), LANES)
        result = ref.at[:, at * LANES : (at + 1) * LANES]
        copies.append(pltpu.make_async_copy(result, out_ref.at[0, :, column], sems.at[len(copies)]))
        copies[-1].start()

    for early, rest, base in (
        (near_early_ref, near_rest_ref, mine ^ 1),
        (own_early_ref, own_rest_ref, mine),
    ):
        for at, partner in enumerate(((0, 0), *neighbours)):
            put(early, at, base, *partner)
        for i, pair in enumerate(zip(*lists)):
            far, k = (jnp.where(base & 1 == 0, zero, one) for zero, one in zip(*pair))
            put(rest, 2 * i, base, far, k)
            put(rest, 2 * i + 1, base, far ^ 1, k)
    for copy in copies:
        copy.wait()


def vmem(count):
    return [pl.BlockSpec(memory_space=pltpu.VMEM)] * count


def hbm(count):
    return [pl.BlockSpec(memory_space=pltpu.HBM)] * count


def in_hbm(x):
    return pltpu.with_memory_space_constraint(x, pltpu.HBM)


def after(count):
    return [pl.BlockSpec(memory_space=pl.ANY)] * count


def call(kernel, ins, out_shape, scratch=(), cost=(1_000_000, 1_000_000)):
    return pl.pallas_call(
        kernel,
        in_specs=ins,
        out_specs=[pl.BlockSpec(memory_space=pltpu.VMEM)] * len(out_shape),
        out_shape=out_shape,
        scratch_shapes=list(scratch),
        compiler_params=pltpu.CompilerParams(vmem_limit_bytes=VMEM_LIMIT),
        cost_estimate=pl.CostEstimate(flops=cost[0], bytes_accessed=cost[1], transcendentals=0),
    )


def gate(x, *others):
    return pl.pallas_call(
        gate_kernel,
        in_specs=after(1 + len(others)),
        out_specs=after(1)[0],
        out_shape=jax.ShapeDtypeStruct(x.shape, x.dtype),
        input_output_aliases={0: 0},
        compiler_params=pltpu.CompilerParams(vmem_limit_bytes=VMEM_LIMIT),
    )(x, *others)


def exchange(x, axis, n, k):
    return lax.ppermute(x, axis, [(i, i ^ k) for i in range(n)])


def on_device(
    n_enc,
    n_seq,
    clip_features,
    clip_shape,
    packing,
    conv_weight,
    embed_weight,
    mod_shift,
    mod_scale,
    qkv_weight,
    q_gain,
    k_gain,
):
    caps = clip_features.shape[2:5]
    depth_all = clip_features.shape[5]
    cols = qkv_weight.shape[2]
    feats = embed_weight.shape[0]
    heads = cols // LANES
    rows = n_enc * BLOCK
    bf16, f32 = jnp.bfloat16, jnp.float32

    def folds(dtype, *lead):
        return jax.ShapeDtypeStruct((*lead, 3 * feats + TAIL, LANES), dtype)

    evens = [0]
    for bit in reversed(range(1, log2(n_enc))):
        evens += [at ^ (1 << bit) for at in evens]
    scale_rows, shift_rows = mod_scale.reshape(-1, LANES), mod_shift.reshape(-1, LANES)
    later = [q_gain.reshape(1, -1), k_gain.reshape(1, -1)]
    features = clip_features.reshape(-1, depth_all)
    conv = conv_weight.reshape(-1, depth_all)
    with jax.named_scope("fold"):
        embed, q_gain, k_gain, keep, *sends = call(
            functools.partial(fold_kernel, len(later)),
            hbm(4 + len(later)),
            [jax.ShapeDtypeStruct(x.shape, x.dtype) for x in (embed_weight, *later)]
            + [folds(f32)]
            + [folds(bf16)] * max(heads - 1, 1),
            [
                pltpu.VMEM(scale_rows.shape, f32),
                pltpu.VMEM(shift_rows.shape, f32),
                pltpu.VMEM(qkv_weight.shape, bf16),
                pltpu.SemaphoreType.DMA((4 + len(later),)),
            ],
            cost=(200_000_000, 1_000_000),
        )(*map(in_hbm, (embed_weight, scale_rows, shift_rows, qkv_weight, *later)))

    with jax.named_scope("encode"):
        own_block = call(
            functools.partial(encode_kernel, caps),
            hbm(4) + after(1),
            [jax.ShapeDtypeStruct((NBS * TOKEN_ROWS, BLOCK), bf16)],
            [
                pltpu.SMEM(clip_shape.shape, jnp.int32),
                pltpu.SMEM(packing.shape, jnp.int32),
                pltpu.VMEM(features.shape, bf16),
                pltpu.VMEM(conv.shape, bf16),
                pltpu.SemaphoreType.DMA((4,)),
            ],
            cost=(500_000_000, 2_000_000),
        )(*map(in_hbm, (clip_shape, packing, features, conv)), keep)[0]

    def add(keep, got, first):
        kernel = functools.partial(add_kernel, len(got))
        return call(kernel, vmem(1 + len(got)) + after(1), [folds(f32), folds(bf16)])(keep, *got, first)

    with jax.named_scope("fold_sum"):
        if heads > 1:
            got = [exchange(sends[k - 1], "seq", n_seq, k) for k in reversed(range(1, heads))]
            keep, send = add(keep, got, own_block)
        else:
            send = sends[0]

    with jax.named_scope("gram"):
        gram = call(gram_kernel, vmem(1) + after(1), [jax.ShapeDtypeStruct((2 * feats, feats), bf16)])(embed, keep)[0]

    with jax.named_scope("tokens"):
        own_block = gate(own_block, keep)
        blocks = [own_block] + [exchange(own_block, "enc", n_enc, k) for k in evens[1:]]

    with jax.named_scope("fold_sum"):
        for bit in range(log2(heads), log2(n_seq)):
            got = exchange(send, "seq", n_seq, 1 << bit)
            if bit + 1 < log2(n_seq):
                keep, send = add(keep, [got], own_block)
            else:
                fresh, swap = call(
                    functools.partial(last_add_kernel, len(blocks)),
                    vmem(2 + len(blocks)) + after(1),
                    [folds(bf16), folds(bf16, 1 + len(blocks))],
                )(keep, got, *blocks, gram)

    partners = [(far, k) for far in evens for k in range(heads) if far or k]
    partners.sort(key=lambda p: (p[0].bit_count() + p[1].bit_count(), p[0]))
    near_count = min(3, len(partners))
    half = (len(partners) - near_count) // 2
    assert len(partners) == near_count + 2 * half
    neighbours = tuple(partners[:near_count])
    lists = (tuple(partners[near_count : near_count + half]), tuple(partners[near_count + half :]))

    def spread(x, partner_of):
        pairs = []
        for e in range(n_enc):
            far, k = partner_of[e & 1]
            pairs += [(e * n_seq + i, (e ^ far) * n_seq + (i ^ k)) for i in range(n_seq)]
        return lax.ppermute(x, ("enc", "seq"), pairs)

    with jax.named_scope("gather"):
        singles = [spread(fresh, (partner, partner)) for partner in neighbours]
        swapped = exchange(swap, "enc", n_enc, 1)
        pair = call(pair_kernel, vmem(2), [folds(bf16, 2)])(fresh, swapped)[0]
        got = [spread(pair, partner_of) for partner_of in zip(*lists)]

    with jax.named_scope("pack"):
        *shared, own_rows, own_mask, far_rows, far_mask = call(
            functools.partial(pack_kernel, tuple(evens), feats),
            vmem(4 + len(evens)),
            [
                jax.ShapeDtypeStruct((APAD, rows), bf16),
                jax.ShapeDtypeStruct((rows, LANES), bf16),
                jax.ShapeDtypeStruct((LANES, rows), bf16),
                jax.ShapeDtypeStruct((1, LANES), f32),
            ]
            + [jax.ShapeDtypeStruct((BLOCK, LANES), bf16)] * 4,
            [pltpu.VMEM((LANES, rows), f32)],
        )(q_gain, k_gain, gram, *blocks, swapped)

    def attend(rows_here, groups, first=()):
        count = sum(group.size for group in groups) // ((3 * feats + TAIL) * LANES)
        return call(
            functools.partial(attend_kernel, len(groups)),
            vmem(6 + len(groups)) + after(len(first)),
            [jax.ShapeDtypeStruct((BLOCK, count * LANES), bf16)],
            cost=(count * 200_000_000, 1_000_000),
        )(*shared, *rows_here, *groups, *first)[0]

    with jax.named_scope("attend"):
        own, other = (own_rows, own_mask), (far_rows, far_mask)
        early, rest = [fresh, *singles], got
        early_other = attend(other, early)
        early_own = attend(own, early, [early_other])
        near_early = exchange(gate(early_other, early_own), "enc", n_enc, 1)
        near_rest = exchange(attend(other, rest, [early_own]), "enc", n_enc, 1)
        rest_own = attend(own, rest)
        return pl.pallas_call(
            functools.partial(output_kernel, heads, neighbours, lists),
            in_specs=vmem(4),
            out_specs=hbm(1)[0],
            out_shape=jax.ShapeDtypeStruct((1, BLOCK, n_enc * cols), bf16),
            scratch_shapes=[pltpu.SemaphoreType.DMA((n_enc * heads,))],
            compiler_params=pltpu.CompilerParams(vmem_limit_bytes=VMEM_LIMIT),
        )(near_early, near_rest, early_own, rest_own)


def solution(mesh):
    return jax.shard_map(
        functools.partial(on_device, mesh.shape["enc"], mesh.shape["seq"]),
        mesh=mesh,
        in_specs=(
            P("enc", "seq", None, None, None, None),
            P("enc", "seq", None),
            P("enc", "seq", None, None),
            P(),
            P(),
            P(),
            P(),
            P(None, "seq", "enc"),
            P(),
            P(),
        ),
        out_specs=P("seq", "enc", None),
        check_vma=False,
    )
```

```python
import functools
import math

import jax
import jax.numpy as jnp
from jax import lax
from jax.experimental import pallas as pl
from jax.experimental.pallas import tpu as pltpu
from jax.sharding import PartitionSpec as P

BLOCK = 128
NBS = 2
LANES = 128
APAD = 72
TAIL = 8
TOKEN_ROWS = 80
eps_norm = 1e-06
FAR = 2.0**20
VMEM_LIMIT = 48 * 1024 * 1024


def mm(a, b, dims=((1,), (0,)), precision=None):
    return lax.dot_general(a, b, (dims, ((), ())), preferred_element_type=jnp.float32, precision=precision)


def split_bf16(x):
    hi = x.astype(jnp.bfloat16)
    return hi, (x - hi.astype(jnp.float32)).astype(jnp.bfloat16)


def log2(n):
    bits = n.bit_length() - 1
    assert 1 << bits == n
    return bits


def fetch(pairs, sems):
    copies = [pltpu.make_async_copy(src, dst, sems.at[i]) for i, (src, dst) in enumerate(pairs)]
    for copy in copies:
        copy.start()
    return copies


def fold_kernel(count, embed_hbm, scale_hbm, shift_hbm, w_hbm, *refs):
    later_hbm, embed_ref, later, keep_ref, sends = refs[:count], refs[count], refs[count + 1 : 2 * count + 1], refs[2 * count + 1], refs[2 * count + 2 : -4]
    scale_ref, shift_ref, w_ref, sems = refs[-4:]
    copies = fetch(
        [(embed_hbm, embed_ref), (scale_hbm, scale_ref), (shift_hbm, shift_ref), (w_hbm, w_ref)]
        + list(zip(later_hbm, later)),
        sems,
    )
    me = lax.axis_index("seq")
    _, depth, cols = w_ref.shape
    feats = embed_ref.shape[0]
    heads = cols // LANES
    for copy in copies[:3]:
        copy.wait()
    mean = jnp.sum(embed_ref[...].astype(jnp.float32), axis=1, keepdims=True) / embed_ref.shape[1]
    span = max(depth, LANES)
    chunks = span // LANES
    first = (me * depth) // LANES
    emb = embed_ref[:, pl.ds(pl.multiple_of(first * LANES, LANES), span)].astype(jnp.float32) - mean
    scale = jnp.concatenate([scale_ref[pl.ds(first + i, 1), :] for i in range(chunks)], axis=1)
    shift = jnp.concatenate([shift_ref[pl.ds(first + i, 1), :] for i in range(chunks)], axis=1)
    left = jnp.concatenate(
        [emb * (1.0 + scale), shift, jnp.zeros((APAD - feats - 1, span), jnp.float32)], axis=0
    )
    if depth < LANES:
        low = me * depth - first * LANES
        lane = lax.broadcasted_iota(jnp.int32, left.shape, 1)
        left = jnp.where((lane >= low) & (lane < low + depth), left, 0.0)
    hi, lo = split_bf16(left)
    both = jnp.concatenate([hi, lo], axis=0)
    copies[3].wait()

    def product(head):
        start = pl.multiple_of(head * LANES, LANES)
        right = jnp.concatenate([w_ref[part, :, pl.ds(start, LANES)] for part in range(3)], axis=1)
        right = jnp.concatenate([right] * (span // depth), axis=0)
        total = mm(both, right)
        total = total[:APAD] + total[APAD:]
        parts = [total[:, part * LANES : (part + 1) * LANES] for part in range(3)]
        row = lax.broadcasted_iota(jnp.int32, (TAIL, LANES), 0)
        tail = jnp.zeros((TAIL, LANES), jnp.float32)
        for part in range(3):
            tail = jnp.where(row == part, parts[part][feats : feats + 1], tail)
        return jnp.concatenate([part[:feats] for part in parts] + [tail], axis=0)

    slot = me & (heads - 1)
    for k in range(1, heads):
        sends[k - 1][...] = product(slot ^ k).astype(jnp.bfloat16)
    total = product(slot)
    keep_ref[...] = total
    if heads == 1:
        sends[0][...] = total.astype(jnp.bfloat16)
    for copy in copies[4:]:
        copy.wait()


def add_kernel(count, keep_in, *refs):
    total = keep_in[...]
    for ref in refs[:count]:
        total = total + ref[...].astype(jnp.float32)
    refs[-2][...] = total
    refs[-1][...] = total.astype(jnp.bfloat16)


def last_add_kernel(count, keep_in, got_ref, *refs):
    total = (keep_in[...] + got_ref[...].astype(jnp.float32)).astype(jnp.bfloat16)
    out_ref, swap_ref = refs[-2:]
    out_ref[...] = total
    swap_ref[0] = total
    for i in range(count):
        block = refs[i][...]
        rest = jnp.zeros((total.shape[0] - block.shape[0], LANES), jnp.bfloat16)
        swap_ref[1 + i] = jnp.concatenate([block, rest], axis=0)


def pair_kernel(own_ref, swapped_ref, out_ref):
    out_ref[0] = own_ref[...]
    out_ref[1] = swapped_ref[0]


def gate_kernel(*refs):
    pass


def encode_kernel(caps, shape_hbm, plan_hbm, feat_ref, conv_ref, out_ref, shape_ref, plan_ref, sems):
    copies = fetch([(shape_hbm, shape_ref), (plan_hbm, plan_ref)], sems)
    frames_cap, height_cap, width_cap = caps
    spots = frames_cap * height_cap * width_cap
    frame_size = height_cap * width_cap
    latent_ch = conv_ref.shape[0] // 27
    feats = 4 * latent_ch
    taps = mm(conv_ref[...], feat_ref[...], ((1,), (1,)))
    copies[0].wait()
    copies[1].wait()
    frames, height, width = shape_ref[0, 0, 0], shape_ref[0, 0, 1], shape_ref[0, 0, 2]
    spot = lax.broadcasted_iota(jnp.int32, (1, spots), 1)
    frame_ix = spot // frame_size
    row_ix = (spot % frame_size) // width_cap
    col_ix = spot % width_cap
    inside = (frame_ix < frames) & (row_ix < height) & (col_ix < width)
    taps = jnp.where(inside, taps, 0.0)

    def tap(a, b, j):
        at = (9 * a + 3 * b + j) * latent_ch
        return taps[at : at + latent_ch]

    def later(x, by):
        zeros = jnp.zeros((latent_ch, by * frame_size), jnp.float32)
        return jnp.concatenate([zeros, x[:, : spots - by * frame_size]], axis=1)

    def over_frames(b, j):
        return tap(2, b, j) + later(tap(1, b, j), 1) + later(tap(0, b, j), 2)

    def over_rows(j):
        above = pltpu.roll(over_frames(0, j), width_cap, 1)
        below = pltpu.roll(over_frames(2, j), spots - width_cap, 1)
        return (
            over_frames(1, j)
            + jnp.where(row_ix >= 1, above, 0.0)
            + jnp.where(row_ix < height_cap - 1, below, 0.0)
        )

    latent = (
        over_rows(1)
        + jnp.where(col_ix >= 1, pltpu.roll(over_rows(0), 1, 1), 0.0)
        + jnp.where(col_ix < width_cap - 1, pltpu.roll(over_rows(2), spots - 1, 1), 0.0)
    )
    latent = latent.astype(jnp.bfloat16).astype(jnp.float32)
    shifted = [latent] + [pltpu.roll(latent, spots - by, 1) for by in (1, width_cap, width_cap + 1)]
    patches = jnp.concatenate(shifted, axis=0).astype(jnp.bfloat16)

    tokens = NBS * BLOCK
    half_w = (width // 2).astype(jnp.float32)
    per_frame_int = (height // 2) * (width // 2)
    per_frame = per_frame_int.astype(jnp.float32)
    live = frames * per_frame_int
    token_int = lax.broadcasted_iota(jnp.int32, (1, tokens), 1)
    token = token_int.astype(jnp.float32)
    frame_of = jnp.floor((token + 0.5) / jnp.full((1, tokens), per_frame))
    within = token - frame_of * per_frame
    row_of = jnp.floor((within + 0.5) / jnp.full((1, tokens), half_w))
    col_of = within - row_of * half_w
    source = (frame_of * frame_size + row_of * (2 * width_cap) + col_of * 2).astype(jnp.int32)
    source = jnp.where(token_int < live, source, -1)
    chosen = lax.broadcasted_iota(jnp.int32, (spots, tokens), 0) == source
    picked = mm(patches, jnp.where(chosen, 1.0, 0.0).astype(jnp.bfloat16))
    kind = lax.broadcasted_iota(jnp.int32, (TOKEN_ROWS - feats, BLOCK), 0)
    pieces = []
    for b in range(NBS):
        count = jnp.clip(live - b * BLOCK, 0, BLOCK)
        info = jnp.where(
            kind == 0,
            plan_ref[0, 0, b, 0],
            jnp.where(kind == 1, plan_ref[0, 0, b, 1], jnp.where(kind == 2, count, 0)),
        )
        pieces += [picked[:, b * BLOCK : (b + 1) * BLOCK], info.astype(jnp.float32)]
    out_ref[...] = jnp.concatenate(pieces, axis=0).astype(jnp.bfloat16)


def gram_kernel(embed_ref, first_ref, out_ref):
    feats, width = embed_ref.shape
    emb = embed_ref[...].astype(jnp.float32)
    emb = emb - jnp.sum(emb, axis=1, keepdims=True) / width
    both = jnp.concatenate(split_bf16(emb), axis=0)
    gram = mm(both, both, ((1,), (1,))) / width
    gram = gram[:feats] + gram[feats:]
    out_ref[...] = jnp.concatenate(split_bf16(gram[:, :feats] + gram[:, feats:]), axis=0)


def pack_kernel(evens, feats, q_gain_ref, k_gain_ref, gram_ref, *refs):
    here, near = refs[: len(evens)], refs[len(evens)]
    x_t_ref, x_ref, key_mask_ref, gain_ref, *row_refs, rows_t = refs[len(evens) + 1 :]
    n_enc = 2 * len(evens)
    mine = lax.axis_index("enc")
    rows = n_enc * BLOCK
    lane = lax.broadcasted_iota(jnp.int32, (1, BLOCK), 1).astype(jnp.float32)
    extra = lax.broadcasted_iota(jnp.int32, (APAD - feats, BLOCK), 0)
    found = []
    blocks = [(at, here[i][...]) for i, at in enumerate(evens)]
    blocks += [(at ^ 1, near[1 + i]) for i, at in enumerate(evens)]
    for distance, block in blocks:
        source = mine ^ distance
        for b in range(NBS):
            tile = block.astype(jnp.float32)[b * TOKEN_ROWS : (b + 1) * TOKEN_ROWS]
            owner, offset, count = (tile[feats + i : feats + i + 1] for i in range(3))
            owner = jnp.where(offset == 0.0, owner, -1.0)
            segment = jnp.where(lane < count, (source + 1).astype(jnp.float32), 0.0)
            found.append((owner, segment, tile[:feats]))
    at = lax.broadcasted_iota(jnp.int32, (feats, feats), 0)
    frm = lax.broadcasted_iota(jnp.int32, (feats, feats), 1)
    order = jnp.where(frm == (at % 4) * (feats // 4) + at // 4, 1.0, 0.0).astype(jnp.bfloat16)
    for o in range(n_enc):
        segment = jnp.zeros((1, BLOCK), jnp.float32)
        body = jnp.zeros((feats, BLOCK), jnp.float32)
        for owner, seg_of, tile in found:
            hit = owner == float(o)
            segment = segment + jnp.where(hit, seg_of, 0.0)
            body = body + jnp.where(hit, tile, 0.0)
        tail = jnp.where(extra == 0, 1.0, jnp.where(extra == 1, segment, 0.0))
        rows_t[:, o * BLOCK : (o + 1) * BLOCK] = jnp.concatenate(
            [body, tail, jnp.zeros((LANES - APAD, BLOCK), jnp.float32)], axis=0
        )
    picked = mm(order, rows_t[:feats].astype(jnp.bfloat16))
    spread = mm(gram_ref[...], picked.astype(jnp.bfloat16))
    variance = jnp.sum((spread[:feats] + spread[feats:]) * picked, axis=0, keepdims=True)
    rows_t[:feats] = picked * lax.rsqrt(jnp.maximum(variance, 0.0) + eps_norm)
    x_t = rows_t[...]
    x_t_ref[...] = x_t[:APAD].astype(jnp.bfloat16)
    x_ref[...] = x_t.T.astype(jnp.bfloat16)
    group_t = lax.broadcasted_iota(jnp.int32, (LANES, rows), 0).astype(jnp.float32)
    key_mask_ref[...] = jnp.where(x_t[feats + 1 : feats + 2] == group_t, 0.0, 1.0).astype(jnp.bfloat16)
    group = lax.broadcasted_iota(jnp.int32, (BLOCK, LANES), 1).astype(jnp.float32)
    for core in range(2):
        rows_ref, mask_ref = row_refs[2 * core : 2 * core + 2]
        own = rows_t[:, pl.ds(pl.multiple_of((mine ^ core) * BLOCK, BLOCK), BLOCK)].T
        rows_ref[...] = own.astype(jnp.bfloat16)
        mask_ref[...] = jnp.where(own[:, feats + 1 : feats + 2] == group, -FAR, 0.0).astype(jnp.bfloat16)
    head_dim = q_gain_ref.shape[1]
    gain_ref[...] = q_gain_ref[...] * k_gain_ref[...] * (head_dim**-0.5 * math.log2(math.e))


def attend_heads(folds, place, x_t_ref, x_ref, key_mask_ref, gain_ref, own_ref, own_mask_ref):
    folds = list(folds)
    heads = range(len(folds))
    feats = (folds[0].shape[0] - TAIL) // 3
    tails = jnp.concatenate([fold[3 * feats :].astype(jnp.float32) for fold in folds], axis=1)
    row = lax.broadcasted_iota(jnp.int32, tails.shape, 0)

    def side(part):
        body = jnp.concatenate([fold[part * feats : (part + 1) * feats] for fold in folds], axis=1)
        shift = jnp.where(row == 0, tails[part : part + 1], 0.0).astype(jnp.bfloat16)
        return jnp.concatenate([body, shift], axis=0)

    def of(i):
        return slice(i * LANES, (i + 1) * LANES)

    keys = mm(side(1), x_t_ref[...], ((0,), (0,)))
    queries = mm(own_ref[:, :APAD], side(0))
    values = mm(x_ref[:, :APAD], side(2)).astype(jnp.bfloat16)
    gain, own_mask, key_mask = gain_ref[...], own_mask_ref[...], key_mask_ref[...]
    left, right = [], []
    for i in heads:
        key = keys[of(i)]
        square = jnp.sum(key * key, axis=0, keepdims=True) / LANES
        key = (key * lax.rsqrt(square + eps_norm)).astype(jnp.bfloat16)
        right.append(jnp.concatenate([key, key_mask], axis=0))
        query = queries[:, of(i)]
        square = jnp.sum(query * query, axis=1, keepdims=True) / LANES
        query = (query * lax.rsqrt(square + eps_norm) * gain).astype(jnp.bfloat16)
        left.append(jnp.concatenate([query, own_mask], axis=1))
    scores = [mm(left[i], right[i]) for i in heads]
    weights = [jnp.exp2(score).astype(jnp.bfloat16) for score in scores]
    ones = jnp.ones((values.shape[0], LANES), jnp.bfloat16)
    mixed = [mm(weights[i], jnp.concatenate([values[:, of(i)], ones], axis=1)) for i in heads]
    for i in heads:
        place(i, (mixed[i][:, :LANES] / mixed[i][:, LANES:]).astype(jnp.bfloat16))


def each_head(refs):
    for ref in refs:
        if len(ref.shape) == 2:
            yield ref[...]
        else:
            for i in range(ref.shape[0]):
                yield ref[i]


def attend_kernel(count, *refs):
    folds, out_ref = refs[6 : 6 + count], refs[-1]

    def place(i, result):
        out_ref[:, i * LANES : (i + 1) * LANES] = result

    attend_heads(each_head(folds), place, *refs[:6])


def output_kernel(heads, neighbours, lists, near_early_ref, near_rest_ref, own_early_ref, own_rest_ref, out_ref, sems):
    mine, slot = lax.axis_index("enc"), lax.axis_index("seq") & (heads - 1)
    copies = []

    def put(ref, at, base, far, k):
        head = (base ^ far) * heads + (slot ^ k)
        column = pl.ds(pl.multiple_of(head * LANES, LANES), LANES)
        result = ref.at[:, at * LANES : (at + 1) * LANES]
        copies.append(pltpu.make_async_copy(result, out_ref.at[0, :, column], sems.at[len(copies)]))
        copies[-1].start()

    for early, rest, base in (
        (near_early_ref, near_rest_ref, mine ^ 1),
        (own_early_ref, own_rest_ref, mine),
    ):
        for at, partner in enumerate(((0, 0), *neighbours)):
            put(early, at, base, *partner)
        for i, pair in enumerate(zip(*lists)):
            far, k = (jnp.where(base & 1 == 0, zero, one) for zero, one in zip(*pair))
            put(rest, 2 * i, base, far, k)
            put(rest, 2 * i + 1, base, far ^ 1, k)
    for copy in copies:
        copy.wait()


def vmem(count):
    return [pl.BlockSpec(memory_space=pltpu.VMEM)] * count


def hbm(count):
    return [pl.BlockSpec(memory_space=pltpu.HBM)] * count


def in_hbm(x):
    return pltpu.with_memory_space_constraint(x, pltpu.HBM)


def after(count):
    return [pl.BlockSpec(memory_space=pl.ANY)] * count


def call(kernel, ins, out_shape, scratch=(), cost=(1_000_000, 1_000_000)):
    return pl.pallas_call(
        kernel,
        in_specs=ins,
        out_specs=[pl.BlockSpec(memory_space=pltpu.VMEM)] * len(out_shape),
        out_shape=out_shape,
        scratch_shapes=list(scratch),
        compiler_params=pltpu.CompilerParams(vmem_limit_bytes=VMEM_LIMIT),
        cost_estimate=pl.CostEstimate(flops=cost[0], bytes_accessed=cost[1], transcendentals=0),
    )


def gate(x, *others):
    return pl.pallas_call(
        gate_kernel,
        in_specs=after(1 + len(others)),
        out_specs=after(1)[0],
        out_shape=jax.ShapeDtypeStruct(x.shape, x.dtype),
        input_output_aliases={0: 0},
        compiler_params=pltpu.CompilerParams(vmem_limit_bytes=VMEM_LIMIT),
    )(x, *others)


def exchange(x, axis, n, k):
    return lax.ppermute(x, axis, [(i, i ^ k) for i in range(n)])


def on_device(
    n_enc,
    n_seq,
    clip_features,
    clip_shape,
    packing,
    conv_weight,
    embed_weight,
    mod_shift,
    mod_scale,
    qkv_weight,
    q_gain,
    k_gain,
):
    caps = clip_features.shape[2:5]
    depth_all = clip_features.shape[5]
    cols = qkv_weight.shape[2]
    feats = embed_weight.shape[0]
    heads = cols // LANES
    rows = n_enc * BLOCK
    bf16, f32 = jnp.bfloat16, jnp.float32

    def folds(dtype, *lead):
        return jax.ShapeDtypeStruct((*lead, 3 * feats + TAIL, LANES), dtype)

    evens = [0]
    for bit in reversed(range(1, log2(n_enc))):
        evens += [at ^ (1 << bit) for at in evens]
    scale_rows, shift_rows = mod_scale.reshape(-1, LANES), mod_shift.reshape(-1, LANES)
    later = [
        clip_features.reshape(-1, depth_all),
        conv_weight.reshape(-1, depth_all),
        q_gain.reshape(1, -1),
        k_gain.reshape(1, -1),
    ]
    with jax.named_scope("fold"):
        embed, features, conv, q_gain, k_gain, keep, *sends = call(
            functools.partial(fold_kernel, len(later)),
            hbm(4 + len(later)),
            [jax.ShapeDtypeStruct(x.shape, x.dtype) for x in (embed_weight, *later)]
            + [folds(f32)]
            + [folds(bf16)] * max(heads - 1, 1),
            [
                pltpu.VMEM(scale_rows.shape, f32),
                pltpu.VMEM(shift_rows.shape, f32),
                pltpu.VMEM(qkv_weight.shape, bf16),
                pltpu.SemaphoreType.DMA((4 + len(later),)),
            ],
            cost=(200_000_000, 1_000_000),
        )(*map(in_hbm, (embed_weight, scale_rows, shift_rows, qkv_weight, *later)))

    with jax.named_scope("encode"):
        own_block = call(
            functools.partial(encode_kernel, caps),
            hbm(2) + vmem(2),
            [jax.ShapeDtypeStruct((NBS * TOKEN_ROWS, BLOCK), bf16)],
            [
                pltpu.SMEM(clip_shape.shape, jnp.int32),
                pltpu.SMEM(packing.shape, jnp.int32),
                pltpu.SemaphoreType.DMA((2,)),
            ],
            cost=(500_000_000, 2_000_000),
        )(in_hbm(clip_shape), in_hbm(packing), features, conv)[0]

    def add(keep, got, first):
        kernel = functools.partial(add_kernel, len(got))
        return call(kernel, vmem(1 + len(got)) + after(1), [folds(f32), folds(bf16)])(keep, *got, first)

    with jax.named_scope("fold_sum"):
        if heads > 1:
            got = [exchange(sends[k - 1], "seq", n_seq, k) for k in reversed(range(1, heads))]
            keep, send = add(keep, got, own_block)
        else:
            send = sends[0]

    with jax.named_scope("gram"):
        gram = call(gram_kernel, vmem(1) + after(1), [jax.ShapeDtypeStruct((2 * feats, feats), bf16)])(embed, keep)[0]

    with jax.named_scope("tokens"):
        own_block = gate(own_block, keep)
        blocks = [own_block] + [exchange(own_block, "enc", n_enc, k) for k in evens[1:]]

    with jax.named_scope("fold_sum"):
        for bit in range(log2(heads), log2(n_seq)):
            got = exchange(send, "seq", n_seq, 1 << bit)
            if bit + 1 < log2(n_seq):
                keep, send = add(keep, [got], own_block)
            else:
                fresh, swap = call(
                    functools.partial(last_add_kernel, len(blocks)),
                    vmem(2 + len(blocks)) + after(1),
                    [folds(bf16), folds(bf16, 1 + len(blocks))],
                )(keep, got, *blocks, gram)

    partners = [(far, k) for far in evens for k in range(heads) if far or k]
    partners.sort(key=lambda p: (p[0].bit_count() + p[1].bit_count(), p[0]))
    near_count = min(3, len(partners))
    half = (len(partners) - near_count) // 2
    assert len(partners) == near_count + 2 * half
    neighbours = tuple(partners[:near_count])
    lists = (tuple(reversed(partners[near_count : near_count + half])), tuple(partners[near_count + half :]))

    def spread(x, partner_of):
        pairs = []
        for e in range(n_enc):
            far, k = partner_of[e & 1]
            pairs += [(e * n_seq + i, (e ^ far) * n_seq + (i ^ k)) for i in range(n_seq)]
        return lax.ppermute(x, ("enc", "seq"), pairs)

    with jax.named_scope("gather"):
        singles = [spread(fresh, (partner, partner)) for partner in neighbours]
        swapped = exchange(swap, "enc", n_enc, 1)
        pair = call(pair_kernel, vmem(2), [folds(bf16, 2)])(fresh, swapped)[0]
        got = [spread(pair, partner_of) for partner_of in zip(*lists)]

    with jax.named_scope("pack"):
        *shared, own_rows, own_mask, far_rows, far_mask = call(
            functools.partial(pack_kernel, tuple(evens), feats),
            vmem(4 + len(evens)),
            [
                jax.ShapeDtypeStruct((APAD, rows), bf16),
                jax.ShapeDtypeStruct((rows, LANES), bf16),
                jax.ShapeDtypeStruct((LANES, rows), bf16),
                jax.ShapeDtypeStruct((1, LANES), f32),
            ]
            + [jax.ShapeDtypeStruct((BLOCK, LANES), bf16)] * 4,
            [pltpu.VMEM((LANES, rows), f32)],
        )(q_gain, k_gain, gram, *blocks, swapped)

    def attend(rows_here, groups, first=()):
        count = sum(group.size for group in groups) // ((3 * feats + TAIL) * LANES)
        return call(
            functools.partial(attend_kernel, len(groups)),
            vmem(6 + len(groups)) + after(len(first)),
            [jax.ShapeDtypeStruct((BLOCK, count * LANES), bf16)],
            cost=(count * 200_000_000, 1_000_000),
        )(*shared, *rows_here, *groups, *first)[0]

    with jax.named_scope("attend"):
        own, other = (own_rows, own_mask), (far_rows, far_mask)
        early, rest = [fresh, *singles], got
        early_other = attend(other, early)
        early_own = attend(own, early, [early_other])
        near_early = exchange(gate(early_other, early_own), "enc", n_enc, 1)
        near_rest = exchange(attend(other, rest, [early_own]), "enc", n_enc, 1)
        rest_own = attend(own, rest)
        return pl.pallas_call(
            functools.partial(output_kernel, heads, neighbours, lists),
            in_specs=vmem(4),
            out_specs=hbm(1)[0],
            out_shape=jax.ShapeDtypeStruct((1, BLOCK, n_enc * cols), bf16),
            scratch_shapes=[pltpu.SemaphoreType.DMA((n_enc * heads,))],
            compiler_params=pltpu.CompilerParams(vmem_limit_bytes=VMEM_LIMIT),
        )(near_early, near_rest, early_own, rest_own)


def solution(mesh):
    return jax.shard_map(
        functools.partial(on_device, mesh.shape["enc"], mesh.shape["seq"]),
        mesh=mesh,
        in_specs=(
            P("enc", "seq", None, None, None, None),
            P("enc", "seq", None),
            P("enc", "seq", None, None),
            P(),
            P(),
            P(),
            P(),
            P(None, "seq", "enc"),
            P(),
            P(),
        ),
        out_specs=P("seq", "enc", None),
        check_vma=False,
    )
```

```python
import functools
import math

import jax
import jax.numpy as jnp
from jax import lax
from jax.experimental import pallas as pl
from jax.experimental.pallas import tpu as pltpu
from jax.sharding import PartitionSpec as P

BLOCK = 128
NBS = 2
LANES = 128
APAD = 72
TAIL = 8
TOKEN_ROWS = 80
eps_norm = 1e-06
FAR = 2.0**20
VMEM_LIMIT = 48 * 1024 * 1024


def mm(a, b, dims=((1,), (0,)), precision=None):
    return lax.dot_general(a, b, (dims, ((), ())), preferred_element_type=jnp.float32, precision=precision)


def split_bf16(x):
    hi = x.astype(jnp.bfloat16)
    return hi, (x - hi.astype(jnp.float32)).astype(jnp.bfloat16)


def log2(n):
    bits = n.bit_length() - 1
    assert 1 << bits == n
    return bits


def fetch(pairs, sems):
    copies = [pltpu.make_async_copy(src, dst, sems.at[i]) for i, (src, dst) in enumerate(pairs)]
    for copy in copies:
        copy.start()
    return copies


def fold_kernel(count, embed_hbm, scale_hbm, shift_hbm, w_hbm, *refs):
    later_hbm, embed_ref, later, keep_ref, sends = refs[:count], refs[count], refs[count + 1 : 2 * count + 1], refs[2 * count + 1], refs[2 * count + 2 : -4]
    scale_ref, shift_ref, w_ref, sems = refs[-4:]
    copies = fetch(
        [(embed_hbm, embed_ref), (scale_hbm, scale_ref), (shift_hbm, shift_ref), (w_hbm, w_ref)]
        + list(zip(later_hbm, later)),
        sems,
    )
    me = lax.axis_index("seq")
    _, depth, cols = w_ref.shape
    feats = embed_ref.shape[0]
    heads = cols // LANES
    for copy in copies[:3]:
        copy.wait()
    mean = jnp.sum(embed_ref[...].astype(jnp.float32), axis=1, keepdims=True) / embed_ref.shape[1]
    span = max(depth, LANES)
    chunks = span // LANES
    first = (me * depth) // LANES
    emb = embed_ref[:, pl.ds(pl.multiple_of(first * LANES, LANES), span)].astype(jnp.float32) - mean
    scale = jnp.concatenate([scale_ref[pl.ds(first + i, 1), :] for i in range(chunks)], axis=1)
    shift = jnp.concatenate([shift_ref[pl.ds(first + i, 1), :] for i in range(chunks)], axis=1)
    left = jnp.concatenate(
        [emb * (1.0 + scale), shift, jnp.zeros((APAD - feats - 1, span), jnp.float32)], axis=0
    )
    if depth < LANES:
        low = me * depth - first * LANES
        lane = lax.broadcasted_iota(jnp.int32, left.shape, 1)
        left = jnp.where((lane >= low) & (lane < low + depth), left, 0.0)
    hi, lo = split_bf16(left)
    both = jnp.concatenate([hi, lo], axis=0)
    copies[3].wait()

    def product(head):
        start = pl.multiple_of(head * LANES, LANES)
        right = jnp.concatenate([w_ref[part, :, pl.ds(start, LANES)] for part in range(3)], axis=1)
        right = jnp.concatenate([right] * (span // depth), axis=0)
        total = mm(both, right)
        total = total[:APAD] + total[APAD:]
        parts = [total[:, part * LANES : (part + 1) * LANES] for part in range(3)]
        row = lax.broadcasted_iota(jnp.int32, (TAIL, LANES), 0)
        tail = jnp.zeros((TAIL, LANES), jnp.float32)
        for part in range(3):
            tail = jnp.where(row == part, parts[part][feats : feats + 1], tail)
        return jnp.concatenate([part[:feats] for part in parts] + [tail], axis=0)

    slot = me & (heads - 1)
    for k in range(1, heads):
        sends[k - 1][...] = product(slot ^ k).astype(jnp.bfloat16)
    total = product(slot)
    keep_ref[...] = total
    if heads == 1:
        sends[0][...] = total.astype(jnp.bfloat16)
    for copy in copies[4:]:
        copy.wait()


def add_kernel(count, keep_in, *refs):
    total = keep_in[...]
    for ref in refs[:count]:
        total = total + ref[...].astype(jnp.float32)
    refs[-2][...] = total
    refs[-1][...] = total.astype(jnp.bfloat16)


def last_add_kernel(count, keep_in, got_ref, *refs):
    total = (keep_in[...] + got_ref[...].astype(jnp.float32)).astype(jnp.bfloat16)
    out_ref, swap_ref = refs[-2:]
    out_ref[...] = total
    swap_ref[0] = total
    for i in range(count):
        block = refs[i][...]
        rest = jnp.zeros((total.shape[0] - block.shape[0], LANES), jnp.bfloat16)
        swap_ref[1 + i] = jnp.concatenate([block, rest], axis=0)


def pair_kernel(own_ref, swapped_ref, out_ref):
    out_ref[0] = own_ref[...]
    out_ref[1] = swapped_ref[0]


def gate_kernel(*refs):
    pass


def encode_kernel(caps, shape_hbm, plan_hbm, feat_ref, conv_ref, out_ref, shape_ref, plan_ref, sems):
    copies = fetch([(shape_hbm, shape_ref), (plan_hbm, plan_ref)], sems)
    frames_cap, height_cap, width_cap = caps
    spots = frames_cap * height_cap * width_cap
    frame_size = height_cap * width_cap
    latent_ch = conv_ref.shape[0] // 27
    feats = 4 * latent_ch
    taps = mm(conv_ref[...], feat_ref[...], ((1,), (1,)))
    copies[0].wait()
    copies[1].wait()
    frames, height, width = shape_ref[0, 0, 0], shape_ref[0, 0, 1], shape_ref[0, 0, 2]
    spot = lax.broadcasted_iota(jnp.int32, (1, spots), 1)
    frame_ix = spot // frame_size
    row_ix = (spot % frame_size) // width_cap
    col_ix = spot % width_cap
    inside = (frame_ix < frames) & (row_ix < height) & (col_ix < width)
    taps = jnp.where(inside, taps, 0.0)

    def tap(a, b, j):
        at = (9 * a + 3 * b + j) * latent_ch
        return taps[at : at + latent_ch]

    def later(x, by):
        zeros = jnp.zeros((latent_ch, by * frame_size), jnp.float32)
        return jnp.concatenate([zeros, x[:, : spots - by * frame_size]], axis=1)

    def over_frames(b, j):
        return tap(2, b, j) + later(tap(1, b, j), 1) + later(tap(0, b, j), 2)

    def over_rows(j):
        above = pltpu.roll(over_frames(0, j), width_cap, 1)
        below = pltpu.roll(over_frames(2, j), spots - width_cap, 1)
        return (
            over_frames(1, j)
            + jnp.where(row_ix >= 1, above, 0.0)
            + jnp.where(row_ix < height_cap - 1, below, 0.0)
        )

    latent = (
        over_rows(1)
        + jnp.where(col_ix >= 1, pltpu.roll(over_rows(0), 1, 1), 0.0)
        + jnp.where(col_ix < width_cap - 1, pltpu.roll(over_rows(2), spots - 1, 1), 0.0)
    )
    latent = latent.astype(jnp.bfloat16).astype(jnp.float32)
    shifted = [latent] + [pltpu.roll(latent, spots - by, 1) for by in (1, width_cap, width_cap + 1)]
    patches = jnp.concatenate(shifted, axis=0).astype(jnp.bfloat16)

    tokens = NBS * BLOCK
    half_w = (width // 2).astype(jnp.float32)
    per_frame_int = (height // 2) * (width // 2)
    per_frame = per_frame_int.astype(jnp.float32)
    live = frames * per_frame_int
    token_int = lax.broadcasted_iota(jnp.int32, (1, tokens), 1)
    token = token_int.astype(jnp.float32)
    frame_of = jnp.floor((token + 0.5) / jnp.full((1, tokens), per_frame))
    within = token - frame_of * per_frame
    row_of = jnp.floor((within + 0.5) / jnp.full((1, tokens), half_w))
    col_of = within - row_of * half_w
    source = (frame_of * frame_size + row_of * (2 * width_cap) + col_of * 2).astype(jnp.int32)
    source = jnp.where(token_int < live, source, -1)
    chosen = lax.broadcasted_iota(jnp.int32, (spots, tokens), 0) == source
    picked = mm(patches, jnp.where(chosen, 1.0, 0.0).astype(jnp.bfloat16))
    kind = lax.broadcasted_iota(jnp.int32, (TOKEN_ROWS - feats, BLOCK), 0)
    pieces = []
    for b in range(NBS):
        count = jnp.clip(live - b * BLOCK, 0, BLOCK)
        info = jnp.where(
            kind == 0,
            plan_ref[0, 0, b, 0],
            jnp.where(kind == 1, plan_ref[0, 0, b, 1], jnp.where(kind == 2, count, 0)),
        )
        pieces += [picked[:, b * BLOCK : (b + 1) * BLOCK], info.astype(jnp.float32)]
    out_ref[...] = jnp.concatenate(pieces, axis=0).astype(jnp.bfloat16)


def gram_kernel(embed_ref, first_ref, out_ref):
    feats, width = embed_ref.shape
    emb = embed_ref[...].astype(jnp.float32)
    emb = emb - jnp.sum(emb, axis=1, keepdims=True) / width
    both = jnp.concatenate(split_bf16(emb), axis=0)
    gram = mm(both, both, ((1,), (1,))) / width
    gram = gram[:feats] + gram[feats:]
    out_ref[...] = jnp.concatenate(split_bf16(gram[:, :feats] + gram[:, feats:]), axis=0)


def pack_kernel(evens, feats, q_gain_ref, k_gain_ref, gram_ref, *refs):
    here, near = refs[: len(evens)], refs[len(evens)]
    x_t_ref, x_ref, key_mask_ref, gain_ref, *row_refs, rows_t = refs[len(evens) + 1 :]
    n_enc = 2 * len(evens)
    mine = lax.axis_index("enc")
    rows = n_enc * BLOCK
    lane = lax.broadcasted_iota(jnp.int32, (1, BLOCK), 1).astype(jnp.float32)
    extra = lax.broadcasted_iota(jnp.int32, (APAD - feats, BLOCK), 0)
    found = []
    blocks = [(at, here[i][...]) for i, at in enumerate(evens)]
    blocks += [(at ^ 1, near[1 + i]) for i, at in enumerate(evens)]
    for distance, block in blocks:
        source = mine ^ distance
        for b in range(NBS):
            tile = block.astype(jnp.float32)[b * TOKEN_ROWS : (b + 1) * TOKEN_ROWS]
            owner, offset, count = (tile[feats + i : feats + i + 1] for i in range(3))
            owner = jnp.where(offset == 0.0, owner, -1.0)
            segment = jnp.where(lane < count, (source + 1).astype(jnp.float32), 0.0)
            found.append((owner, segment, tile[:feats]))
    at = lax.broadcasted_iota(jnp.int32, (feats, feats), 0)
    frm = lax.broadcasted_iota(jnp.int32, (feats, feats), 1)
    order = jnp.where(frm == (at % 4) * (feats // 4) + at // 4, 1.0, 0.0).astype(jnp.bfloat16)
    for o in range(n_enc):
        segment = jnp.zeros((1, BLOCK), jnp.float32)
        body = jnp.zeros((feats, BLOCK), jnp.float32)
        for owner, seg_of, tile in found:
            hit = owner == float(o)
            segment = segment + jnp.where(hit, seg_of, 0.0)
            body = body + jnp.where(hit, tile, 0.0)
        tail = jnp.where(extra == 0, 1.0, jnp.where(extra == 1, segment, 0.0))
        rows_t[:, o * BLOCK : (o + 1) * BLOCK] = jnp.concatenate(
            [body, tail, jnp.zeros((LANES - APAD, BLOCK), jnp.float32)], axis=0
        )
    picked = mm(order, rows_t[:feats].astype(jnp.bfloat16))
    spread = mm(gram_ref[...], picked.astype(jnp.bfloat16))
    variance = jnp.sum((spread[:feats] + spread[feats:]) * picked, axis=0, keepdims=True)
    rows_t[:feats] = picked * lax.rsqrt(jnp.maximum(variance, 0.0) + eps_norm)
    x_t = rows_t[...]
    x_t_ref[...] = x_t[:APAD].astype(jnp.bfloat16)
    x_ref[...] = x_t.T.astype(jnp.bfloat16)
    group_t = lax.broadcasted_iota(jnp.int32, (LANES, rows), 0).astype(jnp.float32)
    key_mask_ref[...] = jnp.where(x_t[feats + 1 : feats + 2] == group_t, 0.0, 1.0).astype(jnp.bfloat16)
    group = lax.broadcasted_iota(jnp.int32, (BLOCK, LANES), 1).astype(jnp.float32)
    for core in range(2):
        rows_ref, mask_ref = row_refs[2 * core : 2 * core + 2]
        own = rows_t[:, pl.ds(pl.multiple_of((mine ^ core) * BLOCK, BLOCK), BLOCK)].T
        rows_ref[...] = own.astype(jnp.bfloat16)
        mask_ref[...] = jnp.where(own[:, feats + 1 : feats + 2] == group, -FAR, 0.0).astype(jnp.bfloat16)
    head_dim = q_gain_ref.shape[1]
    gain_ref[...] = q_gain_ref[...] * k_gain_ref[...] * (head_dim**-0.5 * math.log2(math.e))


def attend_heads(folds, place, x_t_ref, x_ref, key_mask_ref, gain_ref, own_ref, own_mask_ref):
    folds = list(folds)
    heads = range(len(folds))
    feats = (folds[0].shape[0] - TAIL) // 3
    tails = jnp.concatenate([fold[3 * feats :].astype(jnp.float32) for fold in folds], axis=1)
    row = lax.broadcasted_iota(jnp.int32, tails.shape, 0)

    def side(part):
        body = jnp.concatenate([fold[part * feats : (part + 1) * feats] for fold in folds], axis=1)
        shift = jnp.where(row == 0, tails[part : part + 1], 0.0).astype(jnp.bfloat16)
        return jnp.concatenate([body, shift], axis=0)

    def of(i):
        return slice(i * LANES, (i + 1) * LANES)

    keys = mm(side(1), x_t_ref[...], ((0,), (0,)))
    queries = mm(own_ref[:, :APAD], side(0))
    values = mm(x_ref[:, :APAD], side(2)).astype(jnp.bfloat16)
    gain, own_mask, key_mask = gain_ref[...], own_mask_ref[...], key_mask_ref[...]
    left, right = [], []
    for i in heads:
        key = keys[of(i)]
        square = jnp.sum(key * key, axis=0, keepdims=True) / LANES
        key = (key * lax.rsqrt(square + eps_norm)).astype(jnp.bfloat16)
        right.append(jnp.concatenate([key, key_mask], axis=0))
        query = queries[:, of(i)]
        square = jnp.sum(query * query, axis=1, keepdims=True) / LANES
        query = (query * lax.rsqrt(square + eps_norm) * gain).astype(jnp.bfloat16)
        left.append(jnp.concatenate([query, own_mask], axis=1))
    scores = [mm(left[i], right[i]) for i in heads]
    weights = [jnp.exp2(score).astype(jnp.bfloat16) for score in scores]
    ones = jnp.ones((values.shape[0], LANES), jnp.bfloat16)
    mixed = [mm(weights[i], jnp.concatenate([values[:, of(i)], ones], axis=1)) for i in heads]
    for i in heads:
        place(i, (mixed[i][:, :LANES] / mixed[i][:, LANES:]).astype(jnp.bfloat16))


def each_head(refs):
    for ref in refs:
        if len(ref.shape) == 2:
            yield ref[...]
        else:
            for i in range(ref.shape[0]):
                yield ref[i]


def attend_kernel(count, *refs):
    folds, out_ref = refs[6 : 6 + count], refs[-1]

    def place(i, result):
        out_ref[:, i * LANES : (i + 1) * LANES] = result

    attend_heads(each_head(folds), place, *refs[:6])


def output_kernel(heads, neighbours, lists, near_early_ref, near_rest_ref, own_early_ref, own_rest_ref, out_ref, sems):
    mine, slot = lax.axis_index("enc"), lax.axis_index("seq") & (heads - 1)
    copies = []

    def put(ref, at, base, far, k):
        head = (base ^ far) * heads + (slot ^ k)
        column = pl.ds(pl.multiple_of(head * LANES, LANES), LANES)
        result = ref.at[:, at * LANES : (at + 1) * LANES]
        copies.append(pltpu.make_async_copy(result, out_ref.at[0, :, column], sems.at[len(copies)]))
        copies[-1].start()

    for early, rest, base in (
        (near_early_ref, near_rest_ref, mine ^ 1),
        (own_early_ref, own_rest_ref, mine),
    ):
        for at, partner in enumerate(((0, 0), *neighbours)):
            put(early, at, base, *partner)
        for i, pair in enumerate(zip(*lists)):
            far, k = (jnp.where(base & 1 == 0, zero, one) for zero, one in zip(*pair))
            put(rest, 2 * i, base, far, k)
            put(rest, 2 * i + 1, base, far ^ 1, k)
    for copy in copies:
        copy.wait()


def vmem(count):
    return [pl.BlockSpec(memory_space=pltpu.VMEM)] * count


def hbm(count):
    return [pl.BlockSpec(memory_space=pltpu.HBM)] * count


def in_hbm(x):
    return pltpu.with_memory_space_constraint(x, pltpu.HBM)


def after(count):
    return [pl.BlockSpec(memory_space=pl.ANY)] * count


def call(kernel, ins, out_shape, scratch=(), cost=(1_000_000, 1_000_000)):
    return pl.pallas_call(
        kernel,
        in_specs=ins,
        out_specs=[pl.BlockSpec(memory_space=pltpu.VMEM)] * len(out_shape),
        out_shape=out_shape,
        scratch_shapes=list(scratch),
        compiler_params=pltpu.CompilerParams(vmem_limit_bytes=VMEM_LIMIT),
        cost_estimate=pl.CostEstimate(flops=cost[0], bytes_accessed=cost[1], transcendentals=0),
    )


def gate(x, *others):
    return pl.pallas_call(
        gate_kernel,
        in_specs=after(1 + len(others)),
        out_specs=after(1)[0],
        out_shape=jax.ShapeDtypeStruct(x.shape, x.dtype),
        input_output_aliases={0: 0},
        compiler_params=pltpu.CompilerParams(vmem_limit_bytes=VMEM_LIMIT),
    )(x, *others)


def exchange(x, axis, n, k):
    return lax.ppermute(x, axis, [(i, i ^ k) for i in range(n)])


def on_device(
    n_enc,
    n_seq,
    clip_features,
    clip_shape,
    packing,
    conv_weight,
    embed_weight,
    mod_shift,
    mod_scale,
    qkv_weight,
    q_gain,
    k_gain,
):
    caps = clip_features.shape[2:5]
    depth_all = clip_features.shape[5]
    cols = qkv_weight.shape[2]
    feats = embed_weight.shape[0]
    heads = cols // LANES
    rows = n_enc * BLOCK
    bf16, f32 = jnp.bfloat16, jnp.float32

    def folds(dtype, *lead):
        return jax.ShapeDtypeStruct((*lead, 3 * feats + TAIL, LANES), dtype)

    evens = [0]
    for bit in reversed(range(1, log2(n_enc))):
        evens += [at ^ (1 << bit) for at in evens]
    scale_rows, shift_rows = mod_scale.reshape(-1, LANES), mod_shift.reshape(-1, LANES)
    later = [
        clip_features.reshape(-1, depth_all),
        conv_weight.reshape(-1, depth_all),
        q_gain.reshape(1, -1),
        k_gain.reshape(1, -1),
    ]
    with jax.named_scope("fold"):
        embed, features, conv, q_gain, k_gain, keep, *sends = call(
            functools.partial(fold_kernel, len(later)),
            hbm(4 + len(later)),
            [jax.ShapeDtypeStruct(x.shape, x.dtype) for x in (embed_weight, *later)]
            + [folds(f32)]
            + [folds(bf16)] * max(heads - 1, 1),
            [
                pltpu.VMEM(scale_rows.shape, f32),
                pltpu.VMEM(shift_rows.shape, f32),
                pltpu.VMEM(qkv_weight.shape, bf16),
                pltpu.SemaphoreType.DMA((4 + len(later),)),
            ],
            cost=(200_000_000, 1_000_000),
        )(*map(in_hbm, (embed_weight, scale_rows, shift_rows, qkv_weight, *later)))

    with jax.named_scope("encode"):
        own_block = call(
            functools.partial(encode_kernel, caps),
            hbm(2) + vmem(2),
            [jax.ShapeDtypeStruct((NBS * TOKEN_ROWS, BLOCK), bf16)],
            [
                pltpu.SMEM(clip_shape.shape, jnp.int32),
                pltpu.SMEM(packing.shape, jnp.int32),
                pltpu.SemaphoreType.DMA((2,)),
            ],
            cost=(500_000_000, 2_000_000),
        )(in_hbm(clip_shape), in_hbm(packing), features, conv)[0]

    def add(keep, got, first):
        kernel = functools.partial(add_kernel, len(got))
        return call(kernel, vmem(1 + len(got)) + after(1), [folds(f32), folds(bf16)])(keep, *got, first)

    with jax.named_scope("fold_sum"):
        if heads > 1:
            got = [exchange(sends[k - 1], "seq", n_seq, k) for k in reversed(range(1, heads))]
            keep, send = add(keep, got, own_block)
        else:
            send = sends[0]

    with jax.named_scope("gram"):
        gram = call(gram_kernel, vmem(1) + after(1), [jax.ShapeDtypeStruct((2 * feats, feats), bf16)])(embed, keep)[0]

    with jax.named_scope("tokens"):
        own_block = gate(own_block, keep)
        blocks = [own_block] + [exchange(own_block, "enc", n_enc, k) for k in evens[1:]]

    with jax.named_scope("fold_sum"):
        for bit in range(log2(heads), log2(n_seq)):
            got = exchange(send, "seq", n_seq, 1 << bit)
            if bit + 1 < log2(n_seq):
                keep, send = add(keep, [got], own_block)
            else:
                fresh, swap = call(
                    functools.partial(last_add_kernel, len(blocks)),
                    vmem(2 + len(blocks)) + after(1),
                    [folds(bf16), folds(bf16, 1 + len(blocks))],
                )(keep, got, *blocks, gram)

    partners = [(far, k) for far in evens for k in range(heads) if far or k]
    partners.sort(key=lambda p: (p[0].bit_count() + p[1].bit_count(), p[0]))
    near_count = min(3, len(partners))
    half = (len(partners) - near_count) // 2
    assert len(partners) == near_count + 2 * half
    neighbours = tuple(partners[:near_count])
    lists = (tuple(partners[near_count : near_count + half]), tuple(reversed(partners[near_count + half :])))

    def spread(x, partner_of):
        pairs = []
        for e in range(n_enc):
            far, k = partner_of[e & 1]
            pairs += [(e * n_seq + i, (e ^ far) * n_seq + (i ^ k)) for i in range(n_seq)]
        return lax.ppermute(x, ("enc", "seq"), pairs)

    with jax.named_scope("gather"):
        singles = [spread(fresh, (partner, partner)) for partner in neighbours]
        swapped = exchange(swap, "enc", n_enc, 1)
        pair = call(pair_kernel, vmem(2), [folds(bf16, 2)])(fresh, swapped)[0]
        got = [spread(pair, partner_of) for partner_of in zip(*lists)]

    with jax.named_scope("pack"):
        *shared, own_rows, own_mask, far_rows, far_mask = call(
            functools.partial(pack_kernel, tuple(evens), feats),
            vmem(4 + len(evens)),
            [
                jax.ShapeDtypeStruct((APAD, rows), bf16),
                jax.ShapeDtypeStruct((rows, LANES), bf16),
                jax.ShapeDtypeStruct((LANES, rows), bf16),
                jax.ShapeDtypeStruct((1, LANES), f32),
            ]
            + [jax.ShapeDtypeStruct((BLOCK, LANES), bf16)] * 4,
            [pltpu.VMEM((LANES, rows), f32)],
        )(q_gain, k_gain, gram, *blocks, swapped)

    def attend(rows_here, groups, first=()):
        count = sum(group.size for group in groups) // ((3 * feats + TAIL) * LANES)
        return call(
            functools.partial(attend_kernel, len(groups)),
            vmem(6 + len(groups)) + after(len(first)),
            [jax.ShapeDtypeStruct((BLOCK, count * LANES), bf16)],
            cost=(count * 200_000_000, 1_000_000),
        )(*shared, *rows_here, *groups, *first)[0]

    with jax.named_scope("attend"):
        own, other = (own_rows, own_mask), (far_rows, far_mask)
        early, rest = [fresh, *singles], got
        early_other = attend(other, early)
        early_own = attend(own, early, [early_other])
        near_early = exchange(gate(early_other, early_own), "enc", n_enc, 1)
        near_rest = exchange(attend(other, rest, [early_own]), "enc", n_enc, 1)
        rest_own = attend(own, rest)
        return pl.pallas_call(
            functools.partial(output_kernel, heads, neighbours, lists),
            in_specs=vmem(4),
            out_specs=hbm(1)[0],
            out_shape=jax.ShapeDtypeStruct((1, BLOCK, n_enc * cols), bf16),
            scratch_shapes=[pltpu.SemaphoreType.DMA((n_enc * heads,))],
            compiler_params=pltpu.CompilerParams(vmem_limit_bytes=VMEM_LIMIT),
        )(near_early, near_rest, early_own, rest_own)


def solution(mesh):
    return jax.shard_map(
        functools.partial(on_device, mesh.shape["enc"], mesh.shape["seq"]),
        mesh=mesh,
        in_specs=(
            P("enc", "seq", None, None, None, None),
            P("enc", "seq", None),
            P("enc", "seq", None, None),
            P(),
            P(),
            P(),
            P(),
            P(None, "seq", "enc"),
            P(),
            P(),
        ),
        out_specs=P("seq", "enc", None),
        check_vma=False,
    )
```

```python
import functools
import math

import jax
import jax.numpy as jnp
from jax import lax
from jax.experimental import pallas as pl
from jax.experimental.pallas import tpu as pltpu
from jax.sharding import PartitionSpec as P

BLOCK = 128
NBS = 2
LANES = 128
APAD = 72
TAIL = 8
TOKEN_ROWS = 80
TOKEN_MESSAGE = 208
eps_norm = 1e-06
FAR = 2.0**20
VMEM_LIMIT = 48 * 1024 * 1024


def mm(a, b, dims=((1,), (0,)), precision=None):
    return lax.dot_general(a, b, (dims, ((), ())), preferred_element_type=jnp.float32, precision=precision)


def split_bf16(x):
    hi = x.astype(jnp.bfloat16)
    return hi, (x - hi.astype(jnp.float32)).astype(jnp.bfloat16)


def log2(n):
    bits = n.bit_length() - 1
    assert 1 << bits == n
    return bits


def fetch(pairs, sems):
    copies = [pltpu.make_async_copy(src, dst, sems.at[i]) for i, (src, dst) in enumerate(pairs)]
    for copy in copies:
        copy.start()
    return copies


def fold_kernel(count, embed_hbm, scale_hbm, shift_hbm, w_hbm, *refs):
    later_hbm, embed_ref, later, keep_ref, sends = refs[:count], refs[count], refs[count + 1 : 2 * count + 1], refs[2 * count + 1], refs[2 * count + 2 : -4]
    scale_ref, shift_ref, w_ref, sems = refs[-4:]
    copies = fetch(
        [(embed_hbm, embed_ref), (scale_hbm, scale_ref), (shift_hbm, shift_ref), (w_hbm, w_ref)]
        + list(zip(later_hbm, later)),
        sems,
    )
    me = lax.axis_index("seq")
    _, depth, cols = w_ref.shape
    feats = embed_ref.shape[0]
    heads = cols // LANES
    for copy in copies[:3]:
        copy.wait()
    mean = jnp.sum(embed_ref[...].astype(jnp.float32), axis=1, keepdims=True) / embed_ref.shape[1]
    span = max(depth, LANES)
    chunks = span // LANES
    first = (me * depth) // LANES
    emb = embed_ref[:, pl.ds(pl.multiple_of(first * LANES, LANES), span)].astype(jnp.float32) - mean
    scale = jnp.concatenate([scale_ref[pl.ds(first + i, 1), :] for i in range(chunks)], axis=1)
    shift = jnp.concatenate([shift_ref[pl.ds(first + i, 1), :] for i in range(chunks)], axis=1)
    left = jnp.concatenate(
        [emb * (1.0 + scale), shift, jnp.zeros((APAD - feats - 1, span), jnp.float32)], axis=0
    )
    if depth < LANES:
        low = me * depth - first * LANES
        lane = lax.broadcasted_iota(jnp.int32, left.shape, 1)
        left = jnp.where((lane >= low) & (lane < low + depth), left, 0.0)
    hi, lo = split_bf16(left)
    both = jnp.concatenate([hi, lo], axis=0)
    copies[3].wait()

    def product(head):
        start = pl.multiple_of(head * LANES, LANES)
        right = jnp.concatenate([w_ref[part, :, pl.ds(start, LANES)] for part in range(3)], axis=1)
        right = jnp.concatenate([right] * (span // depth), axis=0)
        total = mm(both, right)
        total = total[:APAD] + total[APAD:]
        parts = [total[:, part * LANES : (part + 1) * LANES] for part in range(3)]
        row = lax.broadcasted_iota(jnp.int32, (TAIL, LANES), 0)
        tail = jnp.zeros((TAIL, LANES), jnp.float32)
        for part in range(3):
            tail = jnp.where(row == part, parts[part][feats : feats + 1], tail)
        return jnp.concatenate([part[:feats] for part in parts] + [tail], axis=0)

    slot = me & (heads - 1)
    for k in range(1, heads):
        sends[k - 1][...] = product(slot ^ k).astype(jnp.bfloat16)
    total = product(slot)
    keep_ref[...] = total
    if heads == 1:
        sends[0][...] = total.astype(jnp.bfloat16)
    for copy in copies[4:]:
        copy.wait()


def add_kernel(count, keep_in, *refs):
    total = keep_in[...]
    for ref in refs[:count]:
        total = total + ref[...].astype(jnp.float32)
    refs[-2][...] = total
    refs[-1][...] = total.astype(jnp.bfloat16)


def last_add_kernel(count, keep_in, got_ref, *refs):
    total = (keep_in[...] + got_ref[...].astype(jnp.float32)).astype(jnp.bfloat16)
    out_ref, swap_ref = refs[-2:]
    out_ref[...] = total
    swap_ref[0] = total
    for i in range(count):
        block = refs[i][...][: NBS * TOKEN_ROWS]
        rest = jnp.zeros((total.shape[0] - block.shape[0], LANES), jnp.bfloat16)
        swap_ref[1 + i] = jnp.concatenate([block, rest], axis=0)


def pair_kernel(own_ref, swapped_ref, out_ref):
    out_ref[0] = own_ref[...]
    out_ref[1] = swapped_ref[0]


def gate_kernel(*refs):
    pass


def encode_kernel(caps, shape_hbm, plan_hbm, feat_ref, conv_ref, out_ref, shape_ref, plan_ref, sems):
    copies = fetch([(shape_hbm, shape_ref), (plan_hbm, plan_ref)], sems)
    frames_cap, height_cap, width_cap = caps
    spots = frames_cap * height_cap * width_cap
    frame_size = height_cap * width_cap
    latent_ch = conv_ref.shape[0] // 27
    feats = 4 * latent_ch
    taps = mm(conv_ref[...], feat_ref[...], ((1,), (1,)))
    copies[0].wait()
    copies[1].wait()
    frames, height, width = shape_ref[0, 0, 0], shape_ref[0, 0, 1], shape_ref[0, 0, 2]
    spot = lax.broadcasted_iota(jnp.int32, (1, spots), 1)
    frame_ix = spot // frame_size
    row_ix = (spot % frame_size) // width_cap
    col_ix = spot % width_cap
    inside = (frame_ix < frames) & (row_ix < height) & (col_ix < width)
    taps = jnp.where(inside, taps, 0.0)

    def tap(a, b, j):
        at = (9 * a + 3 * b + j) * latent_ch
        return taps[at : at + latent_ch]

    def later(x, by):
        zeros = jnp.zeros((latent_ch, by * frame_size), jnp.float32)
        return jnp.concatenate([zeros, x[:, : spots - by * frame_size]], axis=1)

    def over_frames(b, j):
        return tap(2, b, j) + later(tap(1, b, j), 1) + later(tap(0, b, j), 2)

    def over_rows(j):
        above = pltpu.roll(over_frames(0, j), width_cap, 1)
        below = pltpu.roll(over_frames(2, j), spots - width_cap, 1)
        return (
            over_frames(1, j)
            + jnp.where(row_ix >= 1, above, 0.0)
            + jnp.where(row_ix < height_cap - 1, below, 0.0)
        )

    latent = (
        over_rows(1)
        + jnp.where(col_ix >= 1, pltpu.roll(over_rows(0), 1, 1), 0.0)
        + jnp.where(col_ix < width_cap - 1, pltpu.roll(over_rows(2), spots - 1, 1), 0.0)
    )
    latent = latent.astype(jnp.bfloat16).astype(jnp.float32)
    shifted = [latent] + [pltpu.roll(latent, spots - by, 1) for by in (1, width_cap, width_cap + 1)]
    patches = jnp.concatenate(shifted, axis=0).astype(jnp.bfloat16)

    tokens = NBS * BLOCK
    half_w = (width // 2).astype(jnp.float32)
    per_frame_int = (height // 2) * (width // 2)
    per_frame = per_frame_int.astype(jnp.float32)
    live = frames * per_frame_int
    token_int = lax.broadcasted_iota(jnp.int32, (1, tokens), 1)
    token = token_int.astype(jnp.float32)
    frame_of = jnp.floor((token + 0.5) / jnp.full((1, tokens), per_frame))
    within = token - frame_of * per_frame
    row_of = jnp.floor((within + 0.5) / jnp.full((1, tokens), half_w))
    col_of = within - row_of * half_w
    source = (frame_of * frame_size + row_of * (2 * width_cap) + col_of * 2).astype(jnp.int32)
    source = jnp.where(token_int < live, source, -1)
    chosen = lax.broadcasted_iota(jnp.int32, (spots, tokens), 0) == source
    picked = mm(patches, jnp.where(chosen, 1.0, 0.0).astype(jnp.bfloat16))
    kind = lax.broadcasted_iota(jnp.int32, (TOKEN_ROWS - feats, BLOCK), 0)
    pieces = []
    for b in range(NBS):
        count = jnp.clip(live - b * BLOCK, 0, BLOCK)
        info = jnp.where(
            kind == 0,
            plan_ref[0, 0, b, 0],
            jnp.where(kind == 1, plan_ref[0, 0, b, 1], jnp.where(kind == 2, count, 0)),
        )
        pieces += [picked[:, b * BLOCK : (b + 1) * BLOCK], info.astype(jnp.float32)]
    rest = out_ref.shape[0] - NBS * TOKEN_ROWS
    if rest > 0:
        pieces.append(jnp.zeros((rest, BLOCK), jnp.float32))
    out_ref[...] = jnp.concatenate(pieces, axis=0).astype(jnp.bfloat16)


def gram_kernel(embed_ref, first_ref, out_ref):
    feats, width = embed_ref.shape
    emb = embed_ref[...].astype(jnp.float32)
    emb = emb - jnp.sum(emb, axis=1, keepdims=True) / width
    both = jnp.concatenate(split_bf16(emb), axis=0)
    gram = mm(both, both, ((1,), (1,))) / width
    gram = gram[:feats] + gram[feats:]
    out_ref[...] = jnp.concatenate(split_bf16(gram[:, :feats] + gram[:, feats:]), axis=0)


def pack_kernel(evens, feats, q_gain_ref, k_gain_ref, gram_ref, *refs):
    here, near = refs[: len(evens)], refs[len(evens)]
    x_t_ref, x_ref, key_mask_ref, gain_ref, *row_refs, rows_t = refs[len(evens) + 1 :]
    n_enc = 2 * len(evens)
    mine = lax.axis_index("enc")
    rows = n_enc * BLOCK
    lane = lax.broadcasted_iota(jnp.int32, (1, BLOCK), 1).astype(jnp.float32)
    extra = lax.broadcasted_iota(jnp.int32, (APAD - feats, BLOCK), 0)
    found = []
    blocks = [(at, here[i][...]) for i, at in enumerate(evens)]
    blocks += [(at ^ 1, near[1 + i]) for i, at in enumerate(evens)]
    for distance, block in blocks:
        source = mine ^ distance
        for b in range(NBS):
            tile = block.astype(jnp.float32)[b * TOKEN_ROWS : (b + 1) * TOKEN_ROWS]
            owner, offset, count = (tile[feats + i : feats + i + 1] for i in range(3))
            owner = jnp.where(offset == 0.0, owner, -1.0)
            segment = jnp.where(lane < count, (source + 1).astype(jnp.float32), 0.0)
            found.append((owner, segment, tile[:feats]))
    at = lax.broadcasted_iota(jnp.int32, (feats, feats), 0)
    frm = lax.broadcasted_iota(jnp.int32, (feats, feats), 1)
    order = jnp.where(frm == (at % 4) * (feats // 4) + at // 4, 1.0, 0.0).astype(jnp.bfloat16)
    for o in range(n_enc):
        segment = jnp.zeros((1, BLOCK), jnp.float32)
        body = jnp.zeros((feats, BLOCK), jnp.float32)
        for owner, seg_of, tile in found:
            hit = owner == float(o)
            segment = segment + jnp.where(hit, seg_of, 0.0)
            body = body + jnp.where(hit, tile, 0.0)
        tail = jnp.where(extra == 0, 1.0, jnp.where(extra == 1, segment, 0.0))
        rows_t[:, o * BLOCK : (o + 1) * BLOCK] = jnp.concatenate(
            [body, tail, jnp.zeros((LANES - APAD, BLOCK), jnp.float32)], axis=0
        )
    picked = mm(order, rows_t[:feats].astype(jnp.bfloat16))
    spread = mm(gram_ref[...], picked.astype(jnp.bfloat16))
    variance = jnp.sum((spread[:feats] + spread[feats:]) * picked, axis=0, keepdims=True)
    rows_t[:feats] = picked * lax.rsqrt(jnp.maximum(variance, 0.0) + eps_norm)
    x_t = rows_t[...]
    x_t_ref[...] = x_t[:APAD].astype(jnp.bfloat16)
    x_ref[...] = x_t.T.astype(jnp.bfloat16)
    group_t = lax.broadcasted_iota(jnp.int32, (LANES, rows), 0).astype(jnp.float32)
    key_mask_ref[...] = jnp.where(x_t[feats + 1 : feats + 2] == group_t, 0.0, 1.0).astype(jnp.bfloat16)
    group = lax.broadcasted_iota(jnp.int32, (BLOCK, LANES), 1).astype(jnp.float32)
    for core in range(2):
        rows_ref, mask_ref = row_refs[2 * core : 2 * core + 2]
        own = rows_t[:, pl.ds(pl.multiple_of((mine ^ core) * BLOCK, BLOCK), BLOCK)].T
        rows_ref[...] = own.astype(jnp.bfloat16)
        mask_ref[...] = jnp.where(own[:, feats + 1 : feats + 2] == group, -FAR, 0.0).astype(jnp.bfloat16)
    head_dim = q_gain_ref.shape[1]
    gain_ref[...] = q_gain_ref[...] * k_gain_ref[...] * (head_dim**-0.5 * math.log2(math.e))


def attend_heads(folds, place, x_t_ref, x_ref, key_mask_ref, gain_ref, own_ref, own_mask_ref):
    folds = list(folds)
    heads = range(len(folds))
    feats = (folds[0].shape[0] - TAIL) // 3
    tails = jnp.concatenate([fold[3 * feats :].astype(jnp.float32) for fold in folds], axis=1)
    row = lax.broadcasted_iota(jnp.int32, tails.shape, 0)

    def side(part):
        body = jnp.concatenate([fold[part * feats : (part + 1) * feats] for fold in folds], axis=1)
        shift = jnp.where(row == 0, tails[part : part + 1], 0.0).astype(jnp.bfloat16)
        return jnp.concatenate([body, shift], axis=0)

    def of(i):
        return slice(i * LANES, (i + 1) * LANES)

    keys = mm(side(1), x_t_ref[...], ((0,), (0,)))
    queries = mm(own_ref[:, :APAD], side(0))
    values = mm(x_ref[:, :APAD], side(2)).astype(jnp.bfloat16)
    gain, own_mask, key_mask = gain_ref[...], own_mask_ref[...], key_mask_ref[...]
    left, right = [], []
    for i in heads:
        key = keys[of(i)]
        square = jnp.sum(key * key, axis=0, keepdims=True) / LANES
        key = (key * lax.rsqrt(square + eps_norm)).astype(jnp.bfloat16)
        right.append(jnp.concatenate([key, key_mask], axis=0))
        query = queries[:, of(i)]
        square = jnp.sum(query * query, axis=1, keepdims=True) / LANES
        query = (query * lax.rsqrt(square + eps_norm) * gain).astype(jnp.bfloat16)
        left.append(jnp.concatenate([query, own_mask], axis=1))
    scores = [mm(left[i], right[i]) for i in heads]
    weights = [jnp.exp2(score).astype(jnp.bfloat16) for score in scores]
    ones = jnp.ones((values.shape[0], LANES), jnp.bfloat16)
    mixed = [mm(weights[i], jnp.concatenate([values[:, of(i)], ones], axis=1)) for i in heads]
    for i in heads:
        place(i, (mixed[i][:, :LANES] / mixed[i][:, LANES:]).astype(jnp.bfloat16))


def each_head(refs):
    for ref in refs:
        if len(ref.shape) == 2:
            yield ref[...]
        else:
            for i in range(ref.shape[0]):
                yield ref[i]


def attend_kernel(count, *refs):
    folds, out_ref = refs[6 : 6 + count], refs[-1]

    def place(i, result):
        out_ref[:, i * LANES : (i + 1) * LANES] = result

    attend_heads(each_head(folds), place, *refs[:6])


def output_kernel(heads, neighbours, lists, near_early_ref, near_rest_ref, own_early_ref, own_rest_ref, out_ref, sems):
    mine, slot = lax.axis_index("enc"), lax.axis_index("seq") & (heads - 1)
    copies = []

    def put(ref, at, base, far, k):
        head = (base ^ far) * heads + (slot ^ k)
        column = pl.ds(pl.multiple_of(head * LANES, LANES), LANES)
        result = ref.at[:, at * LANES : (at + 1) * LANES]
        copies.append(pltpu.make_async_copy(result, out_ref.at[0, :, column], sems.at[len(copies)]))
        copies[-1].start()

    for early, rest, base in (
        (near_early_ref, near_rest_ref, mine ^ 1),
        (own_early_ref, own_rest_ref, mine),
    ):
        for at, partner in enumerate(((0, 0), *neighbours)):
            put(early, at, base, *partner)
        for i, pair in enumerate(zip(*lists)):
            far, k = (jnp.where(base & 1 == 0, zero, one) for zero, one in zip(*pair))
            put(rest, 2 * i, base, far, k)
            put(rest, 2 * i + 1, base, far ^ 1, k)
    for copy in copies:
        copy.wait()


def vmem(count):
    return [pl.BlockSpec(memory_space=pltpu.VMEM)] * count


def hbm(count):
    return [pl.BlockSpec(memory_space=pltpu.HBM)] * count


def in_hbm(x):
    return pltpu.with_memory_space_constraint(x, pltpu.HBM)


def after(count):
    return [pl.BlockSpec(memory_space=pl.ANY)] * count


def call(kernel, ins, out_shape, scratch=(), cost=(1_000_000, 1_000_000)):
    return pl.pallas_call(
        kernel,
        in_specs=ins,
        out_specs=[pl.BlockSpec(memory_space=pltpu.VMEM)] * len(out_shape),
        out_shape=out_shape,
        scratch_shapes=list(scratch),
        compiler_params=pltpu.CompilerParams(vmem_limit_bytes=VMEM_LIMIT),
        cost_estimate=pl.CostEstimate(flops=cost[0], bytes_accessed=cost[1], transcendentals=0),
    )


def gate(x, *others):
    return pl.pallas_call(
        gate_kernel,
        in_specs=after(1 + len(others)),
        out_specs=after(1)[0],
        out_shape=jax.ShapeDtypeStruct(x.shape, x.dtype),
        input_output_aliases={0: 0},
        compiler_params=pltpu.CompilerParams(vmem_limit_bytes=VMEM_LIMIT),
    )(x, *others)


def exchange(x, axis, n, k):
    return lax.ppermute(x, axis, [(i, i ^ k) for i in range(n)])


def on_device(
    n_enc,
    n_seq,
    clip_features,
    clip_shape,
    packing,
    conv_weight,
    embed_weight,
    mod_shift,
    mod_scale,
    qkv_weight,
    q_gain,
    k_gain,
):
    caps = clip_features.shape[2:5]
    depth_all = clip_features.shape[5]
    cols = qkv_weight.shape[2]
    feats = embed_weight.shape[0]
    heads = cols // LANES
    rows = n_enc * BLOCK
    bf16, f32 = jnp.bfloat16, jnp.float32

    def folds(dtype, *lead):
        return jax.ShapeDtypeStruct((*lead, 3 * feats + TAIL, LANES), dtype)

    evens = [0]
    for bit in reversed(range(1, log2(n_enc))):
        evens += [at ^ (1 << bit) for at in evens]
    scale_rows, shift_rows = mod_scale.reshape(-1, LANES), mod_shift.reshape(-1, LANES)
    later = [
        clip_features.reshape(-1, depth_all),
        conv_weight.reshape(-1, depth_all),
        q_gain.reshape(1, -1),
        k_gain.reshape(1, -1),
    ]
    with jax.named_scope("fold"):
        embed, features, conv, q_gain, k_gain, keep, *sends = call(
            functools.partial(fold_kernel, len(later)),
            hbm(4 + len(later)),
            [jax.ShapeDtypeStruct(x.shape, x.dtype) for x in (embed_weight, *later)]
            + [folds(f32)]
            + [folds(bf16)] * max(heads - 1, 1),
            [
                pltpu.VMEM(scale_rows.shape, f32),
                pltpu.VMEM(shift_rows.shape, f32),
                pltpu.VMEM(qkv_weight.shape, bf16),
                pltpu.SemaphoreType.DMA((4 + len(later),)),
            ],
            cost=(200_000_000, 1_000_000),
        )(*map(in_hbm, (embed_weight, scale_rows, shift_rows, qkv_weight, *later)))

    with jax.named_scope("encode"):
        own_block = call(
            functools.partial(encode_kernel, caps),
            hbm(2) + vmem(2),
            [jax.ShapeDtypeStruct((TOKEN_MESSAGE, BLOCK), bf16)],
            [
                pltpu.SMEM(clip_shape.shape, jnp.int32),
                pltpu.SMEM(packing.shape, jnp.int32),
                pltpu.SemaphoreType.DMA((2,)),
            ],
            cost=(500_000_000, 2_000_000),
        )(in_hbm(clip_shape), in_hbm(packing), features, conv)[0]

    def add(keep, got, first):
        kernel = functools.partial(add_kernel, len(got))
        return call(kernel, vmem(1 + len(got)) + after(1), [folds(f32), folds(bf16)])(keep, *got, first)

    with jax.named_scope("fold_sum"):
        if heads > 1:
            got = [exchange(sends[k - 1], "seq", n_seq, k) for k in reversed(range(1, heads))]
            keep, send = add(keep, got, own_block)
        else:
            send = sends[0]

    with jax.named_scope("tokens"):
        blocks = [own_block] + [exchange(own_block, "enc", n_enc, k) for k in evens[1:]]

    with jax.named_scope("fold_sum"):
        for bit in range(log2(heads), log2(n_seq)):
            got = exchange(send, "seq", n_seq, 1 << bit)
            if bit + 1 < log2(n_seq):
                keep, send = add(keep, [got], own_block)
            else:
                fresh, swap = call(
                    functools.partial(last_add_kernel, len(blocks)),
                    vmem(2 + len(blocks)) + after(1),
                    [folds(bf16), folds(bf16, 1 + len(blocks))],
                )(keep, got, *blocks, keep)

    partners = [(far, k) for far in evens for k in range(heads) if far or k]
    partners.sort(key=lambda p: (p[0].bit_count() + p[1].bit_count(), p[0]))
    near_count = min(3, len(partners))
    half = (len(partners) - near_count) // 2
    assert len(partners) == near_count + 2 * half
    neighbours = tuple(partners[:near_count])
    lists = (tuple(partners[near_count : near_count + half]), tuple(partners[near_count + half :]))

    def spread(x, partner_of):
        pairs = []
        for e in range(n_enc):
            far, k = partner_of[e & 1]
            pairs += [(e * n_seq + i, (e ^ far) * n_seq + (i ^ k)) for i in range(n_seq)]
        return lax.ppermute(x, ("enc", "seq"), pairs)

    with jax.named_scope("gather"):
        singles = [spread(fresh, (partner, partner)) for partner in neighbours]
        swapped = exchange(swap, "enc", n_enc, 1)
        pair = call(pair_kernel, vmem(2), [folds(bf16, 2)])(fresh, swapped)[0]
        got = [spread(pair, partner_of) for partner_of in zip(*lists)]

    with jax.named_scope("gram"):
        gram = call(gram_kernel, vmem(1) + after(1), [jax.ShapeDtypeStruct((2 * feats, feats), bf16)])(embed, pair)[0]

    with jax.named_scope("pack"):
        *shared, own_rows, own_mask, far_rows, far_mask = call(
            functools.partial(pack_kernel, tuple(evens), feats),
            vmem(4 + len(evens)),
            [
                jax.ShapeDtypeStruct((APAD, rows), bf16),
                jax.ShapeDtypeStruct((rows, LANES), bf16),
                jax.ShapeDtypeStruct((LANES, rows), bf16),
                jax.ShapeDtypeStruct((1, LANES), f32),
            ]
            + [jax.ShapeDtypeStruct((BLOCK, LANES), bf16)] * 4,
            [pltpu.VMEM((LANES, rows), f32)],
        )(q_gain, k_gain, gram, *blocks, swapped)

    def attend(rows_here, groups, first=()):
        count = sum(group.size for group in groups) // ((3 * feats + TAIL) * LANES)
        return call(
            functools.partial(attend_kernel, len(groups)),
            vmem(6 + len(groups)) + after(len(first)),
            [jax.ShapeDtypeStruct((BLOCK, count * LANES), bf16)],
            cost=(count * 200_000_000, 1_000_000),
        )(*shared, *rows_here, *groups, *first)[0]

    with jax.named_scope("attend"):
        own, other = (own_rows, own_mask), (far_rows, far_mask)
        early, rest = [fresh, *singles], got
        early_other = attend(other, early)
        early_own = attend(own, early, [early_other])
        near_early = exchange(gate(early_other, early_own), "enc", n_enc, 1)
        near_rest = exchange(attend(other, rest, [early_own]), "enc", n_enc, 1)
        rest_own = attend(own, rest)
        return pl.pallas_call(
            functools.partial(output_kernel, heads, neighbours, lists),
            in_specs=vmem(4),
            out_specs=hbm(1)[0],
            out_shape=jax.ShapeDtypeStruct((1, BLOCK, n_enc * cols), bf16),
            scratch_shapes=[pltpu.SemaphoreType.DMA((n_enc * heads,))],
            compiler_params=pltpu.CompilerParams(vmem_limit_bytes=VMEM_LIMIT),
        )(near_early, near_rest, early_own, rest_own)


def solution(mesh):
    return jax.shard_map(
        functools.partial(on_device, mesh.shape["enc"], mesh.shape["seq"]),
        mesh=mesh,
        in_specs=(
            P("enc", "seq", None, None, None, None),
            P("enc", "seq", None),
            P("enc", "seq", None, None),
            P(),
            P(),
            P(),
            P(),
            P(None, "seq", "enc"),
            P(),
            P(),
        ),
        out_specs=P("seq", "enc", None),
        check_vma=False,
    )
```

```python
import functools
import math

import jax
import jax.numpy as jnp
from jax import lax
from jax.experimental import pallas as pl
from jax.experimental.pallas import tpu as pltpu
from jax.sharding import PartitionSpec as P

BLOCK = 128
NBS = 2
LANES = 128
APAD = 72
TAIL = 8
TOKEN_ROWS = 80
TOKEN_MESSAGE = 208
eps_norm = 1e-06
FAR = 2.0**20
VMEM_LIMIT = 48 * 1024 * 1024


def mm(a, b, dims=((1,), (0,)), precision=None):
    return lax.dot_general(a, b, (dims, ((), ())), preferred_element_type=jnp.float32, precision=precision)


def split_bf16(x):
    hi = x.astype(jnp.bfloat16)
    return hi, (x - hi.astype(jnp.float32)).astype(jnp.bfloat16)


def log2(n):
    bits = n.bit_length() - 1
    assert 1 << bits == n
    return bits


def fetch(pairs, sems):
    copies = [pltpu.make_async_copy(src, dst, sems.at[i]) for i, (src, dst) in enumerate(pairs)]
    for copy in copies:
        copy.start()
    return copies


def fold_kernel(count, embed_hbm, scale_hbm, shift_hbm, w_hbm, *refs):
    later_hbm, embed_ref, later, keep_ref, sends = refs[:count], refs[count], refs[count + 1 : 2 * count + 1], refs[2 * count + 1], refs[2 * count + 2 : -4]
    scale_ref, shift_ref, w_ref, sems = refs[-4:]
    copies = fetch(
        [(embed_hbm, embed_ref), (scale_hbm, scale_ref), (shift_hbm, shift_ref), (w_hbm, w_ref)]
        + list(zip(later_hbm, later)),
        sems,
    )
    me = lax.axis_index("seq")
    _, depth, cols = w_ref.shape
    feats = embed_ref.shape[0]
    heads = cols // LANES
    for copy in copies[:3]:
        copy.wait()
    mean = jnp.sum(embed_ref[...].astype(jnp.float32), axis=1, keepdims=True) / embed_ref.shape[1]
    span = max(depth, LANES)
    chunks = span // LANES
    first = (me * depth) // LANES
    emb = embed_ref[:, pl.ds(pl.multiple_of(first * LANES, LANES), span)].astype(jnp.float32) - mean
    scale = jnp.concatenate([scale_ref[pl.ds(first + i, 1), :] for i in range(chunks)], axis=1)
    shift = jnp.concatenate([shift_ref[pl.ds(first + i, 1), :] for i in range(chunks)], axis=1)
    left = jnp.concatenate(
        [emb * (1.0 + scale), shift, jnp.zeros((APAD - feats - 1, span), jnp.float32)], axis=0
    )
    if depth < LANES:
        low = me * depth - first * LANES
        lane = lax.broadcasted_iota(jnp.int32, left.shape, 1)
        left = jnp.where((lane >= low) & (lane < low + depth), left, 0.0)
    hi, lo = split_bf16(left)
    both = jnp.concatenate([hi, lo], axis=0)
    copies[3].wait()

    def product(head):
        start = pl.multiple_of(head * LANES, LANES)
        right = jnp.concatenate([w_ref[part, :, pl.ds(start, LANES)] for part in range(3)], axis=1)
        right = jnp.concatenate([right] * (span // depth), axis=0)
        total = mm(both, right)
        total = total[:APAD] + total[APAD:]
        parts = [total[:, part * LANES : (part + 1) * LANES] for part in range(3)]
        row = lax.broadcasted_iota(jnp.int32, (TAIL, LANES), 0)
        tail = jnp.zeros((TAIL, LANES), jnp.float32)
        for part in range(3):
            tail = jnp.where(row == part, parts[part][feats : feats + 1], tail)
        return jnp.concatenate([part[:feats] for part in parts] + [tail], axis=0)

    slot = me & (heads - 1)
    for k in range(1, heads):
        sends[k - 1][...] = product(slot ^ k).astype(jnp.bfloat16)
    total = product(slot)
    keep_ref[...] = total
    if heads == 1:
        sends[0][...] = total.astype(jnp.bfloat16)
    for copy in copies[4:]:
        copy.wait()


def add_kernel(count, keep_in, *refs):
    total = keep_in[...]
    for ref in refs[:count]:
        total = total + ref[...].astype(jnp.float32)
    refs[-2][...] = total
    refs[-1][...] = total.astype(jnp.bfloat16)


def last_add_kernel(count, keep_in, got_ref, *refs):
    total = (keep_in[...] + got_ref[...].astype(jnp.float32)).astype(jnp.bfloat16)
    out_ref, swap_ref = refs[-2:]
    out_ref[...] = total
    swap_ref[0] = total
    for i in range(count):
        block = refs[i][...][: NBS * TOKEN_ROWS]
        rest = jnp.zeros((total.shape[0] - block.shape[0], LANES), jnp.bfloat16)
        swap_ref[1 + i] = jnp.concatenate([block, rest], axis=0)


def pair_kernel(own_ref, swapped_ref, out_ref):
    out_ref[0] = own_ref[...]
    out_ref[1] = swapped_ref[0]


def gate_kernel(*refs):
    pass


def encode_kernel(caps, shape_hbm, plan_hbm, feat_ref, conv_ref, out_ref, shape_ref, plan_ref, sems):
    copies = fetch([(shape_hbm, shape_ref), (plan_hbm, plan_ref)], sems)
    frames_cap, height_cap, width_cap = caps
    spots = frames_cap * height_cap * width_cap
    frame_size = height_cap * width_cap
    latent_ch = conv_ref.shape[0] // 27
    feats = 4 * latent_ch
    taps = mm(conv_ref[...], feat_ref[...], ((1,), (1,)))
    copies[0].wait()
    copies[1].wait()
    frames, height, width = shape_ref[0, 0, 0], shape_ref[0, 0, 1], shape_ref[0, 0, 2]
    spot = lax.broadcasted_iota(jnp.int32, (1, spots), 1)
    frame_ix = spot // frame_size
    row_ix = (spot % frame_size) // width_cap
    col_ix = spot % width_cap
    inside = (frame_ix < frames) & (row_ix < height) & (col_ix < width)
    taps = jnp.where(inside, taps, 0.0)

    def tap(a, b, j):
        at = (9 * a + 3 * b + j) * latent_ch
        return taps[at : at + latent_ch]

    def later(x, by):
        zeros = jnp.zeros((latent_ch, by * frame_size), jnp.float32)
        return jnp.concatenate([zeros, x[:, : spots - by * frame_size]], axis=1)

    def over_frames(b, j):
        return tap(2, b, j) + later(tap(1, b, j), 1) + later(tap(0, b, j), 2)

    def over_rows(j):
        above = pltpu.roll(over_frames(0, j), width_cap, 1)
        below = pltpu.roll(over_frames(2, j), spots - width_cap, 1)
        return (
            over_frames(1, j)
            + jnp.where(row_ix >= 1, above, 0.0)
            + jnp.where(row_ix < height_cap - 1, below, 0.0)
        )

    latent = (
        over_rows(1)
        + jnp.where(col_ix >= 1, pltpu.roll(over_rows(0), 1, 1), 0.0)
        + jnp.where(col_ix < width_cap - 1, pltpu.roll(over_rows(2), spots - 1, 1), 0.0)
    )
    latent = latent.astype(jnp.bfloat16).astype(jnp.float32)
    shifted = [latent] + [pltpu.roll(latent, spots - by, 1) for by in (1, width_cap, width_cap + 1)]
    patches = jnp.concatenate(shifted, axis=0).astype(jnp.bfloat16)

    tokens = NBS * BLOCK
    half_w = (width // 2).astype(jnp.float32)
    per_frame_int = (height // 2) * (width // 2)
    per_frame = per_frame_int.astype(jnp.float32)
    live = frames * per_frame_int
    token_int = lax.broadcasted_iota(jnp.int32, (1, tokens), 1)
    token = token_int.astype(jnp.float32)
    frame_of = jnp.floor((token + 0.5) / jnp.full((1, tokens), per_frame))
    within = token - frame_of * per_frame
    row_of = jnp.floor((within + 0.5) / jnp.full((1, tokens), half_w))
    col_of = within - row_of * half_w
    source = (frame_of * frame_size + row_of * (2 * width_cap) + col_of * 2).astype(jnp.int32)
    source = jnp.where(token_int < live, source, -1)
    chosen = lax.broadcasted_iota(jnp.int32, (spots, tokens), 0) == source
    picked = mm(patches, jnp.where(chosen, 1.0, 0.0).astype(jnp.bfloat16))
    kind = lax.broadcasted_iota(jnp.int32, (TOKEN_ROWS - feats, BLOCK), 0)
    pieces = []
    for b in range(NBS):
        count = jnp.clip(live - b * BLOCK, 0, BLOCK)
        info = jnp.where(
            kind == 0,
            plan_ref[0, 0, b, 0],
            jnp.where(kind == 1, plan_ref[0, 0, b, 1], jnp.where(kind == 2, count, 0)),
        )
        pieces += [picked[:, b * BLOCK : (b + 1) * BLOCK], info.astype(jnp.float32)]
    rest = out_ref.shape[0] - NBS * TOKEN_ROWS
    if rest > 0:
        pieces.append(jnp.zeros((rest, BLOCK), jnp.float32))
    out_ref[...] = jnp.concatenate(pieces, axis=0).astype(jnp.bfloat16)


def gram_kernel(embed_ref, first_ref, out_ref):
    feats, width = embed_ref.shape
    emb = embed_ref[...].astype(jnp.float32)
    emb = emb - jnp.sum(emb, axis=1, keepdims=True) / width
    both = jnp.concatenate(split_bf16(emb), axis=0)
    gram = mm(both, both, ((1,), (1,))) / width
    gram = gram[:feats] + gram[feats:]
    out_ref[...] = jnp.concatenate(split_bf16(gram[:, :feats] + gram[:, feats:]), axis=0)


def pack_kernel(evens, feats, q_gain_ref, k_gain_ref, gram_ref, *refs):
    here, near = refs[: len(evens)], refs[len(evens)]
    x_t_ref, x_ref, key_mask_ref, gain_ref, *row_refs, rows_t = refs[len(evens) + 1 :]
    n_enc = 2 * len(evens)
    mine = lax.axis_index("enc")
    rows = n_enc * BLOCK
    lane = lax.broadcasted_iota(jnp.int32, (1, BLOCK), 1).astype(jnp.float32)
    extra = lax.broadcasted_iota(jnp.int32, (APAD - feats, BLOCK), 0)
    found = []
    blocks = [(at, here[i][...]) for i, at in enumerate(evens)]
    blocks += [(at ^ 1, near[1 + i]) for i, at in enumerate(evens)]
    for distance, block in blocks:
        source = mine ^ distance
        for b in range(NBS):
            tile = block.astype(jnp.float32)[b * TOKEN_ROWS : (b + 1) * TOKEN_ROWS]
            owner, offset, count = (tile[feats + i : feats + i + 1] for i in range(3))
            owner = jnp.where(offset == 0.0, owner, -1.0)
            segment = jnp.where(lane < count, (source + 1).astype(jnp.float32), 0.0)
            found.append((owner, segment, tile[:feats]))
    at = lax.broadcasted_iota(jnp.int32, (feats, feats), 0)
    frm = lax.broadcasted_iota(jnp.int32, (feats, feats), 1)
    order = jnp.where(frm == (at % 4) * (feats // 4) + at // 4, 1.0, 0.0).astype(jnp.bfloat16)
    for o in range(n_enc):
        segment = jnp.zeros((1, BLOCK), jnp.float32)
        body = jnp.zeros((feats, BLOCK), jnp.float32)
        for owner, seg_of, tile in found:
            hit = owner == float(o)
            segment = segment + jnp.where(hit, seg_of, 0.0)
            body = body + jnp.where(hit, tile, 0.0)
        tail = jnp.where(extra == 0, 1.0, jnp.where(extra == 1, segment, 0.0))
        rows_t[:, o * BLOCK : (o + 1) * BLOCK] = jnp.concatenate(
            [body, tail, jnp.zeros((LANES - APAD, BLOCK), jnp.float32)], axis=0
        )
    picked = mm(order, rows_t[:feats].astype(jnp.bfloat16))
    spread = mm(gram_ref[...], picked.astype(jnp.bfloat16))
    variance = jnp.sum((spread[:feats] + spread[feats:]) * picked, axis=0, keepdims=True)
    rows_t[:feats] = picked * lax.rsqrt(jnp.maximum(variance, 0.0) + eps_norm)
    x_t = rows_t[...]
    x_t_ref[...] = x_t[:APAD].astype(jnp.bfloat16)
    x_ref[...] = x_t.T.astype(jnp.bfloat16)
    group_t = lax.broadcasted_iota(jnp.int32, (LANES, rows), 0).astype(jnp.float32)
    key_mask_ref[...] = jnp.where(x_t[feats + 1 : feats + 2] == group_t, 0.0, 1.0).astype(jnp.bfloat16)
    group = lax.broadcasted_iota(jnp.int32, (BLOCK, LANES), 1).astype(jnp.float32)
    for core in range(2):
        rows_ref, mask_ref = row_refs[2 * core : 2 * core + 2]
        own = rows_t[:, pl.ds(pl.multiple_of((mine ^ core) * BLOCK, BLOCK), BLOCK)].T
        rows_ref[...] = own.astype(jnp.bfloat16)
        mask_ref[...] = jnp.where(own[:, feats + 1 : feats + 2] == group, -FAR, 0.0).astype(jnp.bfloat16)
    head_dim = q_gain_ref.shape[1]
    gain_ref[...] = q_gain_ref[...] * k_gain_ref[...] * (head_dim**-0.5 * math.log2(math.e))


def attend_heads(folds, place, x_t_ref, x_ref, key_mask_ref, gain_ref, own_ref, own_mask_ref):
    folds = list(folds)
    heads = range(len(folds))
    feats = (folds[0].shape[0] - TAIL) // 3
    tails = jnp.concatenate([fold[3 * feats :].astype(jnp.float32) for fold in folds], axis=1)
    row = lax.broadcasted_iota(jnp.int32, tails.shape, 0)

    def side(part):
        body = jnp.concatenate([fold[part * feats : (part + 1) * feats] for fold in folds], axis=1)
        shift = jnp.where(row == 0, tails[part : part + 1], 0.0).astype(jnp.bfloat16)
        return jnp.concatenate([body, shift], axis=0)

    def of(i):
        return slice(i * LANES, (i + 1) * LANES)

    keys = mm(side(1), x_t_ref[...], ((0,), (0,)))
    queries = mm(own_ref[:, :APAD], side(0))
    values = mm(x_ref[:, :APAD], side(2)).astype(jnp.bfloat16)
    gain, own_mask, key_mask = gain_ref[...], own_mask_ref[...], key_mask_ref[...]
    left, right = [], []
    for i in heads:
        key = keys[of(i)]
        square = jnp.sum(key * key, axis=0, keepdims=True) / LANES
        key = (key * lax.rsqrt(square + eps_norm)).astype(jnp.bfloat16)
        right.append(jnp.concatenate([key, key_mask], axis=0))
        query = queries[:, of(i)]
        square = jnp.sum(query * query, axis=1, keepdims=True) / LANES
        query = (query * lax.rsqrt(square + eps_norm) * gain).astype(jnp.bfloat16)
        left.append(jnp.concatenate([query, own_mask], axis=1))
    scores = [mm(left[i], right[i]) for i in heads]
    weights = [jnp.exp2(score).astype(jnp.bfloat16) for score in scores]
    ones = jnp.ones((values.shape[0], LANES), jnp.bfloat16)
    mixed = [mm(weights[i], jnp.concatenate([values[:, of(i)], ones], axis=1)) for i in heads]
    for i in heads:
        place(i, (mixed[i][:, :LANES] / mixed[i][:, LANES:]).astype(jnp.bfloat16))


def each_head(refs):
    for ref in refs:
        if len(ref.shape) == 2:
            yield ref[...]
        else:
            for i in range(ref.shape[0]):
                yield ref[i]


def attend_kernel(count, *refs):
    folds, out_ref = refs[6 : 6 + count], refs[-1]

    def place(i, result):
        out_ref[:, i * LANES : (i + 1) * LANES] = result

    attend_heads(each_head(folds), place, *refs[:6])


def output_kernel(heads, neighbours, lists, near_early_ref, near_rest_ref, own_early_ref, own_rest_ref, out_ref, sems):
    mine, slot = lax.axis_index("enc"), lax.axis_index("seq") & (heads - 1)
    copies = []

    def put(ref, at, base, far, k):
        head = (base ^ far) * heads + (slot ^ k)
        column = pl.ds(pl.multiple_of(head * LANES, LANES), LANES)
        result = ref.at[:, at * LANES : (at + 1) * LANES]
        copies.append(pltpu.make_async_copy(result, out_ref.at[0, :, column], sems.at[len(copies)]))
        copies[-1].start()

    for early, rest, base in (
        (near_early_ref, near_rest_ref, mine ^ 1),
        (own_early_ref, own_rest_ref, mine),
    ):
        for at, partner in enumerate(((0, 0), *neighbours)):
            put(early, at, base, *partner)
        for i, pair in enumerate(zip(*lists)):
            far, k = (jnp.where(base & 1 == 0, zero, one) for zero, one in zip(*pair))
            put(rest, 2 * i, base, far, k)
            put(rest, 2 * i + 1, base, far ^ 1, k)
    for copy in copies:
        copy.wait()


def vmem(count):
    return [pl.BlockSpec(memory_space=pltpu.VMEM)] * count


def hbm(count):
    return [pl.BlockSpec(memory_space=pltpu.HBM)] * count


def in_hbm(x):
    return pltpu.with_memory_space_constraint(x, pltpu.HBM)


def after(count):
    return [pl.BlockSpec(memory_space=pl.ANY)] * count


def call(kernel, ins, out_shape, scratch=(), cost=(1_000_000, 1_000_000)):
    return pl.pallas_call(
        kernel,
        in_specs=ins,
        out_specs=[pl.BlockSpec(memory_space=pltpu.VMEM)] * len(out_shape),
        out_shape=out_shape,
        scratch_shapes=list(scratch),
        compiler_params=pltpu.CompilerParams(vmem_limit_bytes=VMEM_LIMIT),
        cost_estimate=pl.CostEstimate(flops=cost[0], bytes_accessed=cost[1], transcendentals=0),
    )


def gate(x, *others):
    return pl.pallas_call(
        gate_kernel,
        in_specs=after(1 + len(others)),
        out_specs=after(1)[0],
        out_shape=jax.ShapeDtypeStruct(x.shape, x.dtype),
        input_output_aliases={0: 0},
        compiler_params=pltpu.CompilerParams(vmem_limit_bytes=VMEM_LIMIT),
    )(x, *others)


def exchange(x, axis, n, k):
    return lax.ppermute(x, axis, [(i, i ^ k) for i in range(n)])


def on_device(
    n_enc,
    n_seq,
    clip_features,
    clip_shape,
    packing,
    conv_weight,
    embed_weight,
    mod_shift,
    mod_scale,
    qkv_weight,
    q_gain,
    k_gain,
):
    caps = clip_features.shape[2:5]
    depth_all = clip_features.shape[5]
    cols = qkv_weight.shape[2]
    feats = embed_weight.shape[0]
    heads = cols // LANES
    rows = n_enc * BLOCK
    bf16, f32 = jnp.bfloat16, jnp.float32

    def folds(dtype, *lead):
        return jax.ShapeDtypeStruct((*lead, 3 * feats + TAIL, LANES), dtype)

    evens = [0]
    for bit in reversed(range(1, log2(n_enc))):
        evens += [at ^ (1 << bit) for at in evens]
    scale_rows, shift_rows = mod_scale.reshape(-1, LANES), mod_shift.reshape(-1, LANES)
    later = [
        clip_features.reshape(-1, depth_all),
        conv_weight.reshape(-1, depth_all),
        q_gain.reshape(1, -1),
        k_gain.reshape(1, -1),
    ]
    with jax.named_scope("fold"):
        embed, features, conv, q_gain, k_gain, keep, *sends = call(
            functools.partial(fold_kernel, len(later)),
            hbm(4 + len(later)),
            [jax.ShapeDtypeStruct(x.shape, x.dtype) for x in (embed_weight, *later)]
            + [folds(f32)]
            + [folds(bf16)] * max(heads - 1, 1),
            [
                pltpu.VMEM(scale_rows.shape, f32),
                pltpu.VMEM(shift_rows.shape, f32),
                pltpu.VMEM(qkv_weight.shape, bf16),
                pltpu.SemaphoreType.DMA((4 + len(later),)),
            ],
            cost=(200_000_000, 1_000_000),
        )(*map(in_hbm, (embed_weight, scale_rows, shift_rows, qkv_weight, *later)))

    with jax.named_scope("encode"):
        own_block = call(
            functools.partial(encode_kernel, caps),
            hbm(2) + vmem(2),
            [jax.ShapeDtypeStruct((TOKEN_MESSAGE, BLOCK), bf16)],
            [
                pltpu.SMEM(clip_shape.shape, jnp.int32),
                pltpu.SMEM(packing.shape, jnp.int32),
                pltpu.SemaphoreType.DMA((2,)),
            ],
            cost=(500_000_000, 2_000_000),
        )(in_hbm(clip_shape), in_hbm(packing), features, conv)[0]

    def add(keep, got, first):
        kernel = functools.partial(add_kernel, len(got))
        return call(kernel, vmem(1 + len(got)) + after(1), [folds(f32), folds(bf16)])(keep, *got, first)

    with jax.named_scope("fold_sum"):
        if heads > 1:
            got = [exchange(sends[k - 1], "seq", n_seq, k) for k in reversed(range(1, heads))]
            keep, send = add(keep, got, own_block)
        else:
            send = sends[0]

    with jax.named_scope("tokens"):
        blocks = [own_block] + [exchange(own_block, "enc", n_enc, k) for k in evens[1:]]

    with jax.named_scope("gram"):
        gram = call(gram_kernel, vmem(1) + after(1), [jax.ShapeDtypeStruct((2 * feats, feats), bf16)])(embed, keep)[0]

    with jax.named_scope("fold_sum"):
        for bit in range(log2(heads), log2(n_seq)):
            got = exchange(send, "seq", n_seq, 1 << bit)
            if bit + 1 < log2(n_seq):
                keep, send = add(keep, [got], own_block)
            else:
                fresh, swap = call(
                    functools.partial(last_add_kernel, len(blocks)),
                    vmem(2 + len(blocks)) + after(1),
                    [folds(bf16), folds(bf16, 1 + len(blocks))],
                )(keep, got, *blocks, gram)

    partners = [(far, k) for far in evens for k in range(heads) if far or k]
    partners.sort(key=lambda p: (p[0].bit_count() + p[1].bit_count(), p[0]))
    near_count = min(3, len(partners))
    half = (len(partners) - near_count) // 2
    assert len(partners) == near_count + 2 * half
    neighbours = tuple(partners[:near_count])
    lists = (tuple(partners[near_count : near_count + half]), tuple(partners[near_count + half :]))

    def spread(x, partner_of):
        pairs = []
        for e in range(n_enc):
            far, k = partner_of[e & 1]
            pairs += [(e * n_seq + i, (e ^ far) * n_seq + (i ^ k)) for i in range(n_seq)]
        return lax.ppermute(x, ("enc", "seq"), pairs)

    with jax.named_scope("gather"):
        singles = [spread(fresh, (partner, partner)) for partner in neighbours]
        swapped = exchange(swap, "enc", n_enc, 1)
        pair = call(pair_kernel, vmem(2), [folds(bf16, 2)])(fresh, swapped)[0]
        got = [spread(pair, partner_of) for partner_of in zip(*lists)]

    with jax.named_scope("pack"):
        *shared, own_rows, own_mask, far_rows, far_mask = call(
            functools.partial(pack_kernel, tuple(evens), feats),
            vmem(4 + len(evens)),
            [
                jax.ShapeDtypeStruct((APAD, rows), bf16),
                jax.ShapeDtypeStruct((rows, LANES), bf16),
                jax.ShapeDtypeStruct((LANES, rows), bf16),
                jax.ShapeDtypeStruct((1, LANES), f32),
            ]
            + [jax.ShapeDtypeStruct((BLOCK, LANES), bf16)] * 4,
            [pltpu.VMEM((LANES, rows), f32)],
        )(q_gain, k_gain, gram, *blocks, swapped)

    def attend(rows_here, groups, first=()):
        count = sum(group.size for group in groups) // ((3 * feats + TAIL) * LANES)
        return call(
            functools.partial(attend_kernel, len(groups)),
            vmem(6 + len(groups)) + after(len(first)),
            [jax.ShapeDtypeStruct((BLOCK, count * LANES), bf16)],
            cost=(count * 200_000_000, 1_000_000),
        )(*shared, *rows_here, *groups, *first)[0]

    with jax.named_scope("attend"):
        own, other = (own_rows, own_mask), (far_rows, far_mask)
        early, rest = [fresh, *singles], got
        early_other = attend(other, early)
        early_own = attend(own, early, [early_other])
        near_early = exchange(gate(early_other, early_own), "enc", n_enc, 1)
        near_rest = exchange(attend(other, rest, [early_own]), "enc", n_enc, 1)
        rest_own = attend(own, rest)
        return pl.pallas_call(
            functools.partial(output_kernel, heads, neighbours, lists),
            in_specs=vmem(4),
            out_specs=hbm(1)[0],
            out_shape=jax.ShapeDtypeStruct((1, BLOCK, n_enc * cols), bf16),
            scratch_shapes=[pltpu.SemaphoreType.DMA((n_enc * heads,))],
            compiler_params=pltpu.CompilerParams(vmem_limit_bytes=VMEM_LIMIT),
        )(near_early, near_rest, early_own, rest_own)


def solution(mesh):
    return jax.shard_map(
        functools.partial(on_device, mesh.shape["enc"], mesh.shape["seq"]),
        mesh=mesh,
        in_specs=(
            P("enc", "seq", None, None, None, None),
            P("enc", "seq", None),
            P("enc", "seq", None, None),
            P(),
            P(),
            P(),
            P(),
            P(None, "seq", "enc"),
            P(),
            P(),
        ),
        out_specs=P("seq", "enc", None),
        check_vma=False,
    )
```

```python
import functools
import math

import jax
import jax.numpy as jnp
from jax import lax
from jax.experimental import pallas as pl
from jax.experimental.pallas import tpu as pltpu
from jax.sharding import PartitionSpec as P

BLOCK = 128
NBS = 2
LANES = 128
APAD = 72
TAIL = 8
TOKEN_ROWS = 80
TOKEN_MESSAGE = 208
eps_norm = 1e-06
FAR = 2.0**20
VMEM_LIMIT = 48 * 1024 * 1024


def mm(a, b, dims=((1,), (0,)), precision=None):
    return lax.dot_general(a, b, (dims, ((), ())), preferred_element_type=jnp.float32, precision=precision)


def split_bf16(x):
    hi = x.astype(jnp.bfloat16)
    return hi, (x - hi.astype(jnp.float32)).astype(jnp.bfloat16)


def log2(n):
    bits = n.bit_length() - 1
    assert 1 << bits == n
    return bits


def fetch(pairs, sems):
    copies = [pltpu.make_async_copy(src, dst, sems.at[i]) for i, (src, dst) in enumerate(pairs)]
    for copy in copies:
        copy.start()
    return copies


def fold_kernel(count, embed_hbm, scale_hbm, shift_hbm, w_hbm, *refs):
    later_hbm, embed_ref, later, keep_ref, sends = refs[:count], refs[count], refs[count + 1 : 2 * count + 1], refs[2 * count + 1], refs[2 * count + 2 : -4]
    scale_ref, shift_ref, w_ref, sems = refs[-4:]
    copies = fetch(
        [(embed_hbm, embed_ref), (scale_hbm, scale_ref), (shift_hbm, shift_ref), (w_hbm, w_ref)]
        + list(zip(later_hbm, later)),
        sems,
    )
    me = lax.axis_index("seq")
    _, depth, cols = w_ref.shape
    feats = embed_ref.shape[0]
    heads = cols // LANES
    for copy in copies[:3]:
        copy.wait()
    mean = jnp.sum(embed_ref[...].astype(jnp.float32), axis=1, keepdims=True) / embed_ref.shape[1]
    span = max(depth, LANES)
    chunks = span // LANES
    first = (me * depth) // LANES
    emb = embed_ref[:, pl.ds(pl.multiple_of(first * LANES, LANES), span)].astype(jnp.float32) - mean
    scale = jnp.concatenate([scale_ref[pl.ds(first + i, 1), :] for i in range(chunks)], axis=1)
    shift = jnp.concatenate([shift_ref[pl.ds(first + i, 1), :] for i in range(chunks)], axis=1)
    left = jnp.concatenate(
        [emb * (1.0 + scale), shift, jnp.zeros((APAD - feats - 1, span), jnp.float32)], axis=0
    )
    if depth < LANES:
        low = me * depth - first * LANES
        lane = lax.broadcasted_iota(jnp.int32, left.shape, 1)
        left = jnp.where((lane >= low) & (lane < low + depth), left, 0.0)
    hi, lo = split_bf16(left)
    both = jnp.concatenate([hi, lo], axis=0)
    copies[3].wait()

    def product(head):
        start = pl.multiple_of(head * LANES, LANES)
        right = jnp.concatenate([w_ref[part, :, pl.ds(start, LANES)] for part in range(3)], axis=1)
        right = jnp.concatenate([right] * (span // depth), axis=0)
        total = mm(both, right)
        total = total[:APAD] + total[APAD:]
        parts = [total[:, part * LANES : (part + 1) * LANES] for part in range(3)]
        row = lax.broadcasted_iota(jnp.int32, (TAIL, LANES), 0)
        tail = jnp.zeros((TAIL, LANES), jnp.float32)
        for part in range(3):
            tail = jnp.where(row == part, parts[part][feats : feats + 1], tail)
        return jnp.concatenate([part[:feats] for part in parts] + [tail], axis=0)

    slot = me & (heads - 1)
    for k in range(1, heads):
        sends[k - 1][...] = product(slot ^ k).astype(jnp.bfloat16)
    total = product(slot)
    keep_ref[...] = total
    if heads == 1:
        sends[0][...] = total.astype(jnp.bfloat16)
    for copy in copies[4:]:
        copy.wait()


def add_kernel(count, keep_in, *refs):
    total = keep_in[...]
    for ref in refs[:count]:
        total = total + ref[...].astype(jnp.float32)
    refs[-2][...] = total
    refs[-1][...] = total.astype(jnp.bfloat16)


def last_add_kernel(keep_in, got_ref, first_ref, out_ref):
    out_ref[...] = (keep_in[...] + got_ref[...].astype(jnp.float32)).astype(jnp.bfloat16)


def cut_kernel(block_ref, first_ref, out_ref):
    out_ref[...] = block_ref[: NBS * TOKEN_ROWS]


def pair_kernel(own_ref, swapped_ref, out_ref):
    out_ref[0] = own_ref[...]
    out_ref[1] = swapped_ref[...]


def gate_kernel(*refs):
    pass


def encode_kernel(caps, shape_hbm, plan_hbm, feat_ref, conv_ref, out_ref, shape_ref, plan_ref, sems):
    copies = fetch([(shape_hbm, shape_ref), (plan_hbm, plan_ref)], sems)
    frames_cap, height_cap, width_cap = caps
    spots = frames_cap * height_cap * width_cap
    frame_size = height_cap * width_cap
    latent_ch = conv_ref.shape[0] // 27
    feats = 4 * latent_ch
    taps = mm(conv_ref[...], feat_ref[...], ((1,), (1,)))
    copies[0].wait()
    copies[1].wait()
    frames, height, width = shape_ref[0, 0, 0], shape_ref[0, 0, 1], shape_ref[0, 0, 2]
    spot = lax.broadcasted_iota(jnp.int32, (1, spots), 1)
    frame_ix = spot // frame_size
    row_ix = (spot % frame_size) // width_cap
    col_ix = spot % width_cap
    inside = (frame_ix < frames) & (row_ix < height) & (col_ix < width)
    taps = jnp.where(inside, taps, 0.0)

    def tap(a, b, j):
        at = (9 * a + 3 * b + j) * latent_ch
        return taps[at : at + latent_ch]

    def later(x, by):
        zeros = jnp.zeros((latent_ch, by * frame_size), jnp.float32)
        return jnp.concatenate([zeros, x[:, : spots - by * frame_size]], axis=1)

    def over_frames(b, j):
        return tap(2, b, j) + later(tap(1, b, j), 1) + later(tap(0, b, j), 2)

    def over_rows(j):
        above = pltpu.roll(over_frames(0, j), width_cap, 1)
        below = pltpu.roll(over_frames(2, j), spots - width_cap, 1)
        return (
            over_frames(1, j)
            + jnp.where(row_ix >= 1, above, 0.0)
            + jnp.where(row_ix < height_cap - 1, below, 0.0)
        )

    latent = (
        over_rows(1)
        + jnp.where(col_ix >= 1, pltpu.roll(over_rows(0), 1, 1), 0.0)
        + jnp.where(col_ix < width_cap - 1, pltpu.roll(over_rows(2), spots - 1, 1), 0.0)
    )
    latent = latent.astype(jnp.bfloat16).astype(jnp.float32)
    shifted = [latent] + [pltpu.roll(latent, spots - by, 1) for by in (1, width_cap, width_cap + 1)]
    patches = jnp.concatenate(shifted, axis=0).astype(jnp.bfloat16)

    tokens = NBS * BLOCK
    half_w = (width // 2).astype(jnp.float32)
    per_frame_int = (height // 2) * (width // 2)
    per_frame = per_frame_int.astype(jnp.float32)
    live = frames * per_frame_int
    token_int = lax.broadcasted_iota(jnp.int32, (1, tokens), 1)
    token = token_int.astype(jnp.float32)
    frame_of = jnp.floor((token + 0.5) / jnp.full((1, tokens), per_frame))
    within = token - frame_of * per_frame
    row_of = jnp.floor((within + 0.5) / jnp.full((1, tokens), half_w))
    col_of = within - row_of * half_w
    source = (frame_of * frame_size + row_of * (2 * width_cap) + col_of * 2).astype(jnp.int32)
    source = jnp.where(token_int < live, source, -1)
    chosen = lax.broadcasted_iota(jnp.int32, (spots, tokens), 0) == source
    picked = mm(patches, jnp.where(chosen, 1.0, 0.0).astype(jnp.bfloat16))
    kind = lax.broadcasted_iota(jnp.int32, (TOKEN_ROWS - feats, BLOCK), 0)
    pieces = []
    for b in range(NBS):
        count = jnp.clip(live - b * BLOCK, 0, BLOCK)
        info = jnp.where(
            kind == 0,
            plan_ref[0, 0, b, 0],
            jnp.where(kind == 1, plan_ref[0, 0, b, 1], jnp.where(kind == 2, count, 0)),
        )
        pieces += [picked[:, b * BLOCK : (b + 1) * BLOCK], info.astype(jnp.float32)]
    rest = out_ref.shape[0] - NBS * TOKEN_ROWS
    if rest > 0:
        pieces.append(jnp.zeros((rest, BLOCK), jnp.float32))
    out_ref[...] = jnp.concatenate(pieces, axis=0).astype(jnp.bfloat16)


def gram_kernel(embed_ref, first_ref, out_ref):
    feats, width = embed_ref.shape
    emb = embed_ref[...].astype(jnp.float32)
    emb = emb - jnp.sum(emb, axis=1, keepdims=True) / width
    both = jnp.concatenate(split_bf16(emb), axis=0)
    gram = mm(both, both, ((1,), (1,))) / width
    gram = gram[:feats] + gram[feats:]
    out_ref[...] = jnp.concatenate(split_bf16(gram[:, :feats] + gram[:, feats:]), axis=0)


def pack_kernel(evens, feats, q_gain_ref, k_gain_ref, gram_ref, *refs):
    here, near = refs[: len(evens)], refs[len(evens) : 2 * len(evens)]
    x_t_ref, x_ref, key_mask_ref, gain_ref, *row_refs, rows_t = refs[2 * len(evens) :]
    n_enc = 2 * len(evens)
    mine = lax.axis_index("enc")
    rows = n_enc * BLOCK
    lane = lax.broadcasted_iota(jnp.int32, (1, BLOCK), 1).astype(jnp.float32)
    extra = lax.broadcasted_iota(jnp.int32, (APAD - feats, BLOCK), 0)
    found = []
    blocks = [(at, here[i][...]) for i, at in enumerate(evens)]
    blocks += [(at ^ 1, near[i][...]) for i, at in enumerate(evens)]
    for distance, block in blocks:
        source = mine ^ distance
        for b in range(NBS):
            tile = block.astype(jnp.float32)[b * TOKEN_ROWS : (b + 1) * TOKEN_ROWS]
            owner, offset, count = (tile[feats + i : feats + i + 1] for i in range(3))
            owner = jnp.where(offset == 0.0, owner, -1.0)
            segment = jnp.where(lane < count, (source + 1).astype(jnp.float32), 0.0)
            found.append((owner, segment, tile[:feats]))
    at = lax.broadcasted_iota(jnp.int32, (feats, feats), 0)
    frm = lax.broadcasted_iota(jnp.int32, (feats, feats), 1)
    order = jnp.where(frm == (at % 4) * (feats // 4) + at // 4, 1.0, 0.0).astype(jnp.bfloat16)
    for o in range(n_enc):
        segment = jnp.zeros((1, BLOCK), jnp.float32)
        body = jnp.zeros((feats, BLOCK), jnp.float32)
        for owner, seg_of, tile in found:
            hit = owner == float(o)
            segment = segment + jnp.where(hit, seg_of, 0.0)
            body = body + jnp.where(hit, tile, 0.0)
        tail = jnp.where(extra == 0, 1.0, jnp.where(extra == 1, segment, 0.0))
        rows_t[:, o * BLOCK : (o + 1) * BLOCK] = jnp.concatenate(
            [body, tail, jnp.zeros((LANES - APAD, BLOCK), jnp.float32)], axis=0
        )
    picked = mm(order, rows_t[:feats].astype(jnp.bfloat16))
    spread = mm(gram_ref[...], picked.astype(jnp.bfloat16))
    variance = jnp.sum((spread[:feats] + spread[feats:]) * picked, axis=0, keepdims=True)
    rows_t[:feats] = picked * lax.rsqrt(jnp.maximum(variance, 0.0) + eps_norm)
    x_t = rows_t[...]
    x_t_ref[...] = x_t[:APAD].astype(jnp.bfloat16)
    x_ref[...] = x_t.T.astype(jnp.bfloat16)
    group_t = lax.broadcasted_iota(jnp.int32, (LANES, rows), 0).astype(jnp.float32)
    key_mask_ref[...] = jnp.where(x_t[feats + 1 : feats + 2] == group_t, 0.0, 1.0).astype(jnp.bfloat16)
    group = lax.broadcasted_iota(jnp.int32, (BLOCK, LANES), 1).astype(jnp.float32)
    for core in range(2):
        rows_ref, mask_ref = row_refs[2 * core : 2 * core + 2]
        own = rows_t[:, pl.ds(pl.multiple_of((mine ^ core) * BLOCK, BLOCK), BLOCK)].T
        rows_ref[...] = own.astype(jnp.bfloat16)
        mask_ref[...] = jnp.where(own[:, feats + 1 : feats + 2] == group, -FAR, 0.0).astype(jnp.bfloat16)
    head_dim = q_gain_ref.shape[1]
    gain_ref[...] = q_gain_ref[...] * k_gain_ref[...] * (head_dim**-0.5 * math.log2(math.e))


def attend_heads(folds, place, x_t_ref, x_ref, key_mask_ref, gain_ref, own_ref, own_mask_ref):
    folds = list(folds)
    heads = range(len(folds))
    feats = (folds[0].shape[0] - TAIL) // 3
    tails = jnp.concatenate([fold[3 * feats :].astype(jnp.float32) for fold in folds], axis=1)
    row = lax.broadcasted_iota(jnp.int32, tails.shape, 0)

    def side(part):
        body = jnp.concatenate([fold[part * feats : (part + 1) * feats] for fold in folds], axis=1)
        shift = jnp.where(row == 0, tails[part : part + 1], 0.0).astype(jnp.bfloat16)
        return jnp.concatenate([body, shift], axis=0)

    def of(i):
        return slice(i * LANES, (i + 1) * LANES)

    keys = mm(side(1), x_t_ref[...], ((0,), (0,)))
    queries = mm(own_ref[:, :APAD], side(0))
    values = mm(x_ref[:, :APAD], side(2)).astype(jnp.bfloat16)
    gain, own_mask, key_mask = gain_ref[...], own_mask_ref[...], key_mask_ref[...]
    left, right = [], []
    for i in heads:
        key = keys[of(i)]
        square = jnp.sum(key * key, axis=0, keepdims=True) / LANES
        key = (key * lax.rsqrt(square + eps_norm)).astype(jnp.bfloat16)
        right.append(jnp.concatenate([key, key_mask], axis=0))
        query = queries[:, of(i)]
        square = jnp.sum(query * query, axis=1, keepdims=True) / LANES
        query = (query * lax.rsqrt(square + eps_norm) * gain).astype(jnp.bfloat16)
        left.append(jnp.concatenate([query, own_mask], axis=1))
    scores = [mm(left[i], right[i]) for i in heads]
    weights = [jnp.exp2(score).astype(jnp.bfloat16) for score in scores]
    ones = jnp.ones((values.shape[0], LANES), jnp.bfloat16)
    mixed = [mm(weights[i], jnp.concatenate([values[:, of(i)], ones], axis=1)) for i in heads]
    for i in heads:
        place(i, (mixed[i][:, :LANES] / mixed[i][:, LANES:]).astype(jnp.bfloat16))


def each_head(refs):
    for ref in refs:
        if len(ref.shape) == 2:
            yield ref[...]
        else:
            for i in range(ref.shape[0]):
                yield ref[i]


def attend_kernel(count, *refs):
    folds, out_ref = refs[6 : 6 + count], refs[-1]

    def place(i, result):
        out_ref[:, i * LANES : (i + 1) * LANES] = result

    attend_heads(each_head(folds), place, *refs[:6])


def output_kernel(heads, neighbours, lists, near_early_ref, near_rest_ref, own_early_ref, own_rest_ref, out_ref, sems):
    mine, slot = lax.axis_index("enc"), lax.axis_index("seq") & (heads - 1)
    copies = []

    def put(ref, at, base, far, k):
        head = (base ^ far) * heads + (slot ^ k)
        column = pl.ds(pl.multiple_of(head * LANES, LANES), LANES)
        result = ref.at[:, at * LANES : (at + 1) * LANES]
        copies.append(pltpu.make_async_copy(result, out_ref.at[0, :, column], sems.at[len(copies)]))
        copies[-1].start()

    for early, rest, base in (
        (near_early_ref, near_rest_ref, mine ^ 1),
        (own_early_ref, own_rest_ref, mine),
    ):
        for at, partner in enumerate(((0, 0), *neighbours)):
            put(early, at, base, *partner)
        for i, pair in enumerate(zip(*lists)):
            far, k = (jnp.where(base & 1 == 0, zero, one) for zero, one in zip(*pair))
            put(rest, 2 * i, base, far, k)
            put(rest, 2 * i + 1, base, far ^ 1, k)
    for copy in copies:
        copy.wait()


def vmem(count):
    return [pl.BlockSpec(memory_space=pltpu.VMEM)] * count


def hbm(count):
    return [pl.BlockSpec(memory_space=pltpu.HBM)] * count


def in_hbm(x):
    return pltpu.with_memory_space_constraint(x, pltpu.HBM)


def after(count):
    return [pl.BlockSpec(memory_space=pl.ANY)] * count


def call(kernel, ins, out_shape, scratch=(), cost=(1_000_000, 1_000_000)):
    return pl.pallas_call(
        kernel,
        in_specs=ins,
        out_specs=[pl.BlockSpec(memory_space=pltpu.VMEM)] * len(out_shape),
        out_shape=out_shape,
        scratch_shapes=list(scratch),
        compiler_params=pltpu.CompilerParams(vmem_limit_bytes=VMEM_LIMIT),
        cost_estimate=pl.CostEstimate(flops=cost[0], bytes_accessed=cost[1], transcendentals=0),
    )


def gate(x, *others):
    return pl.pallas_call(
        gate_kernel,
        in_specs=after(1 + len(others)),
        out_specs=after(1)[0],
        out_shape=jax.ShapeDtypeStruct(x.shape, x.dtype),
        input_output_aliases={0: 0},
        compiler_params=pltpu.CompilerParams(vmem_limit_bytes=VMEM_LIMIT),
    )(x, *others)


def exchange(x, axis, n, k):
    return lax.ppermute(x, axis, [(i, i ^ k) for i in range(n)])


def on_device(
    n_enc,
    n_seq,
    clip_features,
    clip_shape,
    packing,
    conv_weight,
    embed_weight,
    mod_shift,
    mod_scale,
    qkv_weight,
    q_gain,
    k_gain,
):
    caps = clip_features.shape[2:5]
    depth_all = clip_features.shape[5]
    cols = qkv_weight.shape[2]
    feats = embed_weight.shape[0]
    heads = cols // LANES
    rows = n_enc * BLOCK
    bf16, f32 = jnp.bfloat16, jnp.float32

    def folds(dtype, *lead):
        return jax.ShapeDtypeStruct((*lead, 3 * feats + TAIL, LANES), dtype)

    evens = [0]
    for bit in reversed(range(1, log2(n_enc))):
        evens += [at ^ (1 << bit) for at in evens]
    scale_rows, shift_rows = mod_scale.reshape(-1, LANES), mod_shift.reshape(-1, LANES)
    later = [
        clip_features.reshape(-1, depth_all),
        conv_weight.reshape(-1, depth_all),
        q_gain.reshape(1, -1),
        k_gain.reshape(1, -1),
    ]
    with jax.named_scope("fold"):
        embed, features, conv, q_gain, k_gain, keep, *sends = call(
            functools.partial(fold_kernel, len(later)),
            hbm(4 + len(later)),
            [jax.ShapeDtypeStruct(x.shape, x.dtype) for x in (embed_weight, *later)]
            + [folds(f32)]
            + [folds(bf16)] * max(heads - 1, 1),
            [
                pltpu.VMEM(scale_rows.shape, f32),
                pltpu.VMEM(shift_rows.shape, f32),
                pltpu.VMEM(qkv_weight.shape, bf16),
                pltpu.SemaphoreType.DMA((4 + len(later),)),
            ],
            cost=(200_000_000, 1_000_000),
        )(*map(in_hbm, (embed_weight, scale_rows, shift_rows, qkv_weight, *later)))

    with jax.named_scope("encode"):
        own_block = call(
            functools.partial(encode_kernel, caps),
            hbm(2) + vmem(2),
            [jax.ShapeDtypeStruct((TOKEN_MESSAGE, BLOCK), bf16)],
            [
                pltpu.SMEM(clip_shape.shape, jnp.int32),
                pltpu.SMEM(packing.shape, jnp.int32),
                pltpu.SemaphoreType.DMA((2,)),
            ],
            cost=(500_000_000, 2_000_000),
        )(in_hbm(clip_shape), in_hbm(packing), features, conv)[0]

    def add(keep, got, first):
        kernel = functools.partial(add_kernel, len(got))
        return call(kernel, vmem(1 + len(got)) + after(1), [folds(f32), folds(bf16)])(keep, *got, first)

    with jax.named_scope("fold_sum"):
        if heads > 1:
            got = [exchange(sends[k - 1], "seq", n_seq, k) for k in reversed(range(1, heads))]
            keep, send = add(keep, got, own_block)
        else:
            send = sends[0]

    with jax.named_scope("tokens"):
        blocks = [own_block] + [exchange(own_block, "enc", n_enc, k) for k in evens[1:]]

    with jax.named_scope("gram"):
        gram = call(gram_kernel, vmem(1) + after(1), [jax.ShapeDtypeStruct((2 * feats, feats), bf16)])(embed, keep)[0]

    with jax.named_scope("pack"):
        cut = jax.ShapeDtypeStruct((NBS * TOKEN_ROWS, BLOCK), bf16)
        near_blocks = [
            exchange(call(cut_kernel, vmem(1) + after(1), [cut])(block, keep)[0], "enc", n_enc, 1) for block in blocks
        ]
        *shared, own_rows, own_mask, far_rows, far_mask = call(
            functools.partial(pack_kernel, tuple(evens), feats),
            vmem(3 + 2 * len(evens)),
            [
                jax.ShapeDtypeStruct((APAD, rows), bf16),
                jax.ShapeDtypeStruct((rows, LANES), bf16),
                jax.ShapeDtypeStruct((LANES, rows), bf16),
                jax.ShapeDtypeStruct((1, LANES), f32),
            ]
            + [jax.ShapeDtypeStruct((BLOCK, LANES), bf16)] * 4,
            [pltpu.VMEM((LANES, rows), f32)],
        )(q_gain, k_gain, gram, *blocks, *near_blocks)

    with jax.named_scope("fold_sum"):
        for bit in range(log2(heads), log2(n_seq)):
            got = exchange(send, "seq", n_seq, 1 << bit)
            if bit + 1 < log2(n_seq):
                keep, send = add(keep, [got], own_block)
            else:
                (fresh,) = call(last_add_kernel, vmem(2) + after(1), [folds(bf16)])(keep, got, own_rows)

    partners = [(far, k) for far in evens for k in range(heads) if far or k]
    partners.sort(key=lambda p: (p[0].bit_count() + p[1].bit_count(), p[0]))
    near_count = min(3, len(partners))
    half = (len(partners) - near_count) // 2
    assert len(partners) == near_count + 2 * half
    neighbours = tuple(partners[:near_count])
    lists = (tuple(partners[near_count : near_count + half]), tuple(partners[near_count + half :]))

    def spread(x, partner_of):
        pairs = []
        for e in range(n_enc):
            far, k = partner_of[e & 1]
            pairs += [(e * n_seq + i, (e ^ far) * n_seq + (i ^ k)) for i in range(n_seq)]
        return lax.ppermute(x, ("enc", "seq"), pairs)

    with jax.named_scope("gather"):
        singles = [spread(fresh, (partner, partner)) for partner in neighbours]
        swapped = exchange(fresh, "enc", n_enc, 1)
        pair = call(pair_kernel, vmem(2), [folds(bf16, 2)])(fresh, swapped)[0]
        got = [spread(pair, partner_of) for partner_of in zip(*lists)]

    def attend(rows_here, groups, first=()):
        count = sum(group.size for group in groups) // ((3 * feats + TAIL) * LANES)
        return call(
            functools.partial(attend_kernel, len(groups)),
            vmem(6 + len(groups)) + after(len(first)),
            [jax.ShapeDtypeStruct((BLOCK, count * LANES), bf16)],
            cost=(count * 200_000_000, 1_000_000),
        )(*shared, *rows_here, *groups, *first)[0]

    with jax.named_scope("attend"):
        own, other = (own_rows, own_mask), (far_rows, far_mask)
        early, rest = [fresh, *singles], got
        early_other = attend(other, early)
        early_own = attend(own, early, [early_other])
        near_early = exchange(gate(early_other, early_own), "enc", n_enc, 1)
        near_rest = exchange(attend(other, rest, [early_own]), "enc", n_enc, 1)
        rest_own = attend(own, rest)
        return pl.pallas_call(
            functools.partial(output_kernel, heads, neighbours, lists),
            in_specs=vmem(4),
            out_specs=hbm(1)[0],
            out_shape=jax.ShapeDtypeStruct((1, BLOCK, n_enc * cols), bf16),
            scratch_shapes=[pltpu.SemaphoreType.DMA((n_enc * heads,))],
            compiler_params=pltpu.CompilerParams(vmem_limit_bytes=VMEM_LIMIT),
        )(near_early, near_rest, early_own, rest_own)


def solution(mesh):
    return jax.shard_map(
        functools.partial(on_device, mesh.shape["enc"], mesh.shape["seq"]),
        mesh=mesh,
        in_specs=(
            P("enc", "seq", None, None, None, None),
            P("enc", "seq", None),
            P("enc", "seq", None, None),
            P(),
            P(),
            P(),
            P(),
            P(None, "seq", "enc"),
            P(),
            P(),
        ),
        out_specs=P("seq", "enc", None),
        check_vma=False,
    )
```

```python
import functools
import math

import jax
import jax.numpy as jnp
from jax import lax
from jax.experimental import pallas as pl
from jax.experimental.pallas import tpu as pltpu
from jax.sharding import PartitionSpec as P

BLOCK = 128
NBS = 2
LANES = 128
APAD = 72
TAIL = 8
TOKEN_ROWS = 80
TOKEN_MESSAGE = 208
eps_norm = 1e-06
FAR = 2.0**20
VMEM_LIMIT = 48 * 1024 * 1024


def mm(a, b, dims=((1,), (0,)), precision=None):
    return lax.dot_general(a, b, (dims, ((), ())), preferred_element_type=jnp.float32, precision=precision)


def split_bf16(x):
    hi = x.astype(jnp.bfloat16)
    return hi, (x - hi.astype(jnp.float32)).astype(jnp.bfloat16)


def log2(n):
    bits = n.bit_length() - 1
    assert 1 << bits == n
    return bits


def fetch(pairs, sems):
    copies = [pltpu.make_async_copy(src, dst, sems.at[i]) for i, (src, dst) in enumerate(pairs)]
    for copy in copies:
        copy.start()
    return copies


def fold_kernel(count, embed_hbm, scale_hbm, shift_hbm, w_hbm, *refs):
    later_hbm, embed_ref, later, keep_ref, sends = refs[:count], refs[count], refs[count + 1 : 2 * count + 1], refs[2 * count + 1], refs[2 * count + 2 : -4]
    scale_ref, shift_ref, w_ref, sems = refs[-4:]
    copies = fetch(
        [(embed_hbm, embed_ref), (scale_hbm, scale_ref), (shift_hbm, shift_ref), (w_hbm, w_ref)]
        + list(zip(later_hbm, later)),
        sems,
    )
    me = lax.axis_index("seq")
    _, depth, cols = w_ref.shape
    feats = embed_ref.shape[0]
    heads = cols // LANES
    for copy in copies[:3]:
        copy.wait()
    mean = jnp.sum(embed_ref[...].astype(jnp.float32), axis=1, keepdims=True) / embed_ref.shape[1]
    span = max(depth, LANES)
    chunks = span // LANES
    first = (me * depth) // LANES
    emb = embed_ref[:, pl.ds(pl.multiple_of(first * LANES, LANES), span)].astype(jnp.float32) - mean
    scale = jnp.concatenate([scale_ref[pl.ds(first + i, 1), :] for i in range(chunks)], axis=1)
    shift = jnp.concatenate([shift_ref[pl.ds(first + i, 1), :] for i in range(chunks)], axis=1)
    left = jnp.concatenate(
        [emb * (1.0 + scale), shift, jnp.zeros((APAD - feats - 1, span), jnp.float32)], axis=0
    )
    if depth < LANES:
        low = me * depth - first * LANES
        lane = lax.broadcasted_iota(jnp.int32, left.shape, 1)
        left = jnp.where((lane >= low) & (lane < low + depth), left, 0.0)
    hi, lo = split_bf16(left)
    both = jnp.concatenate([hi, lo], axis=0)
    copies[3].wait()

    def product(head):
        start = pl.multiple_of(head * LANES, LANES)
        right = jnp.concatenate([w_ref[part, :, pl.ds(start, LANES)] for part in range(3)], axis=1)
        right = jnp.concatenate([right] * (span // depth), axis=0)
        total = mm(both, right)
        total = total[:APAD] + total[APAD:]
        parts = [total[:, part * LANES : (part + 1) * LANES] for part in range(3)]
        row = lax.broadcasted_iota(jnp.int32, (TAIL, LANES), 0)
        tail = jnp.zeros((TAIL, LANES), jnp.float32)
        for part in range(3):
            tail = jnp.where(row == part, parts[part][feats : feats + 1], tail)
        return jnp.concatenate([part[:feats] for part in parts] + [tail], axis=0)

    slot = me & (heads - 1)
    for k in range(1, heads):
        sends[k - 1][...] = product(slot ^ k).astype(jnp.bfloat16)
    total = product(slot)
    keep_ref[...] = total
    if heads == 1:
        sends[0][...] = total.astype(jnp.bfloat16)
    for copy in copies[4:]:
        copy.wait()


def add_kernel(count, keep_in, *refs):
    total = keep_in[...]
    for ref in refs[:count]:
        total = total + ref[...].astype(jnp.float32)
    refs[-2][...] = total
    refs[-1][...] = total.astype(jnp.bfloat16)


def last_add_kernel(keep_in, got_ref, first_ref, out_ref):
    out_ref[...] = (keep_in[...] + got_ref[...].astype(jnp.float32)).astype(jnp.bfloat16)


def cut_kernel(block_ref, first_ref, out_ref):
    out_ref[...] = block_ref[: NBS * TOKEN_ROWS]


def pair_kernel(own_ref, swapped_ref, out_ref):
    out_ref[0] = own_ref[...]
    out_ref[1] = swapped_ref[...]


def gate_kernel(*refs):
    pass


def encode_kernel(caps, shape_hbm, plan_hbm, feat_ref, conv_ref, out_ref, shape_ref, plan_ref, sems):
    copies = fetch([(shape_hbm, shape_ref), (plan_hbm, plan_ref)], sems)
    frames_cap, height_cap, width_cap = caps
    spots = frames_cap * height_cap * width_cap
    frame_size = height_cap * width_cap
    latent_ch = conv_ref.shape[0] // 27
    feats = 4 * latent_ch
    taps = mm(conv_ref[...], feat_ref[...], ((1,), (1,)))
    copies[0].wait()
    copies[1].wait()
    frames, height, width = shape_ref[0, 0, 0], shape_ref[0, 0, 1], shape_ref[0, 0, 2]
    spot = lax.broadcasted_iota(jnp.int32, (1, spots), 1)
    frame_ix = spot // frame_size
    row_ix = (spot % frame_size) // width_cap
    col_ix = spot % width_cap
    inside = (frame_ix < frames) & (row_ix < height) & (col_ix < width)
    taps = jnp.where(inside, taps, 0.0)

    def tap(a, b, j):
        at = (9 * a + 3 * b + j) * latent_ch
        return taps[at : at + latent_ch]

    def later(x, by):
        zeros = jnp.zeros((latent_ch, by * frame_size), jnp.float32)
        return jnp.concatenate([zeros, x[:, : spots - by * frame_size]], axis=1)

    def over_frames(b, j):
        return tap(2, b, j) + later(tap(1, b, j), 1) + later(tap(0, b, j), 2)

    def over_rows(j):
        above = pltpu.roll(over_frames(0, j), width_cap, 1)
        below = pltpu.roll(over_frames(2, j), spots - width_cap, 1)
        return (
            over_frames(1, j)
            + jnp.where(row_ix >= 1, above, 0.0)
            + jnp.where(row_ix < height_cap - 1, below, 0.0)
        )

    latent = (
        over_rows(1)
        + jnp.where(col_ix >= 1, pltpu.roll(over_rows(0), 1, 1), 0.0)
        + jnp.where(col_ix < width_cap - 1, pltpu.roll(over_rows(2), spots - 1, 1), 0.0)
    )
    latent = latent.astype(jnp.bfloat16).astype(jnp.float32)
    shifted = [latent] + [pltpu.roll(latent, spots - by, 1) for by in (1, width_cap, width_cap + 1)]
    patches = jnp.concatenate(shifted, axis=0).astype(jnp.bfloat16)

    tokens = NBS * BLOCK
    half_w = (width // 2).astype(jnp.float32)
    per_frame_int = (height // 2) * (width // 2)
    per_frame = per_frame_int.astype(jnp.float32)
    live = frames * per_frame_int
    token_int = lax.broadcasted_iota(jnp.int32, (1, tokens), 1)
    token = token_int.astype(jnp.float32)
    frame_of = jnp.floor((token + 0.5) / jnp.full((1, tokens), per_frame))
    within = token - frame_of * per_frame
    row_of = jnp.floor((within + 0.5) / jnp.full((1, tokens), half_w))
    col_of = within - row_of * half_w
    source = (frame_of * frame_size + row_of * (2 * width_cap) + col_of * 2).astype(jnp.int32)
    source = jnp.where(token_int < live, source, -1)
    chosen = lax.broadcasted_iota(jnp.int32, (spots, tokens), 0) == source
    picked = mm(patches, jnp.where(chosen, 1.0, 0.0).astype(jnp.bfloat16))
    kind = lax.broadcasted_iota(jnp.int32, (TOKEN_ROWS - feats, BLOCK), 0)
    pieces = []
    for b in range(NBS):
        count = jnp.clip(live - b * BLOCK, 0, BLOCK)
        info = jnp.where(
            kind == 0,
            plan_ref[0, 0, b, 0],
            jnp.where(kind == 1, plan_ref[0, 0, b, 1], jnp.where(kind == 2, count, 0)),
        )
        pieces += [picked[:, b * BLOCK : (b + 1) * BLOCK], info.astype(jnp.float32)]
    rest = out_ref.shape[0] - NBS * TOKEN_ROWS
    if rest > 0:
        pieces.append(jnp.zeros((rest, BLOCK), jnp.float32))
    out_ref[...] = jnp.concatenate(pieces, axis=0).astype(jnp.bfloat16)


def gram_kernel(embed_ref, first_ref, out_ref):
    feats, width = embed_ref.shape
    emb = embed_ref[...].astype(jnp.float32)
    emb = emb - jnp.sum(emb, axis=1, keepdims=True) / width
    both = jnp.concatenate(split_bf16(emb), axis=0)
    gram = mm(both, both, ((1,), (1,))) / width
    gram = gram[:feats] + gram[feats:]
    out_ref[...] = jnp.concatenate(split_bf16(gram[:, :feats] + gram[:, feats:]), axis=0)


def pack_kernel(evens, feats, q_gain_ref, k_gain_ref, gram_ref, *refs):
    here, near = refs[: len(evens)], refs[len(evens) : 2 * len(evens)]
    x_t_ref, x_ref, key_mask_ref, gain_ref, *row_refs, rows_t = refs[2 * len(evens) :]
    n_enc = 2 * len(evens)
    mine = lax.axis_index("enc")
    rows = n_enc * BLOCK
    lane = lax.broadcasted_iota(jnp.int32, (1, BLOCK), 1).astype(jnp.float32)
    extra = lax.broadcasted_iota(jnp.int32, (APAD - feats, BLOCK), 0)
    found = []
    blocks = [(at, here[i][...]) for i, at in enumerate(evens)]
    blocks += [(at ^ 1, near[i][...]) for i, at in enumerate(evens)]
    for distance, block in blocks:
        source = mine ^ distance
        for b in range(NBS):
            tile = block.astype(jnp.float32)[b * TOKEN_ROWS : (b + 1) * TOKEN_ROWS]
            owner, offset, count = (tile[feats + i : feats + i + 1] for i in range(3))
            owner = jnp.where(offset == 0.0, owner, -1.0)
            segment = jnp.where(lane < count, (source + 1).astype(jnp.float32), 0.0)
            found.append((owner, segment, tile[:feats]))
    at = lax.broadcasted_iota(jnp.int32, (feats, feats), 0)
    frm = lax.broadcasted_iota(jnp.int32, (feats, feats), 1)
    order = jnp.where(frm == (at % 4) * (feats // 4) + at // 4, 1.0, 0.0).astype(jnp.bfloat16)
    for o in range(n_enc):
        segment = jnp.zeros((1, BLOCK), jnp.float32)
        body = jnp.zeros((feats, BLOCK), jnp.float32)
        for owner, seg_of, tile in found:
            hit = owner == float(o)
            segment = segment + jnp.where(hit, seg_of, 0.0)
            body = body + jnp.where(hit, tile, 0.0)
        tail = jnp.where(extra == 0, 1.0, jnp.where(extra == 1, segment, 0.0))
        rows_t[:, o * BLOCK : (o + 1) * BLOCK] = jnp.concatenate(
            [body, tail, jnp.zeros((LANES - APAD, BLOCK), jnp.float32)], axis=0
        )
    picked = mm(order, rows_t[:feats].astype(jnp.bfloat16))
    spread = mm(gram_ref[...], picked.astype(jnp.bfloat16))
    variance = jnp.sum((spread[:feats] + spread[feats:]) * picked, axis=0, keepdims=True)
    rows_t[:feats] = picked * lax.rsqrt(jnp.maximum(variance, 0.0) + eps_norm)
    x_t = rows_t[...]
    x_t_ref[...] = x_t[:APAD].astype(jnp.bfloat16)
    x_ref[...] = x_t.T.astype(jnp.bfloat16)
    group_t = lax.broadcasted_iota(jnp.int32, (LANES, rows), 0).astype(jnp.float32)
    key_mask_ref[...] = jnp.where(x_t[feats + 1 : feats + 2] == group_t, 0.0, 1.0).astype(jnp.bfloat16)
    group = lax.broadcasted_iota(jnp.int32, (BLOCK, LANES), 1).astype(jnp.float32)
    for core in range(2):
        rows_ref, mask_ref = row_refs[2 * core : 2 * core + 2]
        own = rows_t[:, pl.ds(pl.multiple_of((mine ^ core) * BLOCK, BLOCK), BLOCK)].T
        rows_ref[...] = own.astype(jnp.bfloat16)
        mask_ref[...] = jnp.where(own[:, feats + 1 : feats + 2] == group, -FAR, 0.0).astype(jnp.bfloat16)
    head_dim = q_gain_ref.shape[1]
    gain_ref[...] = q_gain_ref[...] * k_gain_ref[...] * (head_dim**-0.5 * math.log2(math.e))


def attend_heads(folds, place, x_t_ref, x_ref, key_mask_ref, gain_ref, own_ref, own_mask_ref):
    folds = list(folds)
    heads = range(len(folds))
    feats = (folds[0].shape[0] - TAIL) // 3
    tails = jnp.concatenate([fold[3 * feats :].astype(jnp.float32) for fold in folds], axis=1)
    row = lax.broadcasted_iota(jnp.int32, tails.shape, 0)

    def side(part):
        body = jnp.concatenate([fold[part * feats : (part + 1) * feats] for fold in folds], axis=1)
        shift = jnp.where(row == 0, tails[part : part + 1], 0.0).astype(jnp.bfloat16)
        return jnp.concatenate([body, shift], axis=0)

    def of(i):
        return slice(i * LANES, (i + 1) * LANES)

    keys = mm(side(1), x_t_ref[...], ((0,), (0,)))
    queries = mm(own_ref[:, :APAD], side(0))
    values = mm(x_ref[:, :APAD], side(2)).astype(jnp.bfloat16)
    gain, own_mask, key_mask = gain_ref[...], own_mask_ref[...], key_mask_ref[...]
    left, right = [], []
    for i in heads:
        key = keys[of(i)]
        square = jnp.sum(key * key, axis=0, keepdims=True) / LANES
        key = (key * lax.rsqrt(square + eps_norm)).astype(jnp.bfloat16)
        right.append(jnp.concatenate([key, key_mask], axis=0))
        query = queries[:, of(i)]
        square = jnp.sum(query * query, axis=1, keepdims=True) / LANES
        query = (query * lax.rsqrt(square + eps_norm) * gain).astype(jnp.bfloat16)
        left.append(jnp.concatenate([query, own_mask], axis=1))
    scores = [mm(left[i], right[i]) for i in heads]
    weights = [jnp.exp2(score).astype(jnp.bfloat16) for score in scores]
    ones = jnp.ones((values.shape[0], LANES), jnp.bfloat16)
    mixed = [mm(weights[i], jnp.concatenate([values[:, of(i)], ones], axis=1)) for i in heads]
    for i in heads:
        place(i, (mixed[i][:, :LANES] / mixed[i][:, LANES:]).astype(jnp.bfloat16))


def each_head(refs):
    for ref in refs:
        if len(ref.shape) == 2:
            yield ref[...]
        else:
            for i in range(ref.shape[0]):
                yield ref[i]


def attend_kernel(count, *refs):
    folds, out_ref = refs[6 : 6 + count], refs[-1]

    def place(i, result):
        out_ref[:, i * LANES : (i + 1) * LANES] = result

    attend_heads(each_head(folds), place, *refs[:6])


def output_kernel(heads, neighbours, lists, kinds, *refs):
    out_ref, sems = refs[-2:]
    mine, slot = lax.axis_index("enc"), lax.axis_index("seq") & (heads - 1)
    copies = []

    def put(ref, at, base, far, k):
        head = (base ^ far) * heads + (slot ^ k)
        column = pl.ds(pl.multiple_of(head * LANES, LANES), LANES)
        result = ref.at[:, at * LANES : (at + 1) * LANES]
        copies.append(pltpu.make_async_copy(result, out_ref.at[0, :, column], sems.at[len(copies)]))
        copies[-1].start()

    for ref, (other, early) in zip(refs, kinds):
        base = mine ^ other
        if early:
            for at, partner in enumerate(((0, 0), *neighbours)):
                put(ref, at, base, *partner)
        else:
            for i, pair in enumerate(zip(*lists)):
                far, k = (jnp.where(base & 1 == 0, zero, one) for zero, one in zip(*pair))
                put(ref, 2 * i, base, far, k)
                put(ref, 2 * i + 1, base, far ^ 1, k)
    for copy in copies:
        copy.wait()


def vmem(count):
    return [pl.BlockSpec(memory_space=pltpu.VMEM)] * count


def hbm(count):
    return [pl.BlockSpec(memory_space=pltpu.HBM)] * count


def in_hbm(x):
    return pltpu.with_memory_space_constraint(x, pltpu.HBM)


def after(count):
    return [pl.BlockSpec(memory_space=pl.ANY)] * count


def call(kernel, ins, out_shape, scratch=(), cost=(1_000_000, 1_000_000)):
    return pl.pallas_call(
        kernel,
        in_specs=ins,
        out_specs=[pl.BlockSpec(memory_space=pltpu.VMEM)] * len(out_shape),
        out_shape=out_shape,
        scratch_shapes=list(scratch),
        compiler_params=pltpu.CompilerParams(vmem_limit_bytes=VMEM_LIMIT),
        cost_estimate=pl.CostEstimate(flops=cost[0], bytes_accessed=cost[1], transcendentals=0),
    )


def gate(x, *others):
    return pl.pallas_call(
        gate_kernel,
        in_specs=after(1 + len(others)),
        out_specs=after(1)[0],
        out_shape=jax.ShapeDtypeStruct(x.shape, x.dtype),
        input_output_aliases={0: 0},
        compiler_params=pltpu.CompilerParams(vmem_limit_bytes=VMEM_LIMIT),
    )(x, *others)


def exchange(x, axis, n, k):
    return lax.ppermute(x, axis, [(i, i ^ k) for i in range(n)])


def on_device(
    n_enc,
    n_seq,
    clip_features,
    clip_shape,
    packing,
    conv_weight,
    embed_weight,
    mod_shift,
    mod_scale,
    qkv_weight,
    q_gain,
    k_gain,
):
    caps = clip_features.shape[2:5]
    depth_all = clip_features.shape[5]
    cols = qkv_weight.shape[2]
    feats = embed_weight.shape[0]
    heads = cols // LANES
    rows = n_enc * BLOCK
    bf16, f32 = jnp.bfloat16, jnp.float32

    def folds(dtype, *lead):
        return jax.ShapeDtypeStruct((*lead, 3 * feats + TAIL, LANES), dtype)

    evens = [0]
    for bit in reversed(range(1, log2(n_enc))):
        evens += [at ^ (1 << bit) for at in evens]
    scale_rows, shift_rows = mod_scale.reshape(-1, LANES), mod_shift.reshape(-1, LANES)
    later = [
        clip_features.reshape(-1, depth_all),
        conv_weight.reshape(-1, depth_all),
        q_gain.reshape(1, -1),
        k_gain.reshape(1, -1),
    ]
    with jax.named_scope("fold"):
        embed, features, conv, q_gain, k_gain, keep, *sends = call(
            functools.partial(fold_kernel, len(later)),
            hbm(4 + len(later)),
            [jax.ShapeDtypeStruct(x.shape, x.dtype) for x in (embed_weight, *later)]
            + [folds(f32)]
            + [folds(bf16)] * max(heads - 1, 1),
            [
                pltpu.VMEM(scale_rows.shape, f32),
                pltpu.VMEM(shift_rows.shape, f32),
                pltpu.VMEM(qkv_weight.shape, bf16),
                pltpu.SemaphoreType.DMA((4 + len(later),)),
            ],
            cost=(200_000_000, 1_000_000),
        )(*map(in_hbm, (embed_weight, scale_rows, shift_rows, qkv_weight, *later)))

    with jax.named_scope("encode"):
        own_block = call(
            functools.partial(encode_kernel, caps),
            hbm(2) + vmem(2),
            [jax.ShapeDtypeStruct((TOKEN_MESSAGE, BLOCK), bf16)],
            [
                pltpu.SMEM(clip_shape.shape, jnp.int32),
                pltpu.SMEM(packing.shape, jnp.int32),
                pltpu.SemaphoreType.DMA((2,)),
            ],
            cost=(500_000_000, 2_000_000),
        )(in_hbm(clip_shape), in_hbm(packing), features, conv)[0]

    def add(keep, got, first):
        kernel = functools.partial(add_kernel, len(got))
        return call(kernel, vmem(1 + len(got)) + after(1), [folds(f32), folds(bf16)])(keep, *got, first)

    with jax.named_scope("fold_sum"):
        if heads > 1:
            got = [exchange(sends[k - 1], "seq", n_seq, k) for k in reversed(range(1, heads))]
            keep, send = add(keep, got, own_block)
        else:
            send = sends[0]

    with jax.named_scope("tokens"):
        blocks = [own_block] + [exchange(own_block, "enc", n_enc, k) for k in evens[1:]]

    with jax.named_scope("gram"):
        gram = call(gram_kernel, vmem(1) + after(1), [jax.ShapeDtypeStruct((2 * feats, feats), bf16)])(embed, keep)[0]

    with jax.named_scope("pack"):
        cut = jax.ShapeDtypeStruct((NBS * TOKEN_ROWS, BLOCK), bf16)
        near_blocks = [
            exchange(call(cut_kernel, vmem(1) + after(1), [cut])(block, keep)[0], "enc", n_enc, 1) for block in blocks
        ]
        *shared, own_rows, own_mask, far_rows, far_mask = call(
            functools.partial(pack_kernel, tuple(evens), feats),
            vmem(3 + 2 * len(evens)),
            [
                jax.ShapeDtypeStruct((APAD, rows), bf16),
                jax.ShapeDtypeStruct((rows, LANES), bf16),
                jax.ShapeDtypeStruct((LANES, rows), bf16),
                jax.ShapeDtypeStruct((1, LANES), f32),
            ]
            + [jax.ShapeDtypeStruct((BLOCK, LANES), bf16)] * 4,
            [pltpu.VMEM((LANES, rows), f32)],
        )(q_gain, k_gain, gram, *blocks, *near_blocks)

    with jax.named_scope("fold_sum"):
        for bit in range(log2(heads), log2(n_seq)):
            got = exchange(send, "seq", n_seq, 1 << bit)
            if bit + 1 < log2(n_seq):
                keep, send = add(keep, [got], own_block)
            else:
                (fresh,) = call(last_add_kernel, vmem(2) + after(1), [folds(bf16)])(keep, got, own_rows)

    partners = [(far, k) for far in evens for k in range(heads) if far or k]
    partners.sort(key=lambda p: (p[0].bit_count() + p[1].bit_count(), p[0]))
    near_count = min(3, len(partners))
    half = (len(partners) - near_count) // 2
    assert len(partners) == near_count + 2 * half
    neighbours = tuple(partners[:near_count])
    lists = (tuple(partners[near_count : near_count + half]), tuple(partners[near_count + half :]))

    def spread(x, partner_of):
        pairs = []
        for e in range(n_enc):
            far, k = partner_of[e & 1]
            pairs += [(e * n_seq + i, (e ^ far) * n_seq + (i ^ k)) for i in range(n_seq)]
        return lax.ppermute(x, ("enc", "seq"), pairs)

    with jax.named_scope("gather"):
        singles = [spread(fresh, (partner, partner)) for partner in neighbours]
        swapped = exchange(fresh, "enc", n_enc, 1)
        pair = call(pair_kernel, vmem(2), [folds(bf16, 2)])(fresh, swapped)[0]
        got = [spread(pair, partner_of) for partner_of in zip(*lists)]

    def attend(rows_here, groups, first=()):
        count = sum(group.size for group in groups) // ((3 * feats + TAIL) * LANES)
        return call(
            functools.partial(attend_kernel, len(groups)),
            vmem(6 + len(groups)) + after(len(first)),
            [jax.ShapeDtypeStruct((BLOCK, count * LANES), bf16)],
            cost=(count * 200_000_000, 1_000_000),
        )(*shared, *rows_here, *groups, *first)[0]

    def write(kinds, results, out):
        olds = [] if out is None else [in_hbm(out)]
        return pl.pallas_call(
            functools.partial(output_kernel, heads, neighbours, lists, kinds),
            in_specs=vmem(len(results)) + hbm(len(olds)),
            out_specs=hbm(1)[0],
            out_shape=jax.ShapeDtypeStruct((1, BLOCK, n_enc * cols), bf16),
            scratch_shapes=[pltpu.SemaphoreType.DMA((n_enc * heads,))],
            input_output_aliases={len(results): 0} if olds else {},
            compiler_params=pltpu.CompilerParams(vmem_limit_bytes=VMEM_LIMIT),
        )(*results, *olds)

    with jax.named_scope("attend"):
        own, other = (own_rows, own_mask), (far_rows, far_mask)
        early, rest = [fresh, *singles], got
        early_other = attend(other, early)
        early_own = attend(own, early, [early_other])
        near_early = exchange(gate(early_other, early_own), "enc", n_enc, 1)
        out = write(((0, 1),), (early_own,), None)
        near_rest = exchange(attend(other, rest, [in_hbm(out)]), "enc", n_enc, 1)
        rest_own = attend(own, rest)
        return write(((1, 1), (1, 0), (0, 0)), (near_early, near_rest, rest_own), out)


def solution(mesh):
    return jax.shard_map(
        functools.partial(on_device, mesh.shape["enc"], mesh.shape["seq"]),
        mesh=mesh,
        in_specs=(
            P("enc", "seq", None, None, None, None),
            P("enc", "seq", None),
            P("enc", "seq", None, None),
            P(),
            P(),
            P(),
            P(),
            P(None, "seq", "enc"),
            P(),
            P(),
        ),
        out_specs=P("seq", "enc", None),
        check_vma=False,
    )
```

```python
import functools
import math

import jax
import jax.numpy as jnp
from jax import lax
from jax.experimental import pallas as pl
from jax.experimental.pallas import tpu as pltpu
from jax.sharding import PartitionSpec as P

BLOCK = 128
NBS = 2
LANES = 128
APAD = 72
TAIL = 8
TOKEN_ROWS = 80
TOKEN_MESSAGE = 208
eps_norm = 1e-06
FAR = 2.0**20
VMEM_LIMIT = 48 * 1024 * 1024


def mm(a, b, dims=((1,), (0,)), precision=None):
    return lax.dot_general(a, b, (dims, ((), ())), preferred_element_type=jnp.float32, precision=precision)


def split_bf16(x):
    hi = x.astype(jnp.bfloat16)
    return hi, (x - hi.astype(jnp.float32)).astype(jnp.bfloat16)


def log2(n):
    bits = n.bit_length() - 1
    assert 1 << bits == n
    return bits


def fetch(pairs, sems):
    copies = [pltpu.make_async_copy(src, dst, sems.at[i]) for i, (src, dst) in enumerate(pairs)]
    for copy in copies:
        copy.start()
    return copies


def fold_kernel(count, embed_hbm, scale_hbm, shift_hbm, w_hbm, *refs):
    later_hbm, embed_ref, later, keep_ref, sends = refs[:count], refs[count], refs[count + 1 : 2 * count + 1], refs[2 * count + 1], refs[2 * count + 2 : -4]
    scale_ref, shift_ref, w_ref, sems = refs[-4:]
    copies = fetch(
        [(embed_hbm, embed_ref), (scale_hbm, scale_ref), (shift_hbm, shift_ref), (w_hbm, w_ref)]
        + list(zip(later_hbm, later)),
        sems,
    )
    me = lax.axis_index("seq")
    _, depth, cols = w_ref.shape
    feats = embed_ref.shape[0]
    heads = cols // LANES
    for copy in copies[:3]:
        copy.wait()
    mean = jnp.sum(embed_ref[...].astype(jnp.float32), axis=1, keepdims=True) / embed_ref.shape[1]
    span = max(depth, LANES)
    chunks = span // LANES
    first = (me * depth) // LANES
    emb = embed_ref[:, pl.ds(pl.multiple_of(first * LANES, LANES), span)].astype(jnp.float32) - mean
    scale = jnp.concatenate([scale_ref[pl.ds(first + i, 1), :] for i in range(chunks)], axis=1)
    shift = jnp.concatenate([shift_ref[pl.ds(first + i, 1), :] for i in range(chunks)], axis=1)
    left = jnp.concatenate(
        [emb * (1.0 + scale), shift, jnp.zeros((APAD - feats - 1, span), jnp.float32)], axis=0
    )
    if depth < LANES:
        low = me * depth - first * LANES
        lane = lax.broadcasted_iota(jnp.int32, left.shape, 1)
        left = jnp.where((lane >= low) & (lane < low + depth), left, 0.0)
    hi, lo = split_bf16(left)
    both = jnp.concatenate([hi, lo], axis=0)
    copies[3].wait()

    def product(head):
        start = pl.multiple_of(head * LANES, LANES)
        right = jnp.concatenate([w_ref[part, :, pl.ds(start, LANES)] for part in range(3)], axis=1)
        right = jnp.concatenate([right] * (span // depth), axis=0)
        total = mm(both, right)
        total = total[:APAD] + total[APAD:]
        parts = [total[:, part * LANES : (part + 1) * LANES] for part in range(3)]
        row = lax.broadcasted_iota(jnp.int32, (TAIL, LANES), 0)
        tail = jnp.zeros((TAIL, LANES), jnp.float32)
        for part in range(3):
            tail = jnp.where(row == part, parts[part][feats : feats + 1], tail)
        return jnp.concatenate([part[:feats] for part in parts] + [tail], axis=0)

    slot = me & (heads - 1)
    for k in range(1, heads):
        sends[k - 1][...] = product(slot ^ k).astype(jnp.bfloat16)
    total = product(slot)
    keep_ref[...] = total
    if heads == 1:
        sends[0][...] = total.astype(jnp.bfloat16)
    for copy in copies[4:]:
        copy.wait()


def add_kernel(count, keep_in, *refs):
    total = keep_in[...]
    for ref in refs[:count]:
        total = total + ref[...].astype(jnp.float32)
    refs[-2][...] = total
    refs[-1][...] = total.astype(jnp.bfloat16)


def last_add_kernel(count, keep_in, got_ref, *refs):
    total = (keep_in[...] + got_ref[...].astype(jnp.float32)).astype(jnp.bfloat16)
    out_ref, swap_ref = refs[-2:]
    out_ref[...] = total
    swap_ref[0] = total
    for i in range(count):
        block = refs[i][...][: NBS * TOKEN_ROWS]
        rest = jnp.zeros((total.shape[0] - block.shape[0], LANES), jnp.bfloat16)
        swap_ref[1 + i] = jnp.concatenate([block, rest], axis=0)


def pair_kernel(own_ref, swapped_ref, out_ref):
    out_ref[0] = own_ref[...]
    out_ref[1] = swapped_ref[0]


def gate_kernel(*refs):
    pass


def encode_kernel(caps, shape_hbm, plan_hbm, feat_ref, conv_ref, out_ref, shape_ref, plan_ref, sems):
    copies = fetch([(shape_hbm, shape_ref), (plan_hbm, plan_ref)], sems)
    frames_cap, height_cap, width_cap = caps
    spots = frames_cap * height_cap * width_cap
    frame_size = height_cap * width_cap
    latent_ch = conv_ref.shape[0] // 27
    feats = 4 * latent_ch
    taps = mm(conv_ref[...], feat_ref[...], ((1,), (1,)))
    copies[0].wait()
    copies[1].wait()
    frames, height, width = shape_ref[0, 0, 0], shape_ref[0, 0, 1], shape_ref[0, 0, 2]
    spot = lax.broadcasted_iota(jnp.int32, (1, spots), 1)
    frame_ix = spot // frame_size
    row_ix = (spot % frame_size) // width_cap
    col_ix = spot % width_cap
    inside = (frame_ix < frames) & (row_ix < height) & (col_ix < width)
    taps = jnp.where(inside, taps, 0.0)

    def tap(a, b, j):
        at = (9 * a + 3 * b + j) * latent_ch
        return taps[at : at + latent_ch]

    def later(x, by):
        zeros = jnp.zeros((latent_ch, by * frame_size), jnp.float32)
        return jnp.concatenate([zeros, x[:, : spots - by * frame_size]], axis=1)

    def over_frames(b, j):
        return tap(2, b, j) + later(tap(1, b, j), 1) + later(tap(0, b, j), 2)

    def over_rows(j):
        above = pltpu.roll(over_frames(0, j), width_cap, 1)
        below = pltpu.roll(over_frames(2, j), spots - width_cap, 1)
        return (
            over_frames(1, j)
            + jnp.where(row_ix >= 1, above, 0.0)
            + jnp.where(row_ix < height_cap - 1, below, 0.0)
        )

    latent = (
        over_rows(1)
        + jnp.where(col_ix >= 1, pltpu.roll(over_rows(0), 1, 1), 0.0)
        + jnp.where(col_ix < width_cap - 1, pltpu.roll(over_rows(2), spots - 1, 1), 0.0)
    )
    latent = latent.astype(jnp.bfloat16).astype(jnp.float32)
    shifted = [latent] + [pltpu.roll(latent, spots - by, 1) for by in (1, width_cap, width_cap + 1)]
    patches = jnp.concatenate(shifted, axis=0).astype(jnp.bfloat16)

    tokens = NBS * BLOCK
    half_w = (width // 2).astype(jnp.float32)
    per_frame_int = (height // 2) * (width // 2)
    per_frame = per_frame_int.astype(jnp.float32)
    live = frames * per_frame_int
    token_int = lax.broadcasted_iota(jnp.int32, (1, tokens), 1)
    token = token_int.astype(jnp.float32)
    frame_of = jnp.floor((token + 0.5) / jnp.full((1, tokens), per_frame))
    within = token - frame_of * per_frame
    row_of = jnp.floor((within + 0.5) / jnp.full((1, tokens), half_w))
    col_of = within - row_of * half_w
    source = (frame_of * frame_size + row_of * (2 * width_cap) + col_of * 2).astype(jnp.int32)
    source = jnp.where(token_int < live, source, -1)
    chosen = lax.broadcasted_iota(jnp.int32, (spots, tokens), 0) == source
    picked = mm(patches, jnp.where(chosen, 1.0, 0.0).astype(jnp.bfloat16))
    kind = lax.broadcasted_iota(jnp.int32, (TOKEN_ROWS - feats, BLOCK), 0)
    pieces = []
    for b in range(NBS):
        count = jnp.clip(live - b * BLOCK, 0, BLOCK)
        info = jnp.where(
            kind == 0,
            plan_ref[0, 0, b, 0],
            jnp.where(kind == 1, plan_ref[0, 0, b, 1], jnp.where(kind == 2, count, 0)),
        )
        pieces += [picked[:, b * BLOCK : (b + 1) * BLOCK], info.astype(jnp.float32)]
    rest = out_ref.shape[0] - NBS * TOKEN_ROWS
    if rest > 0:
        pieces.append(jnp.zeros((rest, BLOCK), jnp.float32))
    out_ref[...] = jnp.concatenate(pieces, axis=0).astype(jnp.bfloat16)


def gram_kernel(embed_ref, first_ref, out_ref):
    feats, width = embed_ref.shape
    emb = embed_ref[...].astype(jnp.float32)
    emb = emb - jnp.sum(emb, axis=1, keepdims=True) / width
    both = jnp.concatenate(split_bf16(emb), axis=0)
    gram = mm(both, both, ((1,), (1,))) / width
    gram = gram[:feats] + gram[feats:]
    out_ref[...] = jnp.concatenate(split_bf16(gram[:, :feats] + gram[:, feats:]), axis=0)


def pack_kernel(evens, feats, q_gain_ref, k_gain_ref, gram_ref, *refs):
    here, near = refs[: len(evens)], refs[len(evens)]
    x_t_ref, x_ref, key_mask_ref, gain_ref, *row_refs, rows_t = refs[len(evens) + 1 :]
    n_enc = 2 * len(evens)
    mine = lax.axis_index("enc")
    rows = n_enc * BLOCK
    lane = lax.broadcasted_iota(jnp.int32, (1, BLOCK), 1).astype(jnp.float32)
    extra = lax.broadcasted_iota(jnp.int32, (APAD - feats, BLOCK), 0)
    found = []
    blocks = [(at, here[i][...]) for i, at in enumerate(evens)]
    blocks += [(at ^ 1, near[1 + i]) for i, at in enumerate(evens)]
    for distance, block in blocks:
        source = mine ^ distance
        for b in range(NBS):
            tile = block.astype(jnp.float32)[b * TOKEN_ROWS : (b + 1) * TOKEN_ROWS]
            owner, offset, count = (tile[feats + i : feats + i + 1] for i in range(3))
            owner = jnp.where(offset == 0.0, owner, -1.0)
            segment = jnp.where(lane < count, (source + 1).astype(jnp.float32), 0.0)
            found.append((owner, segment, tile[:feats]))
    at = lax.broadcasted_iota(jnp.int32, (feats, feats), 0)
    frm = lax.broadcasted_iota(jnp.int32, (feats, feats), 1)
    order = jnp.where(frm == (at % 4) * (feats // 4) + at // 4, 1.0, 0.0).astype(jnp.bfloat16)
    for o in range(n_enc):
        segment = jnp.zeros((1, BLOCK), jnp.float32)
        body = jnp.zeros((feats, BLOCK), jnp.float32)
        for owner, seg_of, tile in found:
            hit = owner == float(o)
            segment = segment + jnp.where(hit, seg_of, 0.0)
            body = body + jnp.where(hit, tile, 0.0)
        tail = jnp.where(extra == 0, 1.0, jnp.where(extra == 1, segment, 0.0))
        rows_t[:, o * BLOCK : (o + 1) * BLOCK] = jnp.concatenate(
            [body, tail, jnp.zeros((LANES - APAD, BLOCK), jnp.float32)], axis=0
        )
    picked = mm(order, rows_t[:feats].astype(jnp.bfloat16))
    spread = mm(gram_ref[...], picked.astype(jnp.bfloat16))
    variance = jnp.sum((spread[:feats] + spread[feats:]) * picked, axis=0, keepdims=True)
    rows_t[:feats] = picked * lax.rsqrt(jnp.maximum(variance, 0.0) + eps_norm)
    x_t = rows_t[...]
    x_t_ref[...] = x_t[:APAD].astype(jnp.bfloat16)
    x_ref[...] = x_t.T.astype(jnp.bfloat16)
    group_t = lax.broadcasted_iota(jnp.int32, (LANES, rows), 0).astype(jnp.float32)
    key_mask_ref[...] = jnp.where(x_t[feats + 1 : feats + 2] == group_t, 0.0, 1.0).astype(jnp.bfloat16)
    group = lax.broadcasted_iota(jnp.int32, (BLOCK, LANES), 1).astype(jnp.float32)
    for core in range(2):
        rows_ref, mask_ref = row_refs[2 * core : 2 * core + 2]
        own = rows_t[:, pl.ds(pl.multiple_of((mine ^ core) * BLOCK, BLOCK), BLOCK)].T
        rows_ref[...] = own.astype(jnp.bfloat16)
        mask_ref[...] = jnp.where(own[:, feats + 1 : feats + 2] == group, -FAR, 0.0).astype(jnp.bfloat16)
    head_dim = q_gain_ref.shape[1]
    gain_ref[...] = q_gain_ref[...] * k_gain_ref[...] * (head_dim**-0.5 * math.log2(math.e))


def attend_heads(folds, place, x_t_ref, x_ref, key_mask_ref, gain_ref, own_ref, own_mask_ref):
    folds = list(folds)
    heads = range(len(folds))
    feats = (folds[0].shape[0] - TAIL) // 3
    tails = jnp.concatenate([fold[3 * feats :].astype(jnp.float32) for fold in folds], axis=1)
    row = lax.broadcasted_iota(jnp.int32, tails.shape, 0)

    def side(part):
        body = jnp.concatenate([fold[part * feats : (part + 1) * feats] for fold in folds], axis=1)
        shift = jnp.where(row == 0, tails[part : part + 1], 0.0).astype(jnp.bfloat16)
        return jnp.concatenate([body, shift], axis=0)

    def of(i):
        return slice(i * LANES, (i + 1) * LANES)

    keys = mm(side(1), x_t_ref[...], ((0,), (0,)))
    queries = mm(own_ref[:, :APAD], side(0))
    values = mm(x_ref[:, :APAD], side(2)).astype(jnp.bfloat16)
    gain, own_mask, key_mask = gain_ref[...], own_mask_ref[...], key_mask_ref[...]
    left, right = [], []
    for i in heads:
        key = keys[of(i)]
        square = jnp.sum(key * key, axis=0, keepdims=True) / LANES
        key = (key * lax.rsqrt(square + eps_norm)).astype(jnp.bfloat16)
        right.append(jnp.concatenate([key, key_mask], axis=0))
        query = queries[:, of(i)]
        square = jnp.sum(query * query, axis=1, keepdims=True) / LANES
        query = (query * lax.rsqrt(square + eps_norm) * gain).astype(jnp.bfloat16)
        left.append(jnp.concatenate([query, own_mask], axis=1))
    scores = [mm(left[i], right[i]) for i in heads]
    weights = [jnp.exp2(score).astype(jnp.bfloat16) for score in scores]
    ones = jnp.ones((values.shape[0], LANES), jnp.bfloat16)
    mixed = [mm(weights[i], jnp.concatenate([values[:, of(i)], ones], axis=1)) for i in heads]
    for i in heads:
        place(i, (mixed[i][:, :LANES] / mixed[i][:, LANES:]).astype(jnp.bfloat16))


def each_head(refs):
    for ref in refs:
        if len(ref.shape) == 2:
            yield ref[...]
        else:
            for i in range(ref.shape[0]):
                yield ref[i]


def attend_kernel(count, *refs):
    folds, out_ref = refs[6 : 6 + count], refs[-1]

    def place(i, result):
        out_ref[:, i * LANES : (i + 1) * LANES] = result

    attend_heads(each_head(folds), place, *refs[:6])


def output_kernel(heads, neighbours, lists, near_early_ref, near_rest_ref, own_early_ref, own_rest_ref, out_ref, sems):
    mine, slot = lax.axis_index("enc"), lax.axis_index("seq") & (heads - 1)
    copies = []

    def put(ref, at, base, far, k):
        head = (base ^ far) * heads + (slot ^ k)
        column = pl.ds(pl.multiple_of(head * LANES, LANES), LANES)
        result = ref.at[:, at * LANES : (at + 1) * LANES]
        copies.append(pltpu.make_async_copy(result, out_ref.at[0, :, column], sems.at[len(copies)]))
        copies[-1].start()

    for early, rest, base in (
        (near_early_ref, near_rest_ref, mine ^ 1),
        (own_early_ref, own_rest_ref, mine),
    ):
        for at, partner in enumerate(((0, 0), *neighbours)):
            put(early, at, base, *partner)
        for i, pair in enumerate(zip(*lists)):
            far, k = (jnp.where(base & 1 == 0, zero, one) for zero, one in zip(*pair))
            put(rest, 2 * i, base, far, k)
            put(rest, 2 * i + 1, base, far ^ 1, k)
    for copy in copies:
        copy.wait()


def vmem(count):
    return [pl.BlockSpec(memory_space=pltpu.VMEM)] * count


def hbm(count):
    return [pl.BlockSpec(memory_space=pltpu.HBM)] * count


def in_hbm(x):
    return pltpu.with_memory_space_constraint(x, pltpu.HBM)


def after(count):
    return [pl.BlockSpec(memory_space=pl.ANY)] * count


def call(kernel, ins, out_shape, scratch=(), cost=(1_000_000, 1_000_000)):
    return pl.pallas_call(
        kernel,
        in_specs=ins,
        out_specs=[pl.BlockSpec(memory_space=pltpu.VMEM)] * len(out_shape),
        out_shape=out_shape,
        scratch_shapes=list(scratch),
        compiler_params=pltpu.CompilerParams(vmem_limit_bytes=VMEM_LIMIT),
        cost_estimate=pl.CostEstimate(flops=cost[0], bytes_accessed=cost[1], transcendentals=0),
    )


def gate(x, *others):
    return pl.pallas_call(
        gate_kernel,
        in_specs=after(1 + len(others)),
        out_specs=after(1)[0],
        out_shape=jax.ShapeDtypeStruct(x.shape, x.dtype),
        input_output_aliases={0: 0},
        compiler_params=pltpu.CompilerParams(vmem_limit_bytes=VMEM_LIMIT),
    )(x, *others)


def exchange(x, axis, n, k):
    return lax.ppermute(x, axis, [(i, i ^ k) for i in range(n)])


def on_device(
    n_enc,
    n_seq,
    clip_features,
    clip_shape,
    packing,
    conv_weight,
    embed_weight,
    mod_shift,
    mod_scale,
    qkv_weight,
    q_gain,
    k_gain,
):
    caps = clip_features.shape[2:5]
    depth_all = clip_features.shape[5]
    cols = qkv_weight.shape[2]
    feats = embed_weight.shape[0]
    heads = cols // LANES
    rows = n_enc * BLOCK
    bf16, f32 = jnp.bfloat16, jnp.float32

    def folds(dtype, *lead):
        return jax.ShapeDtypeStruct((*lead, 3 * feats + TAIL, LANES), dtype)

    evens = [0]
    for bit in reversed(range(1, log2(n_enc))):
        evens += [at ^ (1 << bit) for at in evens]
    scale_rows, shift_rows = mod_scale.reshape(-1, LANES), mod_shift.reshape(-1, LANES)
    later = [
        clip_features.reshape(-1, depth_all),
        conv_weight.reshape(-1, depth_all),
        q_gain.reshape(1, -1),
        k_gain.reshape(1, -1),
    ]
    with jax.named_scope("fold"):
        embed, features, conv, q_gain, k_gain, keep, *sends = call(
            functools.partial(fold_kernel, len(later)),
            hbm(4 + len(later)),
            [jax.ShapeDtypeStruct(x.shape, x.dtype) for x in (embed_weight, *later)]
            + [folds(f32)]
            + [folds(bf16)] * max(heads - 1, 1),
            [
                pltpu.VMEM(scale_rows.shape, f32),
                pltpu.VMEM(shift_rows.shape, f32),
                pltpu.VMEM(qkv_weight.shape, bf16),
                pltpu.SemaphoreType.DMA((4 + len(later),)),
            ],
            cost=(200_000_000, 1_000_000),
        )(*map(in_hbm, (embed_weight, scale_rows, shift_rows, qkv_weight, *later)))

    with jax.named_scope("encode"):
        own_block = call(
            functools.partial(encode_kernel, caps),
            hbm(2) + vmem(2),
            [jax.ShapeDtypeStruct((TOKEN_MESSAGE, BLOCK), bf16)],
            [
                pltpu.SMEM(clip_shape.shape, jnp.int32),
                pltpu.SMEM(packing.shape, jnp.int32),
                pltpu.SemaphoreType.DMA((2,)),
            ],
            cost=(500_000_000, 2_000_000),
        )(in_hbm(clip_shape), in_hbm(packing), features, conv)[0]

    def add(keep, got, first):
        kernel = functools.partial(add_kernel, len(got))
        return call(kernel, vmem(1 + len(got)) + after(1), [folds(f32), folds(bf16)])(keep, *got, first)

    with jax.named_scope("fold_sum"):
        if heads > 1:
            got = [exchange(sends[k - 1], "seq", n_seq, k) for k in reversed(range(1, heads))]
            keep, send = add(keep, got, own_block)
        else:
            send = sends[0]

    with jax.named_scope("tokens"):
        blocks = [own_block] + [exchange(own_block, "enc", n_enc, k) for k in evens[1:]]

    with jax.named_scope("fold_sum"):
        for bit in range(log2(heads), log2(n_seq)):
            got = exchange(send, "seq", n_seq, 1 << bit)
            if bit + 1 < log2(n_seq):
                keep, send = add(keep, [got], own_block)
            else:
                fresh, swap = call(
                    functools.partial(last_add_kernel, len(blocks)),
                    vmem(2 + len(blocks)) + after(1),
                    [folds(bf16), folds(bf16, 1 + len(blocks))],
                )(keep, got, *blocks, keep)

    partners = [(far, k) for far in evens for k in range(heads) if far or k]
    partners.sort(key=lambda p: (p[0].bit_count() + p[1].bit_count(), p[0]))
    near_count = min(3, len(partners))
    half = (len(partners) - near_count) // 2
    assert len(partners) == near_count + 2 * half
    neighbours = tuple(partners[:near_count])
    lists = (tuple(partners[near_count : near_count + half]), tuple(partners[near_count + half :]))

    def spread(x, partner_of):
        pairs = []
        for e in range(n_enc):
            far, k = partner_of[e & 1]
            pairs += [(e * n_seq + i, (e ^ far) * n_seq + (i ^ k)) for i in range(n_seq)]
        return lax.ppermute(x, ("enc", "seq"), pairs)

    with jax.named_scope("gather"):
        sent = {partner: spread(fresh, (partner, partner)) for partner in (neighbours[0], *neighbours[:0:-1])}
        singles = [sent[partner] for partner in neighbours]
        swapped = exchange(swap, "enc", n_enc, 1)
        pair = call(pair_kernel, vmem(2), [folds(bf16, 2)])(fresh, swapped)[0]
        got = [spread(pair, partner_of) for partner_of in zip(*lists)]

    with jax.named_scope("gram"):
        gram = call(gram_kernel, vmem(1) + after(1), [jax.ShapeDtypeStruct((2 * feats, feats), bf16)])(embed, pair)[0]

    with jax.named_scope("pack"):
        *shared, own_rows, own_mask, far_rows, far_mask = call(
            functools.partial(pack_kernel, tuple(evens), feats),
            vmem(4 + len(evens)),
            [
                jax.ShapeDtypeStruct((APAD, rows), bf16),
                jax.ShapeDtypeStruct((rows, LANES), bf16),
                jax.ShapeDtypeStruct((LANES, rows), bf16),
                jax.ShapeDtypeStruct((1, LANES), f32),
            ]
            + [jax.ShapeDtypeStruct((BLOCK, LANES), bf16)] * 4,
            [pltpu.VMEM((LANES, rows), f32)],
        )(q_gain, k_gain, gram, *blocks, swapped)

    def attend(rows_here, groups, first=()):
        count = sum(group.size for group in groups) // ((3 * feats + TAIL) * LANES)
        return call(
            functools.partial(attend_kernel, len(groups)),
            vmem(6 + len(groups)) + after(len(first)),
            [jax.ShapeDtypeStruct((BLOCK, count * LANES), bf16)],
            cost=(count * 200_000_000, 1_000_000),
        )(*shared, *rows_here, *groups, *first)[0]

    with jax.named_scope("attend"):
        own, other = (own_rows, own_mask), (far_rows, far_mask)
        early, rest = [fresh, *singles], got
        early_other = attend(other, early)
        early_own = attend(own, early, [early_other])
        near_early = exchange(gate(early_other, early_own), "enc", n_enc, 1)
        near_rest = exchange(attend(other, rest, [early_own]), "enc", n_enc, 1)
        rest_own = attend(own, rest)
        return pl.pallas_call(
            functools.partial(output_kernel, heads, neighbours, lists),
            in_specs=vmem(4),
            out_specs=hbm(1)[0],
            out_shape=jax.ShapeDtypeStruct((1, BLOCK, n_enc * cols), bf16),
            scratch_shapes=[pltpu.SemaphoreType.DMA((n_enc * heads,))],
            compiler_params=pltpu.CompilerParams(vmem_limit_bytes=VMEM_LIMIT),
        )(near_early, near_rest, early_own, rest_own)


def solution(mesh):
    return jax.shard_map(
        functools.partial(on_device, mesh.shape["enc"], mesh.shape["seq"]),
        mesh=mesh,
        in_specs=(
            P("enc", "seq", None, None, None, None),
            P("enc", "seq", None),
            P("enc", "seq", None, None),
            P(),
            P(),
            P(),
            P(),
            P(None, "seq", "enc"),
            P(),
            P(),
        ),
        out_specs=P("seq", "enc", None),
        check_vma=False,
    )
```
